32 devices in a mesh: mem: 16 (over z, y, core), band: 2 (over x).
Axes of the slice: x: 2, y: 2, z: 4, core: 2. Of those that a mesh axis runs over, the one named last changes fastest.
Arguments:
- coeffs: float32 [16, 2, 2, 2, 640, 640], P('mem', None, None, None, 'band'), may hold values from -0.0390625 to 0.0390625
Outputs:
- ftle: float32 [2, 640, 1280], P(None, 'band')
The draws below stay inside these ranges and needn't reach their ends.
All inputs are finite; a program needn't handle non-finite values.
Results may differ from the reference program's by a relative error of at most 0.0001.
Values sent between devices are 32-bit elements; how exact they have to be, the bound alone decides.
No kernel may reach another device: no remote copies, remote signals or barrier semaphores. Data moves between devices by JAX's collectives and lax.ppermute only.
A program may use at most 64 MiB of HBM per device.

```python
import jax
import jax.numpy as jnp
from jax import lax

NLAT = 640
NLON = 1280
WAVES = 640
LEVELS = 2
STEPS = 1
MEMBERS = 16


def shard_levels(own_key, dims, split, smallest, high):
    factor_of, own = 1.0, jax.random.fold_in(own_key, 6)
    for dim, shards_of in split:
        heights = jnp.exp(jax.random.uniform(jax.random.fold_in(own, dim), (shards_of,), jnp.float32, smallest / len(split), high / len(split)))
        factor_of = factor_of * jnp.repeat(heights, dims[dim] // shards_of).reshape([-1 if axis == dim else 1 for axis in range(len(dims))])
    return factor_of


def scatter_about(stream_key, shape, deviation, reach, split=(), kind=jnp.bfloat16):
    entries = jax.random.normal(stream_key, shape, jnp.float32) * deviation
    if len(split) > 0:
        entries = shard_levels(stream_key, shape, split, -0.22, 0.18) * entries
    return jnp.clip(entries, min=-reach, max=reach).astype(kind)


def setup_inputs(seed: int = 0) -> dict:
    splits = jax.random.split(jax.random.key(seed), 2)
    return {
        "coeffs": scatter_about(splits[0], (MEMBERS, LEVELS, 2, 2, WAVES, NLAT), (0.175 * WAVES ** -0.5), 0.0390625, ((0, 16), (4, 2)), jnp.float32),
    }


def synthesize(spec):
    wave = spec[:, :, 0] + 1j * spec[:, :, 1]
    wave = jnp.swapaxes(wave, -1, -2)
    wave = jnp.pad(wave, ((0, 0), (0, 0), (0, 0), (0, NLON // 2 + 1 - WAVES)))
    field = jnp.fft.irfft(wave, n=NLON, axis=-1) * NLON
    return field.astype(jnp.float32)

def slope(extended, winds):
    center = extended[:, 1:-1]
    north = (extended[:, 2:] - extended[:, :-2]) * 0.5
    east = (jnp.roll(center, -1, 2) - jnp.roll(center, 1, 2)) * 0.5
    return -winds - (winds[0] * east + winds[1] * north)

def padded(field):
    return jnp.pad(field, ((0, 0), (1, 1), (0, 0)))

def tensor(extended):
    center = extended[:, 1:-1]
    north = (extended[:, 2:] - extended[:, :-2]) * 0.5
    east = (jnp.roll(center, -1, 2) - jnp.roll(center, 1, 2)) * 0.5
    g_xx = 1.0 + east[0]
    g_xy = north[0]
    g_yx = east[1]
    g_yy = 1.0 + north[1]
    return jnp.stack([g_xx * g_xx + g_yx * g_yx, g_xx * g_xy + g_yx * g_yy, g_xy * g_xy + g_yy * g_yy])

def member_tensor(spec):
    winds = synthesize(spec)
    result = []
    for level in range(LEVELS):
        flow = winds[level]
        shift = jnp.zeros_like(flow)
        for step in range(STEPS):
            first = slope(padded(shift), flow)
            second = slope(padded(shift + 0.5 * first), flow)
            third = slope(padded(shift + 0.5 * second), flow)
            fourth = slope(padded(shift + third), flow)
            shift = shift + (first + 2.0 * second + 2.0 * third + fourth) / 6.0
        result.append(tensor(padded(shift)))
    return jnp.stack(result)

def reference(coeffs):

    def add_member(total, spec):
        return (total + member_tensor(spec), None)
    start = jnp.zeros((LEVELS, 3, NLAT, NLON), jnp.float32)
    total, unused = lax.scan(add_member, start, coeffs)
    mean_tensor = total / MEMBERS
    first, cross, second = (mean_tensor[:, 0], mean_tensor[:, 1], mean_tensor[:, 2])
    half = (first + second) * 0.5
    differ = (first - second) * 0.5
    largest = half + jnp.sqrt(differ * differ + cross * cross)
    return jnp.log(largest + 1e-06) / (2.0 * STEPS)
```

```python
import functools
import math

import jax
import jax.numpy as jnp
import ml_dtypes
import numpy as np
from jax import lax
from jax.experimental import pallas as pl
from jax.experimental.pallas import tpu as pltpu
from jax.sharding import PartitionSpec as P

NLON = 1280
STEPS = 1
SUB = 8
LANE = 128
VMEM_LIMIT = 48 * 1024 * 1024


def padded(cells, sides, width):
    for axis, dim in sides:
        count = lax.axis_size(axis)
        ends = count - 1
        head = lax.slice_in_dim(cells, 0, width, axis=dim)
        tail = lax.slice_in_dim(cells, cells.shape[dim] - width, cells.shape[dim], axis=dim)
        cells = jnp.concatenate(
            [
                lax.ppermute(tail, axis, [(i, (i + 1) % count) for i in range(ends)]),
                cells,
                lax.ppermute(head, axis, [((i + 1) % count, i) for i in range(ends)]),
            ],
            axis=dim,
        )
    return cells


def slope(extended, winds):
    center = extended[:, 1:-1]
    north = (extended[:, 2:] - extended[:, :-2]) * 0.5
    east = (jnp.roll(center, -1, 2) - jnp.roll(center, 1, 2)) * 0.5
    return -winds - (winds[0] * east + winds[1] * north)


def rimmed(field):
    return padded(field, (("band", 1),), 1)


def tensor(extended):
    center = extended[:, 1:-1]
    north = (extended[:, 2:] - extended[:, :-2]) * 0.5
    east = (jnp.roll(center, -1, 2) - jnp.roll(center, 1, 2)) * 0.5
    g_xx = 1.0 + east[0]
    g_xy = north[0]
    g_yx = east[1]
    g_yy = 1.0 + north[1]
    return jnp.stack(
        [g_xx * g_xx + g_yx * g_yx, g_xx * g_xy + g_yx * g_yy, g_xy * g_xy + g_yy * g_yy]
    )


def integrate(shift, flow, extend):
    first = slope(extend(shift), flow)
    second = slope(extend(0.5 * first), flow)
    third = slope(extend(0.5 * second), flow)
    fourth = slope(extend(third), flow)
    return (first + 2.0 * second + 2.0 * third + fourth) / 6.0


def exponent_of(summed, members):
    mean = summed / members
    first, cross, second = (mean[..., 0, :, :], mean[..., 1, :, :], mean[..., 2, :, :])
    half = (first + second) * 0.5
    differ = (first - second) * 0.5
    largest = half + jnp.sqrt(differ * differ + cross * cross)
    return jnp.log(largest + 1e-06) / (2.0 * STEPS)


def by_rows(coeffs):
    spec = coeffs[0]
    levels = spec.shape[0]
    nlat = spec.shape[4]
    waves = spec.shape[3] * lax.axis_size("band")
    members = lax.axis_size("mem")
    stacked = spec.reshape(levels * 2, 2, spec.shape[3], nlat)
    wave_index = lax.iota(jnp.int32, waves)
    column = lax.iota(jnp.int32, NLON)
    phase = wave_index[:, None] * column[None, :] % NLON
    angle = phase.astype(jnp.float32) * (2.0 * math.pi / NLON)
    weight = jnp.where(wave_index == 0, 1.0, 2.0).astype(jnp.float32)[:, None]
    table = jnp.stack([weight * jnp.cos(angle), -weight * jnp.sin(angle)], axis=0)
    winds = jnp.einsum(
        "crwh,rwn->chn",
        lax.all_to_all(stacked, "band", split_axis=3, concat_axis=2, tiled=True),
        table,
        precision=lax.Precision.HIGHEST,
        preferred_element_type=jnp.float32,
    )
    height = winds.shape[1]
    winds = winds.reshape(levels, 2, height, NLON)
    partials = []
    for level in range(levels):
        flow = winds[level]
        shift = integrate(jnp.zeros_like(flow), flow, rimmed)
        partials.append(tensor(rimmed(shift)))
    summed = lax.psum_scatter(jnp.stack(partials), "mem", scatter_dimension=3, tiled=True)
    return lax.all_gather(exponent_of(summed, members), "mem", axis=2, tiled=True)


@functools.lru_cache(maxsize=None)
def wave_table(bands, waves_local):
    wave = np.arange(bands * waves_local, dtype=np.int64)
    phase = (wave[:, None] * np.arange(NLON, dtype=np.int64)[None, :]) % NLON
    angle = phase.astype(np.float64) * (2.0 * np.pi / NLON)
    weight = np.where(wave == 0, 1.0, 2.0)[:, None]
    table = np.stack([weight * np.cos(angle), -weight * np.sin(angle)])
    table = table.reshape(2, bands, waves_local, NLON).transpose(1, 0, 2, 3).reshape(-1, NLON)
    high = table.astype(ml_dtypes.bfloat16)
    low = (table - high.astype(np.float64)).astype(ml_dtypes.bfloat16)
    return high, low


class Window:
    def __init__(self, index, count, start, width, nlat):
        self.first = index == 0
        self.last = index == count - 1
        self.width = width
        self.extended = width + 2 * SUB
        low = 0 if self.first else start + SUB
        high = nlat if self.last else start + width + SUB
        self.rows = high - low
        self.row_at = (low, nlat - high)
        base_up, base_down = start - SUB, nlat - start - width - SUB
        self.place = (low - base_up, nlat - high - base_down)
        self.side = "own" if 2 * (start + width) <= nlat else "other" if 2 * start >= nlat else "both"


def plan(nlat, widths):
    starts = np.cumsum([0] + widths[:-1])
    return [Window(k, len(widths), int(starts[k]), widths[k], nlat) for k in range(len(widths))]


def choose(band, pair):
    return jnp.where(band == 0, pair[0], pair[1])


def transpose_kernel(which, spec_ref, out_ref):
    out_ref[0] = spec_ref[0, 0].T


def rows_first(spec, level):
    depth, nlat = spec.shape[2:]
    return pl.pallas_call(
        transpose_kernel,
        grid_spec=pltpu.PrefetchScalarGridSpec(
            num_scalar_prefetch=1,
            grid=(2, nlat // LANE),
            in_specs=[pl.BlockSpec((1, 1, depth, LANE), lambda c, t, which: (which[0], c, 0, t))],
            out_specs=pl.BlockSpec((1, LANE, depth), lambda c, t, which: (c, t, 0)),
        ),
        out_shape=jax.ShapeDtypeStruct((2, nlat, depth), jnp.float32),
        compiler_params=pltpu.CompilerParams(vmem_limit_bytes=VMEM_LIMIT),
        cost_estimate=pl.CostEstimate(
            flops=0, transcendentals=0, bytes_accessed=2 * 2 * nlat * depth * 4
        ),
        name="rows_first",
    )(level.reshape(1), spec)


def east_of(x):
    return pltpu.roll(x, NLON - 1, axis=1) - pltpu.roll(x, 1, axis=1)


def north_of(before, here, after):
    row = lax.broadcasted_iota(jnp.int32, here.shape, 0)
    above = jnp.where(row == SUB - 1, pltpu.roll(after, SUB - 1, axis=0), pltpu.roll(here, SUB - 1, axis=0))
    below = jnp.where(row == 0, pltpu.roll(before, 1, axis=0), pltpu.roll(here, 1, axis=0))
    return above - below


def window_kernel(window, depth, *refs):
    refs = list(refs)
    band_ref, local_ref, remote_ref, high_ref, low_ref = refs[:5]
    refs = refs[5:]
    carry_ref = None if window.first else refs.pop(0)
    tensor_ref = refs.pop(0)
    carried_ref = None if window.last else refs.pop(0)
    local_buf, lhs, lhs_high, lhs_low, wind, second, third, shift, sem = refs
    band = band_ref[0]
    rows, extended = window.rows, window.extended

    def at(pair):
        return pl.multiple_of(choose(band, pair).astype(jnp.int32), SUB)

    fetch = pltpu.make_async_copy(local_ref.at[:, pl.ds(at(window.row_at), rows)], local_buf, sem)
    fetch.start()
    for c in range(2):
        lhs[c * rows : (c + 1) * rows, pl.ds(pl.multiple_of((1 - band) * depth, LANE), depth)] = remote_ref[c]
    fetch.wait()
    for c in range(2):
        lhs[c * rows : (c + 1) * rows, pl.ds(pl.multiple_of(band * depth, LANE), depth)] = local_buf[c]
    lhs_high[...] = lhs[...].astype(jnp.bfloat16)
    lhs_low[...] = (lhs[...] - lhs_high[...].astype(jnp.float32)).astype(jnp.bfloat16)

    place = at(window.place)
    if window.first or window.last:
        for c in range(2):
            if window.first:
                wind[c, pl.ds(at((0, extended - SUB)), SUB), :] = jnp.zeros((SUB, NLON), jnp.float32)
            if window.last:
                wind[c, pl.ds(at((extended - SUB, 0)), SUB), :] = jnp.zeros((SUB, NLON), jnp.float32)
    if not window.first:
        for c in range(2):
            wind[c, pl.ds(at((0, extended - 2 * SUB)), 2 * SUB), :] = carry_ref[c]

    @pl.loop(0, NLON // 256)
    def _(tile):
        columns = pl.ds(pl.multiple_of(tile * 256, 256), 256)
        dot = functools.partial(jnp.dot, preferred_element_type=jnp.float32)
        total = dot(lhs_high[...], high_ref[:, columns])
        total += dot(lhs_low[...], high_ref[:, columns])
        total += dot(lhs_high[...], low_ref[:, columns])
        for c in range(2):
            wind[c, pl.ds(place, rows), columns] = total[c * rows : (c + 1) * rows]

    if not window.last:
        for c in range(2):
            carried_ref[c] = wind[c, pl.ds(at((extended - 2 * SUB, 0)), 2 * SUB), :]

    blocks = extended // SUB

    def rows_of(block):
        return pl.ds(pl.multiple_of(block * SUB, SUB), SUB)

    def derivatives(field, block):
        before, after = jnp.maximum(block - 1, 0), jnp.minimum(block + 1, blocks - 1)
        result = []
        for c in range(2):
            here = field[c, rows_of(block), :]
            result.append((east_of(here), north_of(field[c, rows_of(before), :], here, field[c, rows_of(after), :])))
        return result

    @pl.loop(0, blocks)
    def _(block):
        flow = [wind[c, rows_of(block), :] for c in range(2)]
        for c, (east, north) in enumerate(derivatives(wind, block)):
            second[c, rows_of(block), :] = 0.25 * (flow[0] * east + flow[1] * north) - flow[c]

    @pl.loop(0, blocks)
    def _(block):
        flow = [wind[c, rows_of(block), :] for c in range(2)]
        for c, (east, north) in enumerate(derivatives(second, block)):
            third[c, rows_of(block), :] = -flow[c] - 0.25 * (flow[0] * east + flow[1] * north)

    @pl.loop(0, blocks)
    def _(block):
        flow = [wind[c, rows_of(block), :] for c in range(2)]
        for c, (east, north) in enumerate(derivatives(third, block)):
            fourth = -flow[c] - 0.5 * (flow[0] * east + flow[1] * north)
            both = second[c, rows_of(block), :] + third[c, rows_of(block), :]
            shift[c, rows_of(block), :] = (2.0 * both + (fourth - flow[c])) * (1.0 / 6.0)

    @pl.loop(0, blocks - 2)
    def _(block):
        (e0, n0), (e1, n1) = derivatives(shift, block + 1)
        g_xx, g_xy, g_yx, g_yy = 1.0 + 0.5 * e0, 0.5 * n0, 0.5 * e1, 1.0 + 0.5 * n1
        tensor_ref[0, rows_of(block), :] = g_xx * g_xx + g_yx * g_yx
        tensor_ref[1, rows_of(block), :] = g_xx * g_xy + g_yx * g_yy
        tensor_ref[2, rows_of(block), :] = g_xy * g_xy + g_yy * g_yy


def window_tensor(window, band, local, remote, table, carry):
    depth = local.shape[2]
    vmem = pl.BlockSpec(memory_space=pltpu.VMEM)
    in_specs = [
        pl.BlockSpec(memory_space=pltpu.SMEM),
        pl.BlockSpec(memory_space=pl.ANY),
        vmem,
        vmem,
        vmem,
    ]
    operands = [band.reshape(1), local, remote, *table]
    if not window.first:
        in_specs.append(vmem)
        operands.append(carry)
    out_shape = [jax.ShapeDtypeStruct((3, window.width, NLON), jnp.float32)]
    if not window.last:
        out_shape.append(jax.ShapeDtypeStruct((2, 2 * SUB, NLON), jnp.float32))
    field = pltpu.VMEM((2, window.extended, NLON), jnp.float32)
    lhs_shape = (2 * window.rows, 2 * depth)
    out = pl.pallas_call(
        functools.partial(window_kernel, window, depth),
        out_shape=out_shape,
        in_specs=in_specs,
        out_specs=[vmem] * len(out_shape),
        scratch_shapes=[
            pltpu.VMEM((2, window.rows, depth), jnp.float32),
            pltpu.VMEM(lhs_shape, jnp.float32),
            pltpu.VMEM(lhs_shape, jnp.bfloat16),
            pltpu.VMEM(lhs_shape, jnp.bfloat16),
            field,
            field,
            field,
            field,
            pltpu.SemaphoreType.DMA,
        ],
        compiler_params=pltpu.CompilerParams(vmem_limit_bytes=VMEM_LIMIT),
        cost_estimate=pl.CostEstimate(
            flops=3 * 2 * lhs_shape[0] * lhs_shape[1] * NLON,
            transcendentals=0,
            bytes_accessed=4 * NLON * lhs_shape[1] + 8 * lhs_shape[0] * depth + 12 * window.width * NLON,
        ),
        name="window_tensor",
    )(*operands)
    return out[0], (None if window.last else out[1])


def by_levels(coeffs):
    spec = coeffs[0]
    levels, _, parts, waves_local, nlat = spec.shape
    members = lax.axis_size("mem")
    band = lax.axis_index("band").astype(jnp.int32)
    spec = spec.reshape(levels, 2, parts * waves_local, nlat)
    windows = plan(nlat, [LANE] * (nlat // LANE))
    table = [jnp.asarray(part) for part in wave_table(levels, waves_local)]
    swap = [(0, 1), (1, 0)]

    outgoing = rows_first(spec, 1 - band)
    remotes = []
    for window in windows:
        piece = lax.dynamic_slice_in_dim(outgoing, choose(1 - band, window.row_at), window.rows, axis=1)
        remotes.append(lax.ppermute(piece, "band", swap))
    local = rows_first(spec, band)

    carry = None
    pieces = {"own": [], "both": [], "other": []}
    for window, remote in zip(windows, remotes):
        partial_sum, carry = window_tensor(window, band, local, remote, table, carry)
        summed = lax.psum_scatter(partial_sum, "mem", scatter_dimension=1, tiled=True)
        pieces[window.side].append(exponent_of(summed, members))

    other = lax.ppermute(jnp.stack(pieces["other"]), "band", swap)
    half = members // 2
    trades = []
    for member in range(members):
        for side in range(2):
            keeps = (member < half) == (side == 0)
            mate = (member, side) if keeps else ((member + half) % members, 1 - side)
            trades.append((member * 2 + side, mate[0] * 2 + mate[1]))
    both = lax.ppermute(pieces["both"][0], ("mem", "band"), trades)

    def gathered(stack):
        count, height, _ = stack.shape
        whole = lax.all_gather(stack, "mem", axis=1, tiled=True)
        return whole.reshape(count, members * height, NLON)

    own = gathered(jnp.stack(pieces["own"]))
    late = gathered(jnp.concatenate([other, both[None]]))
    other, both = late[:-1], late[-1]
    middle = both.shape[0] // 2
    low, high = both[:middle], both[middle:]

    up = jnp.stack(
        [
            jnp.concatenate([*own, low]),
            jnp.concatenate([*other[::-1], high]),
        ]
    )
    down = jnp.stack(
        [
            jnp.concatenate([low, *other]),
            jnp.concatenate([high, *own[::-1]]),
        ]
    )
    return jnp.where(band == 0, up, down)


def per_device(coeffs):
    _, levels, _, _, _, nlat = coeffs.shape
    members = lax.axis_size("mem")
    rows = nlat // lax.axis_size("band")
    if levels == lax.axis_size("band") == 2 and LANE % (members * SUB) == 0 and nlat % (2 * LANE) == LANE and rows > LANE:
        return by_levels(coeffs)
    return by_rows(coeffs)


def solution(mesh):
    placed = (P("mem", None, None, None, "band", None),)
    return jax.shard_map(
        per_device, mesh=mesh, in_specs=placed, out_specs=P(None, "band", None), check_vma=False
    )
```

```python
import functools
import math

import jax
import jax.numpy as jnp
import ml_dtypes
import numpy as np
from jax import lax
from jax.experimental import pallas as pl
from jax.experimental.pallas import tpu as pltpu
from jax.sharding import PartitionSpec as P

NLON = 1280
STEPS = 1
SUB = 8
LANE = 128
VMEM_LIMIT = 24 * 1024 * 1024


def padded(cells, sides, width):
    for axis, dim in sides:
        count = lax.axis_size(axis)
        ends = count - 1
        head = lax.slice_in_dim(cells, 0, width, axis=dim)
        tail = lax.slice_in_dim(cells, cells.shape[dim] - width, cells.shape[dim], axis=dim)
        cells = jnp.concatenate(
            [
                lax.ppermute(tail, axis, [(i, (i + 1) % count) for i in range(ends)]),
                cells,
                lax.ppermute(head, axis, [((i + 1) % count, i) for i in range(ends)]),
            ],
            axis=dim,
        )
    return cells


def slope(extended, winds):
    center = extended[:, 1:-1]
    north = (extended[:, 2:] - extended[:, :-2]) * 0.5
    east = (jnp.roll(center, -1, 2) - jnp.roll(center, 1, 2)) * 0.5
    return -winds - (winds[0] * east + winds[1] * north)


def rimmed(field):
    return padded(field, (("band", 1),), 1)


def tensor(extended):
    center = extended[:, 1:-1]
    north = (extended[:, 2:] - extended[:, :-2]) * 0.5
    east = (jnp.roll(center, -1, 2) - jnp.roll(center, 1, 2)) * 0.5
    g_xx = 1.0 + east[0]
    g_xy = north[0]
    g_yx = east[1]
    g_yy = 1.0 + north[1]
    return jnp.stack(
        [g_xx * g_xx + g_yx * g_yx, g_xx * g_xy + g_yx * g_yy, g_xy * g_xy + g_yy * g_yy]
    )


def integrate(shift, flow, extend):
    first = slope(extend(shift), flow)
    second = slope(extend(0.5 * first), flow)
    third = slope(extend(0.5 * second), flow)
    fourth = slope(extend(third), flow)
    return (first + 2.0 * second + 2.0 * third + fourth) / 6.0


def exponent_of(summed, members):
    mean = summed / members
    first, cross, second = (mean[..., 0, :, :], mean[..., 1, :, :], mean[..., 2, :, :])
    half = (first + second) * 0.5
    differ = (first - second) * 0.5
    largest = half + jnp.sqrt(differ * differ + cross * cross)
    return jnp.log(largest + 1e-06) / (2.0 * STEPS)


def by_rows(coeffs):
    spec = coeffs[0]
    levels = spec.shape[0]
    nlat = spec.shape[4]
    waves = spec.shape[3] * lax.axis_size("band")
    members = lax.axis_size("mem")
    stacked = spec.reshape(levels * 2, 2, spec.shape[3], nlat)
    wave_index = lax.iota(jnp.int32, waves)
    column = lax.iota(jnp.int32, NLON)
    phase = wave_index[:, None] * column[None, :] % NLON
    angle = phase.astype(jnp.float32) * (2.0 * math.pi / NLON)
    weight = jnp.where(wave_index == 0, 1.0, 2.0).astype(jnp.float32)[:, None]
    table = jnp.stack([weight * jnp.cos(angle), -weight * jnp.sin(angle)], axis=0)
    winds = jnp.einsum(
        "crwh,rwn->chn",
        lax.all_to_all(stacked, "band", split_axis=3, concat_axis=2, tiled=True),
        table,
        precision=lax.Precision.HIGHEST,
        preferred_element_type=jnp.float32,
    )
    height = winds.shape[1]
    winds = winds.reshape(levels, 2, height, NLON)
    partials = []
    for level in range(levels):
        flow = winds[level]
        shift = integrate(jnp.zeros_like(flow), flow, rimmed)
        partials.append(tensor(rimmed(shift)))
    summed = lax.psum_scatter(jnp.stack(partials), "mem", scatter_dimension=3, tiled=True)
    return lax.all_gather(exponent_of(summed, members), "mem", axis=2, tiled=True)


@functools.lru_cache(maxsize=None)
def wave_table(bands, waves_local):
    wave = np.arange(bands * waves_local, dtype=np.int64)
    phase = (wave[:, None] * np.arange(NLON, dtype=np.int64)[None, :]) % NLON
    angle = phase.astype(np.float64) * (2.0 * np.pi / NLON)
    weight = np.where(wave == 0, 1.0, 2.0)[:, None]
    table = np.stack([weight * np.cos(angle), -weight * np.sin(angle)])
    table = table.reshape(2, bands, waves_local, NLON).transpose(1, 0, 2, 3).reshape(-1, NLON)
    high = table.astype(ml_dtypes.bfloat16)
    low = (table - high.astype(np.float64)).astype(ml_dtypes.bfloat16)
    return high, low


class Window:
    def __init__(self, index, count, start, width, nlat):
        self.first = index == 0
        self.last = index == count - 1
        self.width = width
        self.extended = width + 2 * SUB
        low = 0 if self.first else start + SUB
        high = nlat if self.last else start + width + SUB
        self.rows = high - low
        self.row_at = (low, nlat - high)
        base_up, base_down = start - SUB, nlat - start - width - SUB
        self.place = (low - base_up, nlat - high - base_down)
        self.side = "own" if 2 * (start + width) <= nlat else "other" if 2 * start >= nlat else "both"


def plan(nlat, widths):
    starts = np.cumsum([0] + widths[:-1])
    return [Window(k, len(widths), int(starts[k]), widths[k], nlat) for k in range(len(widths))]


def choose(band, pair):
    return jnp.where(band == 0, pair[0], pair[1])


def transpose_kernel(place, spec_ref, out_ref):
    out_ref[0] = spec_ref[0, 0].T


def rows_first(spec, level, block, width):
    depth = spec.shape[2]
    return pl.pallas_call(
        transpose_kernel,
        grid_spec=pltpu.PrefetchScalarGridSpec(
            num_scalar_prefetch=1,
            grid=(2, width // LANE),
            in_specs=[pl.BlockSpec((1, 1, depth, LANE), lambda c, t, place: (place[0], c, 0, place[1] + t))],
            out_specs=pl.BlockSpec((1, LANE, depth), lambda c, t, place: (c, t, 0)),
        ),
        out_shape=jax.ShapeDtypeStruct((2, width, depth), jnp.float32),
        compiler_params=pltpu.CompilerParams(vmem_limit_bytes=VMEM_LIMIT),
        cost_estimate=pl.CostEstimate(
            flops=0, transcendentals=0, bytes_accessed=8 * 2 * width * depth * 4
        ),
        name="rows_first",
    )(jnp.stack([level, jnp.asarray(block, jnp.int32)]), spec)


def east_of(x):
    return pltpu.roll(x, NLON - 1, axis=1) - pltpu.roll(x, 1, axis=1)


def north_of(before, here, after):
    row = lax.broadcasted_iota(jnp.int32, here.shape, 0)
    above = jnp.where(row == SUB - 1, pltpu.roll(after, SUB - 1, axis=0), pltpu.roll(here, SUB - 1, axis=0))
    below = jnp.where(row == 0, pltpu.roll(before, 1, axis=0), pltpu.roll(here, 1, axis=0))
    return above - below


def window_kernel(window, depth, *refs):
    refs = list(refs)
    place_ref, local_ref, remote_ref, high_ref, low_ref = refs[:5]
    refs = refs[5:]
    carry_ref = None if window.first else refs.pop(0)
    keep_ref, send_ref = refs.pop(0), refs.pop(0)
    carried_ref = None if window.last else refs.pop(0)
    local_buf, lhs, lhs_high, lhs_low, wind, second, third, shift, sem = refs
    band, core = place_ref[0], place_ref[1]
    rows, extended = window.rows, window.extended

    def at(pair):
        return pl.multiple_of(choose(band, pair).astype(jnp.int32), SUB)

    fetch = pltpu.make_async_copy(local_ref.at[:, pl.ds(at(window.row_at), rows)], local_buf, sem)
    fetch.start()
    for c in range(2):
        lhs[c * rows : (c + 1) * rows, pl.ds(pl.multiple_of((1 - band) * depth, LANE), depth)] = remote_ref[c]
    fetch.wait()
    for c in range(2):
        lhs[c * rows : (c + 1) * rows, pl.ds(pl.multiple_of(band * depth, LANE), depth)] = local_buf[c]
    lhs_high[...] = lhs[...].astype(jnp.bfloat16)
    lhs_low[...] = (lhs[...] - lhs_high[...].astype(jnp.float32)).astype(jnp.bfloat16)

    place = at(window.place)
    if window.first or window.last:
        for c in range(2):
            if window.first:
                wind[c, pl.ds(at((0, extended - SUB)), SUB), :] = jnp.zeros((SUB, NLON), jnp.float32)
            if window.last:
                wind[c, pl.ds(at((extended - SUB, 0)), SUB), :] = jnp.zeros((SUB, NLON), jnp.float32)
    if not window.first:
        for c in range(2):
            wind[c, pl.ds(at((0, extended - 2 * SUB)), 2 * SUB), :] = carry_ref[c]

    @pl.loop(0, NLON // 256)
    def _(tile):
        columns = pl.ds(pl.multiple_of(tile * 256, 256), 256)
        dot = functools.partial(jnp.dot, preferred_element_type=jnp.float32)
        total = dot(lhs_high[...], high_ref[:, columns])
        total += dot(lhs_low[...], high_ref[:, columns])
        total += dot(lhs_high[...], low_ref[:, columns])
        for c in range(2):
            wind[c, pl.ds(place, rows), columns] = total[c * rows : (c + 1) * rows]

    if not window.last:
        for c in range(2):
            carried_ref[c] = wind[c, pl.ds(at((extended - 2 * SUB, 0)), 2 * SUB), :]

    blocks = extended // SUB

    def rows_of(block):
        return pl.ds(pl.multiple_of(block * SUB, SUB), SUB)

    def derivatives(field, block):
        before, after = jnp.maximum(block - 1, 0), jnp.minimum(block + 1, blocks - 1)
        result = []
        for c in range(2):
            here = field[c, rows_of(block), :]
            result.append((east_of(here), north_of(field[c, rows_of(before), :], here, field[c, rows_of(after), :])))
        return result

    @pl.loop(0, blocks, unroll=3)
    def _(block):
        flow = [wind[c, rows_of(block), :] for c in range(2)]
        for c, (east, north) in enumerate(derivatives(wind, block)):
            second[c, rows_of(block), :] = 0.25 * (flow[0] * east + flow[1] * north) - flow[c]

    @pl.loop(0, blocks, unroll=3)
    def _(block):
        flow = [wind[c, rows_of(block), :] for c in range(2)]
        for c, (east, north) in enumerate(derivatives(second, block)):
            third[c, rows_of(block), :] = -flow[c] - 0.25 * (flow[0] * east + flow[1] * north)

    @pl.loop(0, blocks, unroll=3)
    def _(block):
        flow = [wind[c, rows_of(block), :] for c in range(2)]
        for c, (east, north) in enumerate(derivatives(third, block)):
            fourth = -flow[c] - 0.5 * (flow[0] * east + flow[1] * north)
            both = second[c, rows_of(block), :] + third[c, rows_of(block), :]
            shift[c, rows_of(block), :] = (2.0 * both + (fourth - flow[c])) * (1.0 / 6.0)

    half = window.width // 2 // SUB

    def entries(out_ref, base):
        @pl.loop(0, half, unroll=2)
        def _(block):
            (e0, n0), (e1, n1) = derivatives(shift, base + block + 1)
            g_xx, g_xy, g_yx, g_yy = 1.0 + 0.5 * e0, 0.5 * n0, 0.5 * e1, 1.0 + 0.5 * n1
            out_ref[0, rows_of(block), :] = g_xx * g_xx + g_yx * g_yx
            out_ref[1, rows_of(block), :] = g_xx * g_xy + g_yx * g_yy
            out_ref[2, rows_of(block), :] = g_xy * g_xy + g_yy * g_yy

    entries(keep_ref, core * half)
    entries(send_ref, (1 - core) * half)


def window_tensor(window, place, local, remote, table, carry):
    depth = local.shape[2]
    vmem = pl.BlockSpec(memory_space=pltpu.VMEM)
    in_specs = [
        pl.BlockSpec(memory_space=pltpu.SMEM),
        pl.BlockSpec(memory_space=pl.ANY),
        vmem,
        vmem,
        vmem,
    ]
    operands = [place, local, remote, *table]
    if not window.first:
        in_specs.append(vmem)
        operands.append(carry)
    out_shape = [jax.ShapeDtypeStruct((3, window.width // 2, NLON), jnp.float32)] * 2
    if not window.last:
        out_shape.append(jax.ShapeDtypeStruct((2, 2 * SUB, NLON), jnp.float32))
    field = pltpu.VMEM((2, window.extended, NLON), jnp.float32)
    lhs_shape = (2 * window.rows, 2 * depth)
    out = pl.pallas_call(
        functools.partial(window_kernel, window, depth),
        out_shape=out_shape,
        in_specs=in_specs,
        out_specs=[vmem] * len(out_shape),
        scratch_shapes=[
            pltpu.VMEM((2, window.rows, depth), jnp.float32),
            pltpu.VMEM(lhs_shape, jnp.float32),
            pltpu.VMEM(lhs_shape, jnp.bfloat16),
            pltpu.VMEM(lhs_shape, jnp.bfloat16),
            field,
            field,
            field,
            field,
            pltpu.SemaphoreType.DMA,
        ],
        compiler_params=pltpu.CompilerParams(vmem_limit_bytes=VMEM_LIMIT),
        cost_estimate=pl.CostEstimate(
            flops=5 * 3 * 2 * lhs_shape[0] * lhs_shape[1] * NLON,
            transcendentals=0,
            bytes_accessed=4 * NLON * lhs_shape[1] + 8 * lhs_shape[0] * depth + 12 * window.width * NLON,
        ),
        name="window_tensor",
    )(*operands)
    return out[0], out[1], (None if window.last else out[2])


def pairs(members, bit):
    return [(member, member ^ bit) for member in range(members)]


def by_levels(coeffs):
    spec = coeffs[0]
    levels, _, parts, waves_local, nlat = spec.shape
    members = lax.axis_size("mem")
    band = lax.axis_index("band").astype(jnp.int32)
    member = lax.axis_index("mem").astype(jnp.int32)
    core, side = member % 2, member // 2 % 2
    columns_of = [[m for m in range(members) if m % 4 == k] for k in range(4)]
    place = jnp.stack([band, core])
    spec = spec.reshape(levels, 2, parts * waves_local, nlat)
    windows = plan(nlat, [LANE] * (nlat // LANE))
    table = [jnp.asarray(part) for part in wave_table(levels, waves_local)]
    swap = [(0, 1), (1, 0)]

    lead = windows[0].rows
    outgoing = rows_first(spec, 1 - band, choose(1 - band, (0, nlat // LANE - 2)), 2 * LANE)
    piece = lax.dynamic_slice_in_dim(outgoing, choose(1 - band, (0, 2 * LANE - lead)), lead, axis=1)
    remotes = [lax.ppermute(piece, "band", swap)]
    outgoing = rows_first(spec, 1 - band, 0, nlat)
    for window in windows[1:]:
        piece = lax.dynamic_slice_in_dim(outgoing, choose(1 - band, window.row_at), window.rows, axis=1)
        remotes.append(lax.ppermute(piece, "band", swap))
    local = rows_first(spec, band, 0, nlat)

    carry = None
    pieces = {"own": [], "both": [], "other": []}
    for window, remote in zip(windows, remotes):
        keep, send, carry = window_tensor(window, place, local, remote, table, carry)
        received = lax.ppermute(send, "mem", pairs(members, 1))
        quarter = window.width // 4

        def of_side(which):
            first = which * quarter
            return lax.dynamic_slice_in_dim(keep, first, quarter, axis=1) + lax.dynamic_slice_in_dim(
                received, first, quarter, axis=1
            )

        total = of_side(side) + lax.ppermute(of_side(1 - side), "mem", pairs(members, 2))
        summed = lax.psum_scatter(total, "mem", scatter_dimension=1, axis_index_groups=columns_of, tiled=True)
        pieces[window.side].append(exponent_of(summed, members))

    other = lax.ppermute(jnp.stack(pieces["other"]), "band", swap)
    trades = []
    for m in range(members):
        for b in range(2):
            mate = (m, b) if m % 2 == b else (m ^ 1, 1 - b)
            trades.append((m * 2 + b, mate[0] * 2 + mate[1]))
    both = lax.ppermute(pieces["both"][0], ("mem", "band"), trades)

    def gathered(stack):
        whole = lax.all_gather(stack, "mem", axis_index_groups=columns_of, axis=1, tiled=True)
        beside = lax.ppermute(whole, "mem", pairs(members, 2))
        whole = jnp.where(side == 0, jnp.concatenate([whole, beside], axis=1), jnp.concatenate([beside, whole], axis=1))
        beside = lax.ppermute(whole, "mem", pairs(members, 1))
        return jnp.where(core == 0, jnp.concatenate([whole, beside], axis=1), jnp.concatenate([beside, whole], axis=1))

    own = gathered(jnp.stack(pieces["own"]))
    late = gathered(jnp.concatenate([other, both[None]]))
    other, both = late[:-1], late[-1]
    middle = both.shape[0] // 2
    low, high = both[:middle], both[middle:]

    up = jnp.stack(
        [
            jnp.concatenate([*own, low]),
            jnp.concatenate([*other[::-1], high]),
        ]
    )
    down = jnp.stack(
        [
            jnp.concatenate([low, *other]),
            jnp.concatenate([high, *own[::-1]]),
        ]
    )
    return jnp.where(band == 0, up, down)


def per_device(coeffs):
    _, levels, _, _, _, nlat = coeffs.shape
    members = lax.axis_size("mem")
    rows = nlat // lax.axis_size("band")
    if levels == lax.axis_size("band") == 2 and members == 16 and nlat % (2 * LANE) == LANE and rows > LANE:
        return by_levels(coeffs)
    return by_rows(coeffs)


def solution(mesh):
    placed = (P("mem", None, None, None, "band", None),)
    return jax.shard_map(
        per_device, mesh=mesh, in_specs=placed, out_specs=P(None, "band", None), check_vma=False
    )
```

```python
import functools
import math

import jax
import jax.numpy as jnp
import ml_dtypes
import numpy as np
from jax import lax
from jax.experimental import pallas as pl
from jax.experimental.pallas import tpu as pltpu
from jax.sharding import PartitionSpec as P

NLON = 1280
STEPS = 1
SUB = 8
LANE = 128
VMEM_LIMIT = 24 * 1024 * 1024


def padded(cells, sides, width):
    for axis, dim in sides:
        count = lax.axis_size(axis)
        ends = count - 1
        head = lax.slice_in_dim(cells, 0, width, axis=dim)
        tail = lax.slice_in_dim(cells, cells.shape[dim] - width, cells.shape[dim], axis=dim)
        cells = jnp.concatenate(
            [
                lax.ppermute(tail, axis, [(i, (i + 1) % count) for i in range(ends)]),
                cells,
                lax.ppermute(head, axis, [((i + 1) % count, i) for i in range(ends)]),
            ],
            axis=dim,
        )
    return cells


def slope(extended, winds):
    center = extended[:, 1:-1]
    north = (extended[:, 2:] - extended[:, :-2]) * 0.5
    east = (jnp.roll(center, -1, 2) - jnp.roll(center, 1, 2)) * 0.5
    return -winds - (winds[0] * east + winds[1] * north)


def rimmed(field):
    return padded(field, (("band", 1),), 1)


def tensor(extended):
    center = extended[:, 1:-1]
    north = (extended[:, 2:] - extended[:, :-2]) * 0.5
    east = (jnp.roll(center, -1, 2) - jnp.roll(center, 1, 2)) * 0.5
    g_xx = 1.0 + east[0]
    g_xy = north[0]
    g_yx = east[1]
    g_yy = 1.0 + north[1]
    return jnp.stack(
        [g_xx * g_xx + g_yx * g_yx, g_xx * g_xy + g_yx * g_yy, g_xy * g_xy + g_yy * g_yy]
    )


def integrate(shift, flow, extend):
    first = slope(extend(shift), flow)
    second = slope(extend(0.5 * first), flow)
    third = slope(extend(0.5 * second), flow)
    fourth = slope(extend(third), flow)
    return (first + 2.0 * second + 2.0 * third + fourth) / 6.0


def exponent_of(summed, members):
    mean = summed / members
    first, cross, second = (mean[..., 0, :, :], mean[..., 1, :, :], mean[..., 2, :, :])
    half = (first + second) * 0.5
    differ = (first - second) * 0.5
    largest = half + jnp.sqrt(differ * differ + cross * cross)
    return jnp.log(largest + 1e-06) / (2.0 * STEPS)


def by_rows(coeffs):
    spec = coeffs[0]
    levels = spec.shape[0]
    nlat = spec.shape[4]
    waves = spec.shape[3] * lax.axis_size("band")
    members = lax.axis_size("mem")
    stacked = spec.reshape(levels * 2, 2, spec.shape[3], nlat)
    wave_index = lax.iota(jnp.int32, waves)
    column = lax.iota(jnp.int32, NLON)
    phase = wave_index[:, None] * column[None, :] % NLON
    angle = phase.astype(jnp.float32) * (2.0 * math.pi / NLON)
    weight = jnp.where(wave_index == 0, 1.0, 2.0).astype(jnp.float32)[:, None]
    table = jnp.stack([weight * jnp.cos(angle), -weight * jnp.sin(angle)], axis=0)
    winds = jnp.einsum(
        "crwh,rwn->chn",
        lax.all_to_all(stacked, "band", split_axis=3, concat_axis=2, tiled=True),
        table,
        precision=lax.Precision.HIGHEST,
        preferred_element_type=jnp.float32,
    )
    height = winds.shape[1]
    winds = winds.reshape(levels, 2, height, NLON)
    partials = []
    for level in range(levels):
        flow = winds[level]
        shift = integrate(jnp.zeros_like(flow), flow, rimmed)
        partials.append(tensor(rimmed(shift)))
    summed = lax.psum_scatter(jnp.stack(partials), "mem", scatter_dimension=3, tiled=True)
    return lax.all_gather(exponent_of(summed, members), "mem", axis=2, tiled=True)


@functools.lru_cache(maxsize=None)
def wave_table(bands, waves_local):
    wave = np.arange(bands * waves_local, dtype=np.int64)
    phase = (wave[:, None] * np.arange(NLON, dtype=np.int64)[None, :]) % NLON
    angle = phase.astype(np.float64) * (2.0 * np.pi / NLON)
    weight = np.where(wave == 0, 1.0, 2.0)[:, None]
    table = np.stack([weight * np.cos(angle), -weight * np.sin(angle)])
    table = table.reshape(2, bands, waves_local, NLON).transpose(1, 0, 2, 3).reshape(-1, NLON)
    high = table.astype(ml_dtypes.bfloat16)
    low = (table - high.astype(np.float64)).astype(ml_dtypes.bfloat16)
    return high, low


class Window:
    def __init__(self, index, count, start, width, nlat):
        self.first = index == 0
        self.last = index == count - 1
        self.width = width
        self.extended = width + 2 * SUB
        low = 0 if self.first else start + SUB
        high = nlat if self.last else start + width + SUB
        self.rows = high - low
        self.row_at = (nlat - high, low)
        base_up, base_down = start - SUB, nlat - start - width - SUB
        self.place = (nlat - high - base_down, low - base_up)
        self.side = "other" if 2 * (start + width) <= nlat else "own" if 2 * start >= nlat else "both"


def plan(nlat, widths):
    starts = np.cumsum([0] + widths[:-1])
    return [Window(k, len(widths), int(starts[k]), widths[k], nlat) for k in range(len(widths))]


def choose(band, pair):
    return jnp.where(band == 0, pair[0], pair[1])


def transpose_kernel(place, spec_ref, out_ref):
    out_ref[0] = spec_ref[0, 0].T


def rows_first(spec, level, block, width):
    depth = spec.shape[2]
    return pl.pallas_call(
        transpose_kernel,
        grid_spec=pltpu.PrefetchScalarGridSpec(
            num_scalar_prefetch=1,
            grid=(2, width // LANE),
            in_specs=[pl.BlockSpec((1, 1, depth, LANE), lambda c, t, place: (place[0], c, 0, place[1] + t))],
            out_specs=pl.BlockSpec((1, LANE, depth), lambda c, t, place: (c, t, 0)),
        ),
        out_shape=jax.ShapeDtypeStruct((2, width, depth), jnp.float32),
        compiler_params=pltpu.CompilerParams(vmem_limit_bytes=2 * VMEM_LIMIT),
        cost_estimate=pl.CostEstimate(
            flops=0, transcendentals=0, bytes_accessed=8 * 2 * width * depth * 4
        ),
        name="rows_first",
    )(jnp.stack([level, jnp.asarray(block, jnp.int32)]), spec)


def piece_kernel(start_ref, from_ref, *refs):
    out_ref, sem = refs[-2:]
    start = pl.multiple_of(start_ref[0], SUB)
    copy = pltpu.make_async_copy(from_ref.at[:, pl.ds(start, out_ref.shape[1])], out_ref, sem)
    copy.start()
    copy.wait()


def piece_of(outgoing, start, rows, waits):
    return pl.pallas_call(
        piece_kernel,
        in_specs=[pl.BlockSpec(memory_space=pltpu.SMEM)] + [pl.BlockSpec(memory_space=pl.ANY)] * (1 + len(waits)),
        out_specs=pl.BlockSpec(memory_space=pl.ANY),
        out_shape=jax.ShapeDtypeStruct((2, rows, outgoing.shape[2]), jnp.float32),
        scratch_shapes=[pltpu.SemaphoreType.DMA],
        cost_estimate=pl.CostEstimate(flops=0, transcendentals=0, bytes_accessed=16 * rows * outgoing.shape[2]),
        name="piece_of",
    )(start.astype(jnp.int32).reshape(1), outgoing, *waits)


def east_of(x):
    return pltpu.roll(x, NLON - 1, axis=1) - pltpu.roll(x, 1, axis=1)


def north_of(before, here, after):
    row = lax.broadcasted_iota(jnp.int32, here.shape, 0)
    above = jnp.where(row == SUB - 1, pltpu.roll(after, SUB - 1, axis=0), pltpu.roll(here, SUB - 1, axis=0))
    below = jnp.where(row == 0, pltpu.roll(before, 1, axis=0), pltpu.roll(here, 1, axis=0))
    return above - below


def window_kernel(window, depth, waits, *refs):
    refs = list(refs)
    place_ref, local_ref, remote_ref, high_ref, low_ref = refs[:5]
    refs = refs[5 + waits :]
    carry_ref = None if window.first else refs.pop(0)
    keep_ref, send_ref = refs.pop(0), refs.pop(0)
    carried_ref = None if window.last else refs.pop(0)
    local_buf, lhs, lhs_high, lhs_low, wind, second, third, shift, sem = refs
    band, core = place_ref[0], place_ref[1]
    rows, extended = window.rows, window.extended

    def at(pair):
        return pl.multiple_of(choose(band, pair).astype(jnp.int32), SUB)

    fetch = pltpu.make_async_copy(local_ref.at[:, pl.ds(at(window.row_at), rows)], local_buf, sem)
    fetch.start()
    for c in range(2):
        lhs[c * rows : (c + 1) * rows, pl.ds(pl.multiple_of((1 - band) * depth, LANE), depth)] = remote_ref[c]
    fetch.wait()
    for c in range(2):
        lhs[c * rows : (c + 1) * rows, pl.ds(pl.multiple_of(band * depth, LANE), depth)] = local_buf[c]
    lhs_high[...] = lhs[...].astype(jnp.bfloat16)
    lhs_low[...] = (lhs[...] - lhs_high[...].astype(jnp.float32)).astype(jnp.bfloat16)

    place = at(window.place)
    if window.first or window.last:
        for c in range(2):
            if window.first:
                wind[c, pl.ds(at((extended - SUB, 0)), SUB), :] = jnp.zeros((SUB, NLON), jnp.float32)
            if window.last:
                wind[c, pl.ds(at((0, extended - SUB)), SUB), :] = jnp.zeros((SUB, NLON), jnp.float32)
    if not window.first:
        for c in range(2):
            wind[c, pl.ds(at((extended - 2 * SUB, 0)), 2 * SUB), :] = carry_ref[c]

    @pl.loop(0, NLON // 256)
    def _(tile):
        columns = pl.ds(pl.multiple_of(tile * 256, 256), 256)
        dot = functools.partial(jnp.dot, preferred_element_type=jnp.float32)
        total = dot(lhs_high[...], high_ref[:, columns])
        total += dot(lhs_low[...], high_ref[:, columns])
        total += dot(lhs_high[...], low_ref[:, columns])
        for c in range(2):
            wind[c, pl.ds(place, rows), columns] = total[c * rows : (c + 1) * rows]

    if not window.last:
        for c in range(2):
            carried_ref[c] = wind[c, pl.ds(at((0, extended - 2 * SUB)), 2 * SUB), :]

    blocks = extended // SUB

    def rows_of(block):
        return pl.ds(pl.multiple_of(block * SUB, SUB), SUB)

    def derivatives(field, block):
        before, after = jnp.maximum(block - 1, 0), jnp.minimum(block + 1, blocks - 1)
        result = []
        for c in range(2):
            here = field[c, rows_of(block), :]
            result.append((east_of(here), north_of(field[c, rows_of(before), :], here, field[c, rows_of(after), :])))
        return result

    @pl.loop(0, blocks, unroll=6)
    def _(block):
        flow = [wind[c, rows_of(block), :] for c in range(2)]
        for c, (east, north) in enumerate(derivatives(wind, block)):
            second[c, rows_of(block), :] = 0.25 * (flow[0] * east + flow[1] * north) - flow[c]

    @pl.loop(0, blocks, unroll=6)
    def _(block):
        flow = [wind[c, rows_of(block), :] for c in range(2)]
        for c, (east, north) in enumerate(derivatives(second, block)):
            third[c, rows_of(block), :] = -flow[c] - 0.25 * (flow[0] * east + flow[1] * north)

    @pl.loop(0, blocks, unroll=6)
    def _(block):
        flow = [wind[c, rows_of(block), :] for c in range(2)]
        for c, (east, north) in enumerate(derivatives(third, block)):
            fourth = -flow[c] - 0.5 * (flow[0] * east + flow[1] * north)
            both = second[c, rows_of(block), :] + third[c, rows_of(block), :]
            shift[c, rows_of(block), :] = (2.0 * both + (fourth - flow[c])) * (1.0 / 6.0)

    half = window.width // 2 // SUB

    def entries(out_ref, base):
        @pl.loop(0, half, unroll=4)
        def _(block):
            (e0, n0), (e1, n1) = derivatives(shift, base + block + 1)
            g_xx, g_xy, g_yx, g_yy = 1.0 + 0.5 * e0, 0.5 * n0, 0.5 * e1, 1.0 + 0.5 * n1
            out_ref[0, rows_of(block), :] = g_xx * g_xx + g_yx * g_yx
            out_ref[1, rows_of(block), :] = g_xx * g_xy + g_yx * g_yy
            out_ref[2, rows_of(block), :] = g_xy * g_xy + g_yy * g_yy

    entries(keep_ref, core * half)
    entries(send_ref, (1 - core) * half)


def window_tensor(window, place, local, remote, table, waits, carry):
    depth = local.shape[2]
    vmem = pl.BlockSpec(memory_space=pltpu.VMEM)
    in_specs = [
        pl.BlockSpec(memory_space=pltpu.SMEM),
        pl.BlockSpec(memory_space=pl.ANY),
        vmem,
        vmem,
        vmem,
    ]
    in_specs += [pl.BlockSpec(memory_space=pl.ANY)] * len(waits)
    operands = [place, local, remote, *table, *waits]
    if not window.first:
        in_specs.append(vmem)
        operands.append(carry)
    out_shape = [jax.ShapeDtypeStruct((3, window.width // 2, NLON), jnp.float32)] * 2
    if not window.last:
        out_shape.append(jax.ShapeDtypeStruct((2, 2 * SUB, NLON), jnp.float32))
    field = pltpu.VMEM((2, window.extended, NLON), jnp.float32)
    lhs_shape = (2 * window.rows, 2 * depth)
    out = pl.pallas_call(
        functools.partial(window_kernel, window, depth, len(waits)),
        out_shape=out_shape,
        in_specs=in_specs,
        out_specs=[vmem] * len(out_shape),
        scratch_shapes=[
            pltpu.VMEM((2, window.rows, depth), jnp.float32),
            pltpu.VMEM(lhs_shape, jnp.float32),
            pltpu.VMEM(lhs_shape, jnp.bfloat16),
            pltpu.VMEM(lhs_shape, jnp.bfloat16),
            field,
            field,
            field,
            field,
            pltpu.SemaphoreType.DMA,
        ],
        compiler_params=pltpu.CompilerParams(vmem_limit_bytes=VMEM_LIMIT),
        cost_estimate=pl.CostEstimate(
            flops=5 * 3 * 2 * lhs_shape[0] * lhs_shape[1] * NLON,
            transcendentals=0,
            bytes_accessed=4 * NLON * lhs_shape[1] + 8 * lhs_shape[0] * depth + 12 * window.width * NLON,
        ),
        name="window_tensor",
    )(*operands)
    return out[0], out[1], (None if window.last else out[2])


def pairs(members, bit):
    return [(member, member ^ bit) for member in range(members)]


def by_levels(coeffs):
    spec = coeffs[0]
    levels, _, parts, waves_local, nlat = spec.shape
    members = lax.axis_size("mem")
    band = lax.axis_index("band").astype(jnp.int32)
    member = lax.axis_index("mem").astype(jnp.int32)
    place = jnp.stack([band, member % 2])
    spec = spec.reshape(levels, 2, parts * waves_local, nlat)
    windows = plan(nlat, [LANE] * (nlat // LANE))
    table = [jnp.asarray(part) for part in wave_table(levels, waves_local)]
    swap = [(0, 1), (1, 0)]

    lead = windows[0].rows
    outgoing = rows_first(spec, 1 - band, choose(1 - band, (nlat // LANE - 2, 0)), 2 * LANE)
    piece = piece_of(outgoing, choose(1 - band, (2 * LANE - lead, 0)), lead, [])
    remotes = [lax.ppermute(piece, "band", swap)]
    outgoing = rows_first(spec, 1 - band, 0, nlat)

    def fetch_rows(k, waits):
        window = windows[k]
        piece = piece_of(outgoing, choose(1 - band, window.row_at), window.rows, waits)
        remotes.append(lax.ppermute(piece, "band", swap))
        return piece

    fetch_rows(1, [])
    local = rows_first(spec, band, 0, nlat)

    bits = [1 << n for n in range(members.bit_length() - 1)]

    def halved(parts_of, bit):
        half = parts_of[0].shape[1] // 2
        mine = (member // bit) % 2

        def total(which):
            return sum(lax.dynamic_slice_in_dim(part, which * half, half, axis=1) for part in parts_of[:2])

        leaves = total(1 - mine)
        return [total(mine), lax.ppermute(leaves, "mem", pairs(members, bit)), leaves]

    def doubled(part, bit):
        beside = lax.ppermute(part, "mem", pairs(members, bit))
        mine = (member // bit) % 2
        return jnp.where(mine == 0, jnp.concatenate([part, beside], axis=1), jnp.concatenate([beside, part], axis=1))

    def gathered(part):
        for bit in reversed(bits):
            part = doubled(part, bit)
        return part

    carry = None
    sums = []
    for k, window in enumerate(windows):
        waits = []
        if k + 2 < len(windows):
            waits.append(fetch_rows(k + 2, [remotes[k]] if carry is None else [remotes[k], carry]))
        for j in range(k - 1):
            sums[j] = halved(sums[j], bits[k - 1 - j])
            waits.append(sums[j][2])
        keep, send, carry = window_tensor(window, place, local, remotes[k], table, waits, carry)
        sums.append([keep, lax.ppermute(send, "mem", pairs(members, bits[0]))])
    pieces = {"own": [], "both": [], "other": []}
    for k, window in enumerate(windows):
        for bit in bits[max(len(windows) - 1 - k, 1) :]:
            sums[k] = halved(sums[k], bit)
        pieces[window.side].append(exponent_of(sums[k][0] + sums[k][1], members))

    other = lax.ppermute(jnp.stack(pieces["other"]), "band", swap)
    trades = []
    for m in range(members):
        for b in range(2):
            mate = (m, b) if m % 2 == b else (m ^ 1, 1 - b)
            trades.append((m * 2 + b, mate[0] * 2 + mate[1]))
    both = lax.ppermute(pieces["both"][0], ("mem", "band"), trades)

    early = gathered(jnp.concatenate([other, both[None]]))
    other, both = early[:-1], early[-1]
    middle = both.shape[0] // 2
    low, high = both[:middle], both[middle:]
    rest = jnp.zeros((nlat // 2 - middle, NLON), jnp.float32)
    down = jnp.stack([jnp.concatenate([rest, low]), jnp.concatenate([*other, high])])
    up = jnp.stack([jnp.concatenate([low, *other[::-1]]), jnp.concatenate([high, rest])])
    out = jnp.where(band == 0, down, up)

    own = gathered(jnp.stack(pieces["own"]))
    for k, block in enumerate(own):
        width = block.shape[0]
        row = choose(band, (nlat // 2 - middle - (k + 1) * width, middle + k * width))
        out = lax.dynamic_update_slice(out, block[None], (band, row.astype(jnp.int32), jnp.int32(0)))
    return out


def per_device(coeffs):
    _, levels, _, _, _, nlat = coeffs.shape
    members = lax.axis_size("mem")
    rows = nlat // lax.axis_size("band")
    if levels == lax.axis_size("band") == 2 and members == 16 and nlat % (2 * LANE) == LANE and rows > LANE:
        return by_levels(coeffs)
    return by_rows(coeffs)


def solution(mesh):
    placed = (P("mem", None, None, None, "band", None),)
    return jax.shard_map(
        per_device, mesh=mesh, in_specs=placed, out_specs=P(None, "band", None), check_vma=False
    )
```

```python
import functools
import math

import jax
import jax.numpy as jnp
import ml_dtypes
import numpy as np
from jax import lax
from jax.experimental import pallas as pl
from jax.experimental.pallas import tpu as pltpu
from jax.sharding import PartitionSpec as P

NLON = 1280
STEPS = 1
SUB = 8
LANE = 128
VMEM_LIMIT = 24 * 1024 * 1024


def padded(cells, sides, width):
    for axis, dim in sides:
        count = lax.axis_size(axis)
        ends = count - 1
        head = lax.slice_in_dim(cells, 0, width, axis=dim)
        tail = lax.slice_in_dim(cells, cells.shape[dim] - width, cells.shape[dim], axis=dim)
        cells = jnp.concatenate(
            [
                lax.ppermute(tail, axis, [(i, (i + 1) % count) for i in range(ends)]),
                cells,
                lax.ppermute(head, axis, [((i + 1) % count, i) for i in range(ends)]),
            ],
            axis=dim,
        )
    return cells


def slope(extended, winds):
    center = extended[:, 1:-1]
    north = (extended[:, 2:] - extended[:, :-2]) * 0.5
    east = (jnp.roll(center, -1, 2) - jnp.roll(center, 1, 2)) * 0.5
    return -winds - (winds[0] * east + winds[1] * north)


def rimmed(field):
    return padded(field, (("band", 1),), 1)


def tensor(extended):
    center = extended[:, 1:-1]
    north = (extended[:, 2:] - extended[:, :-2]) * 0.5
    east = (jnp.roll(center, -1, 2) - jnp.roll(center, 1, 2)) * 0.5
    g_xx = 1.0 + east[0]
    g_xy = north[0]
    g_yx = east[1]
    g_yy = 1.0 + north[1]
    return jnp.stack(
        [g_xx * g_xx + g_yx * g_yx, g_xx * g_xy + g_yx * g_yy, g_xy * g_xy + g_yy * g_yy]
    )


def integrate(shift, flow, extend):
    first = slope(extend(shift), flow)
    second = slope(extend(0.5 * first), flow)
    third = slope(extend(0.5 * second), flow)
    fourth = slope(extend(third), flow)
    return (first + 2.0 * second + 2.0 * third + fourth) / 6.0


def exponent_of(summed, members):
    mean = summed / members
    first, cross, second = (mean[..., 0, :, :], mean[..., 1, :, :], mean[..., 2, :, :])
    half = (first + second) * 0.5
    differ = (first - second) * 0.5
    largest = half + jnp.sqrt(differ * differ + cross * cross)
    return jnp.log(largest + 1e-06) / (2.0 * STEPS)


def by_rows(coeffs):
    spec = coeffs[0]
    levels = spec.shape[0]
    nlat = spec.shape[4]
    waves = spec.shape[3] * lax.axis_size("band")
    members = lax.axis_size("mem")
    stacked = spec.reshape(levels * 2, 2, spec.shape[3], nlat)
    wave_index = lax.iota(jnp.int32, waves)
    column = lax.iota(jnp.int32, NLON)
    phase = wave_index[:, None] * column[None, :] % NLON
    angle = phase.astype(jnp.float32) * (2.0 * math.pi / NLON)
    weight = jnp.where(wave_index == 0, 1.0, 2.0).astype(jnp.float32)[:, None]
    table = jnp.stack([weight * jnp.cos(angle), -weight * jnp.sin(angle)], axis=0)
    winds = jnp.einsum(
        "crwh,rwn->chn",
        lax.all_to_all(stacked, "band", split_axis=3, concat_axis=2, tiled=True),
        table,
        precision=lax.Precision.HIGHEST,
        preferred_element_type=jnp.float32,
    )
    height = winds.shape[1]
    winds = winds.reshape(levels, 2, height, NLON)
    partials = []
    for level in range(levels):
        flow = winds[level]
        shift = integrate(jnp.zeros_like(flow), flow, rimmed)
        partials.append(tensor(rimmed(shift)))
    summed = lax.psum_scatter(jnp.stack(partials), "mem", scatter_dimension=3, tiled=True)
    return lax.all_gather(exponent_of(summed, members), "mem", axis=2, tiled=True)


@functools.lru_cache(maxsize=None)
def wave_table(bands, waves_local):
    wave = np.arange(bands * waves_local, dtype=np.int64)
    phase = (wave[:, None] * np.arange(NLON, dtype=np.int64)[None, :]) % NLON
    angle = phase.astype(np.float64) * (2.0 * np.pi / NLON)
    weight = np.where(wave == 0, 1.0, 2.0)[:, None]
    table = np.stack([weight * np.cos(angle), -weight * np.sin(angle)])
    table = table.reshape(2, bands, waves_local, NLON).transpose(1, 0, 2, 3).reshape(-1, NLON)
    high = table.astype(ml_dtypes.bfloat16)
    low = (table - high.astype(np.float64)).astype(ml_dtypes.bfloat16)
    return high, low


class Window:
    def __init__(self, index, count, start, width, nlat):
        self.first = index == 0
        self.last = index == count - 1
        self.width = width
        self.extended = width + 2 * SUB
        low = 0 if self.first else start + SUB
        high = nlat if self.last else start + width + SUB
        self.rows = high - low
        self.row_at = (nlat - high, low)
        base_up, base_down = start - SUB, nlat - start - width - SUB
        self.place = (nlat - high - base_down, low - base_up)
        self.side = "other" if 2 * (start + width) <= nlat else "own" if 2 * start >= nlat else "both"


def plan(nlat, widths):
    starts = np.cumsum([0] + widths[:-1])
    return [Window(k, len(widths), int(starts[k]), widths[k], nlat) for k in range(len(widths))]


def choose(band, pair):
    return jnp.where(band == 0, pair[0], pair[1])


def transpose_kernel(place, spec_ref, out_ref):
    out_ref[0] = spec_ref[0, 0].T


def rows_first(spec, level, block, width):
    depth = spec.shape[2]
    return pl.pallas_call(
        transpose_kernel,
        grid_spec=pltpu.PrefetchScalarGridSpec(
            num_scalar_prefetch=1,
            grid=(2, width // LANE),
            in_specs=[pl.BlockSpec((1, 1, depth, LANE), lambda c, t, place: (place[0], c, 0, place[1] + t))],
            out_specs=pl.BlockSpec((1, LANE, depth), lambda c, t, place: (c, t, 0)),
        ),
        out_shape=jax.ShapeDtypeStruct((2, width, depth), jnp.float32),
        compiler_params=pltpu.CompilerParams(vmem_limit_bytes=2 * VMEM_LIMIT),
        cost_estimate=pl.CostEstimate(
            flops=0, transcendentals=0, bytes_accessed=8 * 2 * width * depth * 4
        ),
        name="rows_first",
    )(jnp.stack([level, jnp.asarray(block, jnp.int32)]), spec)


def gate_kernel(*refs):
    pass


def gated(part, waits):
    return pl.pallas_call(
        gate_kernel,
        in_specs=[pl.BlockSpec(memory_space=pl.ANY)] * (1 + len(waits)),
        out_specs=pl.BlockSpec(memory_space=pl.ANY),
        out_shape=jax.ShapeDtypeStruct(part.shape, part.dtype),
        input_output_aliases={0: 0},
        cost_estimate=pl.CostEstimate(flops=0, transcendentals=0, bytes_accessed=1024),
        name="gated",
    )(part, *waits)


def east_of(x):
    return pltpu.roll(x, NLON - 1, axis=1) - pltpu.roll(x, 1, axis=1)


def north_of(before, here, after):
    row = lax.broadcasted_iota(jnp.int32, here.shape, 0)
    above = jnp.where(row == SUB - 1, pltpu.roll(after, SUB - 1, axis=0), pltpu.roll(here, SUB - 1, axis=0))
    below = jnp.where(row == 0, pltpu.roll(before, 1, axis=0), pltpu.roll(here, 1, axis=0))
    return above - below


def window_kernel(window, depth, waits, *refs):
    refs = list(refs)
    place_ref, local_ref, remote_ref, high_ref, low_ref = refs[:5]
    refs = refs[5 + waits :]
    carry_ref = None if window.first else refs.pop(0)
    keep_ref, send_ref = refs.pop(0), refs.pop(0)
    carried_ref = None if window.last else refs.pop(0)
    local_buf, lhs, lhs_high, lhs_low, wind, second, third, shift, sem = refs
    band, core = place_ref[0], place_ref[1]
    rows, extended = window.rows, window.extended

    def at(pair):
        return pl.multiple_of(choose(band, pair).astype(jnp.int32), SUB)

    fetch = pltpu.make_async_copy(local_ref.at[:, pl.ds(at(window.row_at), rows)], local_buf, sem)
    fetch.start()
    for c in range(2):
        lhs[c * rows : (c + 1) * rows, pl.ds(pl.multiple_of((1 - band) * depth, LANE), depth)] = remote_ref[c]
    fetch.wait()
    for c in range(2):
        lhs[c * rows : (c + 1) * rows, pl.ds(pl.multiple_of(band * depth, LANE), depth)] = local_buf[c]
    lhs_high[...] = lhs[...].astype(jnp.bfloat16)
    lhs_low[...] = (lhs[...] - lhs_high[...].astype(jnp.float32)).astype(jnp.bfloat16)

    place = at(window.place)
    if window.first or window.last:
        for c in range(2):
            if window.first:
                wind[c, pl.ds(at((extended - SUB, 0)), SUB), :] = jnp.zeros((SUB, NLON), jnp.float32)
            if window.last:
                wind[c, pl.ds(at((0, extended - SUB)), SUB), :] = jnp.zeros((SUB, NLON), jnp.float32)
    if not window.first:
        for c in range(2):
            wind[c, pl.ds(at((extended - 2 * SUB, 0)), 2 * SUB), :] = carry_ref[c]

    @pl.loop(0, NLON // 256)
    def _(tile):
        columns = pl.ds(pl.multiple_of(tile * 256, 256), 256)
        dot = functools.partial(jnp.dot, preferred_element_type=jnp.float32)
        total = dot(lhs_high[...], high_ref[:, columns])
        total += dot(lhs_low[...], high_ref[:, columns])
        total += dot(lhs_high[...], low_ref[:, columns])
        for c in range(2):
            wind[c, pl.ds(place, rows), columns] = total[c * rows : (c + 1) * rows]

    if not window.last:
        for c in range(2):
            carried_ref[c] = wind[c, pl.ds(at((0, extended - 2 * SUB)), 2 * SUB), :]

    blocks = extended // SUB

    def rows_of(block):
        return pl.ds(pl.multiple_of(block * SUB, SUB), SUB)

    def derivatives(field, block):
        before, after = jnp.maximum(block - 1, 0), jnp.minimum(block + 1, blocks - 1)
        result = []
        for c in range(2):
            here = field[c, rows_of(block), :]
            result.append((east_of(here), north_of(field[c, rows_of(before), :], here, field[c, rows_of(after), :])))
        return result

    @pl.loop(0, blocks, unroll=6)
    def _(block):
        flow = [wind[c, rows_of(block), :] for c in range(2)]
        for c, (east, north) in enumerate(derivatives(wind, block)):
            second[c, rows_of(block), :] = 0.25 * (flow[0] * east + flow[1] * north) - flow[c]

    @pl.loop(0, blocks, unroll=6)
    def _(block):
        flow = [wind[c, rows_of(block), :] for c in range(2)]
        for c, (east, north) in enumerate(derivatives(second, block)):
            third[c, rows_of(block), :] = -flow[c] - 0.25 * (flow[0] * east + flow[1] * north)

    @pl.loop(0, blocks, unroll=6)
    def _(block):
        flow = [wind[c, rows_of(block), :] for c in range(2)]
        for c, (east, north) in enumerate(derivatives(third, block)):
            fourth = -flow[c] - 0.5 * (flow[0] * east + flow[1] * north)
            both = second[c, rows_of(block), :] + third[c, rows_of(block), :]
            shift[c, rows_of(block), :] = (2.0 * both + (fourth - flow[c])) * (1.0 / 6.0)

    half = window.width // 2 // SUB

    def entries(out_ref, base):
        @pl.loop(0, half, unroll=4)
        def _(block):
            (e0, n0), (e1, n1) = derivatives(shift, base + block + 1)
            g_xx, g_xy, g_yx, g_yy = 1.0 + 0.5 * e0, 0.5 * n0, 0.5 * e1, 1.0 + 0.5 * n1
            out_ref[0, rows_of(block), :] = g_xx * g_xx + g_yx * g_yx
            out_ref[1, rows_of(block), :] = g_xx * g_xy + g_yx * g_yy
            out_ref[2, rows_of(block), :] = g_xy * g_xy + g_yy * g_yy

    entries(keep_ref, core * half)
    entries(send_ref, (1 - core) * half)


def window_tensor(window, place, local, remote, table, waits, carry):
    depth = local.shape[2]
    vmem = pl.BlockSpec(memory_space=pltpu.VMEM)
    in_specs = [
        pl.BlockSpec(memory_space=pltpu.SMEM),
        pl.BlockSpec(memory_space=pl.ANY),
        vmem,
        vmem,
        vmem,
    ]
    in_specs += [pl.BlockSpec(memory_space=pl.ANY)] * len(waits)
    operands = [place, local, remote, *table, *waits]
    if not window.first:
        in_specs.append(vmem)
        operands.append(carry)
    out_shape = [jax.ShapeDtypeStruct((3, window.width // 2, NLON), jnp.float32)] * 2
    if not window.last:
        out_shape.append(jax.ShapeDtypeStruct((2, 2 * SUB, NLON), jnp.float32))
    field = pltpu.VMEM((2, window.extended, NLON), jnp.float32)
    lhs_shape = (2 * window.rows, 2 * depth)
    out = pl.pallas_call(
        functools.partial(window_kernel, window, depth, len(waits)),
        out_shape=out_shape,
        in_specs=in_specs,
        out_specs=[vmem] * len(out_shape),
        scratch_shapes=[
            pltpu.VMEM((2, window.rows, depth), jnp.float32),
            pltpu.VMEM(lhs_shape, jnp.float32),
            pltpu.VMEM(lhs_shape, jnp.bfloat16),
            pltpu.VMEM(lhs_shape, jnp.bfloat16),
            field,
            field,
            field,
            field,
            pltpu.SemaphoreType.DMA,
        ],
        compiler_params=pltpu.CompilerParams(vmem_limit_bytes=VMEM_LIMIT),
        cost_estimate=pl.CostEstimate(
            flops=5 * 3 * 2 * lhs_shape[0] * lhs_shape[1] * NLON,
            transcendentals=0,
            bytes_accessed=4 * NLON * lhs_shape[1] + 8 * lhs_shape[0] * depth + 12 * window.width * NLON,
        ),
        name="window_tensor",
    )(*operands)
    return out[0], out[1], (None if window.last else out[2])


def pairs(members, bit):
    return [(member, member ^ bit) for member in range(members)]


def by_levels(coeffs):
    spec = coeffs[0]
    levels, _, parts, waves_local, nlat = spec.shape
    members = lax.axis_size("mem")
    band = lax.axis_index("band").astype(jnp.int32)
    member = lax.axis_index("mem").astype(jnp.int32)
    place = jnp.stack([band, member % 2])
    spec = spec.reshape(levels, 2, parts * waves_local, nlat)
    windows = plan(nlat, [LANE] * (nlat // LANE))
    table = [jnp.asarray(part) for part in wave_table(levels, waves_local)]
    swap = [(0, 1), (1, 0)]

    lead = windows[0].rows
    outgoing = rows_first(spec, 1 - band, choose(1 - band, (nlat // LANE - 2, 0)), 2 * LANE)
    piece = lax.dynamic_slice_in_dim(outgoing, choose(1 - band, (2 * LANE - lead, 0)), lead, axis=1)
    remotes = [lax.ppermute(piece, "band", swap)]
    outgoing = rows_first(spec, 1 - band, 0, nlat)
    outgoing = [
        lax.dynamic_slice_in_dim(outgoing, choose(1 - band, window.row_at), window.rows, axis=1) for window in windows
    ]

    def fetch_rows(k, waits):
        piece = gated(outgoing[k], waits) if waits else outgoing[k]
        remotes.append(lax.ppermute(piece, "band", swap))
        return piece

    fetch_rows(1, [])
    local = rows_first(spec, band, 0, nlat)

    bits = [1 << n for n in range(members.bit_length() - 1)]

    def halved(parts_of, bit):
        half = parts_of[0].shape[1] // 2
        mine = (member // bit) % 2

        def total(which):
            return sum(lax.dynamic_slice_in_dim(part, which * half, half, axis=1) for part in parts_of[:2])

        leaves = total(1 - mine)
        return [total(mine), lax.ppermute(leaves, "mem", pairs(members, bit)), leaves]

    def doubled(part, bit):
        beside = lax.ppermute(part, "mem", pairs(members, bit))
        mine = (member // bit) % 2
        return jnp.where(mine == 0, jnp.concatenate([part, beside], axis=1), jnp.concatenate([beside, part], axis=1))

    def gathered(part):
        for bit in reversed(bits):
            part = doubled(part, bit)
        return part

    carry = None
    sums = []
    for k, window in enumerate(windows):
        waits = []
        if k + 2 < len(windows):
            waits.append(fetch_rows(k + 2, [remotes[k]] if carry is None else [remotes[k], carry]))
        for j in range(k - 1):
            sums[j] = halved(sums[j], bits[k - 1 - j])
            waits.append(sums[j][2])
        keep, send, carry = window_tensor(window, place, local, remotes[k], table, waits, carry)
        sums.append([keep, lax.ppermute(send, "mem", pairs(members, bits[0]))])
    pieces = {"own": [], "both": [], "other": []}
    for k, window in enumerate(windows):
        for bit in bits[max(len(windows) - 1 - k, 1) :]:
            sums[k] = halved(sums[k], bit)
        pieces[window.side].append(exponent_of(sums[k][0] + sums[k][1], members))

    other = lax.ppermute(jnp.stack(pieces["other"]), "band", swap)
    trades = []
    for m in range(members):
        for b in range(2):
            mate = (m, b) if m % 2 == b else (m ^ 1, 1 - b)
            trades.append((m * 2 + b, mate[0] * 2 + mate[1]))
    both = lax.ppermute(pieces["both"][0], ("mem", "band"), trades)

    early = gathered(jnp.concatenate([other, both[None]]))
    other, both = early[:-1], early[-1]
    middle = both.shape[0] // 2
    low, high = both[:middle], both[middle:]
    rest = jnp.zeros((nlat // 2 - middle, NLON), jnp.float32)
    down = jnp.stack([jnp.concatenate([rest, low]), jnp.concatenate([*other, high])])
    up = jnp.stack([jnp.concatenate([low, *other[::-1]]), jnp.concatenate([high, rest])])
    out = jnp.where(band == 0, down, up)

    own = gathered(jnp.stack(pieces["own"]))
    for k, block in enumerate(own):
        width = block.shape[0]
        row = choose(band, (nlat // 2 - middle - (k + 1) * width, middle + k * width))
        out = lax.dynamic_update_slice(out, block[None], (band, row.astype(jnp.int32), jnp.int32(0)))
    return out


def per_device(coeffs):
    _, levels, _, _, _, nlat = coeffs.shape
    members = lax.axis_size("mem")
    rows = nlat // lax.axis_size("band")
    if levels == lax.axis_size("band") == 2 and members == 16 and nlat % (2 * LANE) == LANE and rows > LANE:
        return by_levels(coeffs)
    return by_rows(coeffs)


def solution(mesh):
    placed = (P("mem", None, None, None, "band", None),)
    return jax.shard_map(
        per_device, mesh=mesh, in_specs=placed, out_specs=P(None, "band", None), check_vma=False
    )
```

```python
import functools
import math

import jax
import jax.numpy as jnp
import ml_dtypes
import numpy as np
from jax import lax
from jax.experimental import pallas as pl
from jax.experimental.pallas import tpu as pltpu
from jax.sharding import PartitionSpec as P

NLON = 1280
STEPS = 1
SUB = 8
LANE = 128
VMEM_LIMIT = 24 * 1024 * 1024
KERNEL_WORK = 8


def padded(cells, sides, width):
    for axis, dim in sides:
        count = lax.axis_size(axis)
        ends = count - 1
        head = lax.slice_in_dim(cells, 0, width, axis=dim)
        tail = lax.slice_in_dim(cells, cells.shape[dim] - width, cells.shape[dim], axis=dim)
        cells = jnp.concatenate(
            [
                lax.ppermute(tail, axis, [(i, (i + 1) % count) for i in range(ends)]),
                cells,
                lax.ppermute(head, axis, [((i + 1) % count, i) for i in range(ends)]),
            ],
            axis=dim,
        )
    return cells


def slope(extended, winds):
    center = extended[:, 1:-1]
    north = (extended[:, 2:] - extended[:, :-2]) * 0.5
    east = (jnp.roll(center, -1, 2) - jnp.roll(center, 1, 2)) * 0.5
    return -winds - (winds[0] * east + winds[1] * north)


def rimmed(field):
    return padded(field, (("band", 1),), 1)


def tensor(extended):
    center = extended[:, 1:-1]
    north = (extended[:, 2:] - extended[:, :-2]) * 0.5
    east = (jnp.roll(center, -1, 2) - jnp.roll(center, 1, 2)) * 0.5
    g_xx = 1.0 + east[0]
    g_xy = north[0]
    g_yx = east[1]
    g_yy = 1.0 + north[1]
    return jnp.stack(
        [g_xx * g_xx + g_yx * g_yx, g_xx * g_xy + g_yx * g_yy, g_xy * g_xy + g_yy * g_yy]
    )


def integrate(shift, flow, extend):
    first = slope(extend(shift), flow)
    second = slope(extend(0.5 * first), flow)
    third = slope(extend(0.5 * second), flow)
    fourth = slope(extend(third), flow)
    return (first + 2.0 * second + 2.0 * third + fourth) / 6.0


def exponent_of(summed, members):
    mean = summed / members
    first, cross, second = (mean[..., 0, :, :], mean[..., 1, :, :], mean[..., 2, :, :])
    half = (first + second) * 0.5
    differ = (first - second) * 0.5
    largest = half + jnp.sqrt(differ * differ + cross * cross)
    return jnp.log(largest + 1e-06) / (2.0 * STEPS)


def by_rows(coeffs):
    spec = coeffs[0]
    levels = spec.shape[0]
    nlat = spec.shape[4]
    waves = spec.shape[3] * lax.axis_size("band")
    members = lax.axis_size("mem")
    stacked = spec.reshape(levels * 2, 2, spec.shape[3], nlat)
    wave_index = lax.iota(jnp.int32, waves)
    column = lax.iota(jnp.int32, NLON)
    phase = wave_index[:, None] * column[None, :] % NLON
    angle = phase.astype(jnp.float32) * (2.0 * math.pi / NLON)
    weight = jnp.where(wave_index == 0, 1.0, 2.0).astype(jnp.float32)[:, None]
    table = jnp.stack([weight * jnp.cos(angle), -weight * jnp.sin(angle)], axis=0)
    winds = jnp.einsum(
        "crwh,rwn->chn",
        lax.all_to_all(stacked, "band", split_axis=3, concat_axis=2, tiled=True),
        table,
        precision=lax.Precision.HIGHEST,
        preferred_element_type=jnp.float32,
    )
    height = winds.shape[1]
    winds = winds.reshape(levels, 2, height, NLON)
    partials = []
    for level in range(levels):
        flow = winds[level]
        shift = integrate(jnp.zeros_like(flow), flow, rimmed)
        partials.append(tensor(rimmed(shift)))
    summed = lax.psum_scatter(jnp.stack(partials), "mem", scatter_dimension=3, tiled=True)
    return lax.all_gather(exponent_of(summed, members), "mem", axis=2, tiled=True)


def by_parity(waves_local):
    half = waves_local // 2
    whole = 2 * LANE - half
    runs = []
    for parity in range(2):
        runs += [(parity, half, 2), (waves_local + parity, whole, 2)]
    for parity in range(2):
        runs.append((waves_local + parity + 2 * whole, half - whole, 2))
    return runs


@functools.lru_cache(maxsize=None)
def wave_table(bands, waves_local):
    order = np.concatenate([start + step * np.arange(count) for start, count, step in by_parity(waves_local)])
    wave, part = order % waves_local, order // waves_local
    wave = wave[None, :] + waves_local * np.arange(bands)[:, None]
    part = np.broadcast_to(part, wave.shape)
    cut = [0, 2 * LANE, 4 * LANE, 4 * LANE + LANE // 2, 5 * LANE]
    result = []
    for parity in range(2):
        picks = [(band, slice(cut[parity], cut[parity + 1])) for band in range(bands)]
        picks += [(band, slice(cut[parity + 2], cut[parity + 3])) for band in range(bands)]
        waves = np.concatenate([wave[pick] for pick in picks])
        parts = np.concatenate([part[pick] for pick in picks])
        phase = (waves[:, None] * np.arange(NLON // 2)[None, :]) % NLON
        angle = phase.astype(np.float64) * (2.0 * np.pi / NLON)
        weight = np.where(waves == 0, 1.0, 2.0)[:, None]
        table = weight * np.where(parts[:, None] == 0, np.cos(angle), -np.sin(angle))
        high = table.astype(ml_dtypes.bfloat16)
        result += [high, (table - high.astype(np.float64)).astype(ml_dtypes.bfloat16)]
    return np.stack(result)


class Window:
    def __init__(self, index, count, start, width, nlat):
        self.first = index == 0
        self.last = index == count - 1
        self.width = width
        self.extended = width + 2 * SUB
        low = 0 if self.first else start + SUB
        high = nlat if self.last else start + width + SUB
        self.rows = high - low
        self.row_at = (nlat - high, low)
        base_up, base_down = start - SUB, nlat - start - width - SUB
        self.place = (nlat - high - base_down, low - base_up)
        self.side = "other" if 2 * (start + width) <= nlat else "own" if 2 * start >= nlat else "both"


def plan(nlat, widths):
    starts = np.cumsum([0] + widths[:-1])
    return [Window(k, len(widths), int(starts[k]), widths[k], nlat) for k in range(len(widths))]


def choose(band, pair):
    return jnp.where(band == 0, pair[0], pair[1])


def transpose_kernel(place, spec_ref, out_ref):
    runs = by_parity(spec_ref.shape[2] // 2)
    out_ref[0] = jnp.concatenate([spec_ref[0, 0, pl.ds(start, count, step), :] for start, count, step in runs]).T


def rows_first(spec, level, block, width):
    depth = spec.shape[2]
    return pl.pallas_call(
        transpose_kernel,
        grid_spec=pltpu.PrefetchScalarGridSpec(
            num_scalar_prefetch=1,
            grid=(2, width // LANE),
            in_specs=[pl.BlockSpec((1, 1, depth, LANE), lambda c, t, place: (place[0], c, 0, place[1] + t))],
            out_specs=pl.BlockSpec((1, LANE, depth), lambda c, t, place: (c, t, 0)),
        ),
        out_shape=jax.ShapeDtypeStruct((2, width, depth), jnp.float32),
        compiler_params=pltpu.CompilerParams(vmem_limit_bytes=2 * VMEM_LIMIT),
        cost_estimate=pl.CostEstimate(
            flops=0, transcendentals=0, bytes_accessed=8 * 2 * width * depth * 4
        ),
        name="rows_first",
    )(jnp.stack([level, jnp.asarray(block, jnp.int32)]), spec)


def gate_kernel(*refs):
    pass


def gated(part, waits):
    return pl.pallas_call(
        gate_kernel,
        in_specs=[pl.BlockSpec(memory_space=pl.ANY)] * (1 + len(waits)),
        out_specs=pl.BlockSpec(memory_space=pl.ANY),
        out_shape=jax.ShapeDtypeStruct(part.shape, part.dtype),
        input_output_aliases={0: 0},
        cost_estimate=pl.CostEstimate(flops=0, transcendentals=0, bytes_accessed=1024),
        name="gated",
    )(part, *waits)


def east_of(x):
    return pltpu.roll(x, NLON - 1, axis=1) - pltpu.roll(x, 1, axis=1)


def north_of(before, here, after):
    row = lax.broadcasted_iota(jnp.int32, here.shape, 0)
    above = jnp.where(row == SUB - 1, pltpu.roll(after, SUB - 1, axis=0), pltpu.roll(here, SUB - 1, axis=0))
    below = jnp.where(row == 0, pltpu.roll(before, 1, axis=0), pltpu.roll(here, 1, axis=0))
    return above - below


def window_kernel(window, depth, waits, *refs):
    refs = list(refs)
    place_ref, local_ref, remote_ref, table_ref = refs[:4]
    refs = refs[4 + waits :]
    carry_ref = None if window.first else refs.pop(0)
    out_refs = [refs.pop(0) for _ in range(4)]
    carried_ref = None if window.last else refs.pop(0)
    table, local_buf, lhs_high, lhs_low, wind, second, third, shift, sems = refs
    band, core, side = place_ref[0], place_ref[1], place_ref[2]
    rows, extended = window.rows, window.extended

    def at(pair):
        return pl.multiple_of(choose(band, pair).astype(jnp.int32), SUB)

    fetch = pltpu.make_async_copy(local_ref.at[:, pl.ds(at(window.row_at), rows)], local_buf, sems.at[0])
    fetch.start()
    tables = pltpu.make_async_copy(table_ref, table, sems.at[1])
    tables.start()
    fetch.wait()
    lane = lax.broadcasted_iota(jnp.int32, (rows, LANE), 1)
    even, odd = [], []
    for c in range(2):
        mine, theirs = local_buf[c], remote_ref[c]
        low, high = jnp.where(band == 0, mine, theirs), jnp.where(band == 0, theirs, mine)
        low_rest, high_rest = low[:, 4 * LANE :], high[:, 4 * LANE :]
        turn = functools.partial(pltpu.roll, shift=LANE // 2, axis=1)
        even_rest = jnp.where(lane < LANE // 2, low_rest, turn(high_rest))
        odd_rest = jnp.where(lane < LANE // 2, turn(low_rest), high_rest)
        even.append(jnp.concatenate([low[:, : 2 * LANE], high[:, : 2 * LANE], even_rest], axis=1))
        odd.append(jnp.concatenate([low[:, 2 * LANE : 4 * LANE], high[:, 2 * LANE : 4 * LANE], odd_rest], axis=1))
    for parity, parts in enumerate((even, odd)):
        lhs = jnp.concatenate(parts)
        lhs_high[parity] = lhs.astype(jnp.bfloat16)
        lhs_low[parity] = (lhs - lhs_high[parity].astype(jnp.float32)).astype(jnp.bfloat16)
    tables.wait()

    place = at(window.place)
    if window.first or window.last:
        for c in range(2):
            if window.first:
                wind[c, pl.ds(at((extended - SUB, 0)), SUB), :] = jnp.zeros((SUB, NLON), jnp.float32)
            if window.last:
                wind[c, pl.ds(at((0, extended - SUB)), SUB), :] = jnp.zeros((SUB, NLON), jnp.float32)
    if not window.first:
        for c in range(2):
            wind[c, pl.ds(at((extended - 2 * SUB, 0)), 2 * SUB), :] = carry_ref[c]

    dot = functools.partial(jnp.dot, preferred_element_type=jnp.float32)
    for start in range(0, NLON // 2, 2 * LANE):
        stop = min(start + 2 * LANE, NLON // 2)
        columns = slice(start, stop)
        sums = []
        for parity in range(2):
            total = dot(lhs_high[parity], table[2 * parity, :, columns])
            total += dot(lhs_low[parity], table[2 * parity, :, columns])
            total += dot(lhs_high[parity], table[2 * parity + 1, :, columns])
            sums.append(total)
        for c in range(2):
            even_sum, odd_sum = (total[c * rows : (c + 1) * rows] for total in sums)
            wind[c, pl.ds(place, rows), start:stop] = even_sum + odd_sum
            wind[c, pl.ds(place, rows), NLON // 2 + start : NLON // 2 + stop] = even_sum - odd_sum

    if not window.last:
        for c in range(2):
            carried_ref[c] = wind[c, pl.ds(at((0, extended - 2 * SUB)), 2 * SUB), :]

    blocks = extended // SUB

    def rows_of(block):
        return pl.ds(pl.multiple_of(block * SUB, SUB), SUB)

    def derivatives(field, block):
        before, after = jnp.maximum(block - 1, 0), jnp.minimum(block + 1, blocks - 1)
        result = []
        for c in range(2):
            here = field[c, rows_of(block), :]
            result.append((east_of(here), north_of(field[c, rows_of(before), :], here, field[c, rows_of(after), :])))
        return result

    @pl.loop(0, blocks, unroll=6)
    def _(block):
        flow = [wind[c, rows_of(block), :] for c in range(2)]
        for c, (east, north) in enumerate(derivatives(wind, block)):
            second[c, rows_of(block), :] = 0.25 * (flow[0] * east + flow[1] * north) - flow[c]

    @pl.loop(0, blocks, unroll=6)
    def _(block):
        flow = [wind[c, rows_of(block), :] for c in range(2)]
        for c, (east, north) in enumerate(derivatives(second, block)):
            third[c, rows_of(block), :] = -flow[c] - 0.25 * (flow[0] * east + flow[1] * north)

    @pl.loop(0, blocks, unroll=6)
    def _(block):
        flow = [wind[c, rows_of(block), :] for c in range(2)]
        for c, (east, north) in enumerate(derivatives(third, block)):
            fourth = -flow[c] - 0.5 * (flow[0] * east + flow[1] * north)
            both = second[c, rows_of(block), :] + third[c, rows_of(block), :]
            shift[c, rows_of(block), :] = (2.0 * both + (fourth - flow[c])) * (1.0 / 6.0)

    quarter = window.width // 4 // SUB

    def entries(out_ref, base):
        @pl.loop(0, quarter, unroll=4)
        def _(block):
            (e0, n0), (e1, n1) = derivatives(shift, base + block + 1)
            g_xx, g_xy, g_yx, g_yy = 1.0 + 0.5 * e0, 0.5 * n0, 0.5 * e1, 1.0 + 0.5 * n1
            out_ref[0, rows_of(block), :] = g_xx * g_xx + g_yx * g_yx
            out_ref[1, rows_of(block), :] = g_xx * g_xy + g_yx * g_yy
            out_ref[2, rows_of(block), :] = g_xy * g_xy + g_yy * g_yy

    for out_ref, (a, b) in zip(out_refs, QUARTERS):
        entries(out_ref, (2 * (core + a - 2 * core * a) + (side + b - 2 * side * b)) * quarter)


QUARTERS = ((0, 0), (0, 1), (1, 0), (1, 1))


def window_tensor(window, place, local, remote, table, waits, carry):
    depth = local.shape[2]
    vmem = pl.BlockSpec(memory_space=pltpu.VMEM)
    in_specs = [
        pl.BlockSpec(memory_space=pltpu.SMEM),
        pl.BlockSpec(memory_space=pl.ANY),
        vmem,
        pl.BlockSpec(memory_space=pl.ANY),
    ]
    in_specs += [pl.BlockSpec(memory_space=pl.ANY)] * len(waits)
    operands = [place, local, remote, table, *waits]
    if not window.first:
        in_specs.append(vmem)
        operands.append(carry)
    out_shape = [jax.ShapeDtypeStruct((3, window.width // 4, NLON), jnp.float32)] * 4
    if not window.last:
        out_shape.append(jax.ShapeDtypeStruct((2, 2 * SUB, NLON), jnp.float32))
    field = pltpu.VMEM((2, window.extended, NLON), jnp.float32)
    lhs_shape = (2, 2 * window.rows, depth)
    out = pl.pallas_call(
        functools.partial(window_kernel, window, depth, len(waits)),
        out_shape=out_shape,
        in_specs=in_specs,
        out_specs=[vmem] * len(out_shape),
        scratch_shapes=[
            pltpu.VMEM(table.shape, table.dtype),
            pltpu.VMEM((2, window.rows, depth), jnp.float32),
            pltpu.VMEM(lhs_shape, jnp.bfloat16),
            pltpu.VMEM(lhs_shape, jnp.bfloat16),
            field,
            field,
            field,
            field,
            pltpu.SemaphoreType.DMA((2,)),
        ],
        compiler_params=pltpu.CompilerParams(vmem_limit_bytes=2 * VMEM_LIMIT),
        cost_estimate=pl.CostEstimate(
            flops=KERNEL_WORK * 3 * 2 * 2 * window.rows * depth * NLON,
            transcendentals=0,
            bytes_accessed=2 * table.size + 4 * window.rows * depth * 4 + 12 * window.width * NLON,
        ),
        name="window_tensor",
    )(*operands)
    return out[:4], (None if window.last else out[4])


def pairs(members, bit):
    return [(member, member ^ bit) for member in range(members)]


def by_levels(coeffs):
    spec = coeffs[0]
    levels, _, parts, waves_local, nlat = spec.shape
    members = lax.axis_size("mem")
    band = lax.axis_index("band").astype(jnp.int32)
    member = lax.axis_index("mem").astype(jnp.int32)
    place = jnp.stack([band, member % 2, member // 2 % 2])
    spec = spec.reshape(levels, 2, parts * waves_local, nlat)
    windows = plan(nlat, [LANE] * (nlat // LANE))
    table = jnp.asarray(wave_table(levels, waves_local))
    swap = [(0, 1), (1, 0)]

    lead = windows[0].rows
    outgoing = rows_first(spec, 1 - band, choose(1 - band, (nlat // LANE - 2, 0)), 2 * LANE)
    piece = lax.dynamic_slice_in_dim(outgoing, choose(1 - band, (2 * LANE - lead, 0)), lead, axis=1)
    remotes = [lax.ppermute(piece, "band", swap)]
    outgoing = rows_first(spec, 1 - band, 0, nlat)
    outgoing = [
        lax.dynamic_slice_in_dim(outgoing, choose(1 - band, window.row_at), window.rows, axis=1) for window in windows
    ]

    def fetch_rows(k, waits):
        piece = gated(outgoing[k], waits) if waits else outgoing[k]
        remotes.append(lax.ppermute(piece, "band", swap))
        return piece

    fetch_rows(1, [])
    local = rows_first(spec, band, 0, nlat)

    bits = [1 << n for n in range(members.bit_length() - 1)]

    def halved(parts_of, bit):
        half = parts_of[0].shape[1] // 2
        mine = (member // bit) % 2

        def total(which):
            return sum(lax.dynamic_slice_in_dim(part, which * half, half, axis=1) for part in parts_of[:2])

        leaves = total(1 - mine)
        return [total(mine), lax.ppermute(leaves, "mem", pairs(members, bit)), leaves]

    def advanced(parts_of, bit):
        if len(parts_of) == 3:
            return halved(parts_of, bit)
        keep, leaves, keep_more, leaves_more = parts_of
        leaves = leaves + leaves_more
        return [keep + keep_more, lax.ppermute(leaves, "mem", pairs(members, bit)), leaves]

    def doubled(part, bit):
        beside = lax.ppermute(part, "mem", pairs(members, bit))
        mine = (member // bit) % 2
        return jnp.where(mine == 0, jnp.concatenate([part, beside], axis=1), jnp.concatenate([beside, part], axis=1))

    def gathered(part):
        for bit in reversed(bits):
            part = doubled(part, bit)
        return part

    carry = None
    sums = []
    for k, window in enumerate(windows):
        waits = []
        if k + 2 < len(windows):
            waits.append(fetch_rows(k + 2, [remotes[k]] if carry is None else [remotes[k], carry]))
        for j in range(k - 1):
            sums[j] = advanced(sums[j], bits[k - 1 - j])
            waits.append(sums[j][-1])
        quarters, carry = window_tensor(window, place, local, remotes[k], table, waits, carry)
        first = lax.ppermute(quarters[3], "mem", pairs(members, bits[0]))
        second = lax.ppermute(quarters[2], "mem", pairs(members, bits[0]))
        sums.append([quarters[0], quarters[1], second, first])
    pieces = {"own": [], "both": [], "other": []}
    for k, window in enumerate(windows):
        for bit in bits[max(len(windows) - 1 - k, 1) :]:
            sums[k] = advanced(sums[k], bit)
        pieces[window.side].append(exponent_of(sums[k][0] + sums[k][1], members))

    other = lax.ppermute(jnp.stack(pieces["other"]), "band", swap)
    trades = []
    for m in range(members):
        for b in range(2):
            mate = (m, b) if m % 2 == b else (m ^ 1, 1 - b)
            trades.append((m * 2 + b, mate[0] * 2 + mate[1]))
    both = lax.ppermute(pieces["both"][0], ("mem", "band"), trades)

    early = gathered(jnp.concatenate([other, both[None]]))
    other, both = early[:-1], early[-1]
    middle = both.shape[0] // 2
    low, high = both[:middle], both[middle:]
    rest = jnp.zeros((nlat // 2 - middle, NLON), jnp.float32)
    down = jnp.stack([jnp.concatenate([rest, low]), jnp.concatenate([*other, high])])
    up = jnp.stack([jnp.concatenate([low, *other[::-1]]), jnp.concatenate([high, rest])])
    out = jnp.where(band == 0, down, up)

    own = gathered(jnp.stack(pieces["own"]))
    for k, block in enumerate(own):
        width = block.shape[0]
        row = choose(band, (nlat // 2 - middle - (k + 1) * width, middle + k * width))
        out = lax.dynamic_update_slice(out, block[None], (band, row.astype(jnp.int32), jnp.int32(0)))
    return out


def per_device(coeffs):
    _, levels, _, _, _, nlat = coeffs.shape
    members = lax.axis_size("mem")
    rows = nlat // lax.axis_size("band")
    if coeffs.shape[4] == 5 * LANE // 2 and levels == lax.axis_size("band") == 2 and members == 16 and nlat % (2 * LANE) == LANE and rows > LANE:
        return by_levels(coeffs)
    return by_rows(coeffs)


def solution(mesh):
    placed = (P("mem", None, None, None, "band", None),)
    return jax.shard_map(
        per_device, mesh=mesh, in_specs=placed, out_specs=P(None, "band", None), check_vma=False
    )
```

```python
import functools
import math

import jax
import jax.numpy as jnp
import ml_dtypes
import numpy as np
from jax import lax
from jax.experimental import pallas as pl
from jax.experimental.pallas import tpu as pltpu
from jax.sharding import PartitionSpec as P

NLON = 1280
STEPS = 1
SUB = 8
LANE = 128
VMEM_LIMIT = 60 * 1024 * 1024
KERNEL_WORK = 8


def padded(cells, sides, width):
    for axis, dim in sides:
        count = lax.axis_size(axis)
        ends = count - 1
        head = lax.slice_in_dim(cells, 0, width, axis=dim)
        tail = lax.slice_in_dim(cells, cells.shape[dim] - width, cells.shape[dim], axis=dim)
        cells = jnp.concatenate(
            [
                lax.ppermute(tail, axis, [(i, (i + 1) % count) for i in range(ends)]),
                cells,
                lax.ppermute(head, axis, [((i + 1) % count, i) for i in range(ends)]),
            ],
            axis=dim,
        )
    return cells


def slope(extended, winds):
    center = extended[:, 1:-1]
    north = (extended[:, 2:] - extended[:, :-2]) * 0.5
    east = (jnp.roll(center, -1, 2) - jnp.roll(center, 1, 2)) * 0.5
    return -winds - (winds[0] * east + winds[1] * north)


def rimmed(field):
    return padded(field, (("band", 1),), 1)


def tensor(extended):
    center = extended[:, 1:-1]
    north = (extended[:, 2:] - extended[:, :-2]) * 0.5
    east = (jnp.roll(center, -1, 2) - jnp.roll(center, 1, 2)) * 0.5
    g_xx = 1.0 + east[0]
    g_xy = north[0]
    g_yx = east[1]
    g_yy = 1.0 + north[1]
    return jnp.stack(
        [g_xx * g_xx + g_yx * g_yx, g_xx * g_xy + g_yx * g_yy, g_xy * g_xy + g_yy * g_yy]
    )


def integrate(shift, flow, extend):
    first = slope(extend(shift), flow)
    second = slope(extend(0.5 * first), flow)
    third = slope(extend(0.5 * second), flow)
    fourth = slope(extend(third), flow)
    return (first + 2.0 * second + 2.0 * third + fourth) / 6.0


def exponent_of(summed, members):
    mean = summed / members
    first, cross, second = (mean[..., 0, :, :], mean[..., 1, :, :], mean[..., 2, :, :])
    half = (first + second) * 0.5
    differ = (first - second) * 0.5
    largest = half + jnp.sqrt(differ * differ + cross * cross)
    return jnp.log(largest + 1e-06) / (2.0 * STEPS)


def by_rows(coeffs):
    spec = coeffs[0]
    levels = spec.shape[0]
    nlat = spec.shape[4]
    waves = spec.shape[3] * lax.axis_size("band")
    members = lax.axis_size("mem")
    stacked = spec.reshape(levels * 2, 2, spec.shape[3], nlat)
    wave_index = lax.iota(jnp.int32, waves)
    column = lax.iota(jnp.int32, NLON)
    phase = wave_index[:, None] * column[None, :] % NLON
    angle = phase.astype(jnp.float32) * (2.0 * math.pi / NLON)
    weight = jnp.where(wave_index == 0, 1.0, 2.0).astype(jnp.float32)[:, None]
    table = jnp.stack([weight * jnp.cos(angle), -weight * jnp.sin(angle)], axis=0)
    winds = jnp.einsum(
        "crwh,rwn->chn",
        lax.all_to_all(stacked, "band", split_axis=3, concat_axis=2, tiled=True),
        table,
        precision=lax.Precision.HIGHEST,
        preferred_element_type=jnp.float32,
    )
    height = winds.shape[1]
    winds = winds.reshape(levels, 2, height, NLON)
    partials = []
    for level in range(levels):
        flow = winds[level]
        shift = integrate(jnp.zeros_like(flow), flow, rimmed)
        partials.append(tensor(rimmed(shift)))
    summed = lax.psum_scatter(jnp.stack(partials), "mem", scatter_dimension=3, tiled=True)
    return lax.all_gather(exponent_of(summed, members), "mem", axis=2, tiled=True)


def by_parity(waves_local):
    half = waves_local // 2
    whole = 2 * LANE - half
    runs = []
    for parity in range(2):
        runs += [(parity, half, 2), (waves_local + parity, whole, 2)]
    for parity in range(2):
        runs.append((waves_local + parity + 2 * whole, half - whole, 2))
    return runs


@functools.lru_cache(maxsize=None)
def wave_table(bands, waves_local):
    order = np.concatenate([start + step * np.arange(count) for start, count, step in by_parity(waves_local)])
    wave, part = order % waves_local, order // waves_local
    wave = wave[None, :] + waves_local * np.arange(bands)[:, None]
    part = np.broadcast_to(part, wave.shape)
    cut = [0, 2 * LANE, 4 * LANE, 4 * LANE + LANE // 2, 5 * LANE]
    result = []
    for parity in range(2):
        picks = [(band, slice(cut[parity], cut[parity + 1])) for band in range(bands)]
        picks += [(band, slice(cut[parity + 2], cut[parity + 3])) for band in range(bands)]
        waves = np.concatenate([wave[pick] for pick in picks])
        parts = np.concatenate([part[pick] for pick in picks])
        phase = (waves[:, None] * np.arange(NLON // 2)[None, :]) % NLON
        angle = phase.astype(np.float64) * (2.0 * np.pi / NLON)
        weight = np.where(waves == 0, 1.0, 2.0)[:, None]
        table = weight * np.where(parts[:, None] == 0, np.cos(angle), -np.sin(angle))
        high = table.astype(ml_dtypes.bfloat16)
        result += [high, (table - high.astype(np.float64)).astype(ml_dtypes.bfloat16)]
    return np.stack(result)


class Window:
    def __init__(self, index, count):
        self.first = index == 0
        self.last = index == count - 1
        self.index = index
        self.width = LANE
        self.extended = LANE + 2 * SUB
        self.main = LANE if self.first else LANE - SUB
        self.rim = 0 if self.last else SUB
        self.rows = self.main + self.rim
        up = SUB if self.first else 2 * SUB
        self.place = (self.extended - up - self.rows, up)
        self.side = "other" if 2 * (index + 1) <= count else "own" if 2 * index >= count else "both"


def choose(band, pair):
    return jnp.where(band == 0, pair[0], pair[1])


def multiple(value, of):
    return pl.multiple_of(value.astype(jnp.int32), of)


def pieces_kernel(windows, slots, count, level_ref, spec_ref, *refs):
    out_refs, (taken, turned, in_sems, out_sems) = refs[: len(windows)], refs[len(windows) :]
    level = level_ref[0]
    runs = by_parity(spec_ref.shape[2] // 2)

    def arrival(c, n):
        tile = choose(level, (count - 1 - slots[n], slots[n]))
        lanes = pl.ds(multiple(tile * LANE, LANE), LANE)
        return pltpu.make_async_copy(spec_ref.at[level, c, :, lanes], taken.at[c, n], in_sems.at[c, n])

    def departures(c, k):
        window, n = windows[k], slots.index(windows[k].index)
        rows = pl.ds(multiple(choose(level, (0, LANE - window.main)), SUB), window.main)
        at = pl.ds(multiple(choose(level, (window.rim, 0)), SUB), window.main)
        yield pltpu.make_async_copy(turned.at[c, n, rows], out_refs[k].at[c, at], out_sems.at[k, c, 0])
        if window.rim:
            rows = pl.ds(multiple(choose(level, (LANE - SUB, 0)), SUB), SUB)
            at = pl.ds(multiple(choose(level, (0, window.main)), SUB), SUB)
            yield pltpu.make_async_copy(turned.at[c, n + 1, rows], out_refs[k].at[c, at], out_sems.at[k, c, 1])

    for n in range(len(slots)):
        for c in range(2):
            arrival(c, n).start()
    for n in range(len(slots)):
        for c in range(2):
            arrival(c, n).wait()
            turned[c, n] = jnp.concatenate([taken[c, n, pl.ds(start, rows, step), :] for start, rows, step in runs]).T
        for k, window in enumerate(windows):
            if slots[n] == window.index + (1 if window.rim else 0):
                for c in range(2):
                    for copy in departures(c, k):
                        copy.start()
    for k in range(len(windows)):
        for c in range(2):
            for copy in departures(c, k):
                copy.wait()


def pieces_of(spec, level, windows, count):
    depth = spec.shape[2]
    slots = sorted({w.index for w in windows} | {w.index + 1 for w in windows if w.rim})
    return pl.pallas_call(
        functools.partial(pieces_kernel, windows, slots, count),
        in_specs=[pl.BlockSpec(memory_space=pltpu.SMEM), pl.BlockSpec(memory_space=pl.ANY)],
        out_specs=[pl.BlockSpec(memory_space=pl.ANY)] * len(windows),
        out_shape=[jax.ShapeDtypeStruct((2, w.rows, depth), jnp.float32) for w in windows],
        scratch_shapes=[
            pltpu.VMEM((2, len(slots), depth, LANE), jnp.float32),
            pltpu.VMEM((2, len(slots), LANE, depth), jnp.float32),
            pltpu.SemaphoreType.DMA((2, len(slots))),
            pltpu.SemaphoreType.DMA((len(windows), 2, 2)),
        ],
        compiler_params=pltpu.CompilerParams(vmem_limit_bytes=VMEM_LIMIT),
        cost_estimate=pl.CostEstimate(
            flops=0, transcendentals=0, bytes_accessed=4 * 2 * len(slots) * LANE * depth * 4
        ),
        name="pieces_of",
    )(level.reshape(1), spec)


def gate_kernel(*refs):
    pass


def gated(part, waits):
    return pl.pallas_call(
        gate_kernel,
        in_specs=[pl.BlockSpec(memory_space=pl.ANY)] * (1 + len(waits)),
        out_specs=pl.BlockSpec(memory_space=pl.ANY),
        out_shape=jax.ShapeDtypeStruct(part.shape, part.dtype),
        input_output_aliases={0: 0},
        cost_estimate=pl.CostEstimate(flops=0, transcendentals=0, bytes_accessed=1024),
        name="gated",
    )(part, *waits)


def east_of(x):
    return pltpu.roll(x, NLON - 1, axis=1) - pltpu.roll(x, 1, axis=1)


def north_of(before, here, after):
    row = lax.broadcasted_iota(jnp.int32, here.shape, 0)
    above = jnp.where(row == SUB - 1, pltpu.roll(after, SUB - 1, axis=0), pltpu.roll(here, SUB - 1, axis=0))
    below = jnp.where(row == 0, pltpu.roll(before, 1, axis=0), pltpu.roll(here, 1, axis=0))
    return above - below


def window_kernel(window, depth, waits, *refs):
    refs = list(refs)
    place_ref, local_ref, remote_ref, table_ref = refs[:4]
    refs = refs[4 + waits :]
    carry_ref = None if window.first else refs.pop(0)
    out_refs = [refs.pop(0) for _ in range(4)]
    carried_ref = None if window.last else refs.pop(0)
    table, lhs_high, lhs_low, wind, second, third, shift, results, carried, table_sem, out_sems = refs
    band, core, side = place_ref[0], place_ref[1], place_ref[2]
    rows, extended = window.rows, window.extended

    def at(pair):
        return multiple(choose(band, pair), SUB)

    tables = pltpu.make_async_copy(table_ref, table, table_sem)
    tables.start()
    lane = lax.broadcasted_iota(jnp.int32, (rows, LANE), 1)
    even, odd = [], []
    for c in range(2):
        mine, theirs = local_ref[c], remote_ref[c]
        low, high = jnp.where(band == 0, mine, theirs), jnp.where(band == 0, theirs, mine)
        low_rest, high_rest = low[:, 4 * LANE :], high[:, 4 * LANE :]
        turn = functools.partial(pltpu.roll, shift=LANE // 2, axis=1)
        even_rest = jnp.where(lane < LANE // 2, low_rest, turn(high_rest))
        odd_rest = jnp.where(lane < LANE // 2, turn(low_rest), high_rest)
        even.append(jnp.concatenate([low[:, : 2 * LANE], high[:, : 2 * LANE], even_rest], axis=1))
        odd.append(jnp.concatenate([low[:, 2 * LANE : 4 * LANE], high[:, 2 * LANE : 4 * LANE], odd_rest], axis=1))
    for parity, parts in enumerate((even, odd)):
        lhs = jnp.concatenate(parts)
        lhs_high[parity] = lhs.astype(jnp.bfloat16)
        lhs_low[parity] = (lhs - lhs_high[parity].astype(jnp.float32)).astype(jnp.bfloat16)
    tables.wait()

    place = at(window.place)
    if window.first or window.last:
        for c in range(2):
            if window.first:
                wind[c, pl.ds(at((extended - SUB, 0)), SUB), :] = jnp.zeros((SUB, NLON), jnp.float32)
            if window.last:
                wind[c, pl.ds(at((0, extended - SUB)), SUB), :] = jnp.zeros((SUB, NLON), jnp.float32)
    if not window.first:
        for c in range(2):
            wind[c, pl.ds(at((extended - 2 * SUB, 0)), 2 * SUB), :] = carry_ref[c]

    dot = functools.partial(jnp.dot, preferred_element_type=jnp.float32)
    for start in range(0, NLON // 2, 2 * LANE):
        stop = min(start + 2 * LANE, NLON // 2)
        columns = slice(start, stop)
        sums = []
        for parity in range(2):
            total = dot(lhs_high[parity], table[2 * parity, :, columns])
            total += dot(lhs_low[parity], table[2 * parity, :, columns])
            total += dot(lhs_high[parity], table[2 * parity + 1, :, columns])
            sums.append(total)
        for c in range(2):
            even_sum, odd_sum = (total[c * rows : (c + 1) * rows] for total in sums)
            wind[c, pl.ds(place, rows), start:stop] = even_sum + odd_sum
            wind[c, pl.ds(place, rows), NLON // 2 + start : NLON // 2 + stop] = even_sum - odd_sum

    if not window.last:
        for c in range(2):
            carried[c] = wind[c, pl.ds(at((0, extended - 2 * SUB)), 2 * SUB), :]
        carry_on = pltpu.make_async_copy(carried, carried_ref, out_sems.at[4])
        carry_on.start()

    blocks = extended // SUB

    def rows_of(block):
        return pl.ds(pl.multiple_of(block * SUB, SUB), SUB)

    def derivatives(field, block):
        before, after = jnp.maximum(block - 1, 0), jnp.minimum(block + 1, blocks - 1)
        result = []
        for c in range(2):
            here = field[c, rows_of(block), :]
            result.append((east_of(here), north_of(field[c, rows_of(before), :], here, field[c, rows_of(after), :])))
        return result

    @pl.loop(0, blocks, unroll=6)
    def _(block):
        flow = [wind[c, rows_of(block), :] for c in range(2)]
        for c, (east, north) in enumerate(derivatives(wind, block)):
            second[c, rows_of(block), :] = 0.25 * (flow[0] * east + flow[1] * north) - flow[c]

    @pl.loop(0, blocks, unroll=6)
    def _(block):
        flow = [wind[c, rows_of(block), :] for c in range(2)]
        for c, (east, north) in enumerate(derivatives(second, block)):
            third[c, rows_of(block), :] = -flow[c] - 0.25 * (flow[0] * east + flow[1] * north)

    @pl.loop(0, blocks, unroll=6)
    def _(block):
        flow = [wind[c, rows_of(block), :] for c in range(2)]
        for c, (east, north) in enumerate(derivatives(third, block)):
            fourth = -flow[c] - 0.5 * (flow[0] * east + flow[1] * north)
            both = second[c, rows_of(block), :] + third[c, rows_of(block), :]
            shift[c, rows_of(block), :] = (2.0 * both + (fourth - flow[c])) * (1.0 / 6.0)

    quarter = window.width // 4 // SUB

    def entries(out, base):
        @pl.loop(0, quarter, unroll=4)
        def _(block):
            (e0, n0), (e1, n1) = derivatives(shift, base + block + 1)
            g_xx, g_xy, g_yx, g_yy = 1.0 + 0.5 * e0, 0.5 * n0, 0.5 * e1, 1.0 + 0.5 * n1
            out[0, rows_of(block), :] = g_xx * g_xx + g_yx * g_yx
            out[1, rows_of(block), :] = g_xx * g_xy + g_yx * g_yy
            out[2, rows_of(block), :] = g_xy * g_xy + g_yy * g_yy

    copies = []
    for n, (a, b) in reversed(list(enumerate(QUARTERS))):
        entries(results.at[n], (2 * (core + a - 2 * core * a) + (side + b - 2 * side * b)) * quarter)
        copies.append(pltpu.make_async_copy(results.at[n], out_refs[n], out_sems.at[n]))
        copies[-1].start()
    for copy in copies:
        copy.wait()
    if not window.last:
        carry_on.wait()


QUARTERS = ((0, 0), (0, 1), (1, 0), (1, 1))


def window_tensor(window, place, local, remote, table, waits, carry):
    depth = local.shape[2]
    vmem = pl.BlockSpec(memory_space=pltpu.VMEM)
    in_specs = [
        pl.BlockSpec(memory_space=pltpu.SMEM),
        vmem,
        vmem,
        pl.BlockSpec(memory_space=pl.ANY),
    ]
    in_specs += [pl.BlockSpec(memory_space=pl.ANY)] * len(waits)
    operands = [place, local, remote, table, *waits]
    if not window.first:
        in_specs.append(vmem)
        operands.append(carry)
    out_shape = [jax.ShapeDtypeStruct((3, window.width // 4, NLON), jnp.float32)] * 4
    if not window.last:
        out_shape.append(jax.ShapeDtypeStruct((2, 2 * SUB, NLON), jnp.float32))
    field = pltpu.VMEM((2, window.extended, NLON), jnp.float32)
    lhs_shape = (2, 2 * window.rows, depth)
    out = pl.pallas_call(
        functools.partial(window_kernel, window, depth, len(waits)),
        out_shape=out_shape,
        in_specs=in_specs,
        out_specs=[pl.BlockSpec(memory_space=pl.ANY)] * len(out_shape),
        scratch_shapes=[
            pltpu.VMEM(table.shape, table.dtype),
            pltpu.VMEM(lhs_shape, jnp.bfloat16),
            pltpu.VMEM(lhs_shape, jnp.bfloat16),
            field,
            field,
            field,
            field,
            pltpu.VMEM((4, 3, window.width // 4, NLON), jnp.float32),
            pltpu.VMEM((2, 2 * SUB, NLON), jnp.float32),
            pltpu.SemaphoreType.DMA,
            pltpu.SemaphoreType.DMA((5,)),
        ],
        compiler_params=pltpu.CompilerParams(vmem_limit_bytes=VMEM_LIMIT),
        cost_estimate=pl.CostEstimate(
            flops=KERNEL_WORK * 3 * 2 * 2 * window.rows * depth * NLON,
            transcendentals=0,
            bytes_accessed=2 * table.size + 4 * window.rows * depth * 4 + 12 * window.width * NLON,
        ),
        name="window_tensor",
    )(*operands)
    return out[:4], (None if window.last else out[4])


def pairs(members, bit):
    return [(member, member ^ bit) for member in range(members)]


def put_kernel(count, place_ref, *refs):
    parts, out_ref, sem = refs[:4], refs[-2], refs[-1]
    core, side, along = place_ref[0], place_ref[1], place_ref[2]
    around = parts[0].shape[1]
    copies = []
    for a, part in enumerate(parts):
        half = core if a < 2 else 1 - core
        quarter = side if a % 2 == 0 else 1 - side
        for w in range(count):
            level, row = place_ref[3 + 4 * w + half], place_ref[5 + 4 * w + half]
            for n in range(around):
                piece = lax.rem(along + 1 + n, around)
                at = multiple(row + (quarter * around + piece) * SUB, SUB)
                copies.append(pltpu.make_async_copy(part.at[w, n], out_ref.at[level, pl.ds(at, SUB)], sem.at[a, w, n]))
                copies[-1].start()
    for copy in copies:
        copy.wait()


def put(out, shape, places, parts):
    count = parts[0].shape[0]
    extra = [] if out is None else [out]
    return pl.pallas_call(
        functools.partial(put_kernel, count),
        in_specs=[pl.BlockSpec(memory_space=pltpu.SMEM)]
        + [pl.BlockSpec(memory_space=pltpu.VMEM)] * 4
        + [pl.BlockSpec(memory_space=pl.ANY)] * len(extra),
        out_specs=pl.BlockSpec(memory_space=pl.ANY),
        out_shape=jax.ShapeDtypeStruct(shape, jnp.float32),
        input_output_aliases={5: 0} if extra else {},
        scratch_shapes=[pltpu.SemaphoreType.DMA((4, count, parts[0].shape[1]))],
        compiler_params=pltpu.CompilerParams(vmem_limit_bytes=VMEM_LIMIT),
        cost_estimate=pl.CostEstimate(flops=0, transcendentals=0, bytes_accessed=8 * 4 * parts[0].size),
        name="put",
    )(places.astype(jnp.int32), *parts, *extra)


def pairs(members, bit):
    return [(member, member ^ bit) for member in range(members)]


def by_levels(coeffs):
    spec = coeffs[0]
    levels, _, parts, waves_local, nlat = spec.shape
    members = lax.axis_size("mem")
    band = lax.axis_index("band").astype(jnp.int32)
    member = lax.axis_index("mem").astype(jnp.int32)
    core, side, along = member % 2, member // 2 % 2, member // 4
    place = jnp.stack([band, core, side])
    spec = spec.reshape(levels, 2, parts * waves_local, nlat)
    count = nlat // LANE
    windows = [Window(k, count) for k in range(count)]
    table = jnp.asarray(wave_table(levels, waves_local))
    swap = [(0, 1), (1, 0)]

    (piece,) = pieces_of(spec, 1 - band, windows[:1], count)
    remotes = [lax.ppermute(piece, "band", swap)]
    outgoing = [None, *pieces_of(spec, 1 - band, windows[1:], count)]

    def fetch_rows(k, waits):
        piece = gated(outgoing[k], waits) if waits else outgoing[k]
        remotes.append(lax.ppermute(piece, "band", swap))
        return piece

    fetch_rows(1, [])
    local = pieces_of(spec, band, windows, count)

    around = members // 4
    shifts = [[(m, (m + 4 * d) % members) for m in range(members)] for d in range(around)]

    def across(kept, passed, kept_more, passed_more):
        leaves = passed + passed_more
        return [kept, kept_more, lax.ppermute(leaves, "mem", pairs(members, 2))], leaves

    def onward(*parts_of):
        rows = parts_of[0].shape[1] // around

        def total(d):
            first = (along + d) % around * rows
            return sum(lax.dynamic_slice_in_dim(part, first, rows, axis=1) for part in parts_of)

        leaves = [total(d) for d in range(1, around)]
        return [total(0), *(lax.ppermute(leaves[d - 1], "mem", shifts[d]) for d in range(1, around))], leaves[0]

    carry = None
    sums, steps = [], [across, onward]
    for k, window in enumerate(windows):
        waits = []
        if k + 2 < count:
            waits.append(fetch_rows(k + 2, [remotes[k]] if carry is None else [remotes[k], carry]))
        for j in range(max(0, k - len(steps)), k):
            sums[j], left = steps[k - 1 - j](*sums[j])
            waits.append(left)
        quarters, carry = window_tensor(window, place, local[k], remotes[k], table, waits, carry)
        first = lax.ppermute(quarters[3], "mem", pairs(members, 1))
        second = lax.ppermute(quarters[2], "mem", pairs(members, 1))
        sums.append([quarters[0], quarters[1], second, first])
    pieces = {"own": [], "both": [], "other": []}
    for k, window in enumerate(windows):
        for step in steps[min(count - 1 - k, len(steps)) :]:
            sums[k], _ = step(*sums[k])
        pieces[window.side].append(exponent_of(sum(sums[k]), members))

    other = lax.ppermute(jnp.stack(pieces["other"]), "band", swap)
    trades = []
    for m in range(members):
        for b in range(2):
            mate = (m, b) if m % 2 == b else (m ^ 1, 1 - b)
            trades.append((m * 2 + b, mate[0] * 2 + mate[1]))
    both = lax.ppermute(pieces["both"][0], ("mem", "band"), trades)

    def gathered(stack):
        line = [lax.ppermute(stack, "mem", shifts[d]) for d in range(around - 1, 0, -1)] + [stack]
        mine = jnp.stack(line, axis=1)
        beside = lax.ppermute(mine, "mem", pairs(members, 2))
        return [mine, beside, *(lax.ppermute(part, "mem", pairs(members, 1)) for part in (mine, beside))]

    def places(rows):
        return jnp.stack([core, side, along] + [jnp.asarray(value, jnp.int32) for pair in rows for value in pair])

    height = nlat // 2
    half, far = LANE // 2, 1 - band
    early = []
    for k in range(len(pieces["other"])):
        row = choose(band, (k * LANE, height - (k + 1) * LANE))
        early.append((far, far, row, row + half))
    row = choose(band, (height - half, 0))
    early.append((0, 1, row, row))
    late = []
    for k in range(len(pieces["own"])):
        row = choose(band, (height - half - (k + 1) * LANE, half + k * LANE))
        late.append((band, band, row, row + half))
    shape = (levels, height, NLON)
    out = put(None, shape, places(early), gathered(jnp.concatenate([other, both[None]])))
    return put(out, shape, places(late), gathered(jnp.stack(pieces["own"])))


def per_device(coeffs):
    _, levels, _, _, _, nlat = coeffs.shape
    members = lax.axis_size("mem")
    rows = nlat // lax.axis_size("band")
    fits = coeffs.shape[4] == 5 * LANE // 2 and nlat % (2 * LANE) == LANE and rows > LANE
    if fits and levels == lax.axis_size("band") == 2 and members == 16:
        return by_levels(coeffs)
    return by_rows(coeffs)


def solution(mesh):
    placed = (P("mem", None, None, None, "band", None),)
    return jax.shard_map(
        per_device, mesh=mesh, in_specs=placed, out_specs=P(None, "band", None), check_vma=False
    )
```

```python
import functools
import math

import jax
import jax.numpy as jnp
import ml_dtypes
import numpy as np
from jax import lax
from jax.experimental import pallas as pl
from jax.experimental.pallas import tpu as pltpu
from jax.sharding import PartitionSpec as P

NLON = 1280
STEPS = 1
SUB = 8
LANE = 128
VMEM_LIMIT = 60 * 1024 * 1024
KERNEL_WORK = 8
LAG = 1


def padded(cells, sides, width):
    for axis, dim in sides:
        count = lax.axis_size(axis)
        ends = count - 1
        head = lax.slice_in_dim(cells, 0, width, axis=dim)
        tail = lax.slice_in_dim(cells, cells.shape[dim] - width, cells.shape[dim], axis=dim)
        cells = jnp.concatenate(
            [
                lax.ppermute(tail, axis, [(i, (i + 1) % count) for i in range(ends)]),
                cells,
                lax.ppermute(head, axis, [((i + 1) % count, i) for i in range(ends)]),
            ],
            axis=dim,
        )
    return cells


def slope(extended, winds):
    center = extended[:, 1:-1]
    north = (extended[:, 2:] - extended[:, :-2]) * 0.5
    east = (jnp.roll(center, -1, 2) - jnp.roll(center, 1, 2)) * 0.5
    return -winds - (winds[0] * east + winds[1] * north)


def rimmed(field):
    return padded(field, (("band", 1),), 1)


def tensor(extended):
    center = extended[:, 1:-1]
    north = (extended[:, 2:] - extended[:, :-2]) * 0.5
    east = (jnp.roll(center, -1, 2) - jnp.roll(center, 1, 2)) * 0.5
    g_xx = 1.0 + east[0]
    g_xy = north[0]
    g_yx = east[1]
    g_yy = 1.0 + north[1]
    return jnp.stack(
        [g_xx * g_xx + g_yx * g_yx, g_xx * g_xy + g_yx * g_yy, g_xy * g_xy + g_yy * g_yy]
    )


def integrate(shift, flow, extend):
    first = slope(extend(shift), flow)
    second = slope(extend(0.5 * first), flow)
    third = slope(extend(0.5 * second), flow)
    fourth = slope(extend(third), flow)
    return (first + 2.0 * second + 2.0 * third + fourth) / 6.0


def exponent_of(summed, members):
    mean = summed / members
    first, cross, second = (mean[..., 0, :, :], mean[..., 1, :, :], mean[..., 2, :, :])
    half = (first + second) * 0.5
    differ = (first - second) * 0.5
    largest = half + jnp.sqrt(differ * differ + cross * cross)
    return jnp.log(largest + 1e-06) / (2.0 * STEPS)


def by_rows(coeffs):
    spec = coeffs[0]
    levels = spec.shape[0]
    nlat = spec.shape[4]
    waves = spec.shape[3] * lax.axis_size("band")
    members = lax.axis_size("mem")
    stacked = spec.reshape(levels * 2, 2, spec.shape[3], nlat)
    wave_index = lax.iota(jnp.int32, waves)
    column = lax.iota(jnp.int32, NLON)
    phase = wave_index[:, None] * column[None, :] % NLON
    angle = phase.astype(jnp.float32) * (2.0 * math.pi / NLON)
    weight = jnp.where(wave_index == 0, 1.0, 2.0).astype(jnp.float32)[:, None]
    table = jnp.stack([weight * jnp.cos(angle), -weight * jnp.sin(angle)], axis=0)
    winds = jnp.einsum(
        "crwh,rwn->chn",
        lax.all_to_all(stacked, "band", split_axis=3, concat_axis=2, tiled=True),
        table,
        precision=lax.Precision.HIGHEST,
        preferred_element_type=jnp.float32,
    )
    height = winds.shape[1]
    winds = winds.reshape(levels, 2, height, NLON)
    partials = []
    for level in range(levels):
        flow = winds[level]
        shift = integrate(jnp.zeros_like(flow), flow, rimmed)
        partials.append(tensor(rimmed(shift)))
    summed = lax.psum_scatter(jnp.stack(partials), "mem", scatter_dimension=3, tiled=True)
    return lax.all_gather(exponent_of(summed, members), "mem", axis=2, tiled=True)


def by_parity(waves_local):
    half = waves_local // 2
    whole = 2 * LANE - half
    runs = []
    for parity in range(2):
        runs += [(parity, half, 2), (waves_local + parity, whole, 2)]
    for parity in range(2):
        runs.append((waves_local + parity + 2 * whole, half - whole, 2))
    return runs


@functools.lru_cache(maxsize=None)
def wave_table(bands, waves_local):
    order = np.concatenate([start + step * np.arange(count) for start, count, step in by_parity(waves_local)])
    wave, part = order % waves_local, order // waves_local
    wave = wave[None, :] + waves_local * np.arange(bands)[:, None]
    part = np.broadcast_to(part, wave.shape)
    cut = [0, 2 * LANE, 4 * LANE, 4 * LANE + LANE // 2, 5 * LANE]
    result = []
    for parity in range(2):
        picks = [(band, slice(cut[parity], cut[parity + 1])) for band in range(bands)]
        picks += [(band, slice(cut[parity + 2], cut[parity + 3])) for band in range(bands)]
        waves = np.concatenate([wave[pick] for pick in picks])
        parts = np.concatenate([part[pick] for pick in picks])
        phase = (waves[:, None] * np.arange(NLON // 2)[None, :]) % NLON
        angle = phase.astype(np.float64) * (2.0 * np.pi / NLON)
        weight = np.where(waves == 0, 1.0, 2.0)[:, None]
        table = weight * np.where(parts[:, None] == 0, np.cos(angle), -np.sin(angle))
        high = table.astype(ml_dtypes.bfloat16)
        result += [high, (table - high.astype(np.float64)).astype(ml_dtypes.bfloat16)]
    return np.stack(result)


class Piece:
    def __init__(self, index, count):
        self.index = index
        self.main = LANE if index == 0 else LANE - SUB
        self.rim = 0 if index == count - 1 else SUB
        self.rows = self.main + self.rim


class Window:
    def __init__(self, pieces, count):
        self.pieces = pieces
        self.first = pieces[0].index == 0
        self.last = pieces[-1].index == count - 1
        self.width = LANE * len(pieces)
        self.extended = self.width + 2 * SUB
        self.spread = self.extended // SUB
        self.places = []
        up = SUB if self.first else 2 * SUB
        for piece in pieces:
            self.places.append((self.extended - up - piece.rows, up))
            up += piece.rows
        self.side = "other" if 2 * (pieces[-1].index + 1) <= count else "own" if 2 * pieces[0].index >= count else "both"


def choose(band, pair):
    return jnp.where(band == 0, pair[0], pair[1])


def multiple(value, of):
    return pl.multiple_of(value.astype(jnp.int32), of)


def pieces_kernel(pieces, slots, count, level_ref, spec_ref, *refs):
    out_refs, (taken, turned, in_sems, out_sems) = refs[: len(pieces)], refs[len(pieces) :]
    level = level_ref[0]
    runs = by_parity(spec_ref.shape[2] // 2)

    def arrival(c, n):
        tile = choose(level, (count - 1 - slots[n], slots[n]))
        lanes = pl.ds(multiple(tile * LANE, LANE), LANE)
        return pltpu.make_async_copy(spec_ref.at[level, c, :, lanes], taken.at[c, n], in_sems.at[c, n])

    def departures(c, k):
        piece, n = pieces[k], slots.index(pieces[k].index)
        rows = pl.ds(multiple(choose(level, (0, LANE - piece.main)), SUB), piece.main)
        at = pl.ds(multiple(choose(level, (piece.rim, 0)), SUB), piece.main)
        yield pltpu.make_async_copy(turned.at[c, n, rows], out_refs[k].at[c, at], out_sems.at[k, c, 0])
        if piece.rim:
            rows = pl.ds(multiple(choose(level, (LANE - SUB, 0)), SUB), SUB)
            at = pl.ds(multiple(choose(level, (0, piece.main)), SUB), SUB)
            yield pltpu.make_async_copy(turned.at[c, n + 1, rows], out_refs[k].at[c, at], out_sems.at[k, c, 1])

    for n in range(len(slots)):
        for c in range(2):
            arrival(c, n).start()
    for n in range(len(slots)):
        for c in range(2):
            arrival(c, n).wait()
            turned[c, n] = jnp.concatenate([taken[c, n, pl.ds(start, rows, step), :] for start, rows, step in runs]).T
        for k, piece in enumerate(pieces):
            if slots[n] == piece.index + (1 if piece.rim else 0):
                for c in range(2):
                    for copy in departures(c, k):
                        copy.start()
    for k in range(len(pieces)):
        for c in range(2):
            for copy in departures(c, k):
                copy.wait()


def pieces_of(spec, level, pieces, count):
    depth = spec.shape[2]
    slots = sorted({w.index for w in pieces} | {w.index + 1 for w in pieces if w.rim})
    return pl.pallas_call(
        functools.partial(pieces_kernel, pieces, slots, count),
        in_specs=[pl.BlockSpec(memory_space=pltpu.SMEM), pl.BlockSpec(memory_space=pl.ANY)],
        out_specs=[pl.BlockSpec(memory_space=pl.ANY)] * len(pieces),
        out_shape=[jax.ShapeDtypeStruct((2, w.rows, depth), jnp.float32) for w in pieces],
        scratch_shapes=[
            pltpu.VMEM((2, len(slots), depth, LANE), jnp.float32),
            pltpu.VMEM((2, len(slots), LANE, depth), jnp.float32),
            pltpu.SemaphoreType.DMA((2, len(slots))),
            pltpu.SemaphoreType.DMA((len(pieces), 2, 2)),
        ],
        compiler_params=pltpu.CompilerParams(vmem_limit_bytes=VMEM_LIMIT),
        cost_estimate=pl.CostEstimate(
            flops=0, transcendentals=0, bytes_accessed=4 * 2 * len(slots) * LANE * depth * 4
        ),
        name="pieces_of",
    )(level.reshape(1), spec)


def gate_kernel(*refs):
    pass


def gated(part, waits):
    return pl.pallas_call(
        gate_kernel,
        in_specs=[pl.BlockSpec(memory_space=pl.ANY)] * (1 + len(waits)),
        out_specs=pl.BlockSpec(memory_space=pl.ANY),
        out_shape=jax.ShapeDtypeStruct(part.shape, part.dtype),
        input_output_aliases={0: 0},
        cost_estimate=pl.CostEstimate(flops=0, transcendentals=0, bytes_accessed=1024),
        name="gated",
    )(part, *waits)


def east_of(x):
    return pltpu.roll(x, NLON - 1, axis=1) - pltpu.roll(x, 1, axis=1)


def window_kernel(window, waits, *refs):
    refs = list(refs)
    pieces, extended, spread = window.pieces, window.extended, window.spread
    place_ref, table_ref = refs[:2]
    local_refs, remote_refs = refs[2 : 2 + len(pieces)], refs[2 + len(pieces) : 2 + 2 * len(pieces)]
    refs = refs[2 + 2 * len(pieces) + waits :]
    carry_ref = None if window.first else refs.pop(0)
    out_refs = [refs.pop(0) for _ in range(4)]
    carried_ref = None if window.last else refs.pop(0)
    table, lhs_high, lhs_low, natural, wind, second, third, shift, results, carried, table_sem, out_sems = refs
    band, core, side = place_ref[0], place_ref[1], place_ref[2]

    def at(pair):
        return multiple(choose(band, pair), SUB)

    tables = pltpu.make_async_copy(table_ref, table, table_sem)
    tables.start()
    even, odd = [], []
    for local_ref, remote_ref, piece in zip(local_refs, remote_refs, pieces):
        lane = lax.broadcasted_iota(jnp.int32, (piece.rows, LANE), 1)
        turn = functools.partial(pltpu.roll, shift=LANE // 2, axis=1)
        for c in range(2):
            mine, theirs = local_ref[c], remote_ref[c]
            low, high = jnp.where(band == 0, mine, theirs), jnp.where(band == 0, theirs, mine)
            low_rest, high_rest = low[:, 4 * LANE :], high[:, 4 * LANE :]
            even_rest = jnp.where(lane < LANE // 2, low_rest, turn(high_rest))
            odd_rest = jnp.where(lane < LANE // 2, turn(low_rest), high_rest)
            even.append(jnp.concatenate([low[:, : 2 * LANE], high[:, : 2 * LANE], even_rest], axis=1))
            odd.append(jnp.concatenate([low[:, 2 * LANE : 4 * LANE], high[:, 2 * LANE : 4 * LANE], odd_rest], axis=1))
    for parity, parts in enumerate((even, odd)):
        lhs = jnp.concatenate(parts)
        lhs_high[parity] = lhs.astype(jnp.bfloat16)
        lhs_low[parity] = (lhs - lhs_high[parity].astype(jnp.float32)).astype(jnp.bfloat16)

    tiles = NLON // LANE
    for c in range(2):
        for t in range(tiles):
            if window.first:
                natural[c, t, pl.ds(at((extended - SUB, 0)), SUB), :] = jnp.zeros((SUB, LANE), jnp.float32)
            else:
                natural[c, t, pl.ds(at((extended - 2 * SUB, 0)), 2 * SUB), :] = carry_ref[c, t]
            if window.last:
                natural[c, t, pl.ds(at((0, extended - SUB)), SUB), :] = jnp.zeros((SUB, LANE), jnp.float32)
    tables.wait()

    dot = functools.partial(jnp.dot, preferred_element_type=jnp.float32)
    for start in range(0, tiles // 2, 2):
        stop = min(start + 2, tiles // 2)
        columns = slice(start * LANE, stop * LANE)
        sums = []
        for parity in range(2):
            total = dot(lhs_high[parity], table[2 * parity, :, columns])
            total += dot(lhs_low[parity], table[2 * parity, :, columns])
            total += dot(lhs_high[parity], table[2 * parity + 1, :, columns])
            sums.append(total)
        row = 0
        for piece, place in zip(pieces, window.places):
            rows = pl.ds(at(place), piece.rows)
            for c in range(2):
                even_sum, odd_sum = (total[row : row + piece.rows] for total in sums)
                row += piece.rows
                for t in range(start, stop):
                    lanes = slice((t - start) * LANE, (t - start + 1) * LANE)
                    natural[c, t, rows, :] = even_sum[:, lanes] + odd_sum[:, lanes]
                    natural[c, tiles // 2 + t, rows, :] = even_sum[:, lanes] - odd_sum[:, lanes]

    if not window.last:
        for c in range(2):
            for t in range(tiles):
                carried[c, t] = natural[c, t, pl.ds(at((0, extended - 2 * SUB)), 2 * SUB), :]
        carry_on = pltpu.make_async_copy(carried, carried_ref, out_sems.at[4])
        carry_on.start()

    def closed(field):
        for c in range(2):
            field[c, 0] = pltpu.roll(field[c, spread], 1, axis=0)
            field[c, spread + 1] = pltpu.roll(field[c, 1], SUB - 1, axis=0)

    def slopes(field, block):
        return [(east_of(field[c, block]), field[c, block + 1] - field[c, block - 1]) for c in range(2)]

    def each_block(body):
        @pl.loop(0, spread // 2)
        def _(pair):
            body(2 * pair + 1)
            body(2 * pair + 2)

    def spread_out(block):
        for c in range(2):
            rows = pl.ds(block - 1, SUB, spread)
            wind[c, block] = jnp.concatenate([natural[c, t, rows, :] for t in range(tiles)], axis=1)

    each_block(spread_out)
    closed(wind)

    def second_slope(block):
        u, v = wind[0, block], wind[1, block]
        for c, (east, north) in enumerate(slopes(wind, block)):
            second[c, block] = 0.25 * (u * east + v * north) - (u, v)[c]

    each_block(second_slope)
    closed(second)

    def third_slope(block):
        u, v = wind[0, block], wind[1, block]
        for c, (east, north) in enumerate(slopes(second, block)):
            third[c, block] = -(u, v)[c] - 0.25 * (u * east + v * north)

    each_block(third_slope)
    closed(third)

    def whole_step(block):
        u, v = wind[0, block], wind[1, block]
        for c, (east, north) in enumerate(slopes(third, block)):
            fourth = -(u, v)[c] - 0.5 * (u * east + v * north)
            both = second[c, block] + third[c, block]
            shift[c, block] = (2.0 * both + (fourth - (u, v)[c])) * (1.0 / 6.0)

    each_block(whole_step)
    closed(shift)

    def entries(block):
        (e0, n0), (e1, n1) = slopes(shift, block)
        g_xx, g_xy, g_yx, g_yy = 1.0 + 0.5 * e0, 0.5 * n0, 0.5 * e1, 1.0 + 0.5 * n1
        rows = pl.ds(block - 1, SUB, spread)
        for n, entry in enumerate((g_xx * g_xx + g_yx * g_yx, g_xx * g_xy + g_yx * g_yy, g_xy * g_xy + g_yy * g_yy)):
            for t in range(tiles):
                results[n, t, rows, :] = entry[:, t * LANE : (t + 1) * LANE]

    each_block(entries)

    quarter = window.width // 4
    copies = []
    for n, (a, b) in enumerate(QUARTERS):
        base = (2 * (core + a - 2 * core * a) + (side + b - 2 * side * b)) * quarter + SUB
        rows = pl.ds(multiple(base, SUB), quarter)
        copies.append(pltpu.make_async_copy(results.at[:, :, rows], out_refs[n], out_sems.at[n]))
        copies[-1].start()
    for copy in copies:
        copy.wait()
    if not window.last:
        carry_on.wait()


QUARTERS = ((0, 0), (0, 1), (1, 0), (1, 1))


def window_tensor(window, place, table, local, remote, waits, carry):
    depth, tiles = local[0].shape[2], NLON // LANE
    vmem, hbm = pl.BlockSpec(memory_space=pltpu.VMEM), pl.BlockSpec(memory_space=pl.ANY)
    in_specs = [pl.BlockSpec(memory_space=pltpu.SMEM), hbm]
    in_specs += [vmem] * (len(local) + len(remote)) + [hbm] * len(waits)
    operands = [place, table, *local, *remote, *waits]
    if not window.first:
        in_specs.append(vmem)
        operands.append(carry)
    out_shape = [jax.ShapeDtypeStruct((3, tiles, window.width // 4, LANE), jnp.float32)] * 4
    carried = (2, tiles, 2 * SUB, LANE)
    if not window.last:
        out_shape.append(jax.ShapeDtypeStruct(carried, jnp.float32))
    field = pltpu.VMEM((2, window.spread + 2, SUB, NLON), jnp.float32)
    rows = sum(piece.rows for piece in window.pieces)
    lhs_shape = (2, 2 * rows, depth)
    out = pl.pallas_call(
        functools.partial(window_kernel, window, len(waits)),
        out_shape=out_shape,
        in_specs=in_specs,
        out_specs=[hbm] * len(out_shape),
        scratch_shapes=[
            pltpu.VMEM(table.shape, table.dtype),
            pltpu.VMEM(lhs_shape, jnp.bfloat16),
            pltpu.VMEM(lhs_shape, jnp.bfloat16),
            pltpu.VMEM((2, tiles, window.extended, LANE), jnp.float32),
            field,
            field,
            field,
            field,
            pltpu.VMEM((3, tiles, window.extended, LANE), jnp.float32),
            pltpu.VMEM(carried, jnp.float32),
            pltpu.SemaphoreType.DMA,
            pltpu.SemaphoreType.DMA((5,)),
        ],
        compiler_params=pltpu.CompilerParams(vmem_limit_bytes=VMEM_LIMIT),
        cost_estimate=pl.CostEstimate(
            flops=KERNEL_WORK * 3 * 2 * 2 * rows * depth * NLON,
            transcendentals=0,
            bytes_accessed=2 * table.size + 4 * rows * depth * 4 + 12 * window.width * NLON,
        ),
        name="window_tensor",
    )(*operands)
    return out[:4], (None if window.last else out[4])


def pairs(members, bit):
    return [(member, member ^ bit) for member in range(members)]


def by_levels(coeffs):
    spec = coeffs[0]
    levels, _, parts, waves_local, nlat = spec.shape
    members = lax.axis_size("mem")
    band = lax.axis_index("band").astype(jnp.int32)
    member = lax.axis_index("mem").astype(jnp.int32)
    core, side = member % 2, member // 2 % 2
    place = jnp.stack([band, core, side])
    spec = spec.reshape(levels, 2, parts * waves_local, nlat)
    count = nlat // LANE
    pieces = [Piece(k, count) for k in range(count)]
    windows = [Window(pieces[:2], count)] + [Window([piece], count) for piece in pieces[2:]]
    table = jnp.asarray(wave_table(levels, waves_local))
    swap = [(0, 1), (1, 0)]

    (outgoing,) = pieces_of(spec, 1 - band, pieces[:1], count)
    remotes = [lax.ppermute(outgoing, "band", swap)]
    outgoing = [None, *pieces_of(spec, 1 - band, pieces[1:], count)]

    def fetch_rows(k, waits):
        piece = gated(outgoing[k], waits) if waits else outgoing[k]
        remotes.append(lax.ppermute(piece, "band", swap))
        return piece

    fetch_rows(1, [])
    local = pieces_of(spec, band, pieces, count)

    bits = [1 << n for n in range(members.bit_length() - 1)]

    def halved(parts_of, bit):
        half = parts_of[0].shape[2] // 2
        mine = (member // bit) % 2

        def total(which):
            return sum(lax.dynamic_slice_in_dim(part, which * half, half, axis=2) for part in parts_of)

        leaves = total(1 - mine)
        return [total(mine), lax.ppermute(leaves, "mem", pairs(members, bit))], leaves

    def across(parts_of, bit):
        kept, passed, kept_more, passed_more = parts_of
        leaves = passed + passed_more
        return [kept, kept_more, lax.ppermute(leaves, "mem", pairs(members, bit))], leaves

    def advanced(parts_of, bit):
        return (across if len(parts_of) == 4 else halved)(parts_of, bit)

    def doubled(part, bit):
        beside = lax.ppermute(part, "mem", pairs(members, bit))
        mine = (member // bit) % 2
        return jnp.where(mine == 0, jnp.concatenate([part, beside], axis=0), jnp.concatenate([beside, part], axis=0))

    def gathered(part):
        for bit in reversed(bits):
            part = doubled(part, bit)
        return part

    carry = None
    sums, done = [], []
    for k, window in enumerate(windows):
        waits, last = [], window.pieces[-1].index
        while len(remotes) < min(last + 3, count):
            before = len(remotes) - 2
            waits.append(fetch_rows(len(remotes), [remotes[before]] if carry is None else [remotes[before], carry]))
        for j in range(k - LAG):
            sums[j], left = advanced(sums[j], bits[done[j]])
            done[j] += 1
            waits.append(left)
        here = [piece.index for piece in window.pieces]
        quarters, carry = window_tensor(
            window, place, table, [local[p] for p in here], [remotes[p] for p in here], waits, carry
        )
        first = lax.ppermute(quarters[3], "mem", pairs(members, bits[0]))
        second = lax.ppermute(quarters[2], "mem", pairs(members, bits[0]))
        sums.append([quarters[0], quarters[1], second, first])
        done.append(1)
    results = {}
    for k, window in enumerate(windows):
        for bit in bits[done[k] :]:
            sums[k], _ = advanced(sums[k], bit)
        summed = sum(sums[k])
        rows = summed.shape[2]
        summed = summed.transpose(0, 2, 1, 3).reshape(3, rows, NLON)
        results.setdefault(window.side, []).append(exponent_of(summed, members))

    (other,), (both,) = results["other"], results["both"]
    other = lax.ppermute(other, "band", swap)
    trades = []
    for m in range(members):
        for b in range(2):
            mate = (m, b) if m % 2 == b else (m ^ 1, 1 - b)
            trades.append((m * 2 + b, mate[0] * 2 + mate[1]))
    both = lax.ppermute(both, ("mem", "band"), trades)

    def whole(parts):
        heights = [part.shape[0] for part in parts]
        stack = jnp.concatenate(parts, axis=0)[None]
        stack = gathered(stack)
        cuts = np.cumsum([0] + heights)
        return [stack[:, cuts[n] : cuts[n + 1]].reshape(-1, NLON) for n in range(len(parts))]

    other, both = whole([other, both])
    middle = both.shape[0] // 2
    low, high = both[:middle], both[middle:]
    rest = jnp.zeros((nlat // 2 - middle, NLON), jnp.float32)
    down = jnp.stack([jnp.concatenate([rest, low]), jnp.concatenate([other, high])])
    up = jnp.stack([jnp.concatenate([low, other]), jnp.concatenate([high, rest])])
    out = jnp.where(band == 0, down, up)
    for k, block in enumerate(whole(results["own"])):
        width = block.shape[0]
        row = choose(band, (nlat // 2 - middle - (k + 1) * width, middle + k * width))
        out = lax.dynamic_update_slice(out, block[None], (band, row.astype(jnp.int32), jnp.int32(0)))
    return out


def per_device(coeffs):
    _, levels, _, _, _, nlat = coeffs.shape
    members = lax.axis_size("mem")
    rows = nlat // lax.axis_size("band")
    fits = coeffs.shape[4] == 5 * LANE // 2 and nlat % (2 * LANE) == LANE and rows > LANE
    if fits and levels == lax.axis_size("band") == 2 and members == 16:
        return by_levels(coeffs)
    return by_rows(coeffs)


def solution(mesh):
    placed = (P("mem", None, None, None, "band", None),)
    return jax.shard_map(
        per_device, mesh=mesh, in_specs=placed, out_specs=P(None, "band", None), check_vma=False
    )
```

```python
import functools
import math

import jax
import jax.numpy as jnp
import ml_dtypes
import numpy as np
from jax import lax
from jax.experimental import pallas as pl
from jax.experimental.pallas import tpu as pltpu
from jax.sharding import PartitionSpec as P

NLON = 1280
STEPS = 1
SUB = 8
LANE = 128
VMEM_LIMIT = 60 * 1024 * 1024
KERNEL_WORK = 8
GROUP = 9
AHEAD = ((), (0,), (1,), (2, 0))


def padded(cells, sides, width):
    for axis, dim in sides:
        count = lax.axis_size(axis)
        ends = count - 1
        head = lax.slice_in_dim(cells, 0, width, axis=dim)
        tail = lax.slice_in_dim(cells, cells.shape[dim] - width, cells.shape[dim], axis=dim)
        cells = jnp.concatenate(
            [
                lax.ppermute(tail, axis, [(i, (i + 1) % count) for i in range(ends)]),
                cells,
                lax.ppermute(head, axis, [((i + 1) % count, i) for i in range(ends)]),
            ],
            axis=dim,
        )
    return cells


def slope(extended, winds):
    center = extended[:, 1:-1]
    north = (extended[:, 2:] - extended[:, :-2]) * 0.5
    east = (jnp.roll(center, -1, 2) - jnp.roll(center, 1, 2)) * 0.5
    return -winds - (winds[0] * east + winds[1] * north)


def rimmed(field):
    return padded(field, (("band", 1),), 1)


def tensor(extended):
    center = extended[:, 1:-1]
    north = (extended[:, 2:] - extended[:, :-2]) * 0.5
    east = (jnp.roll(center, -1, 2) - jnp.roll(center, 1, 2)) * 0.5
    g_xx = 1.0 + east[0]
    g_xy = north[0]
    g_yx = east[1]
    g_yy = 1.0 + north[1]
    return jnp.stack(
        [g_xx * g_xx + g_yx * g_yx, g_xx * g_xy + g_yx * g_yy, g_xy * g_xy + g_yy * g_yy]
    )


def integrate(shift, flow, extend):
    first = slope(extend(shift), flow)
    second = slope(extend(0.5 * first), flow)
    third = slope(extend(0.5 * second), flow)
    fourth = slope(extend(third), flow)
    return (first + 2.0 * second + 2.0 * third + fourth) / 6.0


def exponent_of(summed, members):
    mean = summed / members
    first, cross, second = (mean[..., 0, :, :], mean[..., 1, :, :], mean[..., 2, :, :])
    half = (first + second) * 0.5
    differ = (first - second) * 0.5
    largest = half + jnp.sqrt(differ * differ + cross * cross)
    return jnp.log(largest + 1e-06) / (2.0 * STEPS)


def by_rows(coeffs):
    spec = coeffs[0]
    levels = spec.shape[0]
    nlat = spec.shape[4]
    waves = spec.shape[3] * lax.axis_size("band")
    members = lax.axis_size("mem")
    stacked = spec.reshape(levels * 2, 2, spec.shape[3], nlat)
    wave_index = lax.iota(jnp.int32, waves)
    column = lax.iota(jnp.int32, NLON)
    phase = wave_index[:, None] * column[None, :] % NLON
    angle = phase.astype(jnp.float32) * (2.0 * math.pi / NLON)
    weight = jnp.where(wave_index == 0, 1.0, 2.0).astype(jnp.float32)[:, None]
    table = jnp.stack([weight * jnp.cos(angle), -weight * jnp.sin(angle)], axis=0)
    winds = jnp.einsum(
        "crwh,rwn->chn",
        lax.all_to_all(stacked, "band", split_axis=3, concat_axis=2, tiled=True),
        table,
        precision=lax.Precision.HIGHEST,
        preferred_element_type=jnp.float32,
    )
    height = winds.shape[1]
    winds = winds.reshape(levels, 2, height, NLON)
    partials = []
    for level in range(levels):
        flow = winds[level]
        shift = integrate(jnp.zeros_like(flow), flow, rimmed)
        partials.append(tensor(rimmed(shift)))
    summed = lax.psum_scatter(jnp.stack(partials), "mem", scatter_dimension=3, tiled=True)
    return lax.all_gather(exponent_of(summed, members), "mem", axis=2, tiled=True)


def by_parity(waves_local):
    half = waves_local // 2
    whole = 2 * LANE - half
    runs = []
    for parity in range(2):
        runs += [(parity, half, 2), (waves_local + parity, whole, 2)]
    for parity in range(2):
        runs.append((waves_local + parity + 2 * whole, half - whole, 2))
    return runs


@functools.lru_cache(maxsize=None)
def wave_table(bands, waves_local):
    order = np.concatenate([start + step * np.arange(count) for start, count, step in by_parity(waves_local)])
    wave, part = order % waves_local, order // waves_local
    wave = wave[None, :] + waves_local * np.arange(bands)[:, None]
    part = np.broadcast_to(part, wave.shape)
    cut = [0, 2 * LANE, 4 * LANE, 4 * LANE + LANE // 2, 5 * LANE]
    result = []
    for parity in range(2):
        picks = [(band, slice(cut[parity], cut[parity + 1])) for band in range(bands)]
        picks += [(band, slice(cut[parity + 2], cut[parity + 3])) for band in range(bands)]
        waves = np.concatenate([wave[pick] for pick in picks])
        parts = np.concatenate([part[pick] for pick in picks])
        phase = (waves[:, None] * np.arange(NLON // 2)[None, :]) % NLON
        angle = phase.astype(np.float64) * (2.0 * np.pi / NLON)
        weight = np.where(waves == 0, 1.0, 2.0)[:, None]
        table = weight * np.where(parts[:, None] == 0, np.cos(angle), -np.sin(angle))
        high = table.astype(ml_dtypes.bfloat16)
        result += [high, (table - high.astype(np.float64)).astype(ml_dtypes.bfloat16)]
    return np.stack(result)


class Piece:
    def __init__(self, index, count):
        self.index = index
        self.main = LANE if index == 0 else LANE - SUB
        self.rim = 0 if index == count - 1 else SUB
        self.rows = self.main + self.rim


class Window:
    def __init__(self, pieces, count):
        self.pieces = pieces
        self.first = pieces[0].index == 0
        self.last = pieces[-1].index == count - 1
        self.width = LANE * len(pieces)
        self.extended = self.width + 2 * SUB
        self.places = []
        up = SUB if self.first else 2 * SUB
        for piece in pieces:
            self.places.append((self.extended - up - piece.rows, up))
            up += piece.rows
        self.side = "other" if 2 * (pieces[-1].index + 1) <= count else "own" if 2 * pieces[0].index >= count else "both"


def choose(band, pair):
    return jnp.where(band == 0, pair[0], pair[1])


def multiple(value, of):
    return pl.multiple_of(value.astype(jnp.int32), of)


def pieces_kernel(pieces, slots, count, level_ref, spec_ref, *refs):
    out_refs, (taken, turned, in_sems, out_sems) = refs[: len(pieces)], refs[len(pieces) :]
    level = level_ref[0]
    runs = by_parity(spec_ref.shape[2] // 2)

    def arrival(c, n):
        tile = choose(level, (count - 1 - slots[n], slots[n]))
        lanes = pl.ds(multiple(tile * LANE, LANE), LANE)
        return pltpu.make_async_copy(spec_ref.at[level, c, :, lanes], taken.at[c, n], in_sems.at[c, n])

    def departures(c, k):
        piece, n = pieces[k], slots.index(pieces[k].index)
        rows = pl.ds(multiple(choose(level, (0, LANE - piece.main)), SUB), piece.main)
        at = pl.ds(multiple(choose(level, (piece.rim, 0)), SUB), piece.main)
        yield pltpu.make_async_copy(turned.at[c, n, rows], out_refs[k].at[c, at], out_sems.at[k, c, 0])
        if piece.rim:
            rows = pl.ds(multiple(choose(level, (LANE - SUB, 0)), SUB), SUB)
            at = pl.ds(multiple(choose(level, (0, piece.main)), SUB), SUB)
            yield pltpu.make_async_copy(turned.at[c, n + 1, rows], out_refs[k].at[c, at], out_sems.at[k, c, 1])

    for n in range(len(slots)):
        for c in range(2):
            arrival(c, n).start()
    for n in range(len(slots)):
        for c in range(2):
            arrival(c, n).wait()
            turned[c, n] = jnp.concatenate([taken[c, n, pl.ds(start, rows, step), :] for start, rows, step in runs]).T
        for k, piece in enumerate(pieces):
            if slots[n] == piece.index + (1 if piece.rim else 0):
                for c in range(2):
                    for copy in departures(c, k):
                        copy.start()
    for k in range(len(pieces)):
        for c in range(2):
            for copy in departures(c, k):
                copy.wait()


def pieces_of(spec, level, pieces, count):
    depth = spec.shape[2]
    slots = sorted({w.index for w in pieces} | {w.index + 1 for w in pieces if w.rim})
    return pl.pallas_call(
        functools.partial(pieces_kernel, pieces, slots, count),
        in_specs=[pl.BlockSpec(memory_space=pltpu.SMEM), pl.BlockSpec(memory_space=pl.ANY)],
        out_specs=[pl.BlockSpec(memory_space=pl.ANY)] * len(pieces),
        out_shape=[jax.ShapeDtypeStruct((2, w.rows, depth), jnp.float32) for w in pieces],
        scratch_shapes=[
            pltpu.VMEM((2, len(slots), depth, LANE), jnp.float32),
            pltpu.VMEM((2, len(slots), LANE, depth), jnp.float32),
            pltpu.SemaphoreType.DMA((2, len(slots))),
            pltpu.SemaphoreType.DMA((len(pieces), 2, 2)),
        ],
        compiler_params=pltpu.CompilerParams(vmem_limit_bytes=VMEM_LIMIT),
        cost_estimate=pl.CostEstimate(
            flops=0, transcendentals=0, bytes_accessed=4 * 2 * len(slots) * LANE * depth * 4
        ),
        name="pieces_of",
    )(level.reshape(1), spec)


def gate_kernel(*refs):
    pass


def gated(part, waits):
    return pl.pallas_call(
        gate_kernel,
        in_specs=[pl.BlockSpec(memory_space=pl.ANY)] * (1 + len(waits)),
        out_specs=pl.BlockSpec(memory_space=pl.ANY),
        out_shape=jax.ShapeDtypeStruct(part.shape, part.dtype),
        input_output_aliases={0: 0},
        cost_estimate=pl.CostEstimate(flops=0, transcendentals=0, bytes_accessed=1024),
        name="gated",
    )(part, *waits)


def east_of(x):
    return pltpu.roll(x, NLON - 1, axis=1) - pltpu.roll(x, 1, axis=1)


def window_kernel(window, waits, *refs):
    refs = list(refs)
    pieces, extended = window.pieces, window.extended
    place_ref, table_ref = refs[:2]
    local_refs, remote_refs = refs[2 : 2 + len(pieces)], refs[2 + len(pieces) : 2 + 2 * len(pieces)]
    refs = refs[2 + 2 * len(pieces) + waits :]
    carry_ref = None if window.first else refs.pop(0)
    out_refs = [refs.pop(0) for _ in PARTS]
    carried_ref = None if window.last else refs.pop(0)
    table, lhs, wind, second, third, shift, results, carried, table_sem, out_sems = refs
    band, core, side = place_ref[0], place_ref[1], place_ref[2]
    half = lhs.shape[1] // 2

    def at(pair):
        return multiple(choose(band, pair), SUB)

    tables = pltpu.make_async_copy(table_ref, table, table_sem)
    tables.start()
    even, odd = [], []
    for local_ref, remote_ref, piece in zip(local_refs, remote_refs, pieces):
        lane = lax.broadcasted_iota(jnp.int32, (piece.rows, LANE), 1)
        turn = functools.partial(pltpu.roll, shift=LANE // 2, axis=1)
        for c in range(2):
            mine, theirs = local_ref[c], remote_ref[c]
            low, high = jnp.where(band == 0, mine, theirs), jnp.where(band == 0, theirs, mine)
            low_rest, high_rest = low[:, 4 * LANE :], high[:, 4 * LANE :]
            even_rest = jnp.where(lane < LANE // 2, low_rest, turn(high_rest))
            odd_rest = jnp.where(lane < LANE // 2, turn(low_rest), high_rest)
            even.append(jnp.concatenate([low[:, : 2 * LANE], high[:, : 2 * LANE], even_rest], axis=1))
            odd.append(jnp.concatenate([low[:, 2 * LANE : 4 * LANE], high[:, 2 * LANE : 4 * LANE], odd_rest], axis=1))
    for parity, parts in enumerate((even, odd)):
        whole = jnp.concatenate(parts)
        high = whole.astype(jnp.bfloat16)
        lhs[parity, :half] = high
        lhs[parity, half:] = (whole - high.astype(jnp.float32)).astype(jnp.bfloat16)

    for c in range(2):
        if window.first:
            wind[c, pl.ds(at((extended - SUB, 0)), SUB), :] = jnp.zeros((SUB, NLON), jnp.float32)
        else:
            wind[c, pl.ds(at((extended - 2 * SUB, 0)), 2 * SUB), :] = carry_ref[c]
        if window.last:
            wind[c, pl.ds(at((0, extended - SUB)), SUB), :] = jnp.zeros((SUB, NLON), jnp.float32)
    tables.wait()

    dot = functools.partial(jnp.dot, preferred_element_type=jnp.float32)
    for start in range(0, NLON // 2, 2 * LANE):
        stop = min(start + 2 * LANE, NLON // 2)
        sums = []
        for parity in range(2):
            both = dot(lhs[parity], table[2 * parity, :, start:stop])
            sums.append(both[:half] + both[half:] + dot(lhs[parity, :half], table[2 * parity + 1, :, start:stop]))
        row = 0
        for piece, place in zip(pieces, window.places):
            rows = pl.ds(at(place), piece.rows)
            for c in range(2):
                even_sum, odd_sum = (total[row : row + piece.rows] for total in sums)
                row += piece.rows
                wind[c, rows, start:stop] = even_sum + odd_sum
                wind[c, rows, NLON // 2 + start : NLON // 2 + stop] = even_sum - odd_sum

    if not window.last:
        for c in range(2):
            carried[c] = wind[c, pl.ds(at((0, extended - 2 * SUB)), 2 * SUB), :]
        carry_on = pltpu.make_async_copy(carried, carried_ref, out_sems.at[len(PARTS)])
        carry_on.start()

    blocks = extended // SUB

    def rows_of(block):
        return pl.ds(multiple(block * SUB, SUB), SUB)

    def slopes(field, first, number):
        row = lax.broadcasted_iota(jnp.int32, (SUB, NLON), 0)
        runs = []
        for c in range(2):
            here = [field[c, rows_of(first + n), :] for n in range(number)]
            before = field[c, rows_of(jnp.maximum(first - 1, 0)), :]
            after = field[c, rows_of(jnp.minimum(first + number, blocks - 1)), :]
            up = [pltpu.roll(x, SUB - 1, axis=0) for x in [*here, after]]
            down = [pltpu.roll(x, 1, axis=0) for x in [before, *here]]
            runs.append(
                [
                    (
                        east_of(here[n]),
                        jnp.where(row == SUB - 1, up[n + 1], up[n]) - jnp.where(row == 0, down[n], down[n + 1]),
                    )
                    for n in range(number)
                ]
            )
        return zip(*runs)

    def each_run(count, number, body):
        @pl.loop(0, count // number)
        def _(run):
            body(run * number, number)

    group = max(n for n in range(1, GROUP + 1) if blocks % n == 0)

    def second_slope(first, number):
        for n, pair in enumerate(slopes(wind, first, number)):
            flow = [wind[c, rows_of(first + n), :] for c in range(2)]
            for c, (east, north) in enumerate(pair):
                second[c, rows_of(first + n), :] = 0.25 * (flow[0] * east + flow[1] * north) - flow[c]

    def third_slope(first, number):
        for n, pair in enumerate(slopes(second, first, number)):
            flow = [wind[c, rows_of(first + n), :] for c in range(2)]
            for c, (east, north) in enumerate(pair):
                third[c, rows_of(first + n), :] = -flow[c] - 0.25 * (flow[0] * east + flow[1] * north)

    def whole_step(first, number):
        for n, pair in enumerate(slopes(third, first, number)):
            here = rows_of(first + n)
            flow = [wind[c, here, :] for c in range(2)]
            for c, (east, north) in enumerate(pair):
                fourth = -flow[c] - 0.5 * (flow[0] * east + flow[1] * north)
                both = second[c, here, :] + third[c, here, :]
                shift[c, here, :] = (2.0 * both + (fourth - flow[c])) * (1.0 / 6.0)

    for body in (second_slope, third_slope, whole_step):
        each_run(blocks, group, body)

    def entries(first, number):
        for n, ((e0, n0), (e1, n1)) in enumerate(slopes(shift, first + 1, number)):
            g_xx, g_xy, g_yx, g_yy = 1.0 + 0.5 * e0, 0.5 * n0, 0.5 * e1, 1.0 + 0.5 * n1
            here = rows_of(first + n)
            results[0, here, :] = g_xx * g_xx + g_yx * g_yx
            results[1, here, :] = g_xx * g_xy + g_yx * g_yy
            results[2, here, :] = g_xy * g_xy + g_yy * g_yy

    each_run(blocks - 2, 8, entries)

    quarter = window.width // 4
    copies = []
    for n, (a, b, p, of) in enumerate(PARTS):
        base = (2 * (core + a - 2 * core * a) + (side + b - 2 * side * b)) * quarter + p * (quarter // of)
        rows = pl.ds(multiple(base, SUB), quarter // of)
        copies.append(pltpu.make_async_copy(results.at[:, rows], out_refs[n], out_sems.at[n]))
        copies[-1].start()
    for copy in copies:
        copy.wait()
    if not window.last:
        carry_on.wait()


PARTS = ((0, 0, 0, 1), (0, 1, 0, 1), (1, 0, 0, 1), (1, 1, 0, 2), (1, 1, 1, 2))


def window_tensor(window, place, table, local, remote, waits, carry):
    depth = local[0].shape[2]
    vmem, hbm = pl.BlockSpec(memory_space=pltpu.VMEM), pl.BlockSpec(memory_space=pl.ANY)
    in_specs = [pl.BlockSpec(memory_space=pltpu.SMEM), hbm]
    in_specs += [vmem] * (len(local) + len(remote)) + [hbm] * len(waits)
    operands = [place, table, *local, *remote, *waits]
    if not window.first:
        in_specs.append(vmem)
        operands.append(carry)
    out_shape = [jax.ShapeDtypeStruct((3, window.width // 4 // of, NLON), jnp.float32) for _, _, _, of in PARTS]
    carried = (2, 2 * SUB, NLON)
    if not window.last:
        out_shape.append(jax.ShapeDtypeStruct(carried, jnp.float32))
    field = pltpu.VMEM((2, window.extended, NLON), jnp.float32)
    rows = sum(piece.rows for piece in window.pieces)
    out = pl.pallas_call(
        functools.partial(window_kernel, window, len(waits)),
        out_shape=out_shape,
        in_specs=in_specs,
        out_specs=[hbm] * len(out_shape),
        scratch_shapes=[
            pltpu.VMEM(table.shape, table.dtype),
            pltpu.VMEM((2, 4 * rows, depth), jnp.bfloat16),
            field,
            field,
            field,
            field,
            pltpu.VMEM((3, window.width, NLON), jnp.float32),
            pltpu.VMEM(carried, jnp.float32),
            pltpu.SemaphoreType.DMA,
            pltpu.SemaphoreType.DMA((len(PARTS) + 1,)),
        ],
        compiler_params=pltpu.CompilerParams(vmem_limit_bytes=VMEM_LIMIT),
        cost_estimate=pl.CostEstimate(
            flops=KERNEL_WORK * 3 * 2 * 2 * rows * depth * NLON,
            transcendentals=0,
            bytes_accessed=2 * table.size + 4 * rows * depth * 4 + 12 * window.width * NLON,
        ),
        name="window_tensor",
    )(*operands)
    return out[: len(PARTS)], (None if window.last else out[len(PARTS)])


def pairs(members, bit):
    return [(member, member ^ bit) for member in range(members)]


def by_levels(coeffs):
    spec = coeffs[0]
    levels, _, parts, waves_local, nlat = spec.shape
    members = lax.axis_size("mem")
    band = lax.axis_index("band").astype(jnp.int32)
    member = lax.axis_index("mem").astype(jnp.int32)
    core, side = member % 2, member // 2 % 2
    place = jnp.stack([band, core, side])
    spec = spec.reshape(levels, 2, parts * waves_local, nlat)
    count = nlat // LANE
    pieces = [Piece(k, count) for k in range(count)]
    windows = [Window(pieces[:2], count)] + [Window([piece], count) for piece in pieces[2:]]
    table = jnp.asarray(wave_table(levels, waves_local))
    swap = [(0, 1), (1, 0)]

    (outgoing,) = pieces_of(spec, 1 - band, pieces[:1], count)
    remotes = [lax.ppermute(outgoing, "band", swap)]
    outgoing = [None, *pieces_of(spec, 1 - band, pieces[1:], count)]

    def fetch_rows(k, waits):
        piece = gated(outgoing[k], waits) if waits else outgoing[k]
        remotes.append(lax.ppermute(piece, "band", swap))
        return piece

    fetch_rows(1, [])
    local = pieces_of(spec, band, pieces, count)

    bits = [1 << n for n in range(members.bit_length() - 1)]

    def halved(parts_of, bit):
        half = parts_of[0].shape[1] // 2
        mine = (member // bit) % 2

        def total(which):
            return sum(lax.dynamic_slice_in_dim(part, which * half, half, axis=1) for part in parts_of)

        leaves = total(1 - mine)
        return [total(mine), lax.ppermute(leaves, "mem", pairs(members, bit))], leaves

    def across(parts_of, bit):
        kept, passed, kept_more, passed_more = parts_of
        leaves = passed + passed_more
        return [kept, kept_more, lax.ppermute(leaves, "mem", pairs(members, bit))], leaves

    def advanced(parts_of, bit):
        return (across if len(parts_of) == 4 else halved)(parts_of, bit)

    def doubled(part, bit):
        beside = lax.ppermute(part, "mem", pairs(members, bit))
        mine = (member // bit) % 2
        return jnp.where(mine == 0, jnp.concatenate([part, beside], axis=0), jnp.concatenate([beside, part], axis=0))

    def gathered(part):
        for bit in reversed(bits):
            part = doubled(part, bit)
        return part

    carry = None
    sums, done = [], []
    for k, window in enumerate(windows):
        waits, last = [], window.pieces[-1].index
        while len(remotes) < min(last + 3, count):
            before = len(remotes) - 2
            waits.append(fetch_rows(len(remotes), [remotes[before]] if carry is None else [remotes[before], carry]))
        for j in AHEAD[k]:
            sums[j], left = advanced(sums[j], bits[done[j]])
            done[j] += 1
            waits.append(left)
        here = [piece.index for piece in window.pieces]
        parts, carry = window_tensor(
            window, place, table, [local[p] for p in here], [remotes[p] for p in here], waits, carry
        )
        swapped = [lax.ppermute(part, "mem", pairs(members, bits[0])) for part in reversed(parts[2:])]
        sums.append([parts[0], parts[1], swapped[2], jnp.concatenate(swapped[1::-1], axis=1)])
        done.append(1)
    results = {}
    for k, window in enumerate(windows):
        for bit in bits[done[k] :]:
            sums[k], _ = advanced(sums[k], bit)
        results.setdefault(window.side, []).append(exponent_of(sum(sums[k]), members))

    (other,), (both,) = results["other"], results["both"]
    other = lax.ppermute(other, "band", swap)
    trades = []
    for m in range(members):
        for b in range(2):
            mate = (m, b) if m % 2 == b else (m ^ 1, 1 - b)
            trades.append((m * 2 + b, mate[0] * 2 + mate[1]))
    both = lax.ppermute(both, ("mem", "band"), trades)

    def whole(parts):
        heights = [part.shape[0] for part in parts]
        stack = jnp.concatenate(parts, axis=0)[None]
        stack = gathered(stack)
        cuts = np.cumsum([0] + heights)
        return [stack[:, cuts[n] : cuts[n + 1]].reshape(-1, NLON) for n in range(len(parts))]

    other, both = whole([other, both])
    middle = both.shape[0] // 2
    low, high = both[:middle], both[middle:]
    rest = jnp.zeros((nlat // 2 - middle, NLON), jnp.float32)
    down = jnp.stack([jnp.concatenate([rest, low]), jnp.concatenate([other, high])])
    up = jnp.stack([jnp.concatenate([low, other]), jnp.concatenate([high, rest])])
    out = jnp.where(band == 0, down, up)
    for k, block in enumerate(whole(results["own"])):
        width = block.shape[0]
        row = choose(band, (nlat // 2 - middle - (k + 1) * width, middle + k * width))
        out = lax.dynamic_update_slice(out, block[None], (band, row.astype(jnp.int32), jnp.int32(0)))
    return out


def per_device(coeffs):
    _, levels, _, _, _, nlat = coeffs.shape
    members = lax.axis_size("mem")
    rows = nlat // lax.axis_size("band")
    fits = coeffs.shape[4] == 5 * LANE // 2 and nlat % (2 * LANE) == LANE and rows > LANE
    if fits and levels == lax.axis_size("band") == 2 and members == 16:
        return by_levels(coeffs)
    return by_rows(coeffs)


def solution(mesh):
    placed = (P("mem", None, None, None, "band", None),)
    return jax.shard_map(
        per_device, mesh=mesh, in_specs=placed, out_specs=P(None, "band", None), check_vma=False
    )
```

```python
import functools
import math

import jax
import jax.numpy as jnp
import ml_dtypes
import numpy as np
from jax import lax
from jax.experimental import pallas as pl
from jax.experimental.pallas import tpu as pltpu
from jax.sharding import PartitionSpec as P

NLON = 1280
STEPS = 1
SUB = 8
LANE = 128
VMEM_LIMIT = 60 * 1024 * 1024
KERNEL_WORK = 8
AHEAD = ((), (), (0,), (1, 0), (2, 1, 0))


def padded(cells, sides, width):
    for axis, dim in sides:
        count = lax.axis_size(axis)
        ends = count - 1
        head = lax.slice_in_dim(cells, 0, width, axis=dim)
        tail = lax.slice_in_dim(cells, cells.shape[dim] - width, cells.shape[dim], axis=dim)
        cells = jnp.concatenate(
            [
                lax.ppermute(tail, axis, [(i, (i + 1) % count) for i in range(ends)]),
                cells,
                lax.ppermute(head, axis, [((i + 1) % count, i) for i in range(ends)]),
            ],
            axis=dim,
        )
    return cells


def slope(extended, winds):
    center = extended[:, 1:-1]
    north = (extended[:, 2:] - extended[:, :-2]) * 0.5
    east = (jnp.roll(center, -1, 2) - jnp.roll(center, 1, 2)) * 0.5
    return -winds - (winds[0] * east + winds[1] * north)


def rimmed(field):
    return padded(field, (("band", 1),), 1)


def tensor(extended):
    center = extended[:, 1:-1]
    north = (extended[:, 2:] - extended[:, :-2]) * 0.5
    east = (jnp.roll(center, -1, 2) - jnp.roll(center, 1, 2)) * 0.5
    g_xx = 1.0 + east[0]
    g_xy = north[0]
    g_yx = east[1]
    g_yy = 1.0 + north[1]
    return jnp.stack(
        [g_xx * g_xx + g_yx * g_yx, g_xx * g_xy + g_yx * g_yy, g_xy * g_xy + g_yy * g_yy]
    )


def integrate(shift, flow, extend):
    first = slope(extend(shift), flow)
    second = slope(extend(0.5 * first), flow)
    third = slope(extend(0.5 * second), flow)
    fourth = slope(extend(third), flow)
    return (first + 2.0 * second + 2.0 * third + fourth) / 6.0


def exponent_of(summed, members):
    mean = summed / members
    first, cross, second = (mean[..., 0, :, :], mean[..., 1, :, :], mean[..., 2, :, :])
    half = (first + second) * 0.5
    differ = (first - second) * 0.5
    largest = half + jnp.sqrt(differ * differ + cross * cross)
    return jnp.log(largest + 1e-06) / (2.0 * STEPS)


def by_rows(coeffs):
    spec = coeffs[0]
    levels = spec.shape[0]
    nlat = spec.shape[4]
    waves = spec.shape[3] * lax.axis_size("band")
    members = lax.axis_size("mem")
    stacked = spec.reshape(levels * 2, 2, spec.shape[3], nlat)
    wave_index = lax.iota(jnp.int32, waves)
    column = lax.iota(jnp.int32, NLON)
    phase = wave_index[:, None] * column[None, :] % NLON
    angle = phase.astype(jnp.float32) * (2.0 * math.pi / NLON)
    weight = jnp.where(wave_index == 0, 1.0, 2.0).astype(jnp.float32)[:, None]
    table = jnp.stack([weight * jnp.cos(angle), -weight * jnp.sin(angle)], axis=0)
    winds = jnp.einsum(
        "crwh,rwn->chn",
        lax.all_to_all(stacked, "band", split_axis=3, concat_axis=2, tiled=True),
        table,
        precision=lax.Precision.HIGHEST,
        preferred_element_type=jnp.float32,
    )
    height = winds.shape[1]
    winds = winds.reshape(levels, 2, height, NLON)
    partials = []
    for level in range(levels):
        flow = winds[level]
        shift = integrate(jnp.zeros_like(flow), flow, rimmed)
        partials.append(tensor(rimmed(shift)))
    summed = lax.psum_scatter(jnp.stack(partials), "mem", scatter_dimension=3, tiled=True)
    return lax.all_gather(exponent_of(summed, members), "mem", axis=2, tiled=True)


def by_parity(waves_local):
    half = waves_local // 2
    whole = 2 * LANE - half
    runs = []
    for parity in range(2):
        runs += [(parity, half, 2), (waves_local + parity, whole, 2)]
    for parity in range(2):
        runs.append((waves_local + parity + 2 * whole, half - whole, 2))
    return runs


@functools.lru_cache(maxsize=None)
def wave_table(bands, waves_local):
    order = np.concatenate([start + step * np.arange(count) for start, count, step in by_parity(waves_local)])
    wave, part = order % waves_local, order // waves_local
    wave = wave[None, :] + waves_local * np.arange(bands)[:, None]
    part = np.broadcast_to(part, wave.shape)
    cut = [0, 2 * LANE, 4 * LANE, 4 * LANE + LANE // 2, 5 * LANE]
    result = []
    for parity in range(2):
        picks = [(band, slice(cut[parity], cut[parity + 1])) for band in range(bands)]
        picks += [(band, slice(cut[parity + 2], cut[parity + 3])) for band in range(bands)]
        waves = np.concatenate([wave[pick] for pick in picks])
        parts = np.concatenate([part[pick] for pick in picks])
        phase = (waves[:, None] * np.arange(NLON // 2)[None, :]) % NLON
        angle = phase.astype(np.float64) * (2.0 * np.pi / NLON)
        weight = np.where(waves == 0, 1.0, 2.0)[:, None]
        table = weight * np.where(parts[:, None] == 0, np.cos(angle), -np.sin(angle))
        high = table.astype(ml_dtypes.bfloat16)
        result += [high, (table - high.astype(np.float64)).astype(ml_dtypes.bfloat16)]
    return np.stack(result)


class Window:
    def __init__(self, index, count):
        self.first = index == 0
        self.last = index == count - 1
        self.index = index
        self.width = LANE
        self.extended = LANE + 2 * SUB
        self.main = LANE if self.first else LANE - SUB
        self.rim = 0 if self.last else SUB
        self.rows = self.main + self.rim
        up = SUB if self.first else 2 * SUB
        self.place = (self.extended - up - self.rows, up)
        self.side = "other" if 2 * (index + 1) <= count else "own" if 2 * index >= count else "both"


def choose(band, pair):
    return jnp.where(band == 0, pair[0], pair[1])


def multiple(value, of):
    return pl.multiple_of(value.astype(jnp.int32), of)


def pieces_kernel(windows, slots, count, level_ref, spec_ref, *refs):
    out_refs, (taken, turned, in_sems, out_sems) = refs[: len(windows)], refs[len(windows) :]
    level = level_ref[0]
    runs = by_parity(spec_ref.shape[2] // 2)

    def arrival(c, n):
        tile = choose(level, (count - 1 - slots[n], slots[n]))
        lanes = pl.ds(multiple(tile * LANE, LANE), LANE)
        return pltpu.make_async_copy(spec_ref.at[level, c, :, lanes], taken.at[c, n], in_sems.at[c, n])

    def departures(c, k):
        window, n = windows[k], slots.index(windows[k].index)
        rows = pl.ds(multiple(choose(level, (0, LANE - window.main)), SUB), window.main)
        at = pl.ds(multiple(choose(level, (window.rim, 0)), SUB), window.main)
        yield pltpu.make_async_copy(turned.at[c, n, rows], out_refs[k].at[c, at], out_sems.at[k, c, 0])
        if window.rim:
            rows = pl.ds(multiple(choose(level, (LANE - SUB, 0)), SUB), SUB)
            at = pl.ds(multiple(choose(level, (0, window.main)), SUB), SUB)
            yield pltpu.make_async_copy(turned.at[c, n + 1, rows], out_refs[k].at[c, at], out_sems.at[k, c, 1])

    for n in range(len(slots)):
        for c in range(2):
            arrival(c, n).start()
    for n in range(len(slots)):
        for c in range(2):
            arrival(c, n).wait()
            turned[c, n] = jnp.concatenate([taken[c, n, pl.ds(start, rows, step), :] for start, rows, step in runs]).T
        for k, window in enumerate(windows):
            if slots[n] == window.index + (1 if window.rim else 0):
                for c in range(2):
                    for copy in departures(c, k):
                        copy.start()
    for k in range(len(windows)):
        for c in range(2):
            for copy in departures(c, k):
                copy.wait()


def pieces_of(spec, level, windows, count):
    depth = spec.shape[2]
    slots = sorted({w.index for w in windows} | {w.index + 1 for w in windows if w.rim})
    return pl.pallas_call(
        functools.partial(pieces_kernel, windows, slots, count),
        in_specs=[pl.BlockSpec(memory_space=pltpu.SMEM), pl.BlockSpec(memory_space=pl.ANY)],
        out_specs=[pl.BlockSpec(memory_space=pl.ANY)] * len(windows),
        out_shape=[jax.ShapeDtypeStruct((2, w.rows, depth), jnp.float32) for w in windows],
        scratch_shapes=[
            pltpu.VMEM((2, len(slots), depth, LANE), jnp.float32),
            pltpu.VMEM((2, len(slots), LANE, depth), jnp.float32),
            pltpu.SemaphoreType.DMA((2, len(slots))),
            pltpu.SemaphoreType.DMA((len(windows), 2, 2)),
        ],
        compiler_params=pltpu.CompilerParams(vmem_limit_bytes=VMEM_LIMIT),
        cost_estimate=pl.CostEstimate(
            flops=0, transcendentals=0, bytes_accessed=4 * 2 * len(slots) * LANE * depth * 4
        ),
        name="pieces_of",
    )(level.reshape(1), spec)


def east_of(x):
    return pltpu.roll(x, NLON - 1, axis=1) - pltpu.roll(x, 1, axis=1)


def north_of(before, here, after):
    row = lax.broadcasted_iota(jnp.int32, here.shape, 0)
    above = jnp.where(row == SUB - 1, pltpu.roll(after, SUB - 1, axis=0), pltpu.roll(here, SUB - 1, axis=0))
    below = jnp.where(row == 0, pltpu.roll(before, 1, axis=0), pltpu.roll(here, 1, axis=0))
    return above - below


def window_kernel(window, depth, waits, *refs):
    refs = list(refs)
    place_ref, local_ref, remote_ref, table_ref = refs[:4]
    refs = refs[4 + waits :]
    carry_ref = None if window.first else refs.pop(0)
    out_refs = [refs.pop(0) for _ in range(4)]
    carried_ref = None if window.last else refs.pop(0)
    table, lhs_high, lhs_low, wind, second, third, shift, results, carried, table_sem, out_sems = refs
    band, core, side = place_ref[0], place_ref[1], place_ref[2]
    rows, extended = window.rows, window.extended

    def at(pair):
        return multiple(choose(band, pair), SUB)

    tables = pltpu.make_async_copy(table_ref, table, table_sem)
    tables.start()
    lane = lax.broadcasted_iota(jnp.int32, (rows, LANE), 1)
    even, odd = [], []
    for c in range(2):
        mine, theirs = local_ref[c], remote_ref[c]
        low, high = jnp.where(band == 0, mine, theirs), jnp.where(band == 0, theirs, mine)
        low_rest, high_rest = low[:, 4 * LANE :], high[:, 4 * LANE :]
        turn = functools.partial(pltpu.roll, shift=LANE // 2, axis=1)
        even_rest = jnp.where(lane < LANE // 2, low_rest, turn(high_rest))
        odd_rest = jnp.where(lane < LANE // 2, turn(low_rest), high_rest)
        even.append(jnp.concatenate([low[:, : 2 * LANE], high[:, : 2 * LANE], even_rest], axis=1))
        odd.append(jnp.concatenate([low[:, 2 * LANE : 4 * LANE], high[:, 2 * LANE : 4 * LANE], odd_rest], axis=1))
    for parity, parts in enumerate((even, odd)):
        lhs = jnp.concatenate(parts)
        lhs_high[parity] = lhs.astype(jnp.bfloat16)
        lhs_low[parity] = (lhs - lhs_high[parity].astype(jnp.float32)).astype(jnp.bfloat16)
    tables.wait()

    place = at(window.place)
    if window.first or window.last:
        for c in range(2):
            if window.first:
                wind[c, pl.ds(at((extended - SUB, 0)), SUB), :] = jnp.zeros((SUB, NLON), jnp.float32)
            if window.last:
                wind[c, pl.ds(at((0, extended - SUB)), SUB), :] = jnp.zeros((SUB, NLON), jnp.float32)
    if not window.first:
        for c in range(2):
            wind[c, pl.ds(at((extended - 2 * SUB, 0)), 2 * SUB), :] = carry_ref[c]

    dot = functools.partial(jnp.dot, preferred_element_type=jnp.float32)
    for start in range(0, NLON // 2, 2 * LANE):
        stop = min(start + 2 * LANE, NLON // 2)
        columns = slice(start, stop)
        sums = []
        for parity in range(2):
            total = dot(lhs_high[parity], table[2 * parity, :, columns])
            total += dot(lhs_low[parity], table[2 * parity, :, columns])
            total += dot(lhs_high[parity], table[2 * parity + 1, :, columns])
            sums.append(total)
        for c in range(2):
            even_sum, odd_sum = (total[c * rows : (c + 1) * rows] for total in sums)
            wind[c, pl.ds(place, rows), start:stop] = even_sum + odd_sum
            wind[c, pl.ds(place, rows), NLON // 2 + start : NLON // 2 + stop] = even_sum - odd_sum

    if not window.last:
        for c in range(2):
            carried[c] = wind[c, pl.ds(at((0, extended - 2 * SUB)), 2 * SUB), :]
        carry_on = pltpu.make_async_copy(carried, carried_ref, out_sems.at[4])
        carry_on.start()

    blocks = extended // SUB

    def rows_of(block):
        return pl.ds(pl.multiple_of(block * SUB, SUB), SUB)

    def derivatives(field, block):
        before, after = jnp.maximum(block - 1, 0), jnp.minimum(block + 1, blocks - 1)
        result = []
        for c in range(2):
            here = field[c, rows_of(block), :]
            result.append((east_of(here), north_of(field[c, rows_of(before), :], here, field[c, rows_of(after), :])))
        return result

    @pl.loop(0, blocks, unroll=6)
    def _(block):
        flow = [wind[c, rows_of(block), :] for c in range(2)]
        for c, (east, north) in enumerate(derivatives(wind, block)):
            second[c, rows_of(block), :] = 0.25 * (flow[0] * east + flow[1] * north) - flow[c]

    @pl.loop(0, blocks, unroll=6)
    def _(block):
        flow = [wind[c, rows_of(block), :] for c in range(2)]
        for c, (east, north) in enumerate(derivatives(second, block)):
            third[c, rows_of(block), :] = -flow[c] - 0.25 * (flow[0] * east + flow[1] * north)

    @pl.loop(0, blocks, unroll=6)
    def _(block):
        flow = [wind[c, rows_of(block), :] for c in range(2)]
        for c, (east, north) in enumerate(derivatives(third, block)):
            fourth = -flow[c] - 0.5 * (flow[0] * east + flow[1] * north)
            both = second[c, rows_of(block), :] + third[c, rows_of(block), :]
            shift[c, rows_of(block), :] = (2.0 * both + (fourth - flow[c])) * (1.0 / 6.0)

    quarter = window.width // 4 // SUB

    def entries(out, base):
        @pl.loop(0, quarter, unroll=4)
        def _(block):
            (e0, n0), (e1, n1) = derivatives(shift, base + block + 1)
            g_xx, g_xy, g_yx, g_yy = 1.0 + 0.5 * e0, 0.5 * n0, 0.5 * e1, 1.0 + 0.5 * n1
            out[0, rows_of(block), :] = g_xx * g_xx + g_yx * g_yx
            out[1, rows_of(block), :] = g_xx * g_xy + g_yx * g_yy
            out[2, rows_of(block), :] = g_xy * g_xy + g_yy * g_yy

    copies = []
    for n, (a, b) in reversed(list(enumerate(QUARTERS))):
        entries(results.at[n], (2 * (core + a - 2 * core * a) + (side + b - 2 * side * b)) * quarter)
        copies.append(pltpu.make_async_copy(results.at[n], out_refs[n], out_sems.at[n]))
        copies[-1].start()
    for copy in copies:
        copy.wait()
    if not window.last:
        carry_on.wait()


QUARTERS = ((0, 0), (0, 1), (1, 0), (1, 1))


def window_tensor(window, place, local, remote, table, waits, carry):
    depth = local.shape[2]
    vmem = pl.BlockSpec(memory_space=pltpu.VMEM)
    in_specs = [
        pl.BlockSpec(memory_space=pltpu.SMEM),
        vmem,
        vmem,
        pl.BlockSpec(memory_space=pl.ANY),
    ]
    in_specs += [pl.BlockSpec(memory_space=pl.ANY)] * len(waits)
    operands = [place, local, remote, table, *waits]
    if not window.first:
        in_specs.append(vmem)
        operands.append(carry)
    out_shape = [jax.ShapeDtypeStruct((3, window.width // 4, NLON), jnp.float32)] * 4
    if not window.last:
        out_shape.append(jax.ShapeDtypeStruct((2, 2 * SUB, NLON), jnp.float32))
    field = pltpu.VMEM((2, window.extended, NLON), jnp.float32)
    lhs_shape = (2, 2 * window.rows, depth)
    out = pl.pallas_call(
        functools.partial(window_kernel, window, depth, len(waits)),
        out_shape=out_shape,
        in_specs=in_specs,
        out_specs=[pl.BlockSpec(memory_space=pl.ANY)] * len(out_shape),
        scratch_shapes=[
            pltpu.VMEM(table.shape, table.dtype),
            pltpu.VMEM(lhs_shape, jnp.bfloat16),
            pltpu.VMEM(lhs_shape, jnp.bfloat16),
            field,
            field,
            field,
            field,
            pltpu.VMEM((4, 3, window.width // 4, NLON), jnp.float32),
            pltpu.VMEM((2, 2 * SUB, NLON), jnp.float32),
            pltpu.SemaphoreType.DMA,
            pltpu.SemaphoreType.DMA((5,)),
        ],
        compiler_params=pltpu.CompilerParams(vmem_limit_bytes=VMEM_LIMIT),
        cost_estimate=pl.CostEstimate(
            flops=KERNEL_WORK * 3 * 2 * 2 * window.rows * depth * NLON,
            transcendentals=0,
            bytes_accessed=2 * table.size + 4 * window.rows * depth * 4 + 12 * window.width * NLON,
        ),
        name="window_tensor",
    )(*operands)
    return out[:4], (None if window.last else out[4])


def pairs(members, bit):
    return [(member, member ^ bit) for member in range(members)]


def pairs(members, bit):
    return [(member, member ^ bit) for member in range(members)]


def put_kernel(count, place_ref, *refs):
    parts, out_ref, sem = refs[:4], refs[-2], refs[-1]
    core, side, along = place_ref[0], place_ref[1], place_ref[2]
    around = parts[0].shape[1]
    copies = []
    for a, part in enumerate(parts):
        half = core if a < 2 else 1 - core
        quarter = side if a % 2 == 0 else 1 - side
        for w in range(count):
            level, row = place_ref[3 + 4 * w + half], place_ref[5 + 4 * w + half]
            for n in range(around):
                piece = lax.rem(along + 1 + n, around)
                at = multiple(row + (quarter * around + piece) * SUB, SUB)
                copies.append(pltpu.make_async_copy(part.at[w, n], out_ref.at[level, pl.ds(at, SUB)], sem.at[a, w, n]))
                copies[-1].start()
    for copy in copies:
        copy.wait()


def put(out, shape, places, parts):
    count = parts[0].shape[0]
    extra = [] if out is None else [out]
    return pl.pallas_call(
        functools.partial(put_kernel, count),
        in_specs=[pl.BlockSpec(memory_space=pltpu.SMEM)]
        + [pl.BlockSpec(memory_space=pltpu.VMEM)] * 4
        + [pl.BlockSpec(memory_space=pl.ANY)] * len(extra),
        out_specs=pl.BlockSpec(memory_space=pl.ANY),
        out_shape=jax.ShapeDtypeStruct(shape, jnp.float32),
        input_output_aliases={5: 0} if extra else {},
        scratch_shapes=[pltpu.SemaphoreType.DMA((4, count, parts[0].shape[1]))],
        compiler_params=pltpu.CompilerParams(vmem_limit_bytes=VMEM_LIMIT),
        cost_estimate=pl.CostEstimate(flops=0, transcendentals=0, bytes_accessed=8 * 4 * parts[0].size),
        name="put",
    )(places.astype(jnp.int32), *parts, *extra)


def pairs(members, bit):
    return [(member, member ^ bit) for member in range(members)]


def by_levels(coeffs):
    spec = coeffs[0]
    levels, _, parts, waves_local, nlat = spec.shape
    members = lax.axis_size("mem")
    band = lax.axis_index("band").astype(jnp.int32)
    member = lax.axis_index("mem").astype(jnp.int32)
    core, side = member % 2, member // 2 % 2
    place = jnp.stack([band, core, side])
    spec = spec.reshape(levels, 2, parts * waves_local, nlat)
    count = nlat // LANE
    windows = [Window(k, count) for k in range(count)]
    table = jnp.asarray(wave_table(levels, waves_local))
    swap = [(0, 1), (1, 0)]

    (piece,) = pieces_of(spec, 1 - band, windows[:1], count)
    remotes = [lax.ppermute(piece, "band", swap)]
    outgoing = pieces_of(spec, 1 - band, windows[1:], count)
    remotes += [lax.ppermute(piece, "band", swap) for piece in outgoing]
    local = pieces_of(spec, band, windows, count)

    bits = [1 << n for n in range(members.bit_length() - 1)]

    def halved(parts_of, bit):
        half = parts_of[0].shape[1] // 2
        mine = (member // bit) % 2

        def total(which):
            return sum(lax.dynamic_slice_in_dim(part, which * half, half, axis=1) for part in parts_of)

        leaves = total(1 - mine)
        return [total(mine), lax.ppermute(leaves, "mem", pairs(members, bit))], leaves

    def across(parts_of, bit):
        kept, passed, kept_more, passed_more = parts_of
        leaves = passed + passed_more
        return [kept, kept_more, lax.ppermute(leaves, "mem", pairs(members, bit))], leaves

    def advanced(parts_of, bit):
        return (across if len(parts_of) == 4 else halved)(parts_of, bit)

    def doubled(part, bit):
        beside = lax.ppermute(part, "mem", pairs(members, bit))
        mine = (member // bit) % 2
        return jnp.where(mine == 0, jnp.concatenate([part, beside], axis=1), jnp.concatenate([beside, part], axis=1))

    def gathered(part):
        for bit in reversed(bits):
            part = doubled(part, bit)
        return part

    carry = None
    sums, done = [], []
    for k, window in enumerate(windows):
        waits = []
        for j in AHEAD[k]:
            sums[j], left = advanced(sums[j], bits[done[j]])
            done[j] += 1
            waits.append(left)
        quarters, carry = window_tensor(window, place, local[k], remotes[k], table, waits, carry)
        first = lax.ppermute(quarters[3], "mem", pairs(members, bits[0]))
        second = lax.ppermute(quarters[2], "mem", pairs(members, bits[0]))
        sums.append([quarters[0], quarters[1], second, first])
        done.append(1)
    pieces = {"own": [], "both": [], "other": []}
    for k, window in enumerate(windows):
        for bit in bits[done[k] :]:
            sums[k], _ = advanced(sums[k], bit)
        pieces[window.side].append(exponent_of(sum(sums[k]), members))

    other = lax.ppermute(jnp.stack(pieces["other"]), "band", swap)
    trades = []
    for m in range(members):
        for b in range(2):
            mate = (m, b) if m % 2 == b else (m ^ 1, 1 - b)
            trades.append((m * 2 + b, mate[0] * 2 + mate[1]))
    both = lax.ppermute(pieces["both"][0], ("mem", "band"), trades)

    early = gathered(jnp.concatenate([other, both[None]]))
    other, both = early[:-1], early[-1]
    middle = both.shape[0] // 2
    low, high = both[:middle], both[middle:]
    rest = jnp.zeros((nlat // 2 - middle, NLON), jnp.float32)
    down = jnp.stack([jnp.concatenate([rest, low]), jnp.concatenate([*other, high])])
    up = jnp.stack([jnp.concatenate([low, *other[::-1]]), jnp.concatenate([high, rest])])
    out = jnp.where(band == 0, down, up)

    own = gathered(jnp.stack(pieces["own"]))
    for k, block in enumerate(own):
        width = block.shape[0]
        row = choose(band, (nlat // 2 - middle - (k + 1) * width, middle + k * width))
        out = lax.dynamic_update_slice(out, block[None], (band, row.astype(jnp.int32), jnp.int32(0)))
    return out


def per_device(coeffs):
    _, levels, _, _, _, nlat = coeffs.shape
    members = lax.axis_size("mem")
    rows = nlat // lax.axis_size("band")
    fits = coeffs.shape[4] == 5 * LANE // 2 and nlat % (2 * LANE) == LANE and rows > LANE
    if fits and levels == lax.axis_size("band") == 2 and members == 16:
        return by_levels(coeffs)
    return by_rows(coeffs)


def solution(mesh):
    placed = (P("mem", None, None, None, "band", None),)
    return jax.shard_map(
        per_device, mesh=mesh, in_specs=placed, out_specs=P(None, "band", None), check_vma=False
    )
```

```python
import functools
import math

import jax
import jax.numpy as jnp
import ml_dtypes
import numpy as np
from jax import lax
from jax.experimental import pallas as pl
from jax.experimental.pallas import tpu as pltpu
from jax.sharding import PartitionSpec as P

NLON = 1280
STEPS = 1
SUB = 8
LANE = 128
VMEM_LIMIT = 60 * 1024 * 1024
KERNEL_WORK = 8
AHEAD = ((), (), (0,), (1, 0), (3, 2, 1, 0))


def padded(cells, sides, width):
    for axis, dim in sides:
        count = lax.axis_size(axis)
        ends = count - 1
        head = lax.slice_in_dim(cells, 0, width, axis=dim)
        tail = lax.slice_in_dim(cells, cells.shape[dim] - width, cells.shape[dim], axis=dim)
        cells = jnp.concatenate(
            [
                lax.ppermute(tail, axis, [(i, (i + 1) % count) for i in range(ends)]),
                cells,
                lax.ppermute(head, axis, [((i + 1) % count, i) for i in range(ends)]),
            ],
            axis=dim,
        )
    return cells


def slope(extended, winds):
    center = extended[:, 1:-1]
    north = (extended[:, 2:] - extended[:, :-2]) * 0.5
    east = (jnp.roll(center, -1, 2) - jnp.roll(center, 1, 2)) * 0.5
    return -winds - (winds[0] * east + winds[1] * north)


def rimmed(field):
    return padded(field, (("band", 1),), 1)


def tensor(extended):
    center = extended[:, 1:-1]
    north = (extended[:, 2:] - extended[:, :-2]) * 0.5
    east = (jnp.roll(center, -1, 2) - jnp.roll(center, 1, 2)) * 0.5
    g_xx = 1.0 + east[0]
    g_xy = north[0]
    g_yx = east[1]
    g_yy = 1.0 + north[1]
    return jnp.stack(
        [g_xx * g_xx + g_yx * g_yx, g_xx * g_xy + g_yx * g_yy, g_xy * g_xy + g_yy * g_yy]
    )


def integrate(shift, flow, extend):
    first = slope(extend(shift), flow)
    second = slope(extend(0.5 * first), flow)
    third = slope(extend(0.5 * second), flow)
    fourth = slope(extend(third), flow)
    return (first + 2.0 * second + 2.0 * third + fourth) / 6.0


def exponent_of(summed, members):
    mean = summed / members
    first, cross, second = (mean[..., 0, :, :], mean[..., 1, :, :], mean[..., 2, :, :])
    half = (first + second) * 0.5
    differ = (first - second) * 0.5
    largest = half + jnp.sqrt(differ * differ + cross * cross)
    return jnp.log(largest + 1e-06) / (2.0 * STEPS)


def by_rows(coeffs):
    spec = coeffs[0]
    levels = spec.shape[0]
    nlat = spec.shape[4]
    waves = spec.shape[3] * lax.axis_size("band")
    members = lax.axis_size("mem")
    stacked = spec.reshape(levels * 2, 2, spec.shape[3], nlat)
    wave_index = lax.iota(jnp.int32, waves)
    column = lax.iota(jnp.int32, NLON)
    phase = wave_index[:, None] * column[None, :] % NLON
    angle = phase.astype(jnp.float32) * (2.0 * math.pi / NLON)
    weight = jnp.where(wave_index == 0, 1.0, 2.0).astype(jnp.float32)[:, None]
    table = jnp.stack([weight * jnp.cos(angle), -weight * jnp.sin(angle)], axis=0)
    winds = jnp.einsum(
        "crwh,rwn->chn",
        lax.all_to_all(stacked, "band", split_axis=3, concat_axis=2, tiled=True),
        table,
        precision=lax.Precision.HIGHEST,
        preferred_element_type=jnp.float32,
    )
    height = winds.shape[1]
    winds = winds.reshape(levels, 2, height, NLON)
    partials = []
    for level in range(levels):
        flow = winds[level]
        shift = integrate(jnp.zeros_like(flow), flow, rimmed)
        partials.append(tensor(rimmed(shift)))
    summed = lax.psum_scatter(jnp.stack(partials), "mem", scatter_dimension=3, tiled=True)
    return lax.all_gather(exponent_of(summed, members), "mem", axis=2, tiled=True)


def by_parity(waves_local):
    half = waves_local // 2
    whole = 2 * LANE - half
    runs = []
    for parity in range(2):
        runs += [(parity, half, 2), (waves_local + parity, whole, 2)]
    for parity in range(2):
        runs.append((waves_local + parity + 2 * whole, half - whole, 2))
    return runs


@functools.lru_cache(maxsize=None)
def wave_table(bands, waves_local):
    order = np.concatenate([start + step * np.arange(count) for start, count, step in by_parity(waves_local)])
    wave, part = order % waves_local, order // waves_local
    wave = wave[None, :] + waves_local * np.arange(bands)[:, None]
    part = np.broadcast_to(part, wave.shape)
    cut = [0, 2 * LANE, 4 * LANE, 4 * LANE + LANE // 2, 5 * LANE]
    result = []
    for parity in range(2):
        picks = [(band, slice(cut[parity], cut[parity + 1])) for band in range(bands)]
        picks += [(band, slice(cut[parity + 2], cut[parity + 3])) for band in range(bands)]
        waves = np.concatenate([wave[pick] for pick in picks])
        parts = np.concatenate([part[pick] for pick in picks])
        phase = (waves[:, None] * np.arange(NLON // 2)[None, :]) % NLON
        angle = phase.astype(np.float64) * (2.0 * np.pi / NLON)
        weight = np.where(waves == 0, 1.0, 2.0)[:, None]
        table = weight * np.where(parts[:, None] == 0, np.cos(angle), -np.sin(angle))
        high = table.astype(ml_dtypes.bfloat16)
        result += [high, (table - high.astype(np.float64)).astype(ml_dtypes.bfloat16)]
    return np.stack(result)


class Window:
    def __init__(self, index, count):
        self.first = index == 0
        self.last = index == count - 1
        self.index = index
        self.width = LANE
        self.extended = LANE + 2 * SUB
        self.main = LANE if self.first else LANE - SUB
        self.rim = 0 if self.last else SUB
        self.rows = self.main + self.rim
        up = SUB if self.first else 2 * SUB
        self.place = (self.extended - up - self.rows, up)
        self.side = "other" if 2 * (index + 1) <= count else "own" if 2 * index >= count else "both"


def choose(band, pair):
    return jnp.where(band == 0, pair[0], pair[1])


def multiple(value, of):
    return pl.multiple_of(value.astype(jnp.int32), of)


def pieces_kernel(windows, slots, count, level_ref, spec_ref, *refs):
    out_refs, (taken, turned, in_sems, out_sems) = refs[: len(windows)], refs[len(windows) :]
    level = level_ref[0]
    runs = by_parity(spec_ref.shape[2] // 2)

    def arrival(c, n):
        tile = choose(level, (count - 1 - slots[n], slots[n]))
        lanes = pl.ds(multiple(tile * LANE, LANE), LANE)
        return pltpu.make_async_copy(spec_ref.at[level, c, :, lanes], taken.at[c, n], in_sems.at[c, n])

    def departures(c, k):
        window, n = windows[k], slots.index(windows[k].index)
        rows = pl.ds(multiple(choose(level, (0, LANE - window.main)), SUB), window.main)
        at = pl.ds(multiple(choose(level, (window.rim, 0)), SUB), window.main)
        yield pltpu.make_async_copy(turned.at[c, n, rows], out_refs[k].at[c, at], out_sems.at[k, c, 0])
        if window.rim:
            rows = pl.ds(multiple(choose(level, (LANE - SUB, 0)), SUB), SUB)
            at = pl.ds(multiple(choose(level, (0, window.main)), SUB), SUB)
            yield pltpu.make_async_copy(turned.at[c, n + 1, rows], out_refs[k].at[c, at], out_sems.at[k, c, 1])

    for n in range(len(slots)):
        for c in range(2):
            arrival(c, n).start()
    for n in range(len(slots)):
        for c in range(2):
            arrival(c, n).wait()
            turned[c, n] = jnp.concatenate([taken[c, n, pl.ds(start, rows, step), :] for start, rows, step in runs]).T
        for k, window in enumerate(windows):
            if slots[n] == window.index + (1 if window.rim else 0):
                for c in range(2):
                    for copy in departures(c, k):
                        copy.start()
    for k in range(len(windows)):
        for c in range(2):
            for copy in departures(c, k):
                copy.wait()


def pieces_of(spec, level, windows, count):
    depth = spec.shape[2]
    slots = sorted({w.index for w in windows} | {w.index + 1 for w in windows if w.rim})
    return pl.pallas_call(
        functools.partial(pieces_kernel, windows, slots, count),
        in_specs=[pl.BlockSpec(memory_space=pltpu.SMEM), pl.BlockSpec(memory_space=pl.ANY)],
        out_specs=[pl.BlockSpec(memory_space=pl.ANY)] * len(windows),
        out_shape=[jax.ShapeDtypeStruct((2, w.rows, depth), jnp.float32) for w in windows],
        scratch_shapes=[
            pltpu.VMEM((2, len(slots), depth, LANE), jnp.float32),
            pltpu.VMEM((2, len(slots), LANE, depth), jnp.float32),
            pltpu.SemaphoreType.DMA((2, len(slots))),
            pltpu.SemaphoreType.DMA((len(windows), 2, 2)),
        ],
        compiler_params=pltpu.CompilerParams(vmem_limit_bytes=VMEM_LIMIT),
        cost_estimate=pl.CostEstimate(
            flops=0, transcendentals=0, bytes_accessed=4 * 2 * len(slots) * LANE * depth * 4
        ),
        name="pieces_of",
    )(level.reshape(1), spec)


def gate_kernel(*refs):
    pass


def gated(part, waits):
    return pl.pallas_call(
        gate_kernel,
        in_specs=[pl.BlockSpec(memory_space=pl.ANY)] * (1 + len(waits)),
        out_specs=pl.BlockSpec(memory_space=pl.ANY),
        out_shape=jax.ShapeDtypeStruct(part.shape, part.dtype),
        input_output_aliases={0: 0},
        cost_estimate=pl.CostEstimate(flops=0, transcendentals=0, bytes_accessed=1024),
        name="gated",
    )(part, *waits)


def east_of(x):
    return pltpu.roll(x, NLON - 1, axis=1) - pltpu.roll(x, 1, axis=1)


def north_of(before, here, after):
    row = lax.broadcasted_iota(jnp.int32, here.shape, 0)
    above = jnp.where(row == SUB - 1, pltpu.roll(after, SUB - 1, axis=0), pltpu.roll(here, SUB - 1, axis=0))
    below = jnp.where(row == 0, pltpu.roll(before, 1, axis=0), pltpu.roll(here, 1, axis=0))
    return above - below


def window_kernel(window, depth, waits, *refs):
    refs = list(refs)
    place_ref, local_ref, remote_ref, table_ref = refs[:4]
    refs = refs[4 + waits :]
    carry_ref = None if window.first else refs.pop(0)
    out_refs = [refs.pop(0) for _ in range(4)]
    carried_ref = None if window.last else refs.pop(0)
    table, lhs_high, lhs_low, wind, second, third, shift, results, carried, table_sem, out_sems = refs
    band, core, side = place_ref[0], place_ref[1], place_ref[2]
    rows, extended = window.rows, window.extended

    def at(pair):
        return multiple(choose(band, pair), SUB)

    tables = pltpu.make_async_copy(table_ref, table, table_sem)
    tables.start()
    lane = lax.broadcasted_iota(jnp.int32, (rows, LANE), 1)
    even, odd = [], []
    for c in range(2):
        mine, theirs = local_ref[c], remote_ref[c]
        low, high = jnp.where(band == 0, mine, theirs), jnp.where(band == 0, theirs, mine)
        low_rest, high_rest = low[:, 4 * LANE :], high[:, 4 * LANE :]
        turn = functools.partial(pltpu.roll, shift=LANE // 2, axis=1)
        even_rest = jnp.where(lane < LANE // 2, low_rest, turn(high_rest))
        odd_rest = jnp.where(lane < LANE // 2, turn(low_rest), high_rest)
        even.append(jnp.concatenate([low[:, : 2 * LANE], high[:, : 2 * LANE], even_rest], axis=1))
        odd.append(jnp.concatenate([low[:, 2 * LANE : 4 * LANE], high[:, 2 * LANE : 4 * LANE], odd_rest], axis=1))
    for parity, parts in enumerate((even, odd)):
        lhs = jnp.concatenate(parts)
        lhs_high[parity] = lhs.astype(jnp.bfloat16)
        lhs_low[parity] = (lhs - lhs_high[parity].astype(jnp.float32)).astype(jnp.bfloat16)
    tables.wait()

    place = at(window.place)
    if window.first or window.last:
        for c in range(2):
            if window.first:
                wind[c, pl.ds(at((extended - SUB, 0)), SUB), :] = jnp.zeros((SUB, NLON), jnp.float32)
            if window.last:
                wind[c, pl.ds(at((0, extended - SUB)), SUB), :] = jnp.zeros((SUB, NLON), jnp.float32)
    if not window.first:
        for c in range(2):
            wind[c, pl.ds(at((extended - 2 * SUB, 0)), 2 * SUB), :] = carry_ref[c]

    dot = functools.partial(jnp.dot, preferred_element_type=jnp.float32)
    for start in range(0, NLON // 2, 2 * LANE):
        stop = min(start + 2 * LANE, NLON // 2)
        columns = slice(start, stop)
        sums = []
        for parity in range(2):
            total = dot(lhs_high[parity], table[2 * parity, :, columns])
            total += dot(lhs_low[parity], table[2 * parity, :, columns])
            total += dot(lhs_high[parity], table[2 * parity + 1, :, columns])
            sums.append(total)
        for c in range(2):
            even_sum, odd_sum = (total[c * rows : (c + 1) * rows] for total in sums)
            wind[c, pl.ds(place, rows), start:stop] = even_sum + odd_sum
            wind[c, pl.ds(place, rows), NLON // 2 + start : NLON // 2 + stop] = even_sum - odd_sum

    if not window.last:
        for c in range(2):
            carried[c] = wind[c, pl.ds(at((0, extended - 2 * SUB)), 2 * SUB), :]
        carry_on = pltpu.make_async_copy(carried, carried_ref, out_sems.at[4])
        carry_on.start()

    blocks = extended // SUB

    def rows_of(block):
        return pl.ds(pl.multiple_of(block * SUB, SUB), SUB)

    def derivatives(field, block):
        before, after = jnp.maximum(block - 1, 0), jnp.minimum(block + 1, blocks - 1)
        result = []
        for c in range(2):
            here = field[c, rows_of(block), :]
            result.append((east_of(here), north_of(field[c, rows_of(before), :], here, field[c, rows_of(after), :])))
        return result

    @pl.loop(0, blocks, unroll=6)
    def _(block):
        flow = [wind[c, rows_of(block), :] for c in range(2)]
        for c, (east, north) in enumerate(derivatives(wind, block)):
            second[c, rows_of(block), :] = 0.25 * (flow[0] * east + flow[1] * north) - flow[c]

    @pl.loop(0, blocks, unroll=6)
    def _(block):
        flow = [wind[c, rows_of(block), :] for c in range(2)]
        for c, (east, north) in enumerate(derivatives(second, block)):
            third[c, rows_of(block), :] = -flow[c] - 0.25 * (flow[0] * east + flow[1] * north)

    @pl.loop(0, blocks, unroll=6)
    def _(block):
        flow = [wind[c, rows_of(block), :] for c in range(2)]
        for c, (east, north) in enumerate(derivatives(third, block)):
            fourth = -flow[c] - 0.5 * (flow[0] * east + flow[1] * north)
            both = second[c, rows_of(block), :] + third[c, rows_of(block), :]
            shift[c, rows_of(block), :] = (2.0 * both + (fourth - flow[c])) * (1.0 / 6.0)

    quarter = window.width // 4 // SUB

    def entries(out, base):
        @pl.loop(0, quarter, unroll=4)
        def _(block):
            (e0, n0), (e1, n1) = derivatives(shift, base + block + 1)
            g_xx, g_xy, g_yx, g_yy = 1.0 + 0.5 * e0, 0.5 * n0, 0.5 * e1, 1.0 + 0.5 * n1
            out[0, rows_of(block), :] = g_xx * g_xx + g_yx * g_yx
            out[1, rows_of(block), :] = g_xx * g_xy + g_yx * g_yy
            out[2, rows_of(block), :] = g_xy * g_xy + g_yy * g_yy

    copies = []
    for n, (a, b) in reversed(list(enumerate(QUARTERS))):
        entries(results.at[n], (2 * (core + a - 2 * core * a) + (side + b - 2 * side * b)) * quarter)
        copies.append(pltpu.make_async_copy(results.at[n], out_refs[n], out_sems.at[n]))
        copies[-1].start()
    for copy in copies:
        copy.wait()
    if not window.last:
        carry_on.wait()


QUARTERS = ((0, 0), (0, 1), (1, 0), (1, 1))


def window_tensor(window, place, local, remote, table, waits, carry):
    depth = local.shape[2]
    vmem = pl.BlockSpec(memory_space=pltpu.VMEM)
    in_specs = [
        pl.BlockSpec(memory_space=pltpu.SMEM),
        vmem,
        vmem,
        pl.BlockSpec(memory_space=pl.ANY),
    ]
    in_specs += [pl.BlockSpec(memory_space=pl.ANY)] * len(waits)
    operands = [place, local, remote, table, *waits]
    if not window.first:
        in_specs.append(vmem)
        operands.append(carry)
    out_shape = [jax.ShapeDtypeStruct((3, window.width // 4, NLON), jnp.float32)] * 4
    if not window.last:
        out_shape.append(jax.ShapeDtypeStruct((2, 2 * SUB, NLON), jnp.float32))
    field = pltpu.VMEM((2, window.extended, NLON), jnp.float32)
    lhs_shape = (2, 2 * window.rows, depth)
    out = pl.pallas_call(
        functools.partial(window_kernel, window, depth, len(waits)),
        out_shape=out_shape,
        in_specs=in_specs,
        out_specs=[pl.BlockSpec(memory_space=pl.ANY)] * len(out_shape),
        scratch_shapes=[
            pltpu.VMEM(table.shape, table.dtype),
            pltpu.VMEM(lhs_shape, jnp.bfloat16),
            pltpu.VMEM(lhs_shape, jnp.bfloat16),
            field,
            field,
            field,
            field,
            pltpu.VMEM((4, 3, window.width // 4, NLON), jnp.float32),
            pltpu.VMEM((2, 2 * SUB, NLON), jnp.float32),
            pltpu.SemaphoreType.DMA,
            pltpu.SemaphoreType.DMA((5,)),
        ],
        compiler_params=pltpu.CompilerParams(vmem_limit_bytes=VMEM_LIMIT),
        cost_estimate=pl.CostEstimate(
            flops=KERNEL_WORK * 3 * 2 * 2 * window.rows * depth * NLON,
            transcendentals=0,
            bytes_accessed=2 * table.size + 4 * window.rows * depth * 4 + 12 * window.width * NLON,
        ),
        name="window_tensor",
    )(*operands)
    return out[:4], (None if window.last else out[4])


def pairs(members, bit):
    return [(member, member ^ bit) for member in range(members)]


def pairs(members, bit):
    return [(member, member ^ bit) for member in range(members)]


def put_kernel(count, place_ref, *refs):
    parts, out_ref, sem = refs[:4], refs[-2], refs[-1]
    core, side, along = place_ref[0], place_ref[1], place_ref[2]
    around = parts[0].shape[1]
    copies = []
    for a, part in enumerate(parts):
        half = core if a < 2 else 1 - core
        quarter = side if a % 2 == 0 else 1 - side
        for w in range(count):
            level, row = place_ref[3 + 4 * w + half], place_ref[5 + 4 * w + half]
            for n in range(around):
                piece = lax.rem(along + 1 + n, around)
                at = multiple(row + (quarter * around + piece) * SUB, SUB)
                copies.append(pltpu.make_async_copy(part.at[w, n], out_ref.at[level, pl.ds(at, SUB)], sem.at[a, w, n]))
                copies[-1].start()
    for copy in copies:
        copy.wait()


def put(out, shape, places, parts):
    count = parts[0].shape[0]
    extra = [] if out is None else [out]
    return pl.pallas_call(
        functools.partial(put_kernel, count),
        in_specs=[pl.BlockSpec(memory_space=pltpu.SMEM)]
        + [pl.BlockSpec(memory_space=pltpu.VMEM)] * 4
        + [pl.BlockSpec(memory_space=pl.ANY)] * len(extra),
        out_specs=pl.BlockSpec(memory_space=pl.ANY),
        out_shape=jax.ShapeDtypeStruct(shape, jnp.float32),
        input_output_aliases={5: 0} if extra else {},
        scratch_shapes=[pltpu.SemaphoreType.DMA((4, count, parts[0].shape[1]))],
        compiler_params=pltpu.CompilerParams(vmem_limit_bytes=VMEM_LIMIT),
        cost_estimate=pl.CostEstimate(flops=0, transcendentals=0, bytes_accessed=8 * 4 * parts[0].size),
        name="put",
    )(places.astype(jnp.int32), *parts, *extra)


def pairs(members, bit):
    return [(member, member ^ bit) for member in range(members)]


def by_levels(coeffs):
    spec = coeffs[0]
    levels, _, parts, waves_local, nlat = spec.shape
    members = lax.axis_size("mem")
    band = lax.axis_index("band").astype(jnp.int32)
    member = lax.axis_index("mem").astype(jnp.int32)
    core, side = member % 2, member // 2 % 2
    place = jnp.stack([band, core, side])
    spec = spec.reshape(levels, 2, parts * waves_local, nlat)
    count = nlat // LANE
    windows = [Window(k, count) for k in range(count)]
    table = jnp.asarray(wave_table(levels, waves_local))
    swap = [(0, 1), (1, 0)]

    (piece,) = pieces_of(spec, 1 - band, windows[:1], count)
    remotes = [lax.ppermute(piece, "band", swap)]
    outgoing = pieces_of(spec, 1 - band, windows[1:], count)
    remotes += [lax.ppermute(piece, "band", swap) for piece in outgoing]
    local = pieces_of(spec, band, windows, count)

    bits = [1 << n for n in range(members.bit_length() - 1)]

    def halved(parts_of, bit):
        half = parts_of[0].shape[1] // 2
        mine = (member // bit) % 2

        def total(which):
            return sum(lax.dynamic_slice_in_dim(part, which * half, half, axis=1) for part in parts_of)

        leaves = total(1 - mine)
        return [total(mine), lax.ppermute(leaves, "mem", pairs(members, bit))], leaves

    def across(parts_of, bit):
        kept, passed, kept_more, passed_more = parts_of
        leaves = passed + passed_more
        return [kept, kept_more, lax.ppermute(leaves, "mem", pairs(members, bit))], leaves

    def advanced(parts_of, bit):
        return (across if len(parts_of) == 4 else halved)(parts_of, bit)

    def doubled(part, bit):
        beside = lax.ppermute(part, "mem", pairs(members, bit))
        mine = (member // bit) % 2
        low, high = jnp.concatenate([part, beside], axis=1), jnp.concatenate([beside, part], axis=1)
        return jnp.where(mine == 0, low, high), beside

    carry = None
    sums, done = [], []
    for k, window in enumerate(windows):
        waits = []
        for j in AHEAD[k]:
            sums[j], left = advanced(sums[j], bits[done[j]])
            done[j] += 1
            waits.append(left)
        quarters, carry = window_tensor(window, place, local[k], remotes[k], table, waits, carry)
        sent = quarters[3] if k + 1 < len(windows) else gated(quarters[3], [sums[2][-1], sums[3][-1]])
        first = lax.ppermute(sent, "mem", pairs(members, bits[0]))
        second = lax.ppermute(quarters[2], "mem", pairs(members, bits[0]))
        sums.append([quarters[0], quarters[1], second, first])
        done.append(1)
    parts_of_last = quarters[0]

    def step(k, waits=()):
        if waits:
            sums[k] = [gated(sums[k][0], list(waits)), *sums[k][1:]]
        sums[k], left = advanced(sums[k], bits[done[k]])
        done[k] += 1
        return left

    def exponent(k):
        return exponent_of(sum(sums[k]), members)

    def arrival(k):
        return sums[k][-1]

    made = [parts_of_last]
    step(1, made)
    step(2, made)
    step(3, made)
    step(4)
    left = step(4, [arrival(3)])
    for k in range(2):
        sums[k] = [gated(sums[k][0], [left]), *sums[k][1:]]
    swapped = lax.ppermute(jnp.stack([exponent(0), exponent(1)]), "band", swap)
    step(2, [left])
    step(3, [left])
    both = exponent(2)
    trades = []
    for m in range(members):
        for b in range(2):
            mate = (m, b) if m % 2 == b else (m ^ 1, 1 - b)
            trades.append((m * 2 + b, mate[0] * 2 + mate[1]))
    both = lax.ppermute(both, ("mem", "band"), trades)
    early = jnp.concatenate([swapped, both[None]])
    orders = [arrival(4)]
    step(4)
    orders.append(arrival(4))
    late = jnp.stack([exponent(3), exponent(4)])
    for n, bit in enumerate(reversed(bits)):
        early, _ = doubled(gated(early, [orders[n]]), bit)
        late, beside = doubled(late, bit)
        orders.append(beside)
    other, both = early[:-1], early[-1]
    middle = both.shape[0] // 2
    low, high = both[:middle], both[middle:]
    rest = jnp.zeros((nlat // 2 - middle, NLON), jnp.float32)
    down = jnp.stack([jnp.concatenate([rest, low]), jnp.concatenate([*other, high])])
    up = jnp.stack([jnp.concatenate([low, *other[::-1]]), jnp.concatenate([high, rest])])
    out = jnp.where(band == 0, down, up)

    for k, block in enumerate(late):
        width = block.shape[0]
        row = choose(band, (nlat // 2 - middle - (k + 1) * width, middle + k * width))
        out = lax.dynamic_update_slice(out, block[None], (band, row.astype(jnp.int32), jnp.int32(0)))
    return out


def per_device(coeffs):
    _, levels, _, _, _, nlat = coeffs.shape
    members = lax.axis_size("mem")
    rows = nlat // lax.axis_size("band")
    fits = coeffs.shape[4] == 5 * LANE // 2 and nlat % (2 * LANE) == LANE and rows > LANE
    if fits and levels == lax.axis_size("band") == 2 and members == 16:
        return by_levels(coeffs)
    return by_rows(coeffs)


def solution(mesh):
    placed = (P("mem", None, None, None, "band", None),)
    return jax.shard_map(
        per_device, mesh=mesh, in_specs=placed, out_specs=P(None, "band", None), check_vma=False
    )
```

```python
import functools
import math

import jax
import jax.numpy as jnp
import ml_dtypes
import numpy as np
from jax import lax
from jax.experimental import pallas as pl
from jax.experimental.pallas import tpu as pltpu
from jax.sharding import PartitionSpec as P

NLON = 1280
STEPS = 1
SUB = 8
LANE = 128
VMEM_LIMIT = 60 * 1024 * 1024
KERNEL_WORK = 8
ORDER = ((2, 4, 8), (4, 8, 2))
AHEAD = ((), (), (0,), (1, 0), (2, 1, 0))


def padded(cells, sides, width):
    for axis, dim in sides:
        count = lax.axis_size(axis)
        ends = count - 1
        head = lax.slice_in_dim(cells, 0, width, axis=dim)
        tail = lax.slice_in_dim(cells, cells.shape[dim] - width, cells.shape[dim], axis=dim)
        cells = jnp.concatenate(
            [
                lax.ppermute(tail, axis, [(i, (i + 1) % count) for i in range(ends)]),
                cells,
                lax.ppermute(head, axis, [((i + 1) % count, i) for i in range(ends)]),
            ],
            axis=dim,
        )
    return cells


def slope(extended, winds):
    center = extended[:, 1:-1]
    north = (extended[:, 2:] - extended[:, :-2]) * 0.5
    east = (jnp.roll(center, -1, 2) - jnp.roll(center, 1, 2)) * 0.5
    return -winds - (winds[0] * east + winds[1] * north)


def rimmed(field):
    return padded(field, (("band", 1),), 1)


def tensor(extended):
    center = extended[:, 1:-1]
    north = (extended[:, 2:] - extended[:, :-2]) * 0.5
    east = (jnp.roll(center, -1, 2) - jnp.roll(center, 1, 2)) * 0.5
    g_xx = 1.0 + east[0]
    g_xy = north[0]
    g_yx = east[1]
    g_yy = 1.0 + north[1]
    return jnp.stack(
        [g_xx * g_xx + g_yx * g_yx, g_xx * g_xy + g_yx * g_yy, g_xy * g_xy + g_yy * g_yy]
    )


def integrate(shift, flow, extend):
    first = slope(extend(shift), flow)
    second = slope(extend(0.5 * first), flow)
    third = slope(extend(0.5 * second), flow)
    fourth = slope(extend(third), flow)
    return (first + 2.0 * second + 2.0 * third + fourth) / 6.0


def exponent_of(summed, members):
    mean = summed / members
    first, cross, second = (mean[..., 0, :, :], mean[..., 1, :, :], mean[..., 2, :, :])
    half = (first + second) * 0.5
    differ = (first - second) * 0.5
    largest = half + jnp.sqrt(differ * differ + cross * cross)
    return jnp.log(largest + 1e-06) / (2.0 * STEPS)


def by_rows(coeffs):
    spec = coeffs[0]
    levels = spec.shape[0]
    nlat = spec.shape[4]
    waves = spec.shape[3] * lax.axis_size("band")
    members = lax.axis_size("mem")
    stacked = spec.reshape(levels * 2, 2, spec.shape[3], nlat)
    wave_index = lax.iota(jnp.int32, waves)
    column = lax.iota(jnp.int32, NLON)
    phase = wave_index[:, None] * column[None, :] % NLON
    angle = phase.astype(jnp.float32) * (2.0 * math.pi / NLON)
    weight = jnp.where(wave_index == 0, 1.0, 2.0).astype(jnp.float32)[:, None]
    table = jnp.stack([weight * jnp.cos(angle), -weight * jnp.sin(angle)], axis=0)
    winds = jnp.einsum(
        "crwh,rwn->chn",
        lax.all_to_all(stacked, "band", split_axis=3, concat_axis=2, tiled=True),
        table,
        precision=lax.Precision.HIGHEST,
        preferred_element_type=jnp.float32,
    )
    height = winds.shape[1]
    winds = winds.reshape(levels, 2, height, NLON)
    partials = []
    for level in range(levels):
        flow = winds[level]
        shift = integrate(jnp.zeros_like(flow), flow, rimmed)
        partials.append(tensor(rimmed(shift)))
    summed = lax.psum_scatter(jnp.stack(partials), "mem", scatter_dimension=3, tiled=True)
    return lax.all_gather(exponent_of(summed, members), "mem", axis=2, tiled=True)


def by_parity(waves_local):
    half = waves_local // 2
    whole = 2 * LANE - half
    runs = []
    for parity in range(2):
        runs += [(parity, half, 2), (waves_local + parity, whole, 2)]
    for parity in range(2):
        runs.append((waves_local + parity + 2 * whole, half - whole, 2))
    return runs


@functools.lru_cache(maxsize=None)
def wave_table(bands, waves_local):
    order = np.concatenate([start + step * np.arange(count) for start, count, step in by_parity(waves_local)])
    wave, part = order % waves_local, order // waves_local
    wave = wave[None, :] + waves_local * np.arange(bands)[:, None]
    part = np.broadcast_to(part, wave.shape)
    cut = [0, 2 * LANE, 4 * LANE, 4 * LANE + LANE // 2, 5 * LANE]
    result = []
    for parity in range(2):
        picks = [(band, slice(cut[parity], cut[parity + 1])) for band in range(bands)]
        picks += [(band, slice(cut[parity + 2], cut[parity + 3])) for band in range(bands)]
        waves = np.concatenate([wave[pick] for pick in picks])
        parts = np.concatenate([part[pick] for pick in picks])
        phase = (waves[:, None] * np.arange(NLON // 2)[None, :]) % NLON
        angle = phase.astype(np.float64) * (2.0 * np.pi / NLON)
        weight = np.where(waves == 0, 1.0, 2.0)[:, None]
        table = weight * np.where(parts[:, None] == 0, np.cos(angle), -np.sin(angle))
        high = table.astype(ml_dtypes.bfloat16)
        result += [high, (table - high.astype(np.float64)).astype(ml_dtypes.bfloat16)]
    return np.stack(result)


class Window:
    def __init__(self, index, count):
        self.first = index == 0
        self.last = index == count - 1
        self.index = index
        self.width = LANE
        self.extended = LANE + 2 * SUB
        self.main = LANE if self.first else LANE - SUB
        self.rim = 0 if self.last else SUB
        self.rows = self.main + self.rim
        up = SUB if self.first else 2 * SUB
        self.place = (self.extended - up - self.rows, up)
        self.side = "other" if 2 * (index + 1) <= count else "own" if 2 * index >= count else "both"


def choose(band, pair):
    return jnp.where(band == 0, pair[0], pair[1])


def multiple(value, of):
    return pl.multiple_of(value.astype(jnp.int32), of)


def pieces_kernel(windows, slots, count, level_ref, spec_ref, *refs):
    out_refs, (taken, turned, in_sems, out_sems) = refs[: len(windows)], refs[len(windows) :]
    level = level_ref[0]
    runs = by_parity(spec_ref.shape[2] // 2)

    def arrival(c, n):
        tile = choose(level, (count - 1 - slots[n], slots[n]))
        lanes = pl.ds(multiple(tile * LANE, LANE), LANE)
        return pltpu.make_async_copy(spec_ref.at[level, c, :, lanes], taken.at[c, n], in_sems.at[c, n])

    def departures(c, k):
        window, n = windows[k], slots.index(windows[k].index)
        rows = pl.ds(multiple(choose(level, (0, LANE - window.main)), SUB), window.main)
        at = pl.ds(multiple(choose(level, (window.rim, 0)), SUB), window.main)
        yield pltpu.make_async_copy(turned.at[c, n, rows], out_refs[k].at[c, at], out_sems.at[k, c, 0])
        if window.rim:
            rows = pl.ds(multiple(choose(level, (LANE - SUB, 0)), SUB), SUB)
            at = pl.ds(multiple(choose(level, (0, window.main)), SUB), SUB)
            yield pltpu.make_async_copy(turned.at[c, n + 1, rows], out_refs[k].at[c, at], out_sems.at[k, c, 1])

    for n in range(len(slots)):
        for c in range(2):
            arrival(c, n).start()
    for n in range(len(slots)):
        for c in range(2):
            arrival(c, n).wait()
            turned[c, n] = jnp.concatenate([taken[c, n, pl.ds(start, rows, step), :] for start, rows, step in runs]).T
        for k, window in enumerate(windows):
            if slots[n] == window.index + (1 if window.rim else 0):
                for c in range(2):
                    for copy in departures(c, k):
                        copy.start()
    for k in range(len(windows)):
        for c in range(2):
            for copy in departures(c, k):
                copy.wait()


def pieces_of(spec, level, windows, count):
    depth = spec.shape[2]
    slots = sorted({w.index for w in windows} | {w.index + 1 for w in windows if w.rim})
    return pl.pallas_call(
        functools.partial(pieces_kernel, windows, slots, count),
        in_specs=[pl.BlockSpec(memory_space=pltpu.SMEM), pl.BlockSpec(memory_space=pl.ANY)],
        out_specs=[pl.BlockSpec(memory_space=pl.ANY)] * len(windows),
        out_shape=[jax.ShapeDtypeStruct((2, w.rows, depth), jnp.float32) for w in windows],
        scratch_shapes=[
            pltpu.VMEM((2, len(slots), depth, LANE), jnp.float32),
            pltpu.VMEM((2, len(slots), LANE, depth), jnp.float32),
            pltpu.SemaphoreType.DMA((2, len(slots))),
            pltpu.SemaphoreType.DMA((len(windows), 2, 2)),
        ],
        compiler_params=pltpu.CompilerParams(vmem_limit_bytes=VMEM_LIMIT),
        cost_estimate=pl.CostEstimate(
            flops=0, transcendentals=0, bytes_accessed=4 * 2 * len(slots) * LANE * depth * 4
        ),
        name="pieces_of",
    )(level.reshape(1), spec)


def gate_kernel(*refs):
    pass


def gated(part, waits):
    return pl.pallas_call(
        gate_kernel,
        in_specs=[pl.BlockSpec(memory_space=pl.ANY)] * (1 + len(waits)),
        out_specs=pl.BlockSpec(memory_space=pl.ANY),
        out_shape=jax.ShapeDtypeStruct(part.shape, part.dtype),
        input_output_aliases={0: 0},
        cost_estimate=pl.CostEstimate(flops=0, transcendentals=0, bytes_accessed=1024),
        name="gated",
    )(part, *waits)


def east_of(x):
    return pltpu.roll(x, NLON - 1, axis=1) - pltpu.roll(x, 1, axis=1)


def north_of(before, here, after):
    row = lax.broadcasted_iota(jnp.int32, here.shape, 0)
    above = jnp.where(row == SUB - 1, pltpu.roll(after, SUB - 1, axis=0), pltpu.roll(here, SUB - 1, axis=0))
    below = jnp.where(row == 0, pltpu.roll(before, 1, axis=0), pltpu.roll(here, 1, axis=0))
    return above - below


def window_kernel(window, depth, waits, *refs):
    refs = list(refs)
    place_ref, local_ref, remote_ref, table_ref = refs[:4]
    refs = refs[4 + waits :]
    carry_ref = None if window.first else refs.pop(0)
    out_refs = [refs.pop(0) for _ in range(4)]
    carried_ref = None if window.last else refs.pop(0)
    table, lhs_high, lhs_low, wind, second, third, shift, results, carried, table_sem, out_sems = refs
    band, core, sides = place_ref[0], place_ref[1], (place_ref[2], place_ref[3])
    rows, extended = window.rows, window.extended

    def at(pair):
        return multiple(choose(band, pair), SUB)

    tables = pltpu.make_async_copy(table_ref, table, table_sem)
    tables.start()
    lane = lax.broadcasted_iota(jnp.int32, (rows, LANE), 1)
    even, odd = [], []
    for c in range(2):
        mine, theirs = local_ref[c], remote_ref[c]
        low, high = jnp.where(band == 0, mine, theirs), jnp.where(band == 0, theirs, mine)
        low_rest, high_rest = low[:, 4 * LANE :], high[:, 4 * LANE :]
        turn = functools.partial(pltpu.roll, shift=LANE // 2, axis=1)
        even_rest = jnp.where(lane < LANE // 2, low_rest, turn(high_rest))
        odd_rest = jnp.where(lane < LANE // 2, turn(low_rest), high_rest)
        even.append(jnp.concatenate([low[:, : 2 * LANE], high[:, : 2 * LANE], even_rest], axis=1))
        odd.append(jnp.concatenate([low[:, 2 * LANE : 4 * LANE], high[:, 2 * LANE : 4 * LANE], odd_rest], axis=1))
    for parity, parts in enumerate((even, odd)):
        lhs = jnp.concatenate(parts)
        lhs_high[parity] = lhs.astype(jnp.bfloat16)
        lhs_low[parity] = (lhs - lhs_high[parity].astype(jnp.float32)).astype(jnp.bfloat16)
    tables.wait()

    place = at(window.place)
    if window.first or window.last:
        for c in range(2):
            if window.first:
                wind[c, pl.ds(at((extended - SUB, 0)), SUB), :] = jnp.zeros((SUB, NLON), jnp.float32)
            if window.last:
                wind[c, pl.ds(at((0, extended - SUB)), SUB), :] = jnp.zeros((SUB, NLON), jnp.float32)
    if not window.first:
        for c in range(2):
            wind[c, pl.ds(at((extended - 2 * SUB, 0)), 2 * SUB), :] = carry_ref[c]

    dot = functools.partial(jnp.dot, preferred_element_type=jnp.float32)
    for start in range(0, NLON // 2, 2 * LANE):
        stop = min(start + 2 * LANE, NLON // 2)
        columns = slice(start, stop)
        sums = []
        for parity in range(2):
            total = dot(lhs_high[parity], table[2 * parity, :, columns])
            total += dot(lhs_low[parity], table[2 * parity, :, columns])
            total += dot(lhs_high[parity], table[2 * parity + 1, :, columns])
            sums.append(total)
        for c in range(2):
            even_sum, odd_sum = (total[c * rows : (c + 1) * rows] for total in sums)
            wind[c, pl.ds(place, rows), start:stop] = even_sum + odd_sum
            wind[c, pl.ds(place, rows), NLON // 2 + start : NLON // 2 + stop] = even_sum - odd_sum

    if not window.last:
        for c in range(2):
            carried[c] = wind[c, pl.ds(at((0, extended - 2 * SUB)), 2 * SUB), :]
        carry_on = pltpu.make_async_copy(carried, carried_ref, out_sems.at[4])
        carry_on.start()

    blocks = extended // SUB

    def rows_of(block):
        return pl.ds(pl.multiple_of(block * SUB, SUB), SUB)

    def derivatives(field, block):
        before, after = jnp.maximum(block - 1, 0), jnp.minimum(block + 1, blocks - 1)
        result = []
        for c in range(2):
            here = field[c, rows_of(block), :]
            result.append((east_of(here), north_of(field[c, rows_of(before), :], here, field[c, rows_of(after), :])))
        return result

    @pl.loop(0, blocks, unroll=6)
    def _(block):
        flow = [wind[c, rows_of(block), :] for c in range(2)]
        for c, (east, north) in enumerate(derivatives(wind, block)):
            second[c, rows_of(block), :] = 0.25 * (flow[0] * east + flow[1] * north) - flow[c]

    @pl.loop(0, blocks, unroll=6)
    def _(block):
        flow = [wind[c, rows_of(block), :] for c in range(2)]
        for c, (east, north) in enumerate(derivatives(second, block)):
            third[c, rows_of(block), :] = -flow[c] - 0.25 * (flow[0] * east + flow[1] * north)

    @pl.loop(0, blocks, unroll=6)
    def _(block):
        flow = [wind[c, rows_of(block), :] for c in range(2)]
        for c, (east, north) in enumerate(derivatives(third, block)):
            fourth = -flow[c] - 0.5 * (flow[0] * east + flow[1] * north)
            both = second[c, rows_of(block), :] + third[c, rows_of(block), :]
            shift[c, rows_of(block), :] = (2.0 * both + (fourth - flow[c])) * (1.0 / 6.0)

    quarter = window.width // 4 // SUB

    def entries(out, base):
        @pl.loop(0, quarter, unroll=4)
        def _(block):
            (e0, n0), (e1, n1) = derivatives(shift, base + block + 1)
            g_xx, g_xy, g_yx, g_yy = 1.0 + 0.5 * e0, 0.5 * n0, 0.5 * e1, 1.0 + 0.5 * n1
            out[0, rows_of(block), :] = g_xx * g_xx + g_yx * g_yx
            out[1, rows_of(block), :] = g_xx * g_xy + g_yx * g_yy
            out[2, rows_of(block), :] = g_xy * g_xy + g_yy * g_yy

    copies = []
    for n, (a, b) in reversed(list(enumerate(QUARTERS))):
        side = sides[a]
        entries(results.at[n], (2 * (core + a - 2 * core * a) + (side + b - 2 * side * b)) * quarter)
        copies.append(pltpu.make_async_copy(results.at[n], out_refs[n], out_sems.at[n]))
        copies[-1].start()
    for copy in copies:
        copy.wait()
    if not window.last:
        carry_on.wait()


QUARTERS = ((0, 0), (0, 1), (1, 0), (1, 1))


def window_tensor(window, place, local, remote, table, waits, carry):
    depth = local.shape[2]
    vmem = pl.BlockSpec(memory_space=pltpu.VMEM)
    in_specs = [
        pl.BlockSpec(memory_space=pltpu.SMEM),
        vmem,
        vmem,
        pl.BlockSpec(memory_space=pl.ANY),
    ]
    in_specs += [pl.BlockSpec(memory_space=pl.ANY)] * len(waits)
    operands = [place, local, remote, table, *waits]
    if not window.first:
        in_specs.append(vmem)
        operands.append(carry)
    out_shape = [jax.ShapeDtypeStruct((3, window.width // 4, NLON), jnp.float32)] * 4
    if not window.last:
        out_shape.append(jax.ShapeDtypeStruct((2, 2 * SUB, NLON), jnp.float32))
    field = pltpu.VMEM((2, window.extended, NLON), jnp.float32)
    lhs_shape = (2, 2 * window.rows, depth)
    out = pl.pallas_call(
        functools.partial(window_kernel, window, depth, len(waits)),
        out_shape=out_shape,
        in_specs=in_specs,
        out_specs=[pl.BlockSpec(memory_space=pl.ANY)] * len(out_shape),
        scratch_shapes=[
            pltpu.VMEM(table.shape, table.dtype),
            pltpu.VMEM(lhs_shape, jnp.bfloat16),
            pltpu.VMEM(lhs_shape, jnp.bfloat16),
            field,
            field,
            field,
            field,
            pltpu.VMEM((4, 3, window.width // 4, NLON), jnp.float32),
            pltpu.VMEM((2, 2 * SUB, NLON), jnp.float32),
            pltpu.SemaphoreType.DMA,
            pltpu.SemaphoreType.DMA((5,)),
        ],
        compiler_params=pltpu.CompilerParams(vmem_limit_bytes=VMEM_LIMIT),
        cost_estimate=pl.CostEstimate(
            flops=KERNEL_WORK * 3 * 2 * 2 * window.rows * depth * NLON,
            transcendentals=0,
            bytes_accessed=2 * table.size + 4 * window.rows * depth * 4 + 12 * window.width * NLON,
        ),
        name="window_tensor",
    )(*operands)
    return out[:4], (None if window.last else out[4])


def put_kernel(count, place_ref, *refs):
    parts, out_ref, sem = refs[:4], refs[-2], refs[-1]
    core, side, along = place_ref[0], place_ref[1], place_ref[2]
    around = parts[0].shape[1]
    copies = []
    for a, part in enumerate(parts):
        half = core if a < 2 else 1 - core
        quarter = side if a % 2 == 0 else 1 - side
        for w in range(count):
            level, row = place_ref[3 + 4 * w + half], place_ref[5 + 4 * w + half]
            for n in range(around):
                piece = lax.rem(along + 1 + n, around)
                at = multiple(row + (quarter * around + piece) * SUB, SUB)
                copies.append(pltpu.make_async_copy(part.at[w, n], out_ref.at[level, pl.ds(at, SUB)], sem.at[a, w, n]))
                copies[-1].start()
    for copy in copies:
        copy.wait()


def put(out, shape, places, parts):
    count = parts[0].shape[0]
    extra = [] if out is None else [out]
    return pl.pallas_call(
        functools.partial(put_kernel, count),
        in_specs=[pl.BlockSpec(memory_space=pltpu.SMEM)]
        + [pl.BlockSpec(memory_space=pltpu.VMEM)] * 4
        + [pl.BlockSpec(memory_space=pl.ANY)] * len(extra),
        out_specs=pl.BlockSpec(memory_space=pl.ANY),
        out_shape=jax.ShapeDtypeStruct(shape, jnp.float32),
        input_output_aliases={5: 0} if extra else {},
        scratch_shapes=[pltpu.SemaphoreType.DMA((4, count, parts[0].shape[1]))],
        compiler_params=pltpu.CompilerParams(vmem_limit_bytes=VMEM_LIMIT),
        cost_estimate=pl.CostEstimate(flops=0, transcendentals=0, bytes_accessed=8 * 4 * parts[0].size),
        name="put",
    )(places.astype(jnp.int32), *parts, *extra)


def by_levels(coeffs):
    spec = coeffs[0]
    levels, _, parts, waves_local, nlat = spec.shape
    members = lax.axis_size("mem")
    band = lax.axis_index("band").astype(jnp.int32)
    member = lax.axis_index("mem").astype(jnp.int32)
    core = member % 2
    half_of = [choose(core, [member // bits[step] % 2 for bits in ORDER]) for step in range(len(ORDER[0]))]
    half_beside = choose(1 - core, [member // bits[0] % 2 for bits in ORDER])
    place = jnp.stack([band, core, half_of[0], half_beside])
    spec = spec.reshape(levels, 2, parts * waves_local, nlat)
    count = nlat // LANE
    windows = [Window(k, count) for k in range(count)]
    table = jnp.asarray(wave_table(levels, waves_local))
    swap = [(0, 1), (1, 0)]

    (piece,) = pieces_of(spec, 1 - band, windows[:1], count)
    remotes = [lax.ppermute(piece, "band", swap)]
    for k, piece in enumerate(pieces_of(spec, 1 - band, windows[1:], count), 1):
        if k > 1:
            piece = gated(piece, [remotes[k - 2]])
        remotes.append(lax.ppermute(piece, "band", swap))
    local = pieces_of(spec, band, windows, count)

    cores = [(m, m ^ 1) for m in range(members)]
    ways = [[(m, m ^ ORDER[m % 2][step]) for m in range(members)] for step in range(len(ORDER[0]))]

    def halved(parts_of, step):
        half = parts_of[0].shape[1] // 2
        mine = half_of[step]

        def total(which):
            return sum(lax.dynamic_slice_in_dim(part, which * half, half, axis=1) for part in parts_of)

        leaves = total(1 - mine)
        return [total(mine), lax.ppermute(leaves, "mem", ways[step])], leaves

    def across(parts_of, step):
        kept, passed, kept_more, passed_more = parts_of
        leaves = passed + passed_more
        return [kept, kept_more, lax.ppermute(leaves, "mem", ways[step])], leaves

    def advanced(parts_of, step):
        return (across if step == 0 else halved)(parts_of, step)

    def doubled(part, step):
        beside = lax.ppermute(part, "mem", cores if step < 0 else ways[step])
        mine = core if step < 0 else half_of[step]
        return jnp.where(mine == 0, jnp.concatenate([part, beside], axis=1), jnp.concatenate([beside, part], axis=1))

    def gathered(part):
        for step in range(len(ways) - 1, -2, -1):
            part = doubled(part, step)
        return part

    carry = None
    sums, done = [], []
    for k, window in enumerate(windows):
        waits = []
        for j in AHEAD[k]:
            sums[j], left = advanced(sums[j], done[j])
            done[j] += 1
            waits.append(left)
        quarters, carry = window_tensor(window, place, local[k], remotes[k], table, waits, carry)
        first = lax.ppermute(quarters[3], "mem", cores)
        second = lax.ppermute(quarters[2], "mem", cores)
        sums.append([quarters[0], quarters[1], second, first])
        done.append(0)
    pieces = {"own": [], "both": [], "other": []}
    for k, window in enumerate(windows):
        for step in range(done[k], len(ways)):
            sums[k], _ = advanced(sums[k], step)
        pieces[window.side].append(exponent_of(sum(sums[k]), members))

    other = lax.ppermute(jnp.stack(pieces["other"]), "band", swap)
    place_of = {}
    for m in range(members):
        for b in range(2):
            bits = ORDER[m % 2]
            piece = functools.reduce(lambda value, bit: 2 * value + m // bit % 2, bits, m % 2)
            place_of[piece, b] = m * 2 + b
    trades, half = [], members // 2
    for (piece, b), index in place_of.items():
        mate = (piece, b) if (piece < half) == (b == 0) else ((piece + half) % members, 1 - b)
        trades.append((index, place_of[mate]))
    both = lax.ppermute(pieces["both"][0], ("mem", "band"), trades)

    early = gathered(jnp.concatenate([other, both[None]]))
    other, both = early[:-1], early[-1]
    middle = both.shape[0] // 2
    low, high = both[:middle], both[middle:]
    rest = jnp.zeros((nlat // 2 - middle, NLON), jnp.float32)
    down = jnp.stack([jnp.concatenate([rest, low]), jnp.concatenate([*other, high])])
    up = jnp.stack([jnp.concatenate([low, *other[::-1]]), jnp.concatenate([high, rest])])
    out = jnp.where(band == 0, down, up)

    own = gathered(jnp.stack(pieces["own"]))
    for k, block in enumerate(own):
        width = block.shape[0]
        row = choose(band, (nlat // 2 - middle - (k + 1) * width, middle + k * width))
        out = lax.dynamic_update_slice(out, block[None], (band, row.astype(jnp.int32), jnp.int32(0)))
    return out


def per_device(coeffs):
    _, levels, _, _, _, nlat = coeffs.shape
    members = lax.axis_size("mem")
    rows = nlat // lax.axis_size("band")
    fits = coeffs.shape[4] == 5 * LANE // 2 and nlat % (2 * LANE) == LANE and rows > LANE
    if fits and levels == lax.axis_size("band") == 2 and members == 16:
        return by_levels(coeffs)
    return by_rows(coeffs)


def solution(mesh):
    placed = (P("mem", None, None, None, "band", None),)
    return jax.shard_map(
        per_device, mesh=mesh, in_specs=placed, out_specs=P(None, "band", None), check_vma=False
    )
```

```python
import functools
import math

import jax
import jax.numpy as jnp
import ml_dtypes
import numpy as np
from jax import lax
from jax.experimental import pallas as pl
from jax.experimental.pallas import tpu as pltpu
from jax.sharding import PartitionSpec as P

NLON = 1280
STEPS = 1
SUB = 8
LANE = 128
VMEM_LIMIT = 60 * 1024 * 1024
KERNEL_WORK = 8
ORDER = ((2, 4, 8), (4, 8, 2))
AHEAD = ((), (), (0,), (1, 0), (3, 2, 1, 0))


def padded(cells, sides, width):
    for axis, dim in sides:
        count = lax.axis_size(axis)
        ends = count - 1
        head = lax.slice_in_dim(cells, 0, width, axis=dim)
        tail = lax.slice_in_dim(cells, cells.shape[dim] - width, cells.shape[dim], axis=dim)
        cells = jnp.concatenate(
            [
                lax.ppermute(tail, axis, [(i, (i + 1) % count) for i in range(ends)]),
                cells,
                lax.ppermute(head, axis, [((i + 1) % count, i) for i in range(ends)]),
            ],
            axis=dim,
        )
    return cells


def slope(extended, winds):
    center = extended[:, 1:-1]
    north = (extended[:, 2:] - extended[:, :-2]) * 0.5
    east = (jnp.roll(center, -1, 2) - jnp.roll(center, 1, 2)) * 0.5
    return -winds - (winds[0] * east + winds[1] * north)


def rimmed(field):
    return padded(field, (("band", 1),), 1)


def tensor(extended):
    center = extended[:, 1:-1]
    north = (extended[:, 2:] - extended[:, :-2]) * 0.5
    east = (jnp.roll(center, -1, 2) - jnp.roll(center, 1, 2)) * 0.5
    g_xx = 1.0 + east[0]
    g_xy = north[0]
    g_yx = east[1]
    g_yy = 1.0 + north[1]
    return jnp.stack(
        [g_xx * g_xx + g_yx * g_yx, g_xx * g_xy + g_yx * g_yy, g_xy * g_xy + g_yy * g_yy]
    )


def integrate(shift, flow, extend):
    first = slope(extend(shift), flow)
    second = slope(extend(0.5 * first), flow)
    third = slope(extend(0.5 * second), flow)
    fourth = slope(extend(third), flow)
    return (first + 2.0 * second + 2.0 * third + fourth) / 6.0


def exponent_of(summed, members):
    mean = summed / members
    first, cross, second = (mean[..., 0, :, :], mean[..., 1, :, :], mean[..., 2, :, :])
    half = (first + second) * 0.5
    differ = (first - second) * 0.5
    largest = half + jnp.sqrt(differ * differ + cross * cross)
    return jnp.log(largest + 1e-06) / (2.0 * STEPS)


def by_rows(coeffs):
    spec = coeffs[0]
    levels = spec.shape[0]
    nlat = spec.shape[4]
    waves = spec.shape[3] * lax.axis_size("band")
    members = lax.axis_size("mem")
    stacked = spec.reshape(levels * 2, 2, spec.shape[3], nlat)
    wave_index = lax.iota(jnp.int32, waves)
    column = lax.iota(jnp.int32, NLON)
    phase = wave_index[:, None] * column[None, :] % NLON
    angle = phase.astype(jnp.float32) * (2.0 * math.pi / NLON)
    weight = jnp.where(wave_index == 0, 1.0, 2.0).astype(jnp.float32)[:, None]
    table = jnp.stack([weight * jnp.cos(angle), -weight * jnp.sin(angle)], axis=0)
    winds = jnp.einsum(
        "crwh,rwn->chn",
        lax.all_to_all(stacked, "band", split_axis=3, concat_axis=2, tiled=True),
        table,
        precision=lax.Precision.HIGHEST,
        preferred_element_type=jnp.float32,
    )
    height = winds.shape[1]
    winds = winds.reshape(levels, 2, height, NLON)
    partials = []
    for level in range(levels):
        flow = winds[level]
        shift = integrate(jnp.zeros_like(flow), flow, rimmed)
        partials.append(tensor(rimmed(shift)))
    summed = lax.psum_scatter(jnp.stack(partials), "mem", scatter_dimension=3, tiled=True)
    return lax.all_gather(exponent_of(summed, members), "mem", axis=2, tiled=True)


def by_parity(waves_local):
    half = waves_local // 2
    whole = 2 * LANE - half
    runs = []
    for parity in range(2):
        runs += [(parity, half, 2), (waves_local + parity, whole, 2)]
    for parity in range(2):
        runs.append((waves_local + parity + 2 * whole, half - whole, 2))
    return runs


@functools.lru_cache(maxsize=None)
def wave_table(bands, waves_local):
    order = np.concatenate([start + step * np.arange(count) for start, count, step in by_parity(waves_local)])
    wave, part = order % waves_local, order // waves_local
    wave = wave[None, :] + waves_local * np.arange(bands)[:, None]
    part = np.broadcast_to(part, wave.shape)
    cut = [0, 2 * LANE, 4 * LANE, 4 * LANE + LANE // 2, 5 * LANE]
    result = []
    for parity in range(2):
        picks = [(band, slice(cut[parity], cut[parity + 1])) for band in range(bands)]
        picks += [(band, slice(cut[parity + 2], cut[parity + 3])) for band in range(bands)]
        waves = np.concatenate([wave[pick] for pick in picks])
        parts = np.concatenate([part[pick] for pick in picks])
        phase = (waves[:, None] * np.arange(NLON // 2)[None, :]) % NLON
        angle = phase.astype(np.float64) * (2.0 * np.pi / NLON)
        weight = np.where(waves == 0, 1.0, 2.0)[:, None]
        table = weight * np.where(parts[:, None] == 0, np.cos(angle), -np.sin(angle))
        high = table.astype(ml_dtypes.bfloat16)
        result += [high, (table - high.astype(np.float64)).astype(ml_dtypes.bfloat16)]
    return np.stack(result)


class Window:
    def __init__(self, index, count):
        self.first = index == 0
        self.last = index == count - 1
        self.index = index
        self.width = LANE
        self.extended = LANE + 2 * SUB
        self.main = LANE if self.first else LANE - SUB
        self.rim = 0 if self.last else SUB
        self.rows = self.main + self.rim
        up = SUB if self.first else 2 * SUB
        self.place = (self.extended - up - self.rows, up)
        self.side = "other" if 2 * (index + 1) <= count else "own" if 2 * index >= count else "both"


def choose(band, pair):
    return jnp.where(band == 0, pair[0], pair[1])


def multiple(value, of):
    return pl.multiple_of(value.astype(jnp.int32), of)


def pieces_kernel(windows, slots, count, level_ref, spec_ref, *refs):
    out_refs, (taken, turned, in_sems, out_sems) = refs[: len(windows)], refs[len(windows) :]
    level = level_ref[0]
    runs = by_parity(spec_ref.shape[2] // 2)

    def arrival(c, n):
        tile = choose(level, (count - 1 - slots[n], slots[n]))
        lanes = pl.ds(multiple(tile * LANE, LANE), LANE)
        return pltpu.make_async_copy(spec_ref.at[level, c, :, lanes], taken.at[c, n], in_sems.at[c, n])

    def departures(c, k):
        window, n = windows[k], slots.index(windows[k].index)
        rows = pl.ds(multiple(choose(level, (0, LANE - window.main)), SUB), window.main)
        at = pl.ds(multiple(choose(level, (window.rim, 0)), SUB), window.main)
        yield pltpu.make_async_copy(turned.at[c, n, rows], out_refs[k].at[c, at], out_sems.at[k, c, 0])
        if window.rim:
            rows = pl.ds(multiple(choose(level, (LANE - SUB, 0)), SUB), SUB)
            at = pl.ds(multiple(choose(level, (0, window.main)), SUB), SUB)
            yield pltpu.make_async_copy(turned.at[c, n + 1, rows], out_refs[k].at[c, at], out_sems.at[k, c, 1])

    for n in range(len(slots)):
        for c in range(2):
            arrival(c, n).start()
    for n in range(len(slots)):
        for c in range(2):
            arrival(c, n).wait()
            turned[c, n] = jnp.concatenate([taken[c, n, pl.ds(start, rows, step), :] for start, rows, step in runs]).T
        for k, window in enumerate(windows):
            if slots[n] == window.index + (1 if window.rim else 0):
                for c in range(2):
                    for copy in departures(c, k):
                        copy.start()
    for k in range(len(windows)):
        for c in range(2):
            for copy in departures(c, k):
                copy.wait()


def pieces_of(spec, level, windows, count):
    depth = spec.shape[2]
    slots = sorted({w.index for w in windows} | {w.index + 1 for w in windows if w.rim})
    return pl.pallas_call(
        functools.partial(pieces_kernel, windows, slots, count),
        in_specs=[pl.BlockSpec(memory_space=pltpu.SMEM), pl.BlockSpec(memory_space=pl.ANY)],
        out_specs=[pl.BlockSpec(memory_space=pl.ANY)] * len(windows),
        out_shape=[jax.ShapeDtypeStruct((2, w.rows, depth), jnp.float32) for w in windows],
        scratch_shapes=[
            pltpu.VMEM((2, len(slots), depth, LANE), jnp.float32),
            pltpu.VMEM((2, len(slots), LANE, depth), jnp.float32),
            pltpu.SemaphoreType.DMA((2, len(slots))),
            pltpu.SemaphoreType.DMA((len(windows), 2, 2)),
        ],
        compiler_params=pltpu.CompilerParams(vmem_limit_bytes=VMEM_LIMIT),
        cost_estimate=pl.CostEstimate(
            flops=0, transcendentals=0, bytes_accessed=4 * 2 * len(slots) * LANE * depth * 4
        ),
        name="pieces_of",
    )(level.reshape(1), spec)


def gate_kernel(*refs):
    pass


def gated(part, waits):
    return pl.pallas_call(
        gate_kernel,
        in_specs=[pl.BlockSpec(memory_space=pl.ANY)] * (1 + len(waits)),
        out_specs=pl.BlockSpec(memory_space=pl.ANY),
        out_shape=jax.ShapeDtypeStruct(part.shape, part.dtype),
        input_output_aliases={0: 0},
        cost_estimate=pl.CostEstimate(flops=0, transcendentals=0, bytes_accessed=1024),
        name="gated",
    )(part, *waits)


def east_of(x):
    return pltpu.roll(x, NLON - 1, axis=1) - pltpu.roll(x, 1, axis=1)


def north_of(before, here, after):
    row = lax.broadcasted_iota(jnp.int32, here.shape, 0)
    above = jnp.where(row == SUB - 1, pltpu.roll(after, SUB - 1, axis=0), pltpu.roll(here, SUB - 1, axis=0))
    below = jnp.where(row == 0, pltpu.roll(before, 1, axis=0), pltpu.roll(here, 1, axis=0))
    return above - below


def window_kernel(window, depth, waits, *refs):
    refs = list(refs)
    place_ref, local_ref, remote_ref, table_ref = refs[:4]
    refs = refs[4 + waits :]
    carry_ref = None if window.first else refs.pop(0)
    out_refs = [refs.pop(0) for _ in range(4)]
    carried_ref = None if window.last else refs.pop(0)
    table, lhs_high, lhs_low, wind, second, third, shift, results, carried, table_sem, out_sems = refs
    band, core, sides = place_ref[0], place_ref[1], (place_ref[2], place_ref[3])
    rows, extended = window.rows, window.extended

    def at(pair):
        return multiple(choose(band, pair), SUB)

    tables = pltpu.make_async_copy(table_ref, table, table_sem)
    tables.start()
    lane = lax.broadcasted_iota(jnp.int32, (rows, LANE), 1)
    even, odd = [], []
    for c in range(2):
        mine, theirs = local_ref[c], remote_ref[c]
        low, high = jnp.where(band == 0, mine, theirs), jnp.where(band == 0, theirs, mine)
        low_rest, high_rest = low[:, 4 * LANE :], high[:, 4 * LANE :]
        turn = functools.partial(pltpu.roll, shift=LANE // 2, axis=1)
        even_rest = jnp.where(lane < LANE // 2, low_rest, turn(high_rest))
        odd_rest = jnp.where(lane < LANE // 2, turn(low_rest), high_rest)
        even.append(jnp.concatenate([low[:, : 2 * LANE], high[:, : 2 * LANE], even_rest], axis=1))
        odd.append(jnp.concatenate([low[:, 2 * LANE : 4 * LANE], high[:, 2 * LANE : 4 * LANE], odd_rest], axis=1))
    for parity, parts in enumerate((even, odd)):
        lhs = jnp.concatenate(parts)
        lhs_high[parity] = lhs.astype(jnp.bfloat16)
        lhs_low[parity] = (lhs - lhs_high[parity].astype(jnp.float32)).astype(jnp.bfloat16)
    tables.wait()

    place = at(window.place)
    if window.first or window.last:
        for c in range(2):
            if window.first:
                wind[c, pl.ds(at((extended - SUB, 0)), SUB), :] = jnp.zeros((SUB, NLON), jnp.float32)
            if window.last:
                wind[c, pl.ds(at((0, extended - SUB)), SUB), :] = jnp.zeros((SUB, NLON), jnp.float32)
    if not window.first:
        for c in range(2):
            wind[c, pl.ds(at((extended - 2 * SUB, 0)), 2 * SUB), :] = carry_ref[c]

    dot = functools.partial(jnp.dot, preferred_element_type=jnp.float32)
    for start in range(0, NLON // 2, 2 * LANE):
        stop = min(start + 2 * LANE, NLON // 2)
        columns = slice(start, stop)
        sums = []
        for parity in range(2):
            total = dot(lhs_high[parity], table[2 * parity, :, columns])
            total += dot(lhs_low[parity], table[2 * parity, :, columns])
            total += dot(lhs_high[parity], table[2 * parity + 1, :, columns])
            sums.append(total)
        for c in range(2):
            even_sum, odd_sum = (total[c * rows : (c + 1) * rows] for total in sums)
            wind[c, pl.ds(place, rows), start:stop] = even_sum + odd_sum
            wind[c, pl.ds(place, rows), NLON // 2 + start : NLON // 2 + stop] = even_sum - odd_sum

    if not window.last:
        for c in range(2):
            carried[c] = wind[c, pl.ds(at((0, extended - 2 * SUB)), 2 * SUB), :]
        carry_on = pltpu.make_async_copy(carried, carried_ref, out_sems.at[4])
        carry_on.start()

    blocks = extended // SUB

    def rows_of(block):
        return pl.ds(pl.multiple_of(block * SUB, SUB), SUB)

    def derivatives(field, block):
        before, after = jnp.maximum(block - 1, 0), jnp.minimum(block + 1, blocks - 1)
        result = []
        for c in range(2):
            here = field[c, rows_of(block), :]
            result.append((east_of(here), north_of(field[c, rows_of(before), :], here, field[c, rows_of(after), :])))
        return result

    @pl.loop(0, blocks, unroll=6)
    def _(block):
        flow = [wind[c, rows_of(block), :] for c in range(2)]
        for c, (east, north) in enumerate(derivatives(wind, block)):
            second[c, rows_of(block), :] = 0.25 * (flow[0] * east + flow[1] * north) - flow[c]

    @pl.loop(0, blocks, unroll=6)
    def _(block):
        flow = [wind[c, rows_of(block), :] for c in range(2)]
        for c, (east, north) in enumerate(derivatives(second, block)):
            third[c, rows_of(block), :] = -flow[c] - 0.25 * (flow[0] * east + flow[1] * north)

    @pl.loop(0, blocks, unroll=6)
    def _(block):
        flow = [wind[c, rows_of(block), :] for c in range(2)]
        for c, (east, north) in enumerate(derivatives(third, block)):
            fourth = -flow[c] - 0.5 * (flow[0] * east + flow[1] * north)
            both = second[c, rows_of(block), :] + third[c, rows_of(block), :]
            shift[c, rows_of(block), :] = (2.0 * both + (fourth - flow[c])) * (1.0 / 6.0)

    quarter = window.width // 4 // SUB

    def entries(out, base):
        @pl.loop(0, quarter, unroll=4)
        def _(block):
            (e0, n0), (e1, n1) = derivatives(shift, base + block + 1)
            g_xx, g_xy, g_yx, g_yy = 1.0 + 0.5 * e0, 0.5 * n0, 0.5 * e1, 1.0 + 0.5 * n1
            out[0, rows_of(block), :] = g_xx * g_xx + g_yx * g_yx
            out[1, rows_of(block), :] = g_xx * g_xy + g_yx * g_yy
            out[2, rows_of(block), :] = g_xy * g_xy + g_yy * g_yy

    copies = []
    for n, (a, b) in reversed(list(enumerate(QUARTERS))):
        side = sides[a]
        entries(results.at[n], (2 * (core + a - 2 * core * a) + (side + b - 2 * side * b)) * quarter)
        copies.append(pltpu.make_async_copy(results.at[n], out_refs[n], out_sems.at[n]))
        copies[-1].start()
    for copy in copies:
        copy.wait()
    if not window.last:
        carry_on.wait()


QUARTERS = ((0, 0), (0, 1), (1, 0), (1, 1))


def window_tensor(window, place, local, remote, table, waits, carry):
    depth = local.shape[2]
    vmem = pl.BlockSpec(memory_space=pltpu.VMEM)
    in_specs = [
        pl.BlockSpec(memory_space=pltpu.SMEM),
        vmem,
        vmem,
        pl.BlockSpec(memory_space=pl.ANY),
    ]
    in_specs += [pl.BlockSpec(memory_space=pl.ANY)] * len(waits)
    operands = [place, local, remote, table, *waits]
    if not window.first:
        in_specs.append(vmem)
        operands.append(carry)
    out_shape = [jax.ShapeDtypeStruct((3, window.width // 4, NLON), jnp.float32)] * 4
    if not window.last:
        out_shape.append(jax.ShapeDtypeStruct((2, 2 * SUB, NLON), jnp.float32))
    field = pltpu.VMEM((2, window.extended, NLON), jnp.float32)
    lhs_shape = (2, 2 * window.rows, depth)
    out = pl.pallas_call(
        functools.partial(window_kernel, window, depth, len(waits)),
        out_shape=out_shape,
        in_specs=in_specs,
        out_specs=[pl.BlockSpec(memory_space=pl.ANY)] * len(out_shape),
        scratch_shapes=[
            pltpu.VMEM(table.shape, table.dtype),
            pltpu.VMEM(lhs_shape, jnp.bfloat16),
            pltpu.VMEM(lhs_shape, jnp.bfloat16),
            field,
            field,
            field,
            field,
            pltpu.VMEM((4, 3, window.width // 4, NLON), jnp.float32),
            pltpu.VMEM((2, 2 * SUB, NLON), jnp.float32),
            pltpu.SemaphoreType.DMA,
            pltpu.SemaphoreType.DMA((5,)),
        ],
        compiler_params=pltpu.CompilerParams(vmem_limit_bytes=VMEM_LIMIT),
        cost_estimate=pl.CostEstimate(
            flops=KERNEL_WORK * 3 * 2 * 2 * window.rows * depth * NLON,
            transcendentals=0,
            bytes_accessed=2 * table.size + 4 * window.rows * depth * 4 + 12 * window.width * NLON,
        ),
        name="window_tensor",
    )(*operands)
    return out[:4], (None if window.last else out[4])


def by_levels(coeffs):
    spec = coeffs[0]
    levels, _, parts, waves_local, nlat = spec.shape
    members = lax.axis_size("mem")
    band = lax.axis_index("band").astype(jnp.int32)
    member = lax.axis_index("mem").astype(jnp.int32)
    core = member % 2
    half_of = [choose(core, [member // bits[step] % 2 for bits in ORDER]) for step in range(len(ORDER[0]))]
    half_beside = choose(1 - core, [member // bits[0] % 2 for bits in ORDER])
    place = jnp.stack([band, core, half_of[0], half_beside])
    spec = spec.reshape(levels, 2, parts * waves_local, nlat)
    count = nlat // LANE
    windows = [Window(k, count) for k in range(count)]
    table = jnp.asarray(wave_table(levels, waves_local))
    swap = [(0, 1), (1, 0)]

    (piece,) = pieces_of(spec, 1 - band, windows[:1], count)
    remotes = [lax.ppermute(piece, "band", swap)]
    for k, piece in enumerate(pieces_of(spec, 1 - band, windows[1:], count), 1):
        if k > 1:
            piece = gated(piece, [remotes[k - 2]])
        remotes.append(lax.ppermute(piece, "band", swap))
    local = pieces_of(spec, band, windows, count)

    cores = [(m, m ^ 1) for m in range(members)]
    ways = [[(m, m ^ ORDER[m % 2][step]) for m in range(members)] for step in range(len(ORDER[0]))]

    def halved(parts_of, step):
        half = parts_of[0].shape[1] // 2
        mine = half_of[step]

        def total(which):
            return sum(lax.dynamic_slice_in_dim(part, which * half, half, axis=1) for part in parts_of)

        leaves = total(1 - mine)
        return [total(mine), lax.ppermute(leaves, "mem", ways[step])], leaves

    def across(parts_of, step):
        kept, passed, kept_more, passed_more = parts_of
        leaves = passed + passed_more
        return [kept, kept_more, lax.ppermute(leaves, "mem", ways[step])], leaves

    def advanced(parts_of, step):
        return (across if step == 0 else halved)(parts_of, step)

    def doubled(part, step):
        beside = lax.ppermute(part, "mem", cores if step < 0 else ways[step])
        mine = core if step < 0 else half_of[step]
        return jnp.where(mine == 0, jnp.concatenate([part, beside], axis=1), jnp.concatenate([beside, part], axis=1))

    carry = None
    sums, done = [], []
    for k, window in enumerate(windows):
        waits = []
        for j in AHEAD[k]:
            sums[j], left = advanced(sums[j], done[j])
            done[j] += 1
            waits.append(left)
        quarters, carry = window_tensor(window, place, local[k], remotes[k], table, waits, carry)
        sent = quarters[3] if k + 1 < count else gated(quarters[3], [sums[k - 2][-1], sums[k - 1][-1]])
        first = lax.ppermute(sent, "mem", cores)
        second = lax.ppermute(quarters[2], "mem", cores)
        sums.append([quarters[0], quarters[1], second, first])
        done.append(0)
    def step(k, waits):
        gate = 1 if done[k] == 0 else 0
        sums[k][gate] = gated(sums[k][gate], waits)
        sums[k], left = advanced(sums[k], done[k])
        done[k] += 1
        return left

    def exponents(some, waits):
        for k in some:
            sums[k] = [gated(sums[k][0], waits), *sums[k][1:]]
        return jnp.stack([exponent_of(sum(sums[k]), members) for k in some])

    left = step(2, [quarters[0]])
    left = step(3, [left])
    left = step(1, [left])
    left = step(4, [left])
    left = step(4, [left])
    far = exponents([0, 1], [left])
    swapped = lax.ppermute(far, "band", swap)
    left = step(2, [far])
    left = step(3, [left])
    left = step(4, [left])
    far = gated(swapped, [left])
    both = exponents([2], [far])
    place_of = {}
    for m in range(members):
        for b in range(2):
            bits = ORDER[m % 2]
            piece = functools.reduce(lambda value, bit: 2 * value + m // bit % 2, bits, m % 2)
            place_of[piece, b] = m * 2 + b
    trades, half = [], members // 2
    for (piece, b), index in place_of.items():
        mate = (piece, b) if (piece < half) == (b == 0) else ((piece + half) % members, 1 - b)
        trades.append((index, place_of[mate]))
    traded = lax.ppermute(both, ("mem", "band"), trades)
    near = jnp.concatenate([traded, exponents([3, 4], [both])])
    for n in (2, 1, 0):
        far = gated(doubled(far, n), [near])
        near = gated(doubled(near, n), [far])
    far, near = doubled(far, -1), doubled(near, -1)

    middle = near.shape[1] // 2
    rest = jnp.zeros((nlat // 2, NLON), jnp.float32)
    down = jnp.stack([rest, jnp.concatenate([*far, rest[:middle]])])
    up = jnp.stack([jnp.concatenate([rest[:middle], *far[::-1]]), rest])
    out = jnp.where(band == 0, down, up)

    def put(block, level, pair):
        return lax.dynamic_update_slice(
            out, block[None], (level, choose(band, pair).astype(jnp.int32), jnp.int32(0))
        )

    edge = nlat // 2 - middle
    out = put(near[0, :middle], 0, (edge, 0))
    out = put(near[0, middle:], 1, (edge, 0))
    for k, block in enumerate(near[1:]):
        out = put(block, band, (edge - (k + 1) * LANE, middle + k * LANE))
    return out


def per_device(coeffs):
    _, levels, _, _, _, nlat = coeffs.shape
    members = lax.axis_size("mem")
    rows = nlat // lax.axis_size("band")
    fits = coeffs.shape[4] == 5 * LANE // 2 and nlat % (2 * LANE) == LANE and rows > LANE
    if fits and levels == lax.axis_size("band") == 2 and members == 16:
        return by_levels(coeffs)
    return by_rows(coeffs)


def solution(mesh):
    placed = (P("mem", None, None, None, "band", None),)
    return jax.shard_map(
        per_device, mesh=mesh, in_specs=placed, out_specs=P(None, "band", None), check_vma=False
    )
```

```python
import functools
import math

import jax
import jax.numpy as jnp
import ml_dtypes
import numpy as np
from jax import lax
from jax.experimental import pallas as pl
from jax.experimental.pallas import tpu as pltpu
from jax.sharding import PartitionSpec as P

NLON = 1280
STEPS = 1
SUB = 8
LANE = 128
VMEM_LIMIT = 60 * 1024 * 1024
KERNEL_WORK = 8
ORDER = ((2, 4, 8), (4, 8, 2))
AHEAD = ((), (), (), (0,), (1, 0))


def padded(cells, sides, width):
    for axis, dim in sides:
        count = lax.axis_size(axis)
        ends = count - 1
        head = lax.slice_in_dim(cells, 0, width, axis=dim)
        tail = lax.slice_in_dim(cells, cells.shape[dim] - width, cells.shape[dim], axis=dim)
        cells = jnp.concatenate(
            [
                lax.ppermute(tail, axis, [(i, (i + 1) % count) for i in range(ends)]),
                cells,
                lax.ppermute(head, axis, [((i + 1) % count, i) for i in range(ends)]),
            ],
            axis=dim,
        )
    return cells


def slope(extended, winds):
    center = extended[:, 1:-1]
    north = (extended[:, 2:] - extended[:, :-2]) * 0.5
    east = (jnp.roll(center, -1, 2) - jnp.roll(center, 1, 2)) * 0.5
    return -winds - (winds[0] * east + winds[1] * north)


def rimmed(field):
    return padded(field, (("band", 1),), 1)


def tensor(extended):
    center = extended[:, 1:-1]
    north = (extended[:, 2:] - extended[:, :-2]) * 0.5
    east = (jnp.roll(center, -1, 2) - jnp.roll(center, 1, 2)) * 0.5
    g_xx = 1.0 + east[0]
    g_xy = north[0]
    g_yx = east[1]
    g_yy = 1.0 + north[1]
    return jnp.stack(
        [g_xx * g_xx + g_yx * g_yx, g_xx * g_xy + g_yx * g_yy, g_xy * g_xy + g_yy * g_yy]
    )


def integrate(shift, flow, extend):
    first = slope(extend(shift), flow)
    second = slope(extend(0.5 * first), flow)
    third = slope(extend(0.5 * second), flow)
    fourth = slope(extend(third), flow)
    return (first + 2.0 * second + 2.0 * third + fourth) / 6.0


def exponent_of(summed, members):
    mean = summed / members
    first, cross, second = (mean[..., 0, :, :], mean[..., 1, :, :], mean[..., 2, :, :])
    half = (first + second) * 0.5
    differ = (first - second) * 0.5
    largest = half + jnp.sqrt(differ * differ + cross * cross)
    return jnp.log(largest + 1e-06) / (2.0 * STEPS)


def by_rows(coeffs):
    spec = coeffs[0]
    levels = spec.shape[0]
    nlat = spec.shape[4]
    waves = spec.shape[3] * lax.axis_size("band")
    members = lax.axis_size("mem")
    stacked = spec.reshape(levels * 2, 2, spec.shape[3], nlat)
    wave_index = lax.iota(jnp.int32, waves)
    column = lax.iota(jnp.int32, NLON)
    phase = wave_index[:, None] * column[None, :] % NLON
    angle = phase.astype(jnp.float32) * (2.0 * math.pi / NLON)
    weight = jnp.where(wave_index == 0, 1.0, 2.0).astype(jnp.float32)[:, None]
    table = jnp.stack([weight * jnp.cos(angle), -weight * jnp.sin(angle)], axis=0)
    winds = jnp.einsum(
        "crwh,rwn->chn",
        lax.all_to_all(stacked, "band", split_axis=3, concat_axis=2, tiled=True),
        table,
        precision=lax.Precision.HIGHEST,
        preferred_element_type=jnp.float32,
    )
    height = winds.shape[1]
    winds = winds.reshape(levels, 2, height, NLON)
    partials = []
    for level in range(levels):
        flow = winds[level]
        shift = integrate(jnp.zeros_like(flow), flow, rimmed)
        partials.append(tensor(rimmed(shift)))
    summed = lax.psum_scatter(jnp.stack(partials), "mem", scatter_dimension=3, tiled=True)
    return lax.all_gather(exponent_of(summed, members), "mem", axis=2, tiled=True)


def by_parity(waves_local):
    half = waves_local // 2
    whole = 2 * LANE - half
    runs = []
    for parity in range(2):
        runs += [(parity, half, 2), (waves_local + parity, whole, 2)]
    for parity in range(2):
        runs.append((waves_local + parity + 2 * whole, half - whole, 2))
    return runs


@functools.lru_cache(maxsize=None)
def wave_table(bands, waves_local):
    order = np.concatenate([start + step * np.arange(count) for start, count, step in by_parity(waves_local)])
    wave, part = order % waves_local, order // waves_local
    wave = wave[None, :] + waves_local * np.arange(bands)[:, None]
    part = np.broadcast_to(part, wave.shape)
    cut = [0, 2 * LANE, 4 * LANE, 4 * LANE + LANE // 2, 5 * LANE]
    result = []
    for parity in range(2):
        picks = [(band, slice(cut[parity], cut[parity + 1])) for band in range(bands)]
        picks += [(band, slice(cut[parity + 2], cut[parity + 3])) for band in range(bands)]
        waves = np.concatenate([wave[pick] for pick in picks])
        parts = np.concatenate([part[pick] for pick in picks])
        phase = (waves[:, None] * np.arange(NLON // 2)[None, :]) % NLON
        angle = phase.astype(np.float64) * (2.0 * np.pi / NLON)
        weight = np.where(waves == 0, 1.0, 2.0)[:, None]
        table = weight * np.where(parts[:, None] == 0, np.cos(angle), -np.sin(angle))
        high = table.astype(ml_dtypes.bfloat16)
        result += [high, (table - high.astype(np.float64)).astype(ml_dtypes.bfloat16)]
    return np.stack(result)


class Window:
    def __init__(self, index, count):
        self.first = index == 0
        self.last = index == count - 1
        self.index = index
        self.width = LANE
        self.extended = LANE + 2 * SUB
        self.main = LANE if self.first else LANE - SUB
        self.rim = 0 if self.last else SUB
        self.rows = self.main + self.rim
        up = SUB if self.first else 2 * SUB
        self.place = (self.extended - up - self.rows, up)
        self.side = "other" if 2 * (index + 1) <= count else "own" if 2 * index >= count else "both"


def choose(band, pair):
    return jnp.where(band == 0, pair[0], pair[1])


def multiple(value, of):
    return pl.multiple_of(value.astype(jnp.int32), of)


def pieces_kernel(windows, slots, count, level_ref, spec_ref, *refs):
    out_refs, (taken, turned, in_sems, out_sems) = refs[: len(windows)], refs[len(windows) :]
    level = level_ref[0]
    runs = by_parity(spec_ref.shape[2] // 2)

    def arrival(c, n):
        tile = choose(level, (count - 1 - slots[n], slots[n]))
        lanes = pl.ds(multiple(tile * LANE, LANE), LANE)
        return pltpu.make_async_copy(spec_ref.at[level, c, :, lanes], taken.at[c, n], in_sems.at[c, n])

    def departures(c, k):
        window, n = windows[k], slots.index(windows[k].index)
        rows = pl.ds(multiple(choose(level, (0, LANE - window.main)), SUB), window.main)
        at = pl.ds(multiple(choose(level, (window.rim, 0)), SUB), window.main)
        yield pltpu.make_async_copy(turned.at[c, n, rows], out_refs[k].at[c, at], out_sems.at[k, c, 0])
        if window.rim:
            rows = pl.ds(multiple(choose(level, (LANE - SUB, 0)), SUB), SUB)
            at = pl.ds(multiple(choose(level, (0, window.main)), SUB), SUB)
            yield pltpu.make_async_copy(turned.at[c, n + 1, rows], out_refs[k].at[c, at], out_sems.at[k, c, 1])

    for n in range(len(slots)):
        for c in range(2):
            arrival(c, n).start()
    for n in range(len(slots)):
        for c in range(2):
            arrival(c, n).wait()
            turned[c, n] = jnp.concatenate([taken[c, n, pl.ds(start, rows, step), :] for start, rows, step in runs]).T
        for k, window in enumerate(windows):
            if slots[n] == window.index + (1 if window.rim else 0):
                for c in range(2):
                    for copy in departures(c, k):
                        copy.start()
    for k in range(len(windows)):
        for c in range(2):
            for copy in departures(c, k):
                copy.wait()


def pieces_of(spec, level, windows, count):
    depth = spec.shape[2]
    slots = sorted({w.index for w in windows} | {w.index + 1 for w in windows if w.rim})
    return pl.pallas_call(
        functools.partial(pieces_kernel, windows, slots, count),
        in_specs=[pl.BlockSpec(memory_space=pltpu.SMEM), pl.BlockSpec(memory_space=pl.ANY)],
        out_specs=[pl.BlockSpec(memory_space=pl.ANY)] * len(windows),
        out_shape=[jax.ShapeDtypeStruct((2, w.rows, depth), jnp.float32) for w in windows],
        scratch_shapes=[
            pltpu.VMEM((2, len(slots), depth, LANE), jnp.float32),
            pltpu.VMEM((2, len(slots), LANE, depth), jnp.float32),
            pltpu.SemaphoreType.DMA((2, len(slots))),
            pltpu.SemaphoreType.DMA((len(windows), 2, 2)),
        ],
        compiler_params=pltpu.CompilerParams(vmem_limit_bytes=VMEM_LIMIT),
        cost_estimate=pl.CostEstimate(
            flops=0, transcendentals=0, bytes_accessed=4 * 2 * len(slots) * LANE * depth * 4
        ),
        name="pieces_of",
    )(level.reshape(1), spec)


def gate_kernel(*refs):
    pass


def gated(part, waits):
    return pl.pallas_call(
        gate_kernel,
        in_specs=[pl.BlockSpec(memory_space=pl.ANY)] * (1 + len(waits)),
        out_specs=pl.BlockSpec(memory_space=pl.ANY),
        out_shape=jax.ShapeDtypeStruct(part.shape, part.dtype),
        input_output_aliases={0: 0},
        cost_estimate=pl.CostEstimate(flops=0, transcendentals=0, bytes_accessed=1024),
        name="gated",
    )(part, *waits)


def east_of(x):
    return pltpu.roll(x, NLON - 1, axis=1) - pltpu.roll(x, 1, axis=1)


def north_of(before, here, after):
    row = lax.broadcasted_iota(jnp.int32, here.shape, 0)
    above = jnp.where(row == SUB - 1, pltpu.roll(after, SUB - 1, axis=0), pltpu.roll(here, SUB - 1, axis=0))
    below = jnp.where(row == 0, pltpu.roll(before, 1, axis=0), pltpu.roll(here, 1, axis=0))
    return above - below


def window_kernel(window, slot, waits, *refs):
    refs = list(refs)
    place_ref, local_ref, remote_ref, table_ref = refs[:4]
    refs = refs[4 + waits + (len(PARTS) if slot else 0) :]
    carry_ref = None if window.first else refs.pop(0)
    out_refs = [refs.pop(0) for _ in range(4)]
    carried_ref = None if window.last else refs.pop(0)
    table, lhs_high, lhs_low, wind, second, third, shift, results, carried, table_sem, carry_sem, out_sems = refs
    band = place_ref[0]
    rows, extended = window.rows, window.extended

    def at(pair):
        return multiple(choose(band, pair), SUB)

    tables = pltpu.make_async_copy(table_ref, table, table_sem)
    tables.start()
    lane = lax.broadcasted_iota(jnp.int32, (rows, LANE), 1)
    even, odd = [], []
    for c in range(2):
        mine, theirs = local_ref[c], remote_ref[c]
        low, high = jnp.where(band == 0, mine, theirs), jnp.where(band == 0, theirs, mine)
        low_rest, high_rest = low[:, 4 * LANE :], high[:, 4 * LANE :]
        turn = functools.partial(pltpu.roll, shift=LANE // 2, axis=1)
        even_rest = jnp.where(lane < LANE // 2, low_rest, turn(high_rest))
        odd_rest = jnp.where(lane < LANE // 2, turn(low_rest), high_rest)
        even.append(jnp.concatenate([low[:, : 2 * LANE], high[:, : 2 * LANE], even_rest], axis=1))
        odd.append(jnp.concatenate([low[:, 2 * LANE : 4 * LANE], high[:, 2 * LANE : 4 * LANE], odd_rest], axis=1))
    for parity, parts in enumerate((even, odd)):
        lhs = jnp.concatenate(parts)
        lhs_high[parity] = lhs.astype(jnp.bfloat16)
        lhs_low[parity] = (lhs - lhs_high[parity].astype(jnp.float32)).astype(jnp.bfloat16)
    tables.wait()

    place = at(window.place)
    if window.first or window.last:
        for c in range(2):
            if window.first:
                wind[c, pl.ds(at((extended - SUB, 0)), SUB), :] = jnp.zeros((SUB, NLON), jnp.float32)
            if window.last:
                wind[c, pl.ds(at((0, extended - SUB)), SUB), :] = jnp.zeros((SUB, NLON), jnp.float32)
    if not window.first:
        for c in range(2):
            wind[c, pl.ds(at((extended - 2 * SUB, 0)), 2 * SUB), :] = carry_ref[c]

    dot = functools.partial(jnp.dot, preferred_element_type=jnp.float32)
    for start in range(0, NLON // 2, 2 * LANE):
        stop = min(start + 2 * LANE, NLON // 2)
        columns = slice(start, stop)
        sums = []
        for parity in range(2):
            total = dot(lhs_high[parity], table[2 * parity, :, columns])
            total += dot(lhs_low[parity], table[2 * parity, :, columns])
            total += dot(lhs_high[parity], table[2 * parity + 1, :, columns])
            sums.append(total)
        for c in range(2):
            even_sum, odd_sum = (total[c * rows : (c + 1) * rows] for total in sums)
            wind[c, pl.ds(place, rows), start:stop] = even_sum + odd_sum
            wind[c, pl.ds(place, rows), NLON // 2 + start : NLON // 2 + stop] = even_sum - odd_sum

    if not window.last:
        for c in range(2):
            carried[c] = wind[c, pl.ds(at((0, extended - 2 * SUB)), 2 * SUB), :]
        carry_on = pltpu.make_async_copy(carried, carried_ref, carry_sem)
        carry_on.start()

    blocks = extended // SUB

    def rows_of(block):
        return pl.ds(pl.multiple_of(block * SUB, SUB), SUB)

    def derivatives(field, block):
        before, after = jnp.maximum(block - 1, 0), jnp.minimum(block + 1, blocks - 1)
        result = []
        for c in range(2):
            here = field[c, rows_of(block), :]
            result.append((east_of(here), north_of(field[c, rows_of(before), :], here, field[c, rows_of(after), :])))
        return result

    @pl.loop(0, blocks, unroll=6)
    def _(block):
        flow = [wind[c, rows_of(block), :] for c in range(2)]
        for c, (east, north) in enumerate(derivatives(wind, block)):
            second[c, rows_of(block), :] = 0.25 * (flow[0] * east + flow[1] * north) - flow[c]

    @pl.loop(0, blocks, unroll=6)
    def _(block):
        flow = [wind[c, rows_of(block), :] for c in range(2)]
        for c, (east, north) in enumerate(derivatives(second, block)):
            third[c, rows_of(block), :] = -flow[c] - 0.25 * (flow[0] * east + flow[1] * north)

    @pl.loop(0, blocks, unroll=6)
    def _(block):
        flow = [wind[c, rows_of(block), :] for c in range(2)]
        for c, (east, north) in enumerate(derivatives(third, block)):
            fourth = -flow[c] - 0.5 * (flow[0] * east + flow[1] * north)
            both = second[c, rows_of(block), :] + third[c, rows_of(block), :]
            shift[c, rows_of(block), :] = (2.0 * both + (fourth - flow[c])) * (1.0 / 6.0)

    quarter = window.width // 4 // SUB

    def entries(out, base):
        @pl.loop(0, quarter, unroll=4)
        def _(block):
            (e0, n0), (e1, n1) = derivatives(shift, base + block + 1)
            g_xx, g_xy, g_yx, g_yy = 1.0 + 0.5 * e0, 0.5 * n0, 0.5 * e1, 1.0 + 0.5 * n1
            out[0, rows_of(block), :] = g_xx * g_xx + g_yx * g_yx
            out[1, rows_of(block), :] = g_xx * g_xy + g_yx * g_yy
            out[2, rows_of(block), :] = g_xy * g_xy + g_yy * g_yy

    copies = []
    for n, (a, b) in reversed(list(enumerate(PARTS))):
        entries(results.at[n], block_of(place_ref, a, b, 0, 0) // 4 * 4)
        for at_part, (e, f) in enumerate(WITHIN):
            rows = pl.ds(multiple(block_of(place_ref, a, b, e, f) % 4 * SUB, SUB), SUB)
            copies.append(
                pltpu.make_async_copy(
                    results.at[n, :, rows],
                    out_refs[n].at[slot, :, pl.ds(at_part * SUB, SUB)],
                    out_sems.at[n, at_part],
                )
            )
            copies[-1].start()
    for copy in copies:
        copy.wait()
    if not window.last:
        carry_on.wait()


PARTS = ((0, 0), (0, 1), (1, 0), (1, 1))
WITHIN = ((0, 0), (0, 1), (1, 0), (1, 1))


def block_of(place_ref, core, *steps):
    block = place_ref[1] + core - 2 * core * place_ref[1]
    for n, differs in enumerate(steps):
        half = place_ref[2 + 3 * core + n]
        block = 2 * block + half + differs - 2 * differs * half
    return block


def window_tensor(window, slot, slots, place, local, remote, table, parts, waits, carry):
    depth = local.shape[2]
    vmem = pl.BlockSpec(memory_space=pltpu.VMEM)
    in_specs = [
        pl.BlockSpec(memory_space=pltpu.SMEM),
        vmem,
        vmem,
        pl.BlockSpec(memory_space=pl.ANY),
    ]
    in_specs += [pl.BlockSpec(memory_space=pl.ANY)] * len(waits)
    operands = [place, local, remote, table, *waits]
    aliases = {}
    if slot:
        aliases = {len(operands) + n: n for n in range(len(PARTS))}
        in_specs += [pl.BlockSpec(memory_space=pl.ANY)] * len(PARTS)
        operands += parts
    if not window.first:
        in_specs.append(vmem)
        operands.append(carry)
    out_shape = [jax.ShapeDtypeStruct((slots, 3, window.width // 4, NLON), jnp.float32)] * len(PARTS)
    if not window.last:
        out_shape.append(jax.ShapeDtypeStruct((2, 2 * SUB, NLON), jnp.float32))
    field = pltpu.VMEM((2, window.extended, NLON), jnp.float32)
    lhs_shape = (2, 2 * window.rows, depth)
    out = pl.pallas_call(
        functools.partial(window_kernel, window, slot, len(waits)),
        out_shape=out_shape,
        in_specs=in_specs,
        out_specs=[pl.BlockSpec(memory_space=pl.ANY)] * len(out_shape),
        scratch_shapes=[
            pltpu.VMEM(table.shape, table.dtype),
            pltpu.VMEM(lhs_shape, jnp.bfloat16),
            pltpu.VMEM(lhs_shape, jnp.bfloat16),
            field,
            field,
            field,
            field,
            pltpu.VMEM((4, 3, window.width // 4, NLON), jnp.float32),
            pltpu.VMEM((2, 2 * SUB, NLON), jnp.float32),
            pltpu.SemaphoreType.DMA,
            pltpu.SemaphoreType.DMA,
            pltpu.SemaphoreType.DMA((len(PARTS), len(WITHIN))),
        ],
        input_output_aliases=aliases,
        compiler_params=pltpu.CompilerParams(vmem_limit_bytes=VMEM_LIMIT),
        cost_estimate=pl.CostEstimate(
            flops=KERNEL_WORK * 3 * 2 * 2 * window.rows * depth * NLON,
            transcendentals=0,
            bytes_accessed=2 * table.size + 4 * window.rows * depth * 4 + 12 * window.width * NLON,
        ),
        name="window_tensor",
    )(*operands)
    return list(out[: len(PARTS)]), (None if window.last else out[len(PARTS)])


def put_kernel(kinds, place_ref, mine_ref, beside_ref, *refs):
    out_ref, held, in_sems, out_sems = refs[-4:]
    band, height = place_ref[0], out_ref.shape[1]
    half = LANE // 2
    arrivals, departures = [], []
    for core, ref in enumerate((mine_ref, beside_ref)):
        for w in range(len(kinds)):
            arrivals.append(pltpu.make_async_copy(ref.at[w], held.at[core, w], in_sems.at[core, w]))
            arrivals[-1].start()
    for core in range(2):
        for w, (kind, k) in enumerate(kinds):
            arrivals[core * len(kinds) + w].wait()
            for n in range(SUB):
                block = block_of(place_ref, core, n // 4, n // 2 % 2, n % 2)
                if kind == "other":
                    level, row = 1 - band, choose(band, (k * LANE, height - (k + 1) * LANE)) + block * SUB
                elif kind == "both":
                    level, row = block // SUB, choose(band, (height - half, 0)) + block % SUB * SUB
                else:
                    row = choose(band, (height - half - (k + 1) * LANE, half + k * LANE)) + block * SUB
                    level = band
                departures.append(
                    pltpu.make_async_copy(
                        held.at[core, w, pl.ds(n * SUB, SUB)],
                        out_ref.at[level, pl.ds(multiple(row, SUB), SUB)],
                        out_sems.at[core, w, n],
                    )
                )
                departures[-1].start()
    for copy in departures:
        copy.wait()


def put(out, shape, place, kinds, mine, beside):
    extra = [] if out is None else [out]
    hbm = pl.BlockSpec(memory_space=pl.ANY)
    return pl.pallas_call(
        functools.partial(put_kernel, kinds),
        in_specs=[pl.BlockSpec(memory_space=pltpu.SMEM), hbm, hbm] + [hbm] * len(extra),
        out_specs=hbm,
        out_shape=jax.ShapeDtypeStruct(shape, jnp.float32),
        input_output_aliases={3: 0} if extra else {},
        scratch_shapes=[
            pltpu.VMEM((2, *mine.shape), jnp.float32),
            pltpu.SemaphoreType.DMA((2, len(kinds))),
            pltpu.SemaphoreType.DMA((2, len(kinds), SUB)),
        ],
        compiler_params=pltpu.CompilerParams(vmem_limit_bytes=VMEM_LIMIT),
        cost_estimate=pl.CostEstimate(flops=0, transcendentals=0, bytes_accessed=16 * mine.size),
        name="put",
    )(place, mine, beside, *extra)


def by_levels(coeffs):
    spec = coeffs[0]
    levels, _, parts, waves_local, nlat = spec.shape
    members = lax.axis_size("mem")
    band = lax.axis_index("band").astype(jnp.int32)
    member = lax.axis_index("mem").astype(jnp.int32)
    core = member % 2
    halves = [[member // bit % 2 for bit in bits] for bits in ORDER]
    place = jnp.stack([band, core] + [choose(c, pair) for c in (core, 1 - core) for pair in zip(*halves)])
    spec = spec.reshape(levels, 2, parts * waves_local, nlat)
    count = nlat // LANE
    windows = [Window(k, count) for k in range(count)]
    table = jnp.asarray(wave_table(levels, waves_local))
    swap = [(0, 1), (1, 0)]
    cores = [(m, m ^ 1) for m in range(members)]
    ways = [[(m, m ^ ORDER[m % 2][step]) for m in range(members)] for step in range(len(ORDER[0]))]

    (piece,) = pieces_of(spec, 1 - band, windows[:1], count)
    remotes = [lax.ppermute(piece, "band", swap)]
    for k, piece in enumerate(pieces_of(spec, 1 - band, windows[1:], count), 1):
        if k > 1:
            piece = gated(piece, [remotes[k - 2]])
        remotes.append(lax.ppermute(piece, "band", swap))
    local = pieces_of(spec, band, windows, count)

    batches = [(0, 1), (2, 3), (4,)]
    sums, done = {}, {}

    def step(n, waits=()):
        terms, at = sums[n], done[n]
        gate = 1 if at == 0 else 0
        if waits:
            terms[gate] = gated(terms[gate], list(waits))
        if at == 0:
            kept, passed, kept_more, passed_more = terms
            kept, leaves = [kept, kept_more], passed + passed_more
        else:
            half = terms[0].shape[2] // 2
            leaves = sum(term[:, :, half:] for term in terms)
            kept = [sum(term[:, :, :half] for term in terms)]
        sums[n], done[n] = [*kept, lax.ppermute(leaves, "mem", ways[at])], at + 1
        return leaves

    def exponents(n, waits):
        sums[n][0] = gated(sums[n][0], waits)
        return exponent_of(sum(sums[n]), members)

    def doubled(part, at):
        return jnp.concatenate([part, lax.ppermute(part, "mem", ways[at])], axis=1)

    carry = None
    for n, batch in enumerate(batches):
        made = None
        for slot, k in enumerate(batch):
            waits = [step(j) for j in AHEAD[k]]
            made, carry = window_tensor(
                windows[k], slot, len(batch), place, local[k], remotes[k], table, made, waits, carry
            )
        sent = made[3]
        if batch[-1] + 1 == count:
            sent = gated(sent, [sums[n - 1][-1]])
        elif batch[-1] + 2 == count:
            sent = gated(sent, [remotes[-1]])
        first = lax.ppermute(sent, "mem", cores)
        second = lax.ppermute(made[2], "mem", cores)
        sums[n], done[n] = [made[0], made[1], second, first], 0
        last_made = made[0]

    left = step(0, [last_made])
    left = step(1, [left])
    left = step(2, [left])
    left = step(2, [left])
    far = exponents(0, [left])
    swapped = lax.ppermute(far, "band", swap)
    left = step(1, [far])
    left = step(2, [left])
    far = gated(swapped, [left])
    near = exponents(1, [far])
    place_of = {}
    for m in range(members):
        for b in range(2):
            bits = ORDER[m % 2]
            piece = functools.reduce(lambda value, bit: 2 * value + m // bit % 2, bits, m % 2)
            place_of[piece, b] = m * 2 + b
    trades, half = [], members // 2
    for (piece, b), index in place_of.items():
        mate = (piece, b) if (piece < half) == (b == 0) else ((piece + half) % members, 1 - b)
        trades.append((index, place_of[mate]))
    traded = lax.ppermute(near[:1], ("mem", "band"), trades)
    near = jnp.concatenate([traded, near[1:], exponents(2, [near])])
    for at in (2, 1, 0):
        far = gated(doubled(far, at), [near])
        near = gated(doubled(near, at), [far])
    shape = (levels, nlat // 2, NLON)
    out = put(None, shape, place, [("other", 0), ("other", 1)], far, lax.ppermute(far, "mem", cores))
    kinds = [("both", 0), ("own", 0), ("own", 1)]
    return put(out, shape, place, kinds, near, lax.ppermute(near, "mem", cores))


def per_device(coeffs):
    _, levels, _, _, _, nlat = coeffs.shape
    members = lax.axis_size("mem")
    rows = nlat // lax.axis_size("band")
    fits = coeffs.shape[4] == 5 * LANE // 2 and nlat % (2 * LANE) == LANE and rows > LANE
    if fits and levels == lax.axis_size("band") == 2 and members == 16:
        return by_levels(coeffs)
    return by_rows(coeffs)


def solution(mesh):
    placed = (P("mem", None, None, None, "band", None),)
    return jax.shard_map(
        per_device, mesh=mesh, in_specs=placed, out_specs=P(None, "band", None), check_vma=False
    )
```

```python
import functools
import math

import jax
import jax.numpy as jnp
import ml_dtypes
import numpy as np
from jax import lax
from jax.experimental import pallas as pl
from jax.experimental.pallas import tpu as pltpu
from jax.sharding import PartitionSpec as P

NLON = 1280
STEPS = 1
SUB = 8
LANE = 128
VMEM_LIMIT = 60 * 1024 * 1024
KERNEL_WORK = 8
ORDER = ((2, 4, 8), (4, 8, 2))
AHEAD = ((), (), (0,), (1, 0), (3, 2, 1))


def padded(cells, sides, width):
    for axis, dim in sides:
        count = lax.axis_size(axis)
        ends = count - 1
        head = lax.slice_in_dim(cells, 0, width, axis=dim)
        tail = lax.slice_in_dim(cells, cells.shape[dim] - width, cells.shape[dim], axis=dim)
        cells = jnp.concatenate(
            [
                lax.ppermute(tail, axis, [(i, (i + 1) % count) for i in range(ends)]),
                cells,
                lax.ppermute(head, axis, [((i + 1) % count, i) for i in range(ends)]),
            ],
            axis=dim,
        )
    return cells


def slope(extended, winds):
    center = extended[:, 1:-1]
    north = (extended[:, 2:] - extended[:, :-2]) * 0.5
    east = (jnp.roll(center, -1, 2) - jnp.roll(center, 1, 2)) * 0.5
    return -winds - (winds[0] * east + winds[1] * north)


def rimmed(field):
    return padded(field, (("band", 1),), 1)


def tensor(extended):
    center = extended[:, 1:-1]
    north = (extended[:, 2:] - extended[:, :-2]) * 0.5
    east = (jnp.roll(center, -1, 2) - jnp.roll(center, 1, 2)) * 0.5
    g_xx = 1.0 + east[0]
    g_xy = north[0]
    g_yx = east[1]
    g_yy = 1.0 + north[1]
    return jnp.stack(
        [g_xx * g_xx + g_yx * g_yx, g_xx * g_xy + g_yx * g_yy, g_xy * g_xy + g_yy * g_yy]
    )


def integrate(shift, flow, extend):
    first = slope(extend(shift), flow)
    second = slope(extend(0.5 * first), flow)
    third = slope(extend(0.5 * second), flow)
    fourth = slope(extend(third), flow)
    return (first + 2.0 * second + 2.0 * third + fourth) / 6.0


def exponent_of(summed, members):
    mean = summed / members
    first, cross, second = (mean[..., 0, :, :], mean[..., 1, :, :], mean[..., 2, :, :])
    half = (first + second) * 0.5
    differ = (first - second) * 0.5
    largest = half + jnp.sqrt(differ * differ + cross * cross)
    return jnp.log(largest + 1e-06) / (2.0 * STEPS)


def by_rows(coeffs):
    spec = coeffs[0]
    levels = spec.shape[0]
    nlat = spec.shape[4]
    waves = spec.shape[3] * lax.axis_size("band")
    members = lax.axis_size("mem")
    stacked = spec.reshape(levels * 2, 2, spec.shape[3], nlat)
    wave_index = lax.iota(jnp.int32, waves)
    column = lax.iota(jnp.int32, NLON)
    phase = wave_index[:, None] * column[None, :] % NLON
    angle = phase.astype(jnp.float32) * (2.0 * math.pi / NLON)
    weight = jnp.where(wave_index == 0, 1.0, 2.0).astype(jnp.float32)[:, None]
    table = jnp.stack([weight * jnp.cos(angle), -weight * jnp.sin(angle)], axis=0)
    winds = jnp.einsum(
        "crwh,rwn->chn",
        lax.all_to_all(stacked, "band", split_axis=3, concat_axis=2, tiled=True),
        table,
        precision=lax.Precision.HIGHEST,
        preferred_element_type=jnp.float32,
    )
    height = winds.shape[1]
    winds = winds.reshape(levels, 2, height, NLON)
    partials = []
    for level in range(levels):
        flow = winds[level]
        shift = integrate(jnp.zeros_like(flow), flow, rimmed)
        partials.append(tensor(rimmed(shift)))
    summed = lax.psum_scatter(jnp.stack(partials), "mem", scatter_dimension=3, tiled=True)
    return lax.all_gather(exponent_of(summed, members), "mem", axis=2, tiled=True)


def by_parity(waves_local):
    half = waves_local // 2
    whole = 2 * LANE - half
    runs = []
    for parity in range(2):
        runs += [(parity, half, 2), (waves_local + parity, whole, 2)]
    for parity in range(2):
        runs.append((waves_local + parity + 2 * whole, half - whole, 2))
    return runs


@functools.lru_cache(maxsize=None)
def wave_table(bands, waves_local):
    order = np.concatenate([start + step * np.arange(count) for start, count, step in by_parity(waves_local)])
    wave, part = order % waves_local, order // waves_local
    wave = wave[None, :] + waves_local * np.arange(bands)[:, None]
    part = np.broadcast_to(part, wave.shape)
    cut = [0, 2 * LANE, 4 * LANE, 4 * LANE + LANE // 2, 5 * LANE]
    result = []
    for parity in range(2):
        picks = [(band, slice(cut[parity], cut[parity + 1])) for band in range(bands)]
        picks += [(band, slice(cut[parity + 2], cut[parity + 3])) for band in range(bands)]
        waves = np.concatenate([wave[pick] for pick in picks])
        parts = np.concatenate([part[pick] for pick in picks])
        phase = (waves[:, None] * np.arange(NLON // 2)[None, :]) % NLON
        angle = phase.astype(np.float64) * (2.0 * np.pi / NLON)
        weight = np.where(waves == 0, 1.0, 2.0)[:, None]
        table = weight * np.where(parts[:, None] == 0, np.cos(angle), -np.sin(angle))
        high = table.astype(ml_dtypes.bfloat16)
        result += [high, (table - high.astype(np.float64)).astype(ml_dtypes.bfloat16)]
    return np.stack(result)


class Window:
    def __init__(self, index, count):
        self.first = index == 0
        self.last = index == count - 1
        self.index = index
        self.width = LANE
        self.extended = LANE + 2 * SUB
        self.main = LANE if self.first else LANE - SUB
        self.rim = 0 if self.last else SUB
        self.rows = self.main + self.rim
        up = SUB if self.first else 2 * SUB
        self.place = (self.extended - up - self.rows, up)
        self.side = "other" if 2 * (index + 1) <= count else "own" if 2 * index >= count else "both"


def choose(band, pair):
    return jnp.where(band == 0, pair[0], pair[1])


def multiple(value, of):
    return pl.multiple_of(value.astype(jnp.int32), of)


def pieces_kernel(windows, slots, count, level_ref, spec_ref, *refs):
    out_refs, (taken, turned, in_sems, out_sems) = refs[: len(windows)], refs[len(windows) :]
    level = level_ref[0]
    runs = by_parity(spec_ref.shape[2] // 2)

    def arrival(c, n):
        tile = choose(level, (count - 1 - slots[n], slots[n]))
        lanes = pl.ds(multiple(tile * LANE, LANE), LANE)
        return pltpu.make_async_copy(spec_ref.at[level, c, :, lanes], taken.at[c, n], in_sems.at[c, n])

    def departures(c, k):
        window, n = windows[k], slots.index(windows[k].index)
        rows = pl.ds(multiple(choose(level, (0, LANE - window.main)), SUB), window.main)
        at = pl.ds(multiple(choose(level, (window.rim, 0)), SUB), window.main)
        yield pltpu.make_async_copy(turned.at[c, n, rows], out_refs[k].at[c, at], out_sems.at[k, c, 0])
        if window.rim:
            rows = pl.ds(multiple(choose(level, (LANE - SUB, 0)), SUB), SUB)
            at = pl.ds(multiple(choose(level, (0, window.main)), SUB), SUB)
            yield pltpu.make_async_copy(turned.at[c, n + 1, rows], out_refs[k].at[c, at], out_sems.at[k, c, 1])

    for n in range(len(slots)):
        for c in range(2):
            arrival(c, n).start()
    for n in range(len(slots)):
        for c in range(2):
            arrival(c, n).wait()
            turned[c, n] = jnp.concatenate([taken[c, n, pl.ds(start, rows, step), :] for start, rows, step in runs]).T
        for k, window in enumerate(windows):
            if slots[n] == window.index + (1 if window.rim else 0):
                for c in range(2):
                    for copy in departures(c, k):
                        copy.start()
    for k in range(len(windows)):
        for c in range(2):
            for copy in departures(c, k):
                copy.wait()


def pieces_of(spec, level, windows, count):
    depth = spec.shape[2]
    slots = sorted({w.index for w in windows} | {w.index + 1 for w in windows if w.rim})
    return pl.pallas_call(
        functools.partial(pieces_kernel, windows, slots, count),
        in_specs=[pl.BlockSpec(memory_space=pltpu.SMEM), pl.BlockSpec(memory_space=pl.ANY)],
        out_specs=[pl.BlockSpec(memory_space=pl.ANY)] * len(windows),
        out_shape=[jax.ShapeDtypeStruct((2, w.rows, depth), jnp.float32) for w in windows],
        scratch_shapes=[
            pltpu.VMEM((2, len(slots), depth, LANE), jnp.float32),
            pltpu.VMEM((2, len(slots), LANE, depth), jnp.float32),
            pltpu.SemaphoreType.DMA((2, len(slots))),
            pltpu.SemaphoreType.DMA((len(windows), 2, 2)),
        ],
        compiler_params=pltpu.CompilerParams(vmem_limit_bytes=VMEM_LIMIT),
        cost_estimate=pl.CostEstimate(
            flops=0, transcendentals=0, bytes_accessed=4 * 2 * len(slots) * LANE * depth * 4
        ),
        name="pieces_of",
    )(level.reshape(1), spec)


def gate_kernel(*refs):
    pass


def gated(part, waits):
    return pl.pallas_call(
        gate_kernel,
        in_specs=[pl.BlockSpec(memory_space=pl.ANY)] * (1 + len(waits)),
        out_specs=pl.BlockSpec(memory_space=pl.ANY),
        out_shape=jax.ShapeDtypeStruct(part.shape, part.dtype),
        input_output_aliases={0: 0},
        cost_estimate=pl.CostEstimate(flops=0, transcendentals=0, bytes_accessed=1024),
        name="gated",
    )(part, *waits)


def east_of(x):
    return pltpu.roll(x, NLON - 1, axis=1) - pltpu.roll(x, 1, axis=1)


def north_of(before, here, after):
    row = lax.broadcasted_iota(jnp.int32, here.shape, 0)
    above = jnp.where(row == SUB - 1, pltpu.roll(after, SUB - 1, axis=0), pltpu.roll(here, SUB - 1, axis=0))
    below = jnp.where(row == 0, pltpu.roll(before, 1, axis=0), pltpu.roll(here, 1, axis=0))
    return above - below


def window_kernel(window, depth, waits, *refs):
    refs = list(refs)
    place_ref, local_ref, remote_ref, table_ref = refs[:4]
    refs = refs[4 + waits :]
    carry_ref = None if window.first else refs.pop(0)
    out_refs = [refs.pop(0) for _ in range(4)]
    carried_ref = None if window.last else refs.pop(0)
    table, lhs_high, lhs_low, wind, second, third, shift, results, carried, table_sem, out_sems = refs
    band, core, sides = place_ref[0], place_ref[1], (place_ref[2], place_ref[3])
    rows, extended = window.rows, window.extended

    def at(pair):
        return multiple(choose(band, pair), SUB)

    tables = pltpu.make_async_copy(table_ref, table, table_sem)
    tables.start()
    lane = lax.broadcasted_iota(jnp.int32, (rows, LANE), 1)
    even, odd = [], []
    for c in range(2):
        mine, theirs = local_ref[c], remote_ref[c]
        low, high = jnp.where(band == 0, mine, theirs), jnp.where(band == 0, theirs, mine)
        low_rest, high_rest = low[:, 4 * LANE :], high[:, 4 * LANE :]
        turn = functools.partial(pltpu.roll, shift=LANE // 2, axis=1)
        even_rest = jnp.where(lane < LANE // 2, low_rest, turn(high_rest))
        odd_rest = jnp.where(lane < LANE // 2, turn(low_rest), high_rest)
        even.append(jnp.concatenate([low[:, : 2 * LANE], high[:, : 2 * LANE], even_rest], axis=1))
        odd.append(jnp.concatenate([low[:, 2 * LANE : 4 * LANE], high[:, 2 * LANE : 4 * LANE], odd_rest], axis=1))
    for parity, parts in enumerate((even, odd)):
        lhs = jnp.concatenate(parts)
        lhs_high[parity] = lhs.astype(jnp.bfloat16)
        lhs_low[parity] = (lhs - lhs_high[parity].astype(jnp.float32)).astype(jnp.bfloat16)
    tables.wait()

    place = at(window.place)
    if window.first or window.last:
        for c in range(2):
            if window.first:
                wind[c, pl.ds(at((extended - SUB, 0)), SUB), :] = jnp.zeros((SUB, NLON), jnp.float32)
            if window.last:
                wind[c, pl.ds(at((0, extended - SUB)), SUB), :] = jnp.zeros((SUB, NLON), jnp.float32)
    if not window.first:
        for c in range(2):
            wind[c, pl.ds(at((extended - 2 * SUB, 0)), 2 * SUB), :] = carry_ref[c]

    dot = functools.partial(jnp.dot, preferred_element_type=jnp.float32)
    for start in range(0, NLON // 2, 2 * LANE):
        stop = min(start + 2 * LANE, NLON // 2)
        columns = slice(start, stop)
        sums = []
        for parity in range(2):
            total = dot(lhs_high[parity], table[2 * parity, :, columns])
            total += dot(lhs_low[parity], table[2 * parity, :, columns])
            total += dot(lhs_high[parity], table[2 * parity + 1, :, columns])
            sums.append(total)
        for c in range(2):
            even_sum, odd_sum = (total[c * rows : (c + 1) * rows] for total in sums)
            wind[c, pl.ds(place, rows), start:stop] = even_sum + odd_sum
            wind[c, pl.ds(place, rows), NLON // 2 + start : NLON // 2 + stop] = even_sum - odd_sum

    if not window.last:
        for c in range(2):
            carried[c] = wind[c, pl.ds(at((0, extended - 2 * SUB)), 2 * SUB), :]
        carry_on = pltpu.make_async_copy(carried, carried_ref, out_sems.at[4])
        carry_on.start()

    blocks = extended // SUB

    def rows_of(block):
        return pl.ds(pl.multiple_of(block * SUB, SUB), SUB)

    def derivatives(field, block):
        before, after = jnp.maximum(block - 1, 0), jnp.minimum(block + 1, blocks - 1)
        result = []
        for c in range(2):
            here = field[c, rows_of(block), :]
            result.append((east_of(here), north_of(field[c, rows_of(before), :], here, field[c, rows_of(after), :])))
        return result

    @pl.loop(0, blocks, unroll=6)
    def _(block):
        flow = [wind[c, rows_of(block), :] for c in range(2)]
        for c, (east, north) in enumerate(derivatives(wind, block)):
            second[c, rows_of(block), :] = 0.25 * (flow[0] * east + flow[1] * north) - flow[c]

    @pl.loop(0, blocks, unroll=6)
    def _(block):
        flow = [wind[c, rows_of(block), :] for c in range(2)]
        for c, (east, north) in enumerate(derivatives(second, block)):
            third[c, rows_of(block), :] = -flow[c] - 0.25 * (flow[0] * east + flow[1] * north)

    @pl.loop(0, blocks, unroll=6)
    def _(block):
        flow = [wind[c, rows_of(block), :] for c in range(2)]
        for c, (east, north) in enumerate(derivatives(third, block)):
            fourth = -flow[c] - 0.5 * (flow[0] * east + flow[1] * north)
            both = second[c, rows_of(block), :] + third[c, rows_of(block), :]
            shift[c, rows_of(block), :] = (2.0 * both + (fourth - flow[c])) * (1.0 / 6.0)

    quarter = window.width // 4 // SUB

    def entries(out, base):
        @pl.loop(0, quarter, unroll=4)
        def _(block):
            (e0, n0), (e1, n1) = derivatives(shift, base + block + 1)
            g_xx, g_xy, g_yx, g_yy = 1.0 + 0.5 * e0, 0.5 * n0, 0.5 * e1, 1.0 + 0.5 * n1
            out[0, rows_of(block), :] = g_xx * g_xx + g_yx * g_yx
            out[1, rows_of(block), :] = g_xx * g_xy + g_yx * g_yy
            out[2, rows_of(block), :] = g_xy * g_xy + g_yy * g_yy

    copies = []
    for n, (a, b) in reversed(list(enumerate(QUARTERS))):
        side = sides[a]
        entries(results.at[n], (2 * (core + a - 2 * core * a) + (side + b - 2 * side * b)) * quarter)
        copies.append(pltpu.make_async_copy(results.at[n], out_refs[n], out_sems.at[n]))
        copies[-1].start()
    for copy in copies:
        copy.wait()
    if not window.last:
        carry_on.wait()


QUARTERS = ((0, 0), (0, 1), (1, 0), (1, 1))


def window_tensor(window, place, local, remote, table, waits, carry):
    depth = local.shape[2]
    vmem = pl.BlockSpec(memory_space=pltpu.VMEM)
    in_specs = [
        pl.BlockSpec(memory_space=pltpu.SMEM),
        vmem,
        vmem,
        pl.BlockSpec(memory_space=pl.ANY),
    ]
    in_specs += [pl.BlockSpec(memory_space=pl.ANY)] * len(waits)
    operands = [place, local, remote, table, *waits]
    if not window.first:
        in_specs.append(vmem)
        operands.append(carry)
    out_shape = [jax.ShapeDtypeStruct((3, window.width // 4, NLON), jnp.float32)] * 4
    if not window.last:
        out_shape.append(jax.ShapeDtypeStruct((2, 2 * SUB, NLON), jnp.float32))
    field = pltpu.VMEM((2, window.extended, NLON), jnp.float32)
    lhs_shape = (2, 2 * window.rows, depth)
    out = pl.pallas_call(
        functools.partial(window_kernel, window, depth, len(waits)),
        out_shape=out_shape,
        in_specs=in_specs,
        out_specs=[pl.BlockSpec(memory_space=pl.ANY)] * len(out_shape),
        scratch_shapes=[
            pltpu.VMEM(table.shape, table.dtype),
            pltpu.VMEM(lhs_shape, jnp.bfloat16),
            pltpu.VMEM(lhs_shape, jnp.bfloat16),
            field,
            field,
            field,
            field,
            pltpu.VMEM((4, 3, window.width // 4, NLON), jnp.float32),
            pltpu.VMEM((2, 2 * SUB, NLON), jnp.float32),
            pltpu.SemaphoreType.DMA,
            pltpu.SemaphoreType.DMA((5,)),
        ],
        compiler_params=pltpu.CompilerParams(vmem_limit_bytes=VMEM_LIMIT),
        cost_estimate=pl.CostEstimate(
            flops=KERNEL_WORK * 3 * 2 * 2 * window.rows * depth * NLON,
            transcendentals=0,
            bytes_accessed=2 * table.size + 4 * window.rows * depth * 4 + 12 * window.width * NLON,
        ),
        name="window_tensor",
    )(*operands)
    return out[:4], (None if window.last else out[4])


def by_levels(coeffs):
    spec = coeffs[0]
    levels, _, parts, waves_local, nlat = spec.shape
    members = lax.axis_size("mem")
    band = lax.axis_index("band").astype(jnp.int32)
    member = lax.axis_index("mem").astype(jnp.int32)
    core = member % 2
    half_of = [choose(core, [member // bits[step] % 2 for bits in ORDER]) for step in range(len(ORDER[0]))]
    half_beside = choose(1 - core, [member // bits[0] % 2 for bits in ORDER])
    place = jnp.stack([band, core, half_of[0], half_beside])
    spec = spec.reshape(levels, 2, parts * waves_local, nlat)
    count = nlat // LANE
    windows = [Window(k, count) for k in range(count)]
    table = jnp.asarray(wave_table(levels, waves_local))
    swap = [(0, 1), (1, 0)]

    (piece,) = pieces_of(spec, 1 - band, windows[:1], count)
    remotes = [lax.ppermute(piece, "band", swap)]
    for k, piece in enumerate(pieces_of(spec, 1 - band, windows[1:], count), 1):
        if k > 1:
            piece = gated(piece, [remotes[k - 2]])
        remotes.append(lax.ppermute(piece, "band", swap))
    local = pieces_of(spec, band, windows, count)

    cores = [(m, m ^ 1) for m in range(members)]
    ways = [[(m, m ^ ORDER[m % 2][step]) for m in range(members)] for step in range(len(ORDER[0]))]

    def halved(parts_of, step, waits=()):
        half = parts_of[0].shape[1] // 2
        mine = half_of[step]

        def total(which):
            return sum(lax.dynamic_slice_in_dim(part, which * half, half, axis=1) for part in parts_of)

        leaves = total(1 - mine)
        if waits:
            leaves = gated(leaves, list(waits))
        return [total(mine), lax.ppermute(leaves, "mem", ways[step])], leaves

    def across(parts_of, step):
        kept, passed, kept_more, passed_more = parts_of
        leaves = passed + passed_more
        return [kept, kept_more, lax.ppermute(leaves, "mem", ways[step])], leaves

    def advanced(parts_of, step):
        return (across if step == 0 else halved)(parts_of, step)

    def doubled(part, step):
        beside = lax.ppermute(part, "mem", cores if step < 0 else ways[step])
        mine = core if step < 0 else half_of[step]
        return jnp.where(mine == 0, jnp.concatenate([part, beside], axis=1), jnp.concatenate([beside, part], axis=1))

    def gathered(part):
        for step in range(len(ways) - 1, -2, -1):
            part = doubled(part, step)
        return part

    carry = None
    sums, done = [], []
    for k, window in enumerate(windows):
        waits = []
        for j in AHEAD[k]:
            sums[j], left = advanced(sums[j], done[j])
            done[j] += 1
            waits.append(left)
        quarters, carry = window_tensor(window, place, local[k], remotes[k], table, waits, carry)
        sent = quarters[3] if k + 1 < count else gated(quarters[3], [sums[k - 1][-1]])
        first = lax.ppermute(sent, "mem", cores)
        second = lax.ppermute(quarters[2], "mem", cores)
        sums.append([quarters[0], quarters[1], second, first])
        done.append(0)
    def further(k, until, waits=()):
        while done[k] < until:
            last = done[k] + 1 == until
            if done[k] == 0:
                sums[k], _ = across(sums[k], 0)
            else:
                sums[k], _ = halved(sums[k], done[k], waits if last else ())
            done[k] += 1

    def exponent(k):
        return exponent_of(sum(sums[k]), members)

    further(0, 3, [first])
    further(1, 3, [first])
    further(2, 2, [first])
    further(4, 1)
    over = [sums[4][-1]]
    further(2, 3, over)
    further(4, 2)
    over_two = [sums[4][-1]]
    further(3, 3, over_two)
    further(4, 3)
    pieces = {
        "other": gated(jnp.stack([exponent(0), exponent(1)]), over),
        "both": exponent(2),
        "own": jnp.stack([exponent(3), exponent(4)]),
    }

    other = lax.ppermute(pieces["other"], "band", swap)
    place_of = {}
    for m in range(members):
        for b in range(2):
            bits = ORDER[m % 2]
            piece = functools.reduce(lambda value, bit: 2 * value + m // bit % 2, bits, m % 2)
            place_of[piece, b] = m * 2 + b
    trades, half = [], members // 2
    for (piece, b), index in place_of.items():
        mate = (piece, b) if (piece < half) == (b == 0) else ((piece + half) % members, 1 - b)
        trades.append((index, place_of[mate]))
    both = lax.ppermute(pieces["both"], ("mem", "band"), trades)

    early = gathered(gated(jnp.concatenate([other, both[None]]), over_two))
    other, both = early[:-1], early[-1]
    middle = both.shape[0] // 2
    low, high = both[:middle], both[middle:]
    rest = jnp.zeros((nlat // 2 - middle, NLON), jnp.float32)
    down = jnp.stack([jnp.concatenate([rest, low]), jnp.concatenate([*other, high])])
    up = jnp.stack([jnp.concatenate([low, *other[::-1]]), jnp.concatenate([high, rest])])
    out = jnp.where(band == 0, down, up)

    own = gathered(pieces["own"])
    for k, block in enumerate(own):
        width = block.shape[0]
        row = choose(band, (nlat // 2 - middle - (k + 1) * width, middle + k * width))
        out = lax.dynamic_update_slice(out, block[None], (band, row.astype(jnp.int32), jnp.int32(0)))
    return out


def per_device(coeffs):
    _, levels, _, _, _, nlat = coeffs.shape
    members = lax.axis_size("mem")
    rows = nlat // lax.axis_size("band")
    fits = coeffs.shape[4] == 5 * LANE // 2 and nlat % (2 * LANE) == LANE and rows > LANE
    if fits and levels == lax.axis_size("band") == 2 and members == 16:
        return by_levels(coeffs)
    return by_rows(coeffs)


def solution(mesh):
    placed = (P("mem", None, None, None, "band", None),)
    return jax.shard_map(
        per_device, mesh=mesh, in_specs=placed, out_specs=P(None, "band", None), check_vma=False
    )
```

```python
import functools
import math

import jax
import jax.numpy as jnp
import ml_dtypes
import numpy as np
from jax import lax
from jax.experimental import pallas as pl
from jax.experimental.pallas import tpu as pltpu
from jax.sharding import PartitionSpec as P

NLON = 1280
STEPS = 1
SUB = 8
LANE = 128
VMEM_LIMIT = 28 * 1024 * 1024
KERNEL_WORK = 8
ORDER = ((2, 4, 8), (4, 8, 2))
AHEAD = ((), (), (0,), (1, 0), (2, 1, 0))


def padded(cells, sides, width):
    for axis, dim in sides:
        count = lax.axis_size(axis)
        ends = count - 1
        head = lax.slice_in_dim(cells, 0, width, axis=dim)
        tail = lax.slice_in_dim(cells, cells.shape[dim] - width, cells.shape[dim], axis=dim)
        cells = jnp.concatenate(
            [
                lax.ppermute(tail, axis, [(i, (i + 1) % count) for i in range(ends)]),
                cells,
                lax.ppermute(head, axis, [((i + 1) % count, i) for i in range(ends)]),
            ],
            axis=dim,
        )
    return cells


def slope(extended, winds):
    center = extended[:, 1:-1]
    north = (extended[:, 2:] - extended[:, :-2]) * 0.5
    east = (jnp.roll(center, -1, 2) - jnp.roll(center, 1, 2)) * 0.5
    return -winds - (winds[0] * east + winds[1] * north)


def rimmed(field):
    return padded(field, (("band", 1),), 1)


def tensor(extended):
    center = extended[:, 1:-1]
    north = (extended[:, 2:] - extended[:, :-2]) * 0.5
    east = (jnp.roll(center, -1, 2) - jnp.roll(center, 1, 2)) * 0.5
    g_xx = 1.0 + east[0]
    g_xy = north[0]
    g_yx = east[1]
    g_yy = 1.0 + north[1]
    return jnp.stack(
        [g_xx * g_xx + g_yx * g_yx, g_xx * g_xy + g_yx * g_yy, g_xy * g_xy + g_yy * g_yy]
    )


def integrate(shift, flow, extend):
    first = slope(extend(shift), flow)
    second = slope(extend(0.5 * first), flow)
    third = slope(extend(0.5 * second), flow)
    fourth = slope(extend(third), flow)
    return (first + 2.0 * second + 2.0 * third + fourth) / 6.0


def exponent_of(summed, members):
    mean = summed / members
    first, cross, second = (mean[..., 0, :, :], mean[..., 1, :, :], mean[..., 2, :, :])
    half = (first + second) * 0.5
    differ = (first - second) * 0.5
    largest = half + jnp.sqrt(differ * differ + cross * cross)
    return jnp.log(largest + 1e-06) / (2.0 * STEPS)


def by_rows(coeffs):
    spec = coeffs[0]
    levels = spec.shape[0]
    nlat = spec.shape[4]
    waves = spec.shape[3] * lax.axis_size("band")
    members = lax.axis_size("mem")
    stacked = spec.reshape(levels * 2, 2, spec.shape[3], nlat)
    wave_index = lax.iota(jnp.int32, waves)
    column = lax.iota(jnp.int32, NLON)
    phase = wave_index[:, None] * column[None, :] % NLON
    angle = phase.astype(jnp.float32) * (2.0 * math.pi / NLON)
    weight = jnp.where(wave_index == 0, 1.0, 2.0).astype(jnp.float32)[:, None]
    table = jnp.stack([weight * jnp.cos(angle), -weight * jnp.sin(angle)], axis=0)
    winds = jnp.einsum(
        "crwh,rwn->chn",
        lax.all_to_all(stacked, "band", split_axis=3, concat_axis=2, tiled=True),
        table,
        precision=lax.Precision.HIGHEST,
        preferred_element_type=jnp.float32,
    )
    height = winds.shape[1]
    winds = winds.reshape(levels, 2, height, NLON)
    partials = []
    for level in range(levels):
        flow = winds[level]
        shift = integrate(jnp.zeros_like(flow), flow, rimmed)
        partials.append(tensor(rimmed(shift)))
    summed = lax.psum_scatter(jnp.stack(partials), "mem", scatter_dimension=3, tiled=True)
    return lax.all_gather(exponent_of(summed, members), "mem", axis=2, tiled=True)


def by_parity(waves_local):
    half = waves_local // 2
    whole = 2 * LANE - half
    runs = []
    for parity in range(2):
        runs += [(parity, half, 2), (waves_local + parity, whole, 2)]
    for parity in range(2):
        runs.append((waves_local + parity + 2 * whole, half - whole, 2))
    return runs


@functools.lru_cache(maxsize=None)
def wave_table(bands, waves_local):
    order = np.concatenate([start + step * np.arange(count) for start, count, step in by_parity(waves_local)])
    wave, part = order % waves_local, order // waves_local
    wave = wave[None, :] + waves_local * np.arange(bands)[:, None]
    part = np.broadcast_to(part, wave.shape)
    cut = [0, 2 * LANE, 4 * LANE, 4 * LANE + LANE // 2, 5 * LANE]
    result = []
    for parity in range(2):
        picks = [(band, slice(cut[parity], cut[parity + 1])) for band in range(bands)]
        picks += [(band, slice(cut[parity + 2], cut[parity + 3])) for band in range(bands)]
        waves = np.concatenate([wave[pick] for pick in picks])
        parts = np.concatenate([part[pick] for pick in picks])
        phase = (waves[:, None] * np.arange(NLON // 2)[None, :]) % NLON
        angle = phase.astype(np.float64) * (2.0 * np.pi / NLON)
        weight = np.where(waves == 0, 1.0, 2.0)[:, None]
        table = weight * np.where(parts[:, None] == 0, np.cos(angle), -np.sin(angle))
        high = table.astype(ml_dtypes.bfloat16)
        result += [high, (table - high.astype(np.float64)).astype(ml_dtypes.bfloat16)]
    return np.stack(result)


class Window:
    def __init__(self, index, count):
        self.first = index == 0
        self.last = index == count - 1
        self.index = index
        self.width = LANE
        self.extended = LANE + 2 * SUB
        self.main = LANE if self.first else LANE - SUB
        self.rim = 0 if self.last else SUB
        self.rows = self.main + self.rim
        up = SUB if self.first else 2 * SUB
        self.place = (self.extended - up - self.rows, up)
        self.side = "other" if 2 * (index + 1) <= count else "own" if 2 * index >= count else "both"


def choose(band, pair):
    return jnp.where(band == 0, pair[0], pair[1])


def multiple(value, of):
    return pl.multiple_of(value.astype(jnp.int32), of)


def pieces_kernel(windows, slots, count, level_ref, spec_ref, *refs):
    out_refs, (taken, turned, in_sems, out_sems) = refs[: len(windows)], refs[len(windows) :]
    level = level_ref[0]
    runs = by_parity(spec_ref.shape[2] // 2)

    def arrival(c, n):
        tile = choose(level, (count - 1 - slots[n], slots[n]))
        lanes = pl.ds(multiple(tile * LANE, LANE), LANE)
        return pltpu.make_async_copy(spec_ref.at[level, c, :, lanes], taken.at[c, n], in_sems.at[c, n])

    def departures(c, k):
        window, n = windows[k], slots.index(windows[k].index)
        rows = pl.ds(multiple(choose(level, (0, LANE - window.main)), SUB), window.main)
        at = pl.ds(multiple(choose(level, (window.rim, 0)), SUB), window.main)
        yield pltpu.make_async_copy(turned.at[c, n, rows], out_refs[k].at[c, at], out_sems.at[k, c, 0])
        if window.rim:
            rows = pl.ds(multiple(choose(level, (LANE - SUB, 0)), SUB), SUB)
            at = pl.ds(multiple(choose(level, (0, window.main)), SUB), SUB)
            yield pltpu.make_async_copy(turned.at[c, n + 1, rows], out_refs[k].at[c, at], out_sems.at[k, c, 1])

    for n in range(len(slots)):
        for c in range(2):
            arrival(c, n).start()
    for n in range(len(slots)):
        for c in range(2):
            arrival(c, n).wait()
            turned[c, n] = jnp.concatenate([taken[c, n, pl.ds(start, rows, step), :] for start, rows, step in runs]).T
        for k, window in enumerate(windows):
            if slots[n] == window.index + (1 if window.rim else 0):
                for c in range(2):
                    for copy in departures(c, k):
                        copy.start()
    for k in range(len(windows)):
        for c in range(2):
            for copy in departures(c, k):
                copy.wait()


def pieces_of(spec, level, windows, count):
    depth = spec.shape[2]
    slots = sorted({w.index for w in windows} | {w.index + 1 for w in windows if w.rim})
    return pl.pallas_call(
        functools.partial(pieces_kernel, windows, slots, count),
        in_specs=[pl.BlockSpec(memory_space=pltpu.SMEM), pl.BlockSpec(memory_space=pl.ANY)],
        out_specs=[pl.BlockSpec(memory_space=pl.ANY)] * len(windows),
        out_shape=[jax.ShapeDtypeStruct((2, w.rows, depth), jnp.float32) for w in windows],
        scratch_shapes=[
            pltpu.VMEM((2, len(slots), depth, LANE), jnp.float32),
            pltpu.VMEM((2, len(slots), LANE, depth), jnp.float32),
            pltpu.SemaphoreType.DMA((2, len(slots))),
            pltpu.SemaphoreType.DMA((len(windows), 2, 2)),
        ],
        compiler_params=pltpu.CompilerParams(vmem_limit_bytes=VMEM_LIMIT),
        cost_estimate=pl.CostEstimate(
            flops=0, transcendentals=0, bytes_accessed=4 * 2 * len(slots) * LANE * depth * 4
        ),
        name="pieces_of",
    )(level.reshape(1), spec)


def gate_kernel(*refs):
    pass


def gated(part, waits):
    return pl.pallas_call(
        gate_kernel,
        in_specs=[pl.BlockSpec(memory_space=pl.ANY)] * (1 + len(waits)),
        out_specs=pl.BlockSpec(memory_space=pl.ANY),
        out_shape=jax.ShapeDtypeStruct(part.shape, part.dtype),
        input_output_aliases={0: 0},
        cost_estimate=pl.CostEstimate(flops=0, transcendentals=0, bytes_accessed=1024),
        name="gated",
    )(part, *waits)


def east_of(x):
    return pltpu.roll(x, NLON - 1, axis=1) - pltpu.roll(x, 1, axis=1)


def north_of(before, here, after):
    row = lax.broadcasted_iota(jnp.int32, here.shape, 0)
    above = jnp.where(row == SUB - 1, pltpu.roll(after, SUB - 1, axis=0), pltpu.roll(here, SUB - 1, axis=0))
    below = jnp.where(row == 0, pltpu.roll(before, 1, axis=0), pltpu.roll(here, 1, axis=0))
    return above - below


def window_kernel(window, depth, waits, *refs):
    refs = list(refs)
    place_ref, local_ref, remote_ref, table_ref = refs[:4]
    refs = refs[4 + waits :]
    carry_ref = None if window.first else refs.pop(0)
    out_refs = [refs.pop(0) for _ in range(4)]
    carried_ref = None if window.last else refs.pop(0)
    table, lhs_high, lhs_low, wind, second, third, shift, results, carried, table_sem, out_sems = refs
    band, core, sides = place_ref[0], place_ref[1], (place_ref[2], place_ref[3])
    rows, extended = window.rows, window.extended

    def at(pair):
        return multiple(choose(band, pair), SUB)

    tables = pltpu.make_async_copy(table_ref, table, table_sem)
    tables.start()
    lane = lax.broadcasted_iota(jnp.int32, (rows, LANE), 1)
    even, odd = [], []
    for c in range(2):
        mine, theirs = local_ref[c], remote_ref[c]
        low, high = jnp.where(band == 0, mine, theirs), jnp.where(band == 0, theirs, mine)
        low_rest, high_rest = low[:, 4 * LANE :], high[:, 4 * LANE :]
        turn = functools.partial(pltpu.roll, shift=LANE // 2, axis=1)
        even_rest = jnp.where(lane < LANE // 2, low_rest, turn(high_rest))
        odd_rest = jnp.where(lane < LANE // 2, turn(low_rest), high_rest)
        even.append(jnp.concatenate([low[:, : 2 * LANE], high[:, : 2 * LANE], even_rest], axis=1))
        odd.append(jnp.concatenate([low[:, 2 * LANE : 4 * LANE], high[:, 2 * LANE : 4 * LANE], odd_rest], axis=1))
    for parity, parts in enumerate((even, odd)):
        lhs = jnp.concatenate(parts)
        lhs_high[parity] = lhs.astype(jnp.bfloat16)
        lhs_low[parity] = (lhs - lhs_high[parity].astype(jnp.float32)).astype(jnp.bfloat16)
    tables.wait()

    place = at(window.place)
    if window.first or window.last:
        for c in range(2):
            if window.first:
                wind[c, pl.ds(at((extended - SUB, 0)), SUB), :] = jnp.zeros((SUB, NLON), jnp.float32)
            if window.last:
                wind[c, pl.ds(at((0, extended - SUB)), SUB), :] = jnp.zeros((SUB, NLON), jnp.float32)
    if not window.first:
        for c in range(2):
            wind[c, pl.ds(at((extended - 2 * SUB, 0)), 2 * SUB), :] = carry_ref[c]

    dot = functools.partial(jnp.dot, preferred_element_type=jnp.float32)
    for start in range(0, NLON // 2, 2 * LANE):
        stop = min(start + 2 * LANE, NLON // 2)
        columns = slice(start, stop)
        sums = []
        for parity in range(2):
            total = dot(lhs_high[parity], table[2 * parity, :, columns])
            total += dot(lhs_low[parity], table[2 * parity, :, columns])
            total += dot(lhs_high[parity], table[2 * parity + 1, :, columns])
            sums.append(total)
        for c in range(2):
            even_sum, odd_sum = (total[c * rows : (c + 1) * rows] for total in sums)
            wind[c, pl.ds(place, rows), start:stop] = even_sum + odd_sum
            wind[c, pl.ds(place, rows), NLON // 2 + start : NLON // 2 + stop] = even_sum - odd_sum

    if not window.last:
        for c in range(2):
            carried[c] = wind[c, pl.ds(at((0, extended - 2 * SUB)), 2 * SUB), :]
        carry_on = pltpu.make_async_copy(carried, carried_ref, out_sems.at[4])
        carry_on.start()

    blocks = extended // SUB

    def rows_of(block):
        return pl.ds(pl.multiple_of(block * SUB, SUB), SUB)

    def derivatives(field, block):
        before, after = jnp.maximum(block - 1, 0), jnp.minimum(block + 1, blocks - 1)
        result = []
        for c in range(2):
            here = field[c, rows_of(block), :]
            result.append((east_of(here), north_of(field[c, rows_of(before), :], here, field[c, rows_of(after), :])))
        return result

    @pl.loop(0, blocks, unroll=6)
    def _(block):
        flow = [wind[c, rows_of(block), :] for c in range(2)]
        for c, (east, north) in enumerate(derivatives(wind, block)):
            second[c, rows_of(block), :] = 0.25 * (flow[0] * east + flow[1] * north) - flow[c]

    @pl.loop(0, blocks, unroll=6)
    def _(block):
        flow = [wind[c, rows_of(block), :] for c in range(2)]
        for c, (east, north) in enumerate(derivatives(second, block)):
            third[c, rows_of(block), :] = -flow[c] - 0.25 * (flow[0] * east + flow[1] * north)

    @pl.loop(0, blocks, unroll=6)
    def _(block):
        flow = [wind[c, rows_of(block), :] for c in range(2)]
        for c, (east, north) in enumerate(derivatives(third, block)):
            fourth = -flow[c] - 0.5 * (flow[0] * east + flow[1] * north)
            both = second[c, rows_of(block), :] + third[c, rows_of(block), :]
            shift[c, rows_of(block), :] = (2.0 * both + (fourth - flow[c])) * (1.0 / 6.0)

    quarter = window.width // 4 // SUB

    def entries(out, base):
        @pl.loop(0, quarter, unroll=4)
        def _(block):
            (e0, n0), (e1, n1) = derivatives(shift, base + block + 1)
            g_xx, g_xy, g_yx, g_yy = 1.0 + 0.5 * e0, 0.5 * n0, 0.5 * e1, 1.0 + 0.5 * n1
            out[0, rows_of(block), :] = g_xx * g_xx + g_yx * g_yx
            out[1, rows_of(block), :] = g_xx * g_xy + g_yx * g_yy
            out[2, rows_of(block), :] = g_xy * g_xy + g_yy * g_yy

    copies = []
    for n, (a, b) in reversed(list(enumerate(QUARTERS))):
        side = sides[a]
        entries(results.at[n], (2 * (core + a - 2 * core * a) + (side + b - 2 * side * b)) * quarter)
        copies.append(pltpu.make_async_copy(results.at[n], out_refs[n], out_sems.at[n]))
        copies[-1].start()
    for copy in copies:
        copy.wait()
    if not window.last:
        carry_on.wait()


QUARTERS = ((0, 0), (0, 1), (1, 0), (1, 1))


def window_tensor(window, place, local, remote, table, waits, carry):
    depth = local.shape[2]
    vmem = pl.BlockSpec(memory_space=pltpu.VMEM)
    in_specs = [
        pl.BlockSpec(memory_space=pltpu.SMEM),
        vmem,
        vmem,
        pl.BlockSpec(memory_space=pl.ANY),
    ]
    in_specs += [pl.BlockSpec(memory_space=pl.ANY)] * len(waits)
    operands = [place, local, remote, table, *waits]
    if not window.first:
        in_specs.append(vmem)
        operands.append(carry)
    out_shape = [jax.ShapeDtypeStruct((3, window.width // 4, NLON), jnp.float32)] * 4
    if not window.last:
        out_shape.append(jax.ShapeDtypeStruct((2, 2 * SUB, NLON), jnp.float32))
    field = pltpu.VMEM((2, window.extended, NLON), jnp.float32)
    lhs_shape = (2, 2 * window.rows, depth)
    out = pl.pallas_call(
        functools.partial(window_kernel, window, depth, len(waits)),
        out_shape=out_shape,
        in_specs=in_specs,
        out_specs=[pl.BlockSpec(memory_space=pl.ANY)] * len(out_shape),
        scratch_shapes=[
            pltpu.VMEM(table.shape, table.dtype),
            pltpu.VMEM(lhs_shape, jnp.bfloat16),
            pltpu.VMEM(lhs_shape, jnp.bfloat16),
            field,
            field,
            field,
            field,
            pltpu.VMEM((4, 3, window.width // 4, NLON), jnp.float32),
            pltpu.VMEM((2, 2 * SUB, NLON), jnp.float32),
            pltpu.SemaphoreType.DMA,
            pltpu.SemaphoreType.DMA((5,)),
        ],
        compiler_params=pltpu.CompilerParams(vmem_limit_bytes=VMEM_LIMIT),
        cost_estimate=pl.CostEstimate(
            flops=KERNEL_WORK * 3 * 2 * 2 * window.rows * depth * NLON,
            transcendentals=0,
            bytes_accessed=2 * table.size + 4 * window.rows * depth * 4 + 12 * window.width * NLON,
        ),
        name="window_tensor",
    )(*operands)
    return out[:4], (None if window.last else out[4])


def by_levels(coeffs):
    spec = coeffs[0]
    levels, _, parts, waves_local, nlat = spec.shape
    members = lax.axis_size("mem")
    band = lax.axis_index("band").astype(jnp.int32)
    member = lax.axis_index("mem").astype(jnp.int32)
    core = member % 2
    half_of = [choose(core, [member // bits[step] % 2 for bits in ORDER]) for step in range(len(ORDER[0]))]
    half_beside = choose(1 - core, [member // bits[0] % 2 for bits in ORDER])
    place = jnp.stack([band, core, half_of[0], half_beside])
    spec = spec.reshape(levels, 2, parts * waves_local, nlat)
    count = nlat // LANE
    windows = [Window(k, count) for k in range(count)]
    table = jnp.asarray(wave_table(levels, waves_local))
    swap = [(0, 1), (1, 0)]

    (piece,) = pieces_of(spec, 1 - band, windows[:1], count)
    remotes = [lax.ppermute(piece, "band", swap)]
    for k, piece in enumerate(pieces_of(spec, 1 - band, windows[1:], count), 1):
        if k > 1:
            piece = gated(piece, [remotes[k - 2]])
        remotes.append(lax.ppermute(piece, "band", swap))
    local = pieces_of(spec, band, windows, count)

    cores = [(m, m ^ 1) for m in range(members)]
    ways = [[(m, m ^ ORDER[m % 2][step]) for m in range(members)] for step in range(len(ORDER[0]))]

    def halved(parts_of, step):
        half = parts_of[0].shape[1] // 2
        mine = half_of[step]

        def total(which):
            return sum(lax.dynamic_slice_in_dim(part, which * half, half, axis=1) for part in parts_of)

        leaves = total(1 - mine)
        return [total(mine), lax.ppermute(leaves, "mem", ways[step])], leaves

    def across(parts_of, step):
        kept, passed, kept_more, passed_more = parts_of
        leaves = passed + passed_more
        return [kept, kept_more, lax.ppermute(leaves, "mem", ways[step])], leaves

    def advanced(parts_of, step):
        return (across if step == 0 else halved)(parts_of, step)

    def doubled(part, step):
        beside = lax.ppermute(part, "mem", cores if step < 0 else ways[step])
        mine = core if step < 0 else half_of[step]
        return jnp.where(mine == 0, jnp.concatenate([part, beside], axis=1), jnp.concatenate([beside, part], axis=1))

    def gathered(part):
        for step in range(len(ways) - 1, -2, -1):
            part = doubled(part, step)
        return part

    carry = None
    sums, done = [], []
    for k, window in enumerate(windows):
        waits = []
        for j in AHEAD[k]:
            sums[j], left = advanced(sums[j], done[j])
            done[j] += 1
            waits.append(left)
        quarters, carry = window_tensor(window, place, local[k], remotes[k], table, waits, carry)
        first = lax.ppermute(quarters[3], "mem", cores)
        second = lax.ppermute(quarters[2], "mem", cores)
        sums.append([quarters[0], quarters[1], second, first])
        done.append(0)
    pieces = {"own": [], "both": [], "other": []}
    for k, window in enumerate(windows):
        for step in range(done[k], len(ways)):
            sums[k], _ = advanced(sums[k], step)
        pieces[window.side].append(exponent_of(sum(sums[k]), members))

    other = lax.ppermute(jnp.stack(pieces["other"]), "band", swap)
    place_of = {}
    for m in range(members):
        for b in range(2):
            bits = ORDER[m % 2]
            piece = functools.reduce(lambda value, bit: 2 * value + m // bit % 2, bits, m % 2)
            place_of[piece, b] = m * 2 + b
    trades, half = [], members // 2
    for (piece, b), index in place_of.items():
        mate = (piece, b) if (piece < half) == (b == 0) else ((piece + half) % members, 1 - b)
        trades.append((index, place_of[mate]))
    both = lax.ppermute(pieces["both"][0], ("mem", "band"), trades)

    early = gathered(jnp.concatenate([other, both[None]]))
    other, both = early[:-1], early[-1]
    middle = both.shape[0] // 2
    low, high = both[:middle], both[middle:]
    rest = jnp.zeros((nlat // 2 - middle, NLON), jnp.float32)
    down = jnp.stack([jnp.concatenate([rest, low]), jnp.concatenate([*other, high])])
    up = jnp.stack([jnp.concatenate([low, *other[::-1]]), jnp.concatenate([high, rest])])
    out = jnp.where(band == 0, down, up)

    own = gathered(jnp.stack(pieces["own"]))
    for k, block in enumerate(own):
        width = block.shape[0]
        row = choose(band, (nlat // 2 - middle - (k + 1) * width, middle + k * width))
        out = lax.dynamic_update_slice(out, block[None], (band, row.astype(jnp.int32), jnp.int32(0)))
    return out


def per_device(coeffs):
    _, levels, _, _, _, nlat = coeffs.shape
    members = lax.axis_size("mem")
    rows = nlat // lax.axis_size("band")
    fits = coeffs.shape[4] == 5 * LANE // 2 and nlat % (2 * LANE) == LANE and rows > LANE
    if fits and levels == lax.axis_size("band") == 2 and members == 16:
        return by_levels(coeffs)
    return by_rows(coeffs)


def solution(mesh):
    placed = (P("mem", None, None, None, "band", None),)
    return jax.shard_map(
        per_device, mesh=mesh, in_specs=placed, out_specs=P(None, "band", None), check_vma=False
    )
```

```python
import functools
import math

import jax
import jax.numpy as jnp
import ml_dtypes
import numpy as np
from jax import lax
from jax.experimental import pallas as pl
from jax.experimental.pallas import tpu as pltpu
from jax.sharding import PartitionSpec as P

NLON = 1280
STEPS = 1
SUB = 8
LANE = 128
VMEM_LIMIT = 60 * 1024 * 1024
KERNEL_WORK = 8
ORDER = ((2, 4, 8), (4, 8, 2))
AHEAD = ((), (), (0,), (1, 0), (2, 1, 0))


def padded(cells, sides, width):
    for axis, dim in sides:
        count = lax.axis_size(axis)
        ends = count - 1
        head = lax.slice_in_dim(cells, 0, width, axis=dim)
        tail = lax.slice_in_dim(cells, cells.shape[dim] - width, cells.shape[dim], axis=dim)
        cells = jnp.concatenate(
            [
                lax.ppermute(tail, axis, [(i, (i + 1) % count) for i in range(ends)]),
                cells,
                lax.ppermute(head, axis, [((i + 1) % count, i) for i in range(ends)]),
            ],
            axis=dim,
        )
    return cells


def slope(extended, winds):
    center = extended[:, 1:-1]
    north = (extended[:, 2:] - extended[:, :-2]) * 0.5
    east = (jnp.roll(center, -1, 2) - jnp.roll(center, 1, 2)) * 0.5
    return -winds - (winds[0] * east + winds[1] * north)


def rimmed(field):
    return padded(field, (("band", 1),), 1)


def tensor(extended):
    center = extended[:, 1:-1]
    north = (extended[:, 2:] - extended[:, :-2]) * 0.5
    east = (jnp.roll(center, -1, 2) - jnp.roll(center, 1, 2)) * 0.5
    g_xx = 1.0 + east[0]
    g_xy = north[0]
    g_yx = east[1]
    g_yy = 1.0 + north[1]
    return jnp.stack(
        [g_xx * g_xx + g_yx * g_yx, g_xx * g_xy + g_yx * g_yy, g_xy * g_xy + g_yy * g_yy]
    )


def integrate(shift, flow, extend):
    first = slope(extend(shift), flow)
    second = slope(extend(0.5 * first), flow)
    third = slope(extend(0.5 * second), flow)
    fourth = slope(extend(third), flow)
    return (first + 2.0 * second + 2.0 * third + fourth) / 6.0


def exponent_of(summed, members):
    mean = summed / members
    first, cross, second = (mean[..., 0, :, :], mean[..., 1, :, :], mean[..., 2, :, :])
    half = (first + second) * 0.5
    differ = (first - second) * 0.5
    largest = half + jnp.sqrt(differ * differ + cross * cross)
    return jnp.log(largest + 1e-06) / (2.0 * STEPS)


def by_rows(coeffs):
    spec = coeffs[0]
    levels = spec.shape[0]
    nlat = spec.shape[4]
    waves = spec.shape[3] * lax.axis_size("band")
    members = lax.axis_size("mem")
    stacked = spec.reshape(levels * 2, 2, spec.shape[3], nlat)
    wave_index = lax.iota(jnp.int32, waves)
    column = lax.iota(jnp.int32, NLON)
    phase = wave_index[:, None] * column[None, :] % NLON
    angle = phase.astype(jnp.float32) * (2.0 * math.pi / NLON)
    weight = jnp.where(wave_index == 0, 1.0, 2.0).astype(jnp.float32)[:, None]
    table = jnp.stack([weight * jnp.cos(angle), -weight * jnp.sin(angle)], axis=0)
    winds = jnp.einsum(
        "crwh,rwn->chn",
        lax.all_to_all(stacked, "band", split_axis=3, concat_axis=2, tiled=True),
        table,
        precision=lax.Precision.HIGHEST,
        preferred_element_type=jnp.float32,
    )
    height = winds.shape[1]
    winds = winds.reshape(levels, 2, height, NLON)
    partials = []
    for level in range(levels):
        flow = winds[level]
        shift = integrate(jnp.zeros_like(flow), flow, rimmed)
        partials.append(tensor(rimmed(shift)))
    summed = lax.psum_scatter(jnp.stack(partials), "mem", scatter_dimension=3, tiled=True)
    return lax.all_gather(exponent_of(summed, members), "mem", axis=2, tiled=True)


def by_parity(waves_local):
    half = waves_local // 2
    whole = 2 * LANE - half
    runs = []
    for parity in range(2):
        runs += [(parity, half, 2), (waves_local + parity, whole, 2)]
    for parity in range(2):
        runs.append((waves_local + parity + 2 * whole, half - whole, 2))
    return runs


@functools.lru_cache(maxsize=None)
def wave_table(bands, waves_local):
    order = np.concatenate([start + step * np.arange(count) for start, count, step in by_parity(waves_local)])
    wave, part = order % waves_local, order // waves_local
    wave = wave[None, :] + waves_local * np.arange(bands)[:, None]
    part = np.broadcast_to(part, wave.shape)
    cut = [0, 2 * LANE, 4 * LANE, 4 * LANE + LANE // 2, 5 * LANE]
    result = []
    for parity in range(2):
        picks = [(band, slice(cut[parity], cut[parity + 1])) for band in range(bands)]
        picks += [(band, slice(cut[parity + 2], cut[parity + 3])) for band in range(bands)]
        waves = np.concatenate([wave[pick] for pick in picks])
        parts = np.concatenate([part[pick] for pick in picks])
        phase = (waves[:, None] * np.arange(NLON // 2)[None, :]) % NLON
        angle = phase.astype(np.float64) * (2.0 * np.pi / NLON)
        weight = np.where(waves == 0, 1.0, 2.0)[:, None]
        table = weight * np.where(parts[:, None] == 0, np.cos(angle), -np.sin(angle))
        high = table.astype(ml_dtypes.bfloat16)
        result += [high, (table - high.astype(np.float64)).astype(ml_dtypes.bfloat16)]
    return np.stack(result)


class Window:
    def __init__(self, index, count):
        self.first = index == 0
        self.last = index == count - 1
        self.index = index
        self.width = LANE
        self.extended = LANE + 2 * SUB
        self.main = LANE if self.first else LANE - SUB
        self.rim = 0 if self.last else SUB
        self.rows = self.main + self.rim
        up = SUB if self.first else 2 * SUB
        self.place = (self.extended - up - self.rows, up)
        self.side = "other" if 2 * (index + 1) <= count else "own" if 2 * index >= count else "both"


def choose(band, pair):
    return jnp.where(band == 0, pair[0], pair[1])


def multiple(value, of):
    return pl.multiple_of(value.astype(jnp.int32), of)


def pieces_kernel(windows, slots, count, level_ref, spec_ref, *refs):
    out_refs, (taken, turned, in_sems, out_sems) = refs[: len(windows)], refs[len(windows) :]
    level = level_ref[0]
    runs = by_parity(spec_ref.shape[2] // 2)

    def arrival(c, n):
        tile = choose(level, (count - 1 - slots[n], slots[n]))
        lanes = pl.ds(multiple(tile * LANE, LANE), LANE)
        return pltpu.make_async_copy(spec_ref.at[level, c, :, lanes], taken.at[c, n], in_sems.at[c, n])

    def departures(c, k):
        window, n = windows[k], slots.index(windows[k].index)
        rows = pl.ds(multiple(choose(level, (0, LANE - window.main)), SUB), window.main)
        at = pl.ds(multiple(choose(level, (window.rim, 0)), SUB), window.main)
        yield pltpu.make_async_copy(turned.at[c, n, rows], out_refs[k].at[c, at], out_sems.at[k, c, 0])
        if window.rim:
            rows = pl.ds(multiple(choose(level, (LANE - SUB, 0)), SUB), SUB)
            at = pl.ds(multiple(choose(level, (0, window.main)), SUB), SUB)
            yield pltpu.make_async_copy(turned.at[c, n + 1, rows], out_refs[k].at[c, at], out_sems.at[k, c, 1])

    for n in range(len(slots)):
        for c in range(2):
            arrival(c, n).start()
    for n in range(len(slots)):
        for c in range(2):
            arrival(c, n).wait()
            turned[c, n] = jnp.concatenate([taken[c, n, pl.ds(start, rows, step), :] for start, rows, step in runs]).T
        for k, window in enumerate(windows):
            if slots[n] == window.index + (1 if window.rim else 0):
                for c in range(2):
                    for copy in departures(c, k):
                        copy.start()
    for k in range(len(windows)):
        for c in range(2):
            for copy in departures(c, k):
                copy.wait()


def pieces_of(spec, level, windows, count):
    depth = spec.shape[2]
    slots = sorted({w.index for w in windows} | {w.index + 1 for w in windows if w.rim})
    return pl.pallas_call(
        functools.partial(pieces_kernel, windows, slots, count),
        in_specs=[pl.BlockSpec(memory_space=pltpu.SMEM), pl.BlockSpec(memory_space=pl.ANY)],
        out_specs=[pl.BlockSpec(memory_space=pl.ANY)] * len(windows),
        out_shape=[jax.ShapeDtypeStruct((2, w.rows, depth), jnp.float32) for w in windows],
        scratch_shapes=[
            pltpu.VMEM((2, len(slots), depth, LANE), jnp.float32),
            pltpu.VMEM((2, len(slots), LANE, depth), jnp.float32),
            pltpu.SemaphoreType.DMA((2, len(slots))),
            pltpu.SemaphoreType.DMA((len(windows), 2, 2)),
        ],
        compiler_params=pltpu.CompilerParams(vmem_limit_bytes=VMEM_LIMIT),
        cost_estimate=pl.CostEstimate(
            flops=0, transcendentals=0, bytes_accessed=4 * 2 * len(slots) * LANE * depth * 4
        ),
        name="pieces_of",
    )(level.reshape(1), spec)


def gate_kernel(*refs):
    pass


def gated(part, waits):
    return pl.pallas_call(
        gate_kernel,
        in_specs=[pl.BlockSpec(memory_space=pl.ANY)] * (1 + len(waits)),
        out_specs=pl.BlockSpec(memory_space=pl.ANY),
        out_shape=jax.ShapeDtypeStruct(part.shape, part.dtype),
        input_output_aliases={0: 0},
        cost_estimate=pl.CostEstimate(flops=0, transcendentals=0, bytes_accessed=1024),
        name="gated",
    )(part, *waits)


def east_of(x):
    return pltpu.roll(x, NLON - 1, axis=1) - pltpu.roll(x, 1, axis=1)


def north_of(before, here, after):
    row = lax.broadcasted_iota(jnp.int32, here.shape, 0)
    above = jnp.where(row == SUB - 1, pltpu.roll(after, SUB - 1, axis=0), pltpu.roll(here, SUB - 1, axis=0))
    below = jnp.where(row == 0, pltpu.roll(before, 1, axis=0), pltpu.roll(here, 1, axis=0))
    return above - below


def window_kernel(window, waits, *refs):
    refs = list(refs)
    place_ref, local_ref, remote_ref, table_ref = refs[:4]
    refs = refs[4 + waits :]
    carry_ref = None if window.first else refs.pop(0)
    out_refs = [refs.pop(0) for _ in range(4)]
    carried_ref = None if window.last else refs.pop(0)
    table, mine_buf, theirs_buf, lhs_high, lhs_low, wind, second, third, shift, results, carried, in_sems, out_sems = refs
    band, core, sides = place_ref[0], place_ref[1], (place_ref[2], place_ref[3])
    rows, extended = window.rows, window.extended

    def at(pair):
        return multiple(choose(band, pair), SUB)

    inputs = [pltpu.make_async_copy(local_ref, mine_buf, in_sems.at[0])]
    inputs.append(pltpu.make_async_copy(remote_ref, theirs_buf, in_sems.at[1]))
    tables = pltpu.make_async_copy(table_ref, table, in_sems.at[2])
    if not window.first:
        rows_before = wind.at[:, pl.ds(at((extended - 2 * SUB, 0)), 2 * SUB)]
        inputs.append(pltpu.make_async_copy(carry_ref, rows_before, in_sems.at[3]))
    for copy in [*inputs, tables]:
        copy.start()
    for copy in inputs:
        copy.wait()
    lane = lax.broadcasted_iota(jnp.int32, (rows, LANE), 1)
    even, odd = [], []
    for c in range(2):
        mine, theirs = mine_buf[c], theirs_buf[c]
        low, high = jnp.where(band == 0, mine, theirs), jnp.where(band == 0, theirs, mine)
        low_rest, high_rest = low[:, 4 * LANE :], high[:, 4 * LANE :]
        turn = functools.partial(pltpu.roll, shift=LANE // 2, axis=1)
        even_rest = jnp.where(lane < LANE // 2, low_rest, turn(high_rest))
        odd_rest = jnp.where(lane < LANE // 2, turn(low_rest), high_rest)
        even.append(jnp.concatenate([low[:, : 2 * LANE], high[:, : 2 * LANE], even_rest], axis=1))
        odd.append(jnp.concatenate([low[:, 2 * LANE : 4 * LANE], high[:, 2 * LANE : 4 * LANE], odd_rest], axis=1))
    for parity, parts in enumerate((even, odd)):
        lhs = jnp.concatenate(parts)
        lhs_high[parity] = lhs.astype(jnp.bfloat16)
        lhs_low[parity] = (lhs - lhs_high[parity].astype(jnp.float32)).astype(jnp.bfloat16)

    place = at(window.place)
    if window.first or window.last:
        for c in range(2):
            if window.first:
                wind[c, pl.ds(at((extended - SUB, 0)), SUB), :] = jnp.zeros((SUB, NLON), jnp.float32)
            if window.last:
                wind[c, pl.ds(at((0, extended - SUB)), SUB), :] = jnp.zeros((SUB, NLON), jnp.float32)
    tables.wait()

    dot = functools.partial(jnp.dot, preferred_element_type=jnp.float32)
    for start in range(0, NLON // 2, 2 * LANE):
        stop = min(start + 2 * LANE, NLON // 2)
        columns = slice(start, stop)
        sums = []
        for parity in range(2):
            total = dot(lhs_high[parity], table[2 * parity, :, columns])
            total += dot(lhs_low[parity], table[2 * parity, :, columns])
            total += dot(lhs_high[parity], table[2 * parity + 1, :, columns])
            sums.append(total)
        for c in range(2):
            even_sum, odd_sum = (total[c * rows : (c + 1) * rows] for total in sums)
            wind[c, pl.ds(place, rows), start:stop] = even_sum + odd_sum
            wind[c, pl.ds(place, rows), NLON // 2 + start : NLON // 2 + stop] = even_sum - odd_sum

    if not window.last:
        for c in range(2):
            carried[c] = wind[c, pl.ds(at((0, extended - 2 * SUB)), 2 * SUB), :]
        carry_on = pltpu.make_async_copy(carried, carried_ref, out_sems.at[4])
        carry_on.start()

    blocks = extended // SUB

    def rows_of(block):
        return pl.ds(pl.multiple_of(block * SUB, SUB), SUB)

    def derivatives(field, block):
        before, after = jnp.maximum(block - 1, 0), jnp.minimum(block + 1, blocks - 1)
        result = []
        for c in range(2):
            here = field[c, rows_of(block), :]
            result.append((east_of(here), north_of(field[c, rows_of(before), :], here, field[c, rows_of(after), :])))
        return result

    @pl.loop(0, blocks, unroll=6)
    def _(block):
        flow = [wind[c, rows_of(block), :] for c in range(2)]
        for c, (east, north) in enumerate(derivatives(wind, block)):
            second[c, rows_of(block), :] = 0.25 * (flow[0] * east + flow[1] * north) - flow[c]

    @pl.loop(0, blocks, unroll=6)
    def _(block):
        flow = [wind[c, rows_of(block), :] for c in range(2)]
        for c, (east, north) in enumerate(derivatives(second, block)):
            third[c, rows_of(block), :] = -flow[c] - 0.25 * (flow[0] * east + flow[1] * north)

    @pl.loop(0, blocks, unroll=6)
    def _(block):
        flow = [wind[c, rows_of(block), :] for c in range(2)]
        for c, (east, north) in enumerate(derivatives(third, block)):
            fourth = -flow[c] - 0.5 * (flow[0] * east + flow[1] * north)
            both = second[c, rows_of(block), :] + third[c, rows_of(block), :]
            shift[c, rows_of(block), :] = (2.0 * both + (fourth - flow[c])) * (1.0 / 6.0)

    quarter = window.width // 4 // SUB

    def entries(out, base):
        @pl.loop(0, quarter, unroll=4)
        def _(block):
            (e0, n0), (e1, n1) = derivatives(shift, base + block + 1)
            g_xx, g_xy, g_yx, g_yy = 1.0 + 0.5 * e0, 0.5 * n0, 0.5 * e1, 1.0 + 0.5 * n1
            out[0, rows_of(block), :] = g_xx * g_xx + g_yx * g_yx
            out[1, rows_of(block), :] = g_xx * g_xy + g_yx * g_yy
            out[2, rows_of(block), :] = g_xy * g_xy + g_yy * g_yy

    copies = []
    for n, (a, b) in reversed(list(enumerate(QUARTERS))):
        side = sides[a]
        entries(results.at[n], (2 * (core + a - 2 * core * a) + (side + b - 2 * side * b)) * quarter)
        copies.append(pltpu.make_async_copy(results.at[n], out_refs[n], out_sems.at[n]))
        copies[-1].start()
    for copy in copies:
        copy.wait()
    if not window.last:
        carry_on.wait()


QUARTERS = ((0, 0), (0, 1), (1, 0), (1, 1))


def window_tensor(window, place, local, remote, table, waits, carry):
    depth = local.shape[2]
    operands = [place, local, remote, table, *waits]
    if not window.first:
        operands.append(carry)
    in_specs = [pl.BlockSpec(memory_space=pltpu.SMEM)] + [pl.BlockSpec(memory_space=pl.ANY)] * (len(operands) - 1)
    out_shape = [jax.ShapeDtypeStruct((3, window.width // 4, NLON), jnp.float32)] * 4
    if not window.last:
        out_shape.append(jax.ShapeDtypeStruct((2, 2 * SUB, NLON), jnp.float32))
    field = pltpu.VMEM((2, window.extended, NLON), jnp.float32)
    lhs_shape = (2, 2 * window.rows, depth)
    out = pl.pallas_call(
        functools.partial(window_kernel, window, len(waits)),
        out_shape=out_shape,
        in_specs=in_specs,
        out_specs=[pl.BlockSpec(memory_space=pl.ANY)] * len(out_shape),
        scratch_shapes=[
            pltpu.VMEM(table.shape, table.dtype),
            pltpu.VMEM(local.shape, jnp.float32),
            pltpu.VMEM(local.shape, jnp.float32),
            pltpu.VMEM(lhs_shape, jnp.bfloat16),
            pltpu.VMEM(lhs_shape, jnp.bfloat16),
            field,
            field,
            field,
            field,
            pltpu.VMEM((4, 3, window.width // 4, NLON), jnp.float32),
            pltpu.VMEM((2, 2 * SUB, NLON), jnp.float32),
            pltpu.SemaphoreType.DMA((4,)),
            pltpu.SemaphoreType.DMA((5,)),
        ],
        compiler_params=pltpu.CompilerParams(vmem_limit_bytes=VMEM_LIMIT),
        cost_estimate=pl.CostEstimate(
            flops=KERNEL_WORK * 3 * 2 * 2 * window.rows * depth * NLON,
            transcendentals=0,
            bytes_accessed=2 * table.size + 4 * window.rows * depth * 4 + 12 * window.width * NLON,
        ),
        name="window_tensor",
    )(*operands)
    return out[:4], (None if window.last else out[4])


def by_levels(coeffs):
    spec = coeffs[0]
    levels, _, parts, waves_local, nlat = spec.shape
    members = lax.axis_size("mem")
    band = lax.axis_index("band").astype(jnp.int32)
    member = lax.axis_index("mem").astype(jnp.int32)
    core = member % 2
    half_of = [choose(core, [member // bits[step] % 2 for bits in ORDER]) for step in range(len(ORDER[0]))]
    half_beside = choose(1 - core, [member // bits[0] % 2 for bits in ORDER])
    place = jnp.stack([band, core, half_of[0], half_beside])
    spec = spec.reshape(levels, 2, parts * waves_local, nlat)
    count = nlat // LANE
    windows = [Window(k, count) for k in range(count)]
    table = jnp.asarray(wave_table(levels, waves_local))
    swap = [(0, 1), (1, 0)]

    (piece,) = pieces_of(spec, 1 - band, windows[:1], count)
    remotes = [lax.ppermute(piece, "band", swap)]
    for k, piece in enumerate(pieces_of(spec, 1 - band, windows[1:], count), 1):
        if k > 1:
            piece = gated(piece, [remotes[k - 2]])
        remotes.append(lax.ppermute(piece, "band", swap))
    local = pieces_of(spec, band, windows, count)

    cores = [(m, m ^ 1) for m in range(members)]
    ways = [[(m, m ^ ORDER[m % 2][step]) for m in range(members)] for step in range(len(ORDER[0]))]

    def halved(parts_of, step):
        half = parts_of[0].shape[1] // 2
        mine = half_of[step]

        def total(which):
            return sum(lax.dynamic_slice_in_dim(part, which * half, half, axis=1) for part in parts_of)

        leaves = total(1 - mine)
        return [total(mine), lax.ppermute(leaves, "mem", ways[step])], leaves

    def across(parts_of, step):
        kept, passed, kept_more, passed_more = parts_of
        leaves = passed + passed_more
        return [kept, kept_more, lax.ppermute(leaves, "mem", ways[step])], leaves

    def shared(parts_of, step):
        total = sum(parts_of)
        return [total, lax.ppermute(total, "mem", ways[step])], total

    def advanced(parts_of, step):
        return (across if step == 0 else halved if step + 1 < len(ways) else shared)(parts_of, step)

    def doubled(part, step):
        beside = lax.ppermute(part, "mem", cores if step < 0 else ways[step])
        mine = core if step < 0 else half_of[step]
        return jnp.where(mine == 0, jnp.concatenate([part, beside], axis=1), jnp.concatenate([beside, part], axis=1))

    def gathered(part):
        for step in range(len(ways) - 2, -2, -1):
            part = doubled(part, step)
        return part

    carry = None
    sums, done = [], []
    for k, window in enumerate(windows):
        waits = []
        for j in AHEAD[k]:
            sums[j], left = advanced(sums[j], done[j])
            done[j] += 1
            waits.append(left)
        quarters, carry = window_tensor(window, place, local[k], remotes[k], table, waits, carry)
        first = lax.ppermute(quarters[3], "mem", cores)
        second = lax.ppermute(quarters[2], "mem", cores)
        sums.append([quarters[0], quarters[1], second, first])
        done.append(0)
    pieces = {"own": [], "both": [], "other": []}
    for k, window in enumerate(windows):
        for step in range(done[k], len(ways)):
            sums[k], _ = advanced(sums[k], step)
        pieces[window.side].append(exponent_of(sum(sums[k]), members))

    other = lax.ppermute(jnp.stack(pieces["other"]), "band", swap)
    place_of = {}
    for m in range(members):
        for b in range(2):
            *bits, last = ORDER[m % 2]
            piece = functools.reduce(lambda value, bit: 2 * value + m // bit % 2, bits, m % 2)
            place_of[piece, m // last % 2, b] = m * 2 + b
    trades, half = [], members // 4
    for (piece, twin, b), index in place_of.items():
        mate = (piece, b) if (piece < half) == (b == 0) else ((piece + half) % (2 * half), 1 - b)
        trades.append((index, place_of[mate[0], twin, mate[1]]))
    both = lax.ppermute(pieces["both"][0], ("mem", "band"), trades)

    early = gathered(jnp.concatenate([other, both[None]]))
    other, both = early[:-1], early[-1]
    middle = both.shape[0] // 2
    low, high = both[:middle], both[middle:]
    rest = jnp.zeros((nlat // 2 - middle, NLON), jnp.float32)
    down = jnp.stack([jnp.concatenate([rest, low]), jnp.concatenate([*other, high])])
    up = jnp.stack([jnp.concatenate([low, *other[::-1]]), jnp.concatenate([high, rest])])
    out = jnp.where(band == 0, down, up)

    own = gathered(jnp.stack(pieces["own"]))
    for k, block in enumerate(own):
        width = block.shape[0]
        row = choose(band, (nlat // 2 - middle - (k + 1) * width, middle + k * width))
        out = lax.dynamic_update_slice(out, block[None], (band, row.astype(jnp.int32), jnp.int32(0)))
    return out


def per_device(coeffs):
    _, levels, _, _, _, nlat = coeffs.shape
    members = lax.axis_size("mem")
    rows = nlat // lax.axis_size("band")
    fits = coeffs.shape[4] == 5 * LANE // 2 and nlat % (2 * LANE) == LANE and rows > LANE
    if fits and levels == lax.axis_size("band") == 2 and members == 16:
        return by_levels(coeffs)
    return by_rows(coeffs)


def solution(mesh):
    placed = (P("mem", None, None, None, "band", None),)
    return jax.shard_map(
        per_device, mesh=mesh, in_specs=placed, out_specs=P(None, "band", None), check_vma=False
    )
```

```python
import functools
import math

import jax
import jax.numpy as jnp
import ml_dtypes
import numpy as np
from jax import lax
from jax.experimental import pallas as pl
from jax.experimental.pallas import tpu as pltpu
from jax.sharding import PartitionSpec as P

NLON = 1280
STEPS = 1
SUB = 8
LANE = 128
VMEM_LIMIT = 60 * 1024 * 1024
KERNEL_WORK = 8
ORDER = ((2, 4, 8), (4, 8, 2))
BATCHES = ((0, 1, 2), (3, 4))
AHEAD = ((), (), (), (), (0,))


def padded(cells, sides, width):
    for axis, dim in sides:
        count = lax.axis_size(axis)
        ends = count - 1
        head = lax.slice_in_dim(cells, 0, width, axis=dim)
        tail = lax.slice_in_dim(cells, cells.shape[dim] - width, cells.shape[dim], axis=dim)
        cells = jnp.concatenate(
            [
                lax.ppermute(tail, axis, [(i, (i + 1) % count) for i in range(ends)]),
                cells,
                lax.ppermute(head, axis, [((i + 1) % count, i) for i in range(ends)]),
            ],
            axis=dim,
        )
    return cells


def slope(extended, winds):
    center = extended[:, 1:-1]
    north = (extended[:, 2:] - extended[:, :-2]) * 0.5
    east = (jnp.roll(center, -1, 2) - jnp.roll(center, 1, 2)) * 0.5
    return -winds - (winds[0] * east + winds[1] * north)


def rimmed(field):
    return padded(field, (("band", 1),), 1)


def tensor(extended):
    center = extended[:, 1:-1]
    north = (extended[:, 2:] - extended[:, :-2]) * 0.5
    east = (jnp.roll(center, -1, 2) - jnp.roll(center, 1, 2)) * 0.5
    g_xx = 1.0 + east[0]
    g_xy = north[0]
    g_yx = east[1]
    g_yy = 1.0 + north[1]
    return jnp.stack(
        [g_xx * g_xx + g_yx * g_yx, g_xx * g_xy + g_yx * g_yy, g_xy * g_xy + g_yy * g_yy]
    )


def integrate(shift, flow, extend):
    first = slope(extend(shift), flow)
    second = slope(extend(0.5 * first), flow)
    third = slope(extend(0.5 * second), flow)
    fourth = slope(extend(third), flow)
    return (first + 2.0 * second + 2.0 * third + fourth) / 6.0


def exponent_of(summed, members):
    mean = summed / members
    first, cross, second = (mean[..., 0, :, :], mean[..., 1, :, :], mean[..., 2, :, :])
    half = (first + second) * 0.5
    differ = (first - second) * 0.5
    largest = half + jnp.sqrt(differ * differ + cross * cross)
    return jnp.log(largest + 1e-06) / (2.0 * STEPS)


def by_rows(coeffs):
    spec = coeffs[0]
    levels = spec.shape[0]
    nlat = spec.shape[4]
    waves = spec.shape[3] * lax.axis_size("band")
    members = lax.axis_size("mem")
    stacked = spec.reshape(levels * 2, 2, spec.shape[3], nlat)
    wave_index = lax.iota(jnp.int32, waves)
    column = lax.iota(jnp.int32, NLON)
    phase = wave_index[:, None] * column[None, :] % NLON
    angle = phase.astype(jnp.float32) * (2.0 * math.pi / NLON)
    weight = jnp.where(wave_index == 0, 1.0, 2.0).astype(jnp.float32)[:, None]
    table = jnp.stack([weight * jnp.cos(angle), -weight * jnp.sin(angle)], axis=0)
    winds = jnp.einsum(
        "crwh,rwn->chn",
        lax.all_to_all(stacked, "band", split_axis=3, concat_axis=2, tiled=True),
        table,
        precision=lax.Precision.HIGHEST,
        preferred_element_type=jnp.float32,
    )
    height = winds.shape[1]
    winds = winds.reshape(levels, 2, height, NLON)
    partials = []
    for level in range(levels):
        flow = winds[level]
        shift = integrate(jnp.zeros_like(flow), flow, rimmed)
        partials.append(tensor(rimmed(shift)))
    summed = lax.psum_scatter(jnp.stack(partials), "mem", scatter_dimension=3, tiled=True)
    return lax.all_gather(exponent_of(summed, members), "mem", axis=2, tiled=True)


def by_parity(waves_local):
    half = waves_local // 2
    whole = 2 * LANE - half
    runs = []
    for parity in range(2):
        runs += [(parity, half, 2), (waves_local + parity, whole, 2)]
    for parity in range(2):
        runs.append((waves_local + parity + 2 * whole, half - whole, 2))
    return runs


@functools.lru_cache(maxsize=None)
def wave_table(bands, waves_local):
    order = np.concatenate([start + step * np.arange(count) for start, count, step in by_parity(waves_local)])
    wave, part = order % waves_local, order // waves_local
    wave = wave[None, :] + waves_local * np.arange(bands)[:, None]
    part = np.broadcast_to(part, wave.shape)
    cut = [0, 2 * LANE, 4 * LANE, 4 * LANE + LANE // 2, 5 * LANE]
    result = []
    for parity in range(2):
        picks = [(band, slice(cut[parity], cut[parity + 1])) for band in range(bands)]
        picks += [(band, slice(cut[parity + 2], cut[parity + 3])) for band in range(bands)]
        waves = np.concatenate([wave[pick] for pick in picks])
        parts = np.concatenate([part[pick] for pick in picks])
        phase = (waves[:, None] * np.arange(NLON // 2)[None, :]) % NLON
        angle = phase.astype(np.float64) * (2.0 * np.pi / NLON)
        weight = np.where(waves == 0, 1.0, 2.0)[:, None]
        table = weight * np.where(parts[:, None] == 0, np.cos(angle), -np.sin(angle))
        high = table.astype(ml_dtypes.bfloat16)
        result += [high, (table - high.astype(np.float64)).astype(ml_dtypes.bfloat16)]
    return np.stack(result)


class Window:
    def __init__(self, index, count):
        self.first = index == 0
        self.last = index == count - 1
        self.index = index
        self.width = LANE
        self.extended = LANE + 2 * SUB
        self.main = LANE if self.first else LANE - SUB
        self.rim = 0 if self.last else SUB
        self.rows = self.main + self.rim
        up = SUB if self.first else 2 * SUB
        self.place = (self.extended - up - self.rows, up)
        self.side = "other" if 2 * (index + 1) <= count else "own" if 2 * index >= count else "both"


def choose(band, pair):
    return jnp.where(band == 0, pair[0], pair[1])


def multiple(value, of):
    return pl.multiple_of(value.astype(jnp.int32), of)


def pieces_kernel(windows, slots, count, level_ref, spec_ref, *refs):
    out_refs, (taken, turned, in_sems, out_sems) = refs[: len(windows)], refs[len(windows) :]
    level = level_ref[0]
    runs = by_parity(spec_ref.shape[2] // 2)

    def arrival(c, n):
        tile = choose(level, (count - 1 - slots[n], slots[n]))
        lanes = pl.ds(multiple(tile * LANE, LANE), LANE)
        return pltpu.make_async_copy(spec_ref.at[level, c, :, lanes], taken.at[c, n], in_sems.at[c, n])

    def departures(c, k):
        window, n = windows[k], slots.index(windows[k].index)
        rows = pl.ds(multiple(choose(level, (0, LANE - window.main)), SUB), window.main)
        at = pl.ds(multiple(choose(level, (window.rim, 0)), SUB), window.main)
        yield pltpu.make_async_copy(turned.at[c, n, rows], out_refs[k].at[c, at], out_sems.at[k, c, 0])
        if window.rim:
            rows = pl.ds(multiple(choose(level, (LANE - SUB, 0)), SUB), SUB)
            at = pl.ds(multiple(choose(level, (0, window.main)), SUB), SUB)
            yield pltpu.make_async_copy(turned.at[c, n + 1, rows], out_refs[k].at[c, at], out_sems.at[k, c, 1])

    for n in range(len(slots)):
        for c in range(2):
            arrival(c, n).start()
    for n in range(len(slots)):
        for c in range(2):
            arrival(c, n).wait()
            turned[c, n] = jnp.concatenate([taken[c, n, pl.ds(start, rows, step), :] for start, rows, step in runs]).T
        for k, window in enumerate(windows):
            if slots[n] == window.index + (1 if window.rim else 0):
                for c in range(2):
                    for copy in departures(c, k):
                        copy.start()
    for k in range(len(windows)):
        for c in range(2):
            for copy in departures(c, k):
                copy.wait()


def pieces_of(spec, level, windows, count):
    depth = spec.shape[2]
    slots = sorted({w.index for w in windows} | {w.index + 1 for w in windows if w.rim})
    return pl.pallas_call(
        functools.partial(pieces_kernel, windows, slots, count),
        in_specs=[pl.BlockSpec(memory_space=pltpu.SMEM), pl.BlockSpec(memory_space=pl.ANY)],
        out_specs=[pl.BlockSpec(memory_space=pl.ANY)] * len(windows),
        out_shape=[jax.ShapeDtypeStruct((2, w.rows, depth), jnp.float32) for w in windows],
        scratch_shapes=[
            pltpu.VMEM((2, len(slots), depth, LANE), jnp.float32),
            pltpu.VMEM((2, len(slots), LANE, depth), jnp.float32),
            pltpu.SemaphoreType.DMA((2, len(slots))),
            pltpu.SemaphoreType.DMA((len(windows), 2, 2)),
        ],
        compiler_params=pltpu.CompilerParams(vmem_limit_bytes=VMEM_LIMIT),
        cost_estimate=pl.CostEstimate(
            flops=0, transcendentals=0, bytes_accessed=4 * 2 * len(slots) * LANE * depth * 4
        ),
        name="pieces_of",
    )(level.reshape(1), spec)


def gate_kernel(*refs):
    pass


def gated(part, waits):
    return pl.pallas_call(
        gate_kernel,
        in_specs=[pl.BlockSpec(memory_space=pl.ANY)] * (1 + len(waits)),
        out_specs=pl.BlockSpec(memory_space=pl.ANY),
        out_shape=jax.ShapeDtypeStruct(part.shape, part.dtype),
        input_output_aliases={0: 0},
        cost_estimate=pl.CostEstimate(flops=0, transcendentals=0, bytes_accessed=1024),
        name="gated",
    )(part, *waits)


def east_of(x):
    return pltpu.roll(x, NLON - 1, axis=1) - pltpu.roll(x, 1, axis=1)


def north_of(before, here, after):
    row = lax.broadcasted_iota(jnp.int32, here.shape, 0)
    above = jnp.where(row == SUB - 1, pltpu.roll(after, SUB - 1, axis=0), pltpu.roll(here, SUB - 1, axis=0))
    below = jnp.where(row == 0, pltpu.roll(before, 1, axis=0), pltpu.roll(here, 1, axis=0))
    return above - below


def window_kernel(window, slot, waits, *refs):
    refs = list(refs)
    place_ref, local_ref, remote_ref, table_ref = refs[:4]
    refs = refs[4 + waits + (len(QUARTERS) if slot else 0) :]
    carry_ref = None if window.first else refs.pop(0)
    out_refs = [refs.pop(0) for _ in range(4)]
    carried_ref = None if window.last else refs.pop(0)
    table, lhs_high, lhs_low, wind, second, third, shift, results, carried, table_sem, out_sems = refs
    band, core, sides = place_ref[0], place_ref[1], (place_ref[2], place_ref[3])
    rows, extended = window.rows, window.extended

    def at(pair):
        return multiple(choose(band, pair), SUB)

    tables = pltpu.make_async_copy(table_ref, table, table_sem)
    tables.start()
    lane = lax.broadcasted_iota(jnp.int32, (rows, LANE), 1)
    even, odd = [], []
    for c in range(2):
        mine, theirs = local_ref[c], remote_ref[c]
        low, high = jnp.where(band == 0, mine, theirs), jnp.where(band == 0, theirs, mine)
        low_rest, high_rest = low[:, 4 * LANE :], high[:, 4 * LANE :]
        turn = functools.partial(pltpu.roll, shift=LANE // 2, axis=1)
        even_rest = jnp.where(lane < LANE // 2, low_rest, turn(high_rest))
        odd_rest = jnp.where(lane < LANE // 2, turn(low_rest), high_rest)
        even.append(jnp.concatenate([low[:, : 2 * LANE], high[:, : 2 * LANE], even_rest], axis=1))
        odd.append(jnp.concatenate([low[:, 2 * LANE : 4 * LANE], high[:, 2 * LANE : 4 * LANE], odd_rest], axis=1))
    for parity, parts in enumerate((even, odd)):
        lhs = jnp.concatenate(parts)
        lhs_high[parity] = lhs.astype(jnp.bfloat16)
        lhs_low[parity] = (lhs - lhs_high[parity].astype(jnp.float32)).astype(jnp.bfloat16)
    tables.wait()

    place = at(window.place)
    if window.first or window.last:
        for c in range(2):
            if window.first:
                wind[c, pl.ds(at((extended - SUB, 0)), SUB), :] = jnp.zeros((SUB, NLON), jnp.float32)
            if window.last:
                wind[c, pl.ds(at((0, extended - SUB)), SUB), :] = jnp.zeros((SUB, NLON), jnp.float32)
    if not window.first:
        for c in range(2):
            wind[c, pl.ds(at((extended - 2 * SUB, 0)), 2 * SUB), :] = carry_ref[c]

    dot = functools.partial(jnp.dot, preferred_element_type=jnp.float32)
    for start in range(0, NLON // 2, 2 * LANE):
        stop = min(start + 2 * LANE, NLON // 2)
        columns = slice(start, stop)
        sums = []
        for parity in range(2):
            total = dot(lhs_high[parity], table[2 * parity, :, columns])
            total += dot(lhs_low[parity], table[2 * parity, :, columns])
            total += dot(lhs_high[parity], table[2 * parity + 1, :, columns])
            sums.append(total)
        for c in range(2):
            even_sum, odd_sum = (total[c * rows : (c + 1) * rows] for total in sums)
            wind[c, pl.ds(place, rows), start:stop] = even_sum + odd_sum
            wind[c, pl.ds(place, rows), NLON // 2 + start : NLON // 2 + stop] = even_sum - odd_sum

    if not window.last:
        for c in range(2):
            carried[c] = wind[c, pl.ds(at((0, extended - 2 * SUB)), 2 * SUB), :]
        carry_on = pltpu.make_async_copy(carried, carried_ref, out_sems.at[4])
        carry_on.start()

    blocks = extended // SUB

    def rows_of(block):
        return pl.ds(pl.multiple_of(block * SUB, SUB), SUB)

    def derivatives(field, block):
        before, after = jnp.maximum(block - 1, 0), jnp.minimum(block + 1, blocks - 1)
        result = []
        for c in range(2):
            here = field[c, rows_of(block), :]
            result.append((east_of(here), north_of(field[c, rows_of(before), :], here, field[c, rows_of(after), :])))
        return result

    @pl.loop(0, blocks, unroll=6)
    def _(block):
        flow = [wind[c, rows_of(block), :] for c in range(2)]
        for c, (east, north) in enumerate(derivatives(wind, block)):
            second[c, rows_of(block), :] = 0.25 * (flow[0] * east + flow[1] * north) - flow[c]

    @pl.loop(0, blocks, unroll=6)
    def _(block):
        flow = [wind[c, rows_of(block), :] for c in range(2)]
        for c, (east, north) in enumerate(derivatives(second, block)):
            third[c, rows_of(block), :] = -flow[c] - 0.25 * (flow[0] * east + flow[1] * north)

    @pl.loop(0, blocks, unroll=6)
    def _(block):
        flow = [wind[c, rows_of(block), :] for c in range(2)]
        for c, (east, north) in enumerate(derivatives(third, block)):
            fourth = -flow[c] - 0.5 * (flow[0] * east + flow[1] * north)
            both = second[c, rows_of(block), :] + third[c, rows_of(block), :]
            shift[c, rows_of(block), :] = (2.0 * both + (fourth - flow[c])) * (1.0 / 6.0)

    quarter = window.width // 4 // SUB

    def entries(out, base):
        @pl.loop(0, quarter, unroll=4)
        def _(block):
            (e0, n0), (e1, n1) = derivatives(shift, base + block + 1)
            g_xx, g_xy, g_yx, g_yy = 1.0 + 0.5 * e0, 0.5 * n0, 0.5 * e1, 1.0 + 0.5 * n1
            out[0, rows_of(block), :] = g_xx * g_xx + g_yx * g_yx
            out[1, rows_of(block), :] = g_xx * g_xy + g_yx * g_yy
            out[2, rows_of(block), :] = g_xy * g_xy + g_yy * g_yy

    copies = []
    for n, (a, b) in reversed(list(enumerate(QUARTERS))):
        side = sides[a]
        entries(results.at[n], (2 * (core + a - 2 * core * a) + (side + b - 2 * side * b)) * quarter)
        copies.append(pltpu.make_async_copy(results.at[n], out_refs[n].at[slot], out_sems.at[n]))
        copies[-1].start()
    for copy in copies:
        copy.wait()
    if not window.last:
        carry_on.wait()


QUARTERS = ((0, 0), (0, 1), (1, 0), (1, 1))


def window_tensor(window, slot, slots, place, local, remote, table, made, waits, carry):
    depth = local.shape[2]
    vmem = pl.BlockSpec(memory_space=pltpu.VMEM)
    in_specs = [
        pl.BlockSpec(memory_space=pltpu.SMEM),
        vmem,
        vmem,
        pl.BlockSpec(memory_space=pl.ANY),
    ]
    in_specs += [pl.BlockSpec(memory_space=pl.ANY)] * len(waits)
    operands = [place, local, remote, table, *waits]
    aliases = {}
    if slot:
        aliases = {len(operands) + n: n for n in range(len(QUARTERS))}
        in_specs += [pl.BlockSpec(memory_space=pl.ANY)] * len(QUARTERS)
        operands += made
    if not window.first:
        in_specs.append(vmem)
        operands.append(carry)
    out_shape = [jax.ShapeDtypeStruct((slots, 3, window.width // 4, NLON), jnp.float32)] * len(QUARTERS)
    if not window.last:
        out_shape.append(jax.ShapeDtypeStruct((2, 2 * SUB, NLON), jnp.float32))
    field = pltpu.VMEM((2, window.extended, NLON), jnp.float32)
    lhs_shape = (2, 2 * window.rows, depth)
    out = pl.pallas_call(
        functools.partial(window_kernel, window, slot, len(waits)),
        out_shape=out_shape,
        in_specs=in_specs,
        out_specs=[pl.BlockSpec(memory_space=pl.ANY)] * len(out_shape),
        scratch_shapes=[
            pltpu.VMEM(table.shape, table.dtype),
            pltpu.VMEM(lhs_shape, jnp.bfloat16),
            pltpu.VMEM(lhs_shape, jnp.bfloat16),
            field,
            field,
            field,
            field,
            pltpu.VMEM((4, 3, window.width // 4, NLON), jnp.float32),
            pltpu.VMEM((2, 2 * SUB, NLON), jnp.float32),
            pltpu.SemaphoreType.DMA,
            pltpu.SemaphoreType.DMA((5,)),
        ],
        input_output_aliases=aliases,
        compiler_params=pltpu.CompilerParams(vmem_limit_bytes=VMEM_LIMIT),
        cost_estimate=pl.CostEstimate(
            flops=KERNEL_WORK * 3 * 2 * 2 * window.rows * depth * NLON,
            transcendentals=0,
            bytes_accessed=2 * table.size + 4 * window.rows * depth * 4 + 12 * window.width * NLON,
        ),
        name="window_tensor",
    )(*operands)
    return list(out[:4]), (None if window.last else out[4])


def by_levels(coeffs):
    spec = coeffs[0]
    levels, _, parts, waves_local, nlat = spec.shape
    members = lax.axis_size("mem")
    band = lax.axis_index("band").astype(jnp.int32)
    member = lax.axis_index("mem").astype(jnp.int32)
    core = member % 2
    half_of = [choose(core, [member // bits[step] % 2 for bits in ORDER]) for step in range(len(ORDER[0]))]
    half_beside = choose(1 - core, [member // bits[0] % 2 for bits in ORDER])
    place = jnp.stack([band, core, half_of[0], half_beside])
    spec = spec.reshape(levels, 2, parts * waves_local, nlat)
    count = nlat // LANE
    windows = [Window(k, count) for k in range(count)]
    table = jnp.asarray(wave_table(levels, waves_local))
    swap = [(0, 1), (1, 0)]

    (piece,) = pieces_of(spec, 1 - band, windows[:1], count)
    remotes = [lax.ppermute(piece, "band", swap)]
    outgoing = [None, *pieces_of(spec, 1 - band, windows[1:], count)]
    remotes.append(lax.ppermute(outgoing[1], "band", swap))
    local = pieces_of(spec, band, windows, count)

    cores = [(m, m ^ 1) for m in range(members)]
    ways = [[(m, m ^ ORDER[m % 2][step]) for m in range(members)] for step in range(len(ORDER[0]))]

    def halved(parts_of, step):
        half = parts_of[0].shape[2] // 2
        mine = half_of[step]

        def total(which):
            return sum(lax.dynamic_slice_in_dim(part, which * half, half, axis=2) for part in parts_of)

        leaves = total(1 - mine)
        return [total(mine), lax.ppermute(leaves, "mem", ways[step])], leaves

    def across(parts_of, step):
        kept, passed, kept_more, passed_more = parts_of
        leaves = passed + passed_more
        if len(sums) == 1:
            leaves = gated(leaves, [remotes[-1]])
        return [kept, kept_more, lax.ppermute(leaves, "mem", ways[step])], leaves

    def advanced(parts_of, step):
        return (across if step == 0 else halved)(parts_of, step)

    def doubled(part, step):
        beside = lax.ppermute(part, "mem", cores if step < 0 else ways[step])
        mine = core if step < 0 else half_of[step]
        return jnp.where(mine == 0, jnp.concatenate([part, beside], axis=1), jnp.concatenate([beside, part], axis=1))

    def gathered(part):
        for step in range(len(ways) - 1, -2, -1):
            part = doubled(part, step)
        return part

    carry = None
    sums, done = [], []
    for batch in BATCHES:
        made = None
        for slot, k in enumerate(batch):
            if k + 2 < count:
                piece = gated(outgoing[k + 2], [remotes[k]] if carry is None else [remotes[k], carry])
                remotes.append(lax.ppermute(piece, "band", swap))
            waits = []
            for j in AHEAD[k]:
                sums[j], left = advanced(sums[j], done[j])
                done[j] += 1
                waits.append(left)
            made, carry = window_tensor(
                windows[k], slot, len(batch), place, local[k], remotes[k], table, made, waits, carry
            )
        first = lax.ppermute(made[3], "mem", cores)
        second = lax.ppermute(made[2], "mem", cores)
        sums.append([made[0], made[1], second, first])
        done.append(0)
    results = []
    for j in range(len(BATCHES)):
        for step in range(done[j], len(ways)):
            sums[j], _ = advanced(sums[j], step)
        results.append(exponent_of(sum(sums[j]), members))

    other = lax.ppermute(results[0][:2], "band", swap)
    place_of = {}
    for m in range(members):
        for b in range(2):
            bits = ORDER[m % 2]
            piece = functools.reduce(lambda value, bit: 2 * value + m // bit % 2, bits, m % 2)
            place_of[piece, b] = m * 2 + b
    trades, half = [], members // 2
    for (piece, b), index in place_of.items():
        mate = (piece, b) if (piece < half) == (b == 0) else ((piece + half) % members, 1 - b)
        trades.append((index, place_of[mate]))
    both = lax.ppermute(results[0][2:], ("mem", "band"), trades)

    early = gathered(jnp.concatenate([other, both]))
    other, both = early[:-1], early[-1]
    middle = both.shape[0] // 2
    low, high = both[:middle], both[middle:]
    rest = jnp.zeros((nlat // 2 - middle, NLON), jnp.float32)
    down = jnp.stack([jnp.concatenate([rest, low]), jnp.concatenate([*other, high])])
    up = jnp.stack([jnp.concatenate([low, *other[::-1]]), jnp.concatenate([high, rest])])
    out = jnp.where(band == 0, down, up)

    own = gathered(results[1])
    for k, block in enumerate(own):
        width = block.shape[0]
        row = choose(band, (nlat // 2 - middle - (k + 1) * width, middle + k * width))
        out = lax.dynamic_update_slice(out, block[None], (band, row.astype(jnp.int32), jnp.int32(0)))
    return out


def per_device(coeffs):
    _, levels, _, _, _, nlat = coeffs.shape
    members = lax.axis_size("mem")
    rows = nlat // lax.axis_size("band")
    fits = coeffs.shape[4] == 5 * LANE // 2 and nlat % (2 * LANE) == LANE and rows > LANE
    if fits and levels == lax.axis_size("band") == 2 and members == 16:
        return by_levels(coeffs)
    return by_rows(coeffs)


def solution(mesh):
    placed = (P("mem", None, None, None, "band", None),)
    return jax.shard_map(
        per_device, mesh=mesh, in_specs=placed, out_specs=P(None, "band", None), check_vma=False
    )
```

```python
import functools
import math

import jax
import jax.numpy as jnp
import ml_dtypes
import numpy as np
from jax import lax
from jax.experimental import pallas as pl
from jax.experimental.pallas import tpu as pltpu
from jax.sharding import PartitionSpec as P

NLON = 1280
STEPS = 1
SUB = 8
LANE = 128
VMEM_LIMIT = 60 * 1024 * 1024
KERNEL_WORK = 8
ORDER = ((2, 4, 8), (4, 2, 8))
AHEAD = ((), (), (0,), (1, 0), (2, 1, 0))


def padded(cells, sides, width):
    for axis, dim in sides:
        count = lax.axis_size(axis)
        ends = count - 1
        head = lax.slice_in_dim(cells, 0, width, axis=dim)
        tail = lax.slice_in_dim(cells, cells.shape[dim] - width, cells.shape[dim], axis=dim)
        cells = jnp.concatenate(
            [
                lax.ppermute(tail, axis, [(i, (i + 1) % count) for i in range(ends)]),
                cells,
                lax.ppermute(head, axis, [((i + 1) % count, i) for i in range(ends)]),
            ],
            axis=dim,
        )
    return cells


def slope(extended, winds):
    center = extended[:, 1:-1]
    north = (extended[:, 2:] - extended[:, :-2]) * 0.5
    east = (jnp.roll(center, -1, 2) - jnp.roll(center, 1, 2)) * 0.5
    return -winds - (winds[0] * east + winds[1] * north)


def rimmed(field):
    return padded(field, (("band", 1),), 1)


def tensor(extended):
    center = extended[:, 1:-1]
    north = (extended[:, 2:] - extended[:, :-2]) * 0.5
    east = (jnp.roll(center, -1, 2) - jnp.roll(center, 1, 2)) * 0.5
    g_xx = 1.0 + east[0]
    g_xy = north[0]
    g_yx = east[1]
    g_yy = 1.0 + north[1]
    return jnp.stack(
        [g_xx * g_xx + g_yx * g_yx, g_xx * g_xy + g_yx * g_yy, g_xy * g_xy + g_yy * g_yy]
    )


def integrate(shift, flow, extend):
    first = slope(extend(shift), flow)
    second = slope(extend(0.5 * first), flow)
    third = slope(extend(0.5 * second), flow)
    fourth = slope(extend(third), flow)
    return (first + 2.0 * second + 2.0 * third + fourth) / 6.0


def exponent_of(summed, members):
    mean = summed / members
    first, cross, second = (mean[..., 0, :, :], mean[..., 1, :, :], mean[..., 2, :, :])
    half = (first + second) * 0.5
    differ = (first - second) * 0.5
    largest = half + jnp.sqrt(differ * differ + cross * cross)
    return jnp.log(largest + 1e-06) / (2.0 * STEPS)


def by_rows(coeffs):
    spec = coeffs[0]
    levels = spec.shape[0]
    nlat = spec.shape[4]
    waves = spec.shape[3] * lax.axis_size("band")
    members = lax.axis_size("mem")
    stacked = spec.reshape(levels * 2, 2, spec.shape[3], nlat)
    wave_index = lax.iota(jnp.int32, waves)
    column = lax.iota(jnp.int32, NLON)
    phase = wave_index[:, None] * column[None, :] % NLON
    angle = phase.astype(jnp.float32) * (2.0 * math.pi / NLON)
    weight = jnp.where(wave_index == 0, 1.0, 2.0).astype(jnp.float32)[:, None]
    table = jnp.stack([weight * jnp.cos(angle), -weight * jnp.sin(angle)], axis=0)
    winds = jnp.einsum(
        "crwh,rwn->chn",
        lax.all_to_all(stacked, "band", split_axis=3, concat_axis=2, tiled=True),
        table,
        precision=lax.Precision.HIGHEST,
        preferred_element_type=jnp.float32,
    )
    height = winds.shape[1]
    winds = winds.reshape(levels, 2, height, NLON)
    partials = []
    for level in range(levels):
        flow = winds[level]
        shift = integrate(jnp.zeros_like(flow), flow, rimmed)
        partials.append(tensor(rimmed(shift)))
    summed = lax.psum_scatter(jnp.stack(partials), "mem", scatter_dimension=3, tiled=True)
    return lax.all_gather(exponent_of(summed, members), "mem", axis=2, tiled=True)


def by_parity(waves_local):
    half = waves_local // 2
    whole = 2 * LANE - half
    runs = []
    for parity in range(2):
        runs += [(parity, half, 2), (waves_local + parity, whole, 2)]
    for parity in range(2):
        runs.append((waves_local + parity + 2 * whole, half - whole, 2))
    return runs


@functools.lru_cache(maxsize=None)
def wave_table(bands, waves_local):
    order = np.concatenate([start + step * np.arange(count) for start, count, step in by_parity(waves_local)])
    wave, part = order % waves_local, order // waves_local
    wave = wave[None, :] + waves_local * np.arange(bands)[:, None]
    part = np.broadcast_to(part, wave.shape)
    cut = [0, 2 * LANE, 4 * LANE, 4 * LANE + LANE // 2, 5 * LANE]
    result = []
    for parity in range(2):
        picks = [(band, slice(cut[parity], cut[parity + 1])) for band in range(bands)]
        picks += [(band, slice(cut[parity + 2], cut[parity + 3])) for band in range(bands)]
        waves = np.concatenate([wave[pick] for pick in picks])
        parts = np.concatenate([part[pick] for pick in picks])
        phase = (waves[:, None] * np.arange(NLON // 2)[None, :]) % NLON
        angle = phase.astype(np.float64) * (2.0 * np.pi / NLON)
        weight = np.where(waves == 0, 1.0, 2.0)[:, None]
        table = weight * np.where(parts[:, None] == 0, np.cos(angle), -np.sin(angle))
        high = table.astype(ml_dtypes.bfloat16)
        result += [high, (table - high.astype(np.float64)).astype(ml_dtypes.bfloat16)]
    return np.stack(result)


class Window:
    def __init__(self, index, count):
        self.first = index == 0
        self.last = index == count - 1
        self.index = index
        self.width = LANE
        self.extended = LANE + 2 * SUB
        self.main = LANE if self.first else LANE - SUB
        self.rim = 0 if self.last else SUB
        self.rows = self.main + self.rim
        up = SUB if self.first else 2 * SUB
        self.place = (self.extended - up - self.rows, up)
        self.side = "other" if 2 * (index + 1) <= count else "own" if 2 * index >= count else "both"


def choose(band, pair):
    return jnp.where(band == 0, pair[0], pair[1])


def multiple(value, of):
    return pl.multiple_of(value.astype(jnp.int32), of)


def pieces_kernel(windows, slots, count, level_ref, spec_ref, *refs):
    out_refs, (taken, turned, in_sems, out_sems) = refs[: len(windows)], refs[len(windows) :]
    level = level_ref[0]
    runs = by_parity(spec_ref.shape[2] // 2)

    def arrival(c, n):
        tile = choose(level, (count - 1 - slots[n], slots[n]))
        lanes = pl.ds(multiple(tile * LANE, LANE), LANE)
        return pltpu.make_async_copy(spec_ref.at[level, c, :, lanes], taken.at[c, n], in_sems.at[c, n])

    def departures(c, k):
        window, n = windows[k], slots.index(windows[k].index)
        rows = pl.ds(multiple(choose(level, (0, LANE - window.main)), SUB), window.main)
        at = pl.ds(multiple(choose(level, (window.rim, 0)), SUB), window.main)
        yield pltpu.make_async_copy(turned.at[c, n, rows], out_refs[k].at[c, at], out_sems.at[k, c, 0])
        if window.rim:
            rows = pl.ds(multiple(choose(level, (LANE - SUB, 0)), SUB), SUB)
            at = pl.ds(multiple(choose(level, (0, window.main)), SUB), SUB)
            yield pltpu.make_async_copy(turned.at[c, n + 1, rows], out_refs[k].at[c, at], out_sems.at[k, c, 1])

    for n in range(len(slots)):
        for c in range(2):
            arrival(c, n).start()
    for n in range(len(slots)):
        for c in range(2):
            arrival(c, n).wait()
            turned[c, n] = jnp.concatenate([taken[c, n, pl.ds(start, rows, step), :] for start, rows, step in runs]).T
        for k, window in enumerate(windows):
            if slots[n] == window.index + (1 if window.rim else 0):
                for c in range(2):
                    for copy in departures(c, k):
                        copy.start()
    for k in range(len(windows)):
        for c in range(2):
            for copy in departures(c, k):
                copy.wait()


def pieces_of(spec, level, windows, count):
    depth = spec.shape[2]
    slots = sorted({w.index for w in windows} | {w.index + 1 for w in windows if w.rim})
    return pl.pallas_call(
        functools.partial(pieces_kernel, windows, slots, count),
        in_specs=[pl.BlockSpec(memory_space=pltpu.SMEM), pl.BlockSpec(memory_space=pl.ANY)],
        out_specs=[pl.BlockSpec(memory_space=pl.ANY)] * len(windows),
        out_shape=[jax.ShapeDtypeStruct((2, w.rows, depth), jnp.float32) for w in windows],
        scratch_shapes=[
            pltpu.VMEM((2, len(slots), depth, LANE), jnp.float32),
            pltpu.VMEM((2, len(slots), LANE, depth), jnp.float32),
            pltpu.SemaphoreType.DMA((2, len(slots))),
            pltpu.SemaphoreType.DMA((len(windows), 2, 2)),
        ],
        compiler_params=pltpu.CompilerParams(vmem_limit_bytes=VMEM_LIMIT),
        cost_estimate=pl.CostEstimate(
            flops=0, transcendentals=0, bytes_accessed=4 * 2 * len(slots) * LANE * depth * 4
        ),
        name="pieces_of",
    )(level.reshape(1), spec)


def gate_kernel(*refs):
    pass


def gated(part, waits):
    return pl.pallas_call(
        gate_kernel,
        in_specs=[pl.BlockSpec(memory_space=pl.ANY)] * (1 + len(waits)),
        out_specs=pl.BlockSpec(memory_space=pl.ANY),
        out_shape=jax.ShapeDtypeStruct(part.shape, part.dtype),
        input_output_aliases={0: 0},
        cost_estimate=pl.CostEstimate(flops=0, transcendentals=0, bytes_accessed=1024),
        name="gated",
    )(part, *waits)


def east_of(x):
    return pltpu.roll(x, NLON - 1, axis=1) - pltpu.roll(x, 1, axis=1)


def north_of(before, here, after):
    row = lax.broadcasted_iota(jnp.int32, here.shape, 0)
    above = jnp.where(row == SUB - 1, pltpu.roll(after, SUB - 1, axis=0), pltpu.roll(here, SUB - 1, axis=0))
    below = jnp.where(row == 0, pltpu.roll(before, 1, axis=0), pltpu.roll(here, 1, axis=0))
    return above - below


def window_kernel(window, depth, waits, *refs):
    refs = list(refs)
    place_ref, local_ref, remote_ref, table_ref = refs[:4]
    refs = refs[4 + waits :]
    carry_ref = None if window.first else refs.pop(0)
    out_refs = [refs.pop(0) for _ in range(4)]
    carried_ref = None if window.last else refs.pop(0)
    table, lhs_high, lhs_low, wind, second, third, shift, results, carried, table_sem, out_sems = refs
    band, core, sides = place_ref[0], place_ref[1], (place_ref[2], place_ref[3])
    rows, extended = window.rows, window.extended

    def at(pair):
        return multiple(choose(band, pair), SUB)

    tables = pltpu.make_async_copy(table_ref, table, table_sem)
    tables.start()
    lane = lax.broadcasted_iota(jnp.int32, (rows, LANE), 1)
    even, odd = [], []
    for c in range(2):
        mine, theirs = local_ref[c], remote_ref[c]
        low, high = jnp.where(band == 0, mine, theirs), jnp.where(band == 0, theirs, mine)
        low_rest, high_rest = low[:, 4 * LANE :], high[:, 4 * LANE :]
        turn = functools.partial(pltpu.roll, shift=LANE // 2, axis=1)
        even_rest = jnp.where(lane < LANE // 2, low_rest, turn(high_rest))
        odd_rest = jnp.where(lane < LANE // 2, turn(low_rest), high_rest)
        even.append(jnp.concatenate([low[:, : 2 * LANE], high[:, : 2 * LANE], even_rest], axis=1))
        odd.append(jnp.concatenate([low[:, 2 * LANE : 4 * LANE], high[:, 2 * LANE : 4 * LANE], odd_rest], axis=1))
    for parity, parts in enumerate((even, odd)):
        lhs = jnp.concatenate(parts)
        lhs_high[parity] = lhs.astype(jnp.bfloat16)
        lhs_low[parity] = (lhs - lhs_high[parity].astype(jnp.float32)).astype(jnp.bfloat16)
    tables.wait()

    place = at(window.place)
    if window.first or window.last:
        for c in range(2):
            if window.first:
                wind[c, pl.ds(at((extended - SUB, 0)), SUB), :] = jnp.zeros((SUB, NLON), jnp.float32)
            if window.last:
                wind[c, pl.ds(at((0, extended - SUB)), SUB), :] = jnp.zeros((SUB, NLON), jnp.float32)
    if not window.first:
        for c in range(2):
            wind[c, pl.ds(at((extended - 2 * SUB, 0)), 2 * SUB), :] = carry_ref[c]

    dot = functools.partial(jnp.dot, preferred_element_type=jnp.float32)
    for start in range(0, NLON // 2, 2 * LANE):
        stop = min(start + 2 * LANE, NLON // 2)
        columns = slice(start, stop)
        sums = []
        for parity in range(2):
            total = dot(lhs_high[parity], table[2 * parity, :, columns])
            total += dot(lhs_low[parity], table[2 * parity, :, columns])
            total += dot(lhs_high[parity], table[2 * parity + 1, :, columns])
            sums.append(total)
        for c in range(2):
            even_sum, odd_sum = (total[c * rows : (c + 1) * rows] for total in sums)
            wind[c, pl.ds(place, rows), start:stop] = even_sum + odd_sum
            wind[c, pl.ds(place, rows), NLON // 2 + start : NLON // 2 + stop] = even_sum - odd_sum

    if not window.last:
        for c in range(2):
            carried[c] = wind[c, pl.ds(at((0, extended - 2 * SUB)), 2 * SUB), :]
        carry_on = pltpu.make_async_copy(carried, carried_ref, out_sems.at[4])
        carry_on.start()

    blocks = extended // SUB

    def rows_of(block):
        return pl.ds(pl.multiple_of(block * SUB, SUB), SUB)

    def derivatives(field, block):
        before, after = jnp.maximum(block - 1, 0), jnp.minimum(block + 1, blocks - 1)
        result = []
        for c in range(2):
            here = field[c, rows_of(block), :]
            result.append((east_of(here), north_of(field[c, rows_of(before), :], here, field[c, rows_of(after), :])))
        return result

    @pl.loop(0, blocks, unroll=6)
    def _(block):
        flow = [wind[c, rows_of(block), :] for c in range(2)]
        for c, (east, north) in enumerate(derivatives(wind, block)):
            second[c, rows_of(block), :] = 0.25 * (flow[0] * east + flow[1] * north) - flow[c]

    @pl.loop(0, blocks, unroll=6)
    def _(block):
        flow = [wind[c, rows_of(block), :] for c in range(2)]
        for c, (east, north) in enumerate(derivatives(second, block)):
            third[c, rows_of(block), :] = -flow[c] - 0.25 * (flow[0] * east + flow[1] * north)

    @pl.loop(0, blocks, unroll=6)
    def _(block):
        flow = [wind[c, rows_of(block), :] for c in range(2)]
        for c, (east, north) in enumerate(derivatives(third, block)):
            fourth = -flow[c] - 0.5 * (flow[0] * east + flow[1] * north)
            both = second[c, rows_of(block), :] + third[c, rows_of(block), :]
            shift[c, rows_of(block), :] = (2.0 * both + (fourth - flow[c])) * (1.0 / 6.0)

    quarter = window.width // 4 // SUB

    def entries(out, base):
        @pl.loop(0, quarter, unroll=4)
        def _(block):
            (e0, n0), (e1, n1) = derivatives(shift, base + block + 1)
            g_xx, g_xy, g_yx, g_yy = 1.0 + 0.5 * e0, 0.5 * n0, 0.5 * e1, 1.0 + 0.5 * n1
            out[0, rows_of(block), :] = g_xx * g_xx + g_yx * g_yx
            out[1, rows_of(block), :] = g_xx * g_xy + g_yx * g_yy
            out[2, rows_of(block), :] = g_xy * g_xy + g_yy * g_yy

    copies = []
    for n, (a, b) in reversed(list(enumerate(QUARTERS))):
        side = sides[a]
        entries(results.at[n], (2 * (core + a - 2 * core * a) + (side + b - 2 * side * b)) * quarter)
        copies.append(pltpu.make_async_copy(results.at[n], out_refs[n], out_sems.at[n]))
        copies[-1].start()
    for copy in copies:
        copy.wait()
    if not window.last:
        carry_on.wait()


QUARTERS = ((0, 0), (0, 1), (1, 0), (1, 1))


def window_tensor(window, place, local, remote, table, waits, carry):
    depth = local.shape[2]
    vmem = pl.BlockSpec(memory_space=pltpu.VMEM)
    in_specs = [
        pl.BlockSpec(memory_space=pltpu.SMEM),
        vmem,
        vmem,
        pl.BlockSpec(memory_space=pl.ANY),
    ]
    in_specs += [pl.BlockSpec(memory_space=pl.ANY)] * len(waits)
    operands = [place, local, remote, table, *waits]
    if not window.first:
        in_specs.append(vmem)
        operands.append(carry)
    out_shape = [jax.ShapeDtypeStruct((3, window.width // 4, NLON), jnp.float32)] * 4
    if not window.last:
        out_shape.append(jax.ShapeDtypeStruct((2, 2 * SUB, NLON), jnp.float32))
    field = pltpu.VMEM((2, window.extended, NLON), jnp.float32)
    lhs_shape = (2, 2 * window.rows, depth)
    out = pl.pallas_call(
        functools.partial(window_kernel, window, depth, len(waits)),
        out_shape=out_shape,
        in_specs=in_specs,
        out_specs=[pl.BlockSpec(memory_space=pl.ANY)] * len(out_shape),
        scratch_shapes=[
            pltpu.VMEM(table.shape, table.dtype),
            pltpu.VMEM(lhs_shape, jnp.bfloat16),
            pltpu.VMEM(lhs_shape, jnp.bfloat16),
            field,
            field,
            field,
            field,
            pltpu.VMEM((4, 3, window.width // 4, NLON), jnp.float32),
            pltpu.VMEM((2, 2 * SUB, NLON), jnp.float32),
            pltpu.SemaphoreType.DMA,
            pltpu.SemaphoreType.DMA((5,)),
        ],
        compiler_params=pltpu.CompilerParams(vmem_limit_bytes=VMEM_LIMIT),
        cost_estimate=pl.CostEstimate(
            flops=KERNEL_WORK * 3 * 2 * 2 * window.rows * depth * NLON,
            transcendentals=0,
            bytes_accessed=2 * table.size + 4 * window.rows * depth * 4 + 12 * window.width * NLON,
        ),
        name="window_tensor",
    )(*operands)
    return out[:4], (None if window.last else out[4])


def by_levels(coeffs):
    spec = coeffs[0]
    levels, _, parts, waves_local, nlat = spec.shape
    members = lax.axis_size("mem")
    band = lax.axis_index("band").astype(jnp.int32)
    member = lax.axis_index("mem").astype(jnp.int32)
    core = member % 2
    half_of = [choose(core, [member // bits[step] % 2 for bits in ORDER]) for step in range(len(ORDER[0]))]
    half_beside = choose(1 - core, [member // bits[0] % 2 for bits in ORDER])
    place = jnp.stack([band, core, half_of[0], half_beside])
    spec = spec.reshape(levels, 2, parts * waves_local, nlat)
    count = nlat // LANE
    windows = [Window(k, count) for k in range(count)]
    table = jnp.asarray(wave_table(levels, waves_local))
    swap = [(0, 1), (1, 0)]

    (piece,) = pieces_of(spec, 1 - band, windows[:1], count)
    remotes = [lax.ppermute(piece, "band", swap)]
    for k, piece in enumerate(pieces_of(spec, 1 - band, windows[1:], count), 1):
        if k > 1:
            piece = gated(piece, [remotes[k - 2]])
        remotes.append(lax.ppermute(piece, "band", swap))
    local = pieces_of(spec, band, windows, count)

    cores = [(m, m ^ 1) for m in range(members)]
    ways = [[(m, m ^ ORDER[m % 2][step]) for m in range(members)] for step in range(len(ORDER[0]))]

    def halved(parts_of, step):
        half = parts_of[0].shape[1] // 2
        mine = half_of[step]

        def total(which):
            return sum(lax.dynamic_slice_in_dim(part, which * half, half, axis=1) for part in parts_of)

        leaves = total(1 - mine)
        return [total(mine), lax.ppermute(leaves, "mem", ways[step])], leaves

    def across(parts_of, step):
        kept, passed, kept_more, passed_more = parts_of
        leaves = passed + passed_more
        return [kept, kept_more, lax.ppermute(leaves, "mem", ways[step])], leaves

    def advanced(parts_of, step):
        return (across if step == 0 else halved)(parts_of, step)

    def doubled(part, step):
        beside = lax.ppermute(part, "mem", cores if step < 0 else ways[step])
        mine = core if step < 0 else half_of[step]
        return jnp.where(mine == 0, jnp.concatenate([part, beside], axis=1), jnp.concatenate([beside, part], axis=1))

    def gathered(part):
        for step in range(len(ways) - 1, -2, -1):
            part = doubled(part, step)
        return part

    carry = None
    sums, done = [], []
    for k, window in enumerate(windows):
        waits = []
        for j in AHEAD[k]:
            sums[j], left = advanced(sums[j], done[j])
            done[j] += 1
            waits.append(left)
        quarters, carry = window_tensor(window, place, local[k], remotes[k], table, waits, carry)
        first = lax.ppermute(quarters[3], "mem", cores)
        second = lax.ppermute(quarters[2], "mem", cores)
        sums.append([quarters[0], quarters[1], second, first])
        done.append(0)
    pieces = {"own": [], "both": [], "other": []}
    for k, window in enumerate(windows):
        for step in range(done[k], len(ways)):
            sums[k], _ = advanced(sums[k], step)
        pieces[window.side].append(exponent_of(sum(sums[k]), members))

    other = lax.ppermute(jnp.stack(pieces["other"]), "band", swap)
    place_of = {}
    for m in range(members):
        for b in range(2):
            bits = ORDER[m % 2]
            piece = functools.reduce(lambda value, bit: 2 * value + m // bit % 2, bits, m % 2)
            place_of[piece, b] = m * 2 + b
    trades, half = [], members // 2
    for (piece, b), index in place_of.items():
        mate = (piece, b) if (piece < half) == (b == 0) else ((piece + half) % members, 1 - b)
        trades.append((index, place_of[mate]))
    both = lax.ppermute(pieces["both"][0], ("mem", "band"), trades)

    early = gathered(jnp.concatenate([other, both[None]]))
    other, both = early[:-1], early[-1]
    middle = both.shape[0] // 2
    low, high = both[:middle], both[middle:]
    rest = jnp.zeros((nlat // 2 - middle, NLON), jnp.float32)
    down = jnp.stack([jnp.concatenate([rest, low]), jnp.concatenate([*other, high])])
    up = jnp.stack([jnp.concatenate([low, *other[::-1]]), jnp.concatenate([high, rest])])
    out = jnp.where(band == 0, down, up)

    own = gathered(jnp.stack(pieces["own"]))
    for k, block in enumerate(own):
        width = block.shape[0]
        row = choose(band, (nlat // 2 - middle - (k + 1) * width, middle + k * width))
        out = lax.dynamic_update_slice(out, block[None], (band, row.astype(jnp.int32), jnp.int32(0)))
    return out


def per_device(coeffs):
    _, levels, _, _, _, nlat = coeffs.shape
    members = lax.axis_size("mem")
    rows = nlat // lax.axis_size("band")
    fits = coeffs.shape[4] == 5 * LANE // 2 and nlat % (2 * LANE) == LANE and rows > LANE
    if fits and levels == lax.axis_size("band") == 2 and members == 16:
        return by_levels(coeffs)
    return by_rows(coeffs)


def solution(mesh):
    placed = (P("mem", None, None, None, "band", None),)
    return jax.shard_map(
        per_device, mesh=mesh, in_specs=placed, out_specs=P(None, "band", None), check_vma=False
    )
```

```python
import functools
import math

import jax
import jax.numpy as jnp
import ml_dtypes
import numpy as np
from jax import lax
from jax.experimental import pallas as pl
from jax.experimental.pallas import tpu as pltpu
from jax.sharding import PartitionSpec as P

NLON = 1280
STEPS = 1
SUB = 8
LANE = 128
VMEM_LIMIT = 60 * 1024 * 1024
KERNEL_WORK = 8
ORDER = ((2, 4, 8), (4, 2, 8))
BATCHES = ((0, 1, 2), (3, 4))
AHEAD = ((), (), (), (), (0,))


def padded(cells, sides, width):
    for axis, dim in sides:
        count = lax.axis_size(axis)
        ends = count - 1
        head = lax.slice_in_dim(cells, 0, width, axis=dim)
        tail = lax.slice_in_dim(cells, cells.shape[dim] - width, cells.shape[dim], axis=dim)
        cells = jnp.concatenate(
            [
                lax.ppermute(tail, axis, [(i, (i + 1) % count) for i in range(ends)]),
                cells,
                lax.ppermute(head, axis, [((i + 1) % count, i) for i in range(ends)]),
            ],
            axis=dim,
        )
    return cells


def slope(extended, winds):
    center = extended[:, 1:-1]
    north = (extended[:, 2:] - extended[:, :-2]) * 0.5
    east = (jnp.roll(center, -1, 2) - jnp.roll(center, 1, 2)) * 0.5
    return -winds - (winds[0] * east + winds[1] * north)


def rimmed(field):
    return padded(field, (("band", 1),), 1)


def tensor(extended):
    center = extended[:, 1:-1]
    north = (extended[:, 2:] - extended[:, :-2]) * 0.5
    east = (jnp.roll(center, -1, 2) - jnp.roll(center, 1, 2)) * 0.5
    g_xx = 1.0 + east[0]
    g_xy = north[0]
    g_yx = east[1]
    g_yy = 1.0 + north[1]
    return jnp.stack(
        [g_xx * g_xx + g_yx * g_yx, g_xx * g_xy + g_yx * g_yy, g_xy * g_xy + g_yy * g_yy]
    )


def integrate(shift, flow, extend):
    first = slope(extend(shift), flow)
    second = slope(extend(0.5 * first), flow)
    third = slope(extend(0.5 * second), flow)
    fourth = slope(extend(third), flow)
    return (first + 2.0 * second + 2.0 * third + fourth) / 6.0


def exponent_of(summed, members):
    mean = summed / members
    first, cross, second = (mean[..., 0, :, :], mean[..., 1, :, :], mean[..., 2, :, :])
    half = (first + second) * 0.5
    differ = (first - second) * 0.5
    largest = half + jnp.sqrt(differ * differ + cross * cross)
    return jnp.log(largest + 1e-06) / (2.0 * STEPS)


def by_rows(coeffs):
    spec = coeffs[0]
    levels = spec.shape[0]
    nlat = spec.shape[4]
    waves = spec.shape[3] * lax.axis_size("band")
    members = lax.axis_size("mem")
    stacked = spec.reshape(levels * 2, 2, spec.shape[3], nlat)
    wave_index = lax.iota(jnp.int32, waves)
    column = lax.iota(jnp.int32, NLON)
    phase = wave_index[:, None] * column[None, :] % NLON
    angle = phase.astype(jnp.float32) * (2.0 * math.pi / NLON)
    weight = jnp.where(wave_index == 0, 1.0, 2.0).astype(jnp.float32)[:, None]
    table = jnp.stack([weight * jnp.cos(angle), -weight * jnp.sin(angle)], axis=0)
    winds = jnp.einsum(
        "crwh,rwn->chn",
        lax.all_to_all(stacked, "band", split_axis=3, concat_axis=2, tiled=True),
        table,
        precision=lax.Precision.HIGHEST,
        preferred_element_type=jnp.float32,
    )
    height = winds.shape[1]
    winds = winds.reshape(levels, 2, height, NLON)
    partials = []
    for level in range(levels):
        flow = winds[level]
        shift = integrate(jnp.zeros_like(flow), flow, rimmed)
        partials.append(tensor(rimmed(shift)))
    summed = lax.psum_scatter(jnp.stack(partials), "mem", scatter_dimension=3, tiled=True)
    return lax.all_gather(exponent_of(summed, members), "mem", axis=2, tiled=True)


def by_parity(waves_local):
    half = waves_local // 2
    whole = 2 * LANE - half
    runs = []
    for parity in range(2):
        runs += [(parity, half, 2), (waves_local + parity, whole, 2)]
    for parity in range(2):
        runs.append((waves_local + parity + 2 * whole, half - whole, 2))
    return runs


@functools.lru_cache(maxsize=None)
def wave_table(bands, waves_local):
    order = np.concatenate([start + step * np.arange(count) for start, count, step in by_parity(waves_local)])
    wave, part = order % waves_local, order // waves_local
    wave = wave[None, :] + waves_local * np.arange(bands)[:, None]
    part = np.broadcast_to(part, wave.shape)
    cut = [0, 2 * LANE, 4 * LANE, 4 * LANE + LANE // 2, 5 * LANE]
    result = []
    for parity in range(2):
        picks = [(band, slice(cut[parity], cut[parity + 1])) for band in range(bands)]
        picks += [(band, slice(cut[parity + 2], cut[parity + 3])) for band in range(bands)]
        waves = np.concatenate([wave[pick] for pick in picks])
        parts = np.concatenate([part[pick] for pick in picks])
        phase = (waves[:, None] * np.arange(NLON // 2)[None, :]) % NLON
        angle = phase.astype(np.float64) * (2.0 * np.pi / NLON)
        weight = np.where(waves == 0, 1.0, 2.0)[:, None]
        table = weight * np.where(parts[:, None] == 0, np.cos(angle), -np.sin(angle))
        high = table.astype(ml_dtypes.bfloat16)
        result += [high, (table - high.astype(np.float64)).astype(ml_dtypes.bfloat16)]
    return np.stack(result)


class Window:
    def __init__(self, index, count):
        self.first = index == 0
        self.last = index == count - 1
        self.index = index
        self.width = LANE
        self.extended = LANE + 2 * SUB
        self.main = LANE if self.first else LANE - SUB
        self.rim = 0 if self.last else SUB
        self.rows = self.main + self.rim
        up = SUB if self.first else 2 * SUB
        self.place = (self.extended - up - self.rows, up)
        self.side = "other" if 2 * (index + 1) <= count else "own" if 2 * index >= count else "both"


def choose(band, pair):
    return jnp.where(band == 0, pair[0], pair[1])


def multiple(value, of):
    return pl.multiple_of(value.astype(jnp.int32), of)


def pieces_kernel(windows, slots, count, level_ref, spec_ref, *refs):
    out_refs, (taken, turned, in_sems, out_sems) = refs[: len(windows)], refs[len(windows) :]
    level = level_ref[0]
    runs = by_parity(spec_ref.shape[2] // 2)

    def arrival(c, n):
        tile = choose(level, (count - 1 - slots[n], slots[n]))
        lanes = pl.ds(multiple(tile * LANE, LANE), LANE)
        return pltpu.make_async_copy(spec_ref.at[level, c, :, lanes], taken.at[c, n], in_sems.at[c, n])

    def departures(c, k):
        window, n = windows[k], slots.index(windows[k].index)
        rows = pl.ds(multiple(choose(level, (0, LANE - window.main)), SUB), window.main)
        at = pl.ds(multiple(choose(level, (window.rim, 0)), SUB), window.main)
        yield pltpu.make_async_copy(turned.at[c, n, rows], out_refs[k].at[c, at], out_sems.at[k, c, 0])
        if window.rim:
            rows = pl.ds(multiple(choose(level, (LANE - SUB, 0)), SUB), SUB)
            at = pl.ds(multiple(choose(level, (0, window.main)), SUB), SUB)
            yield pltpu.make_async_copy(turned.at[c, n + 1, rows], out_refs[k].at[c, at], out_sems.at[k, c, 1])

    for n in range(len(slots)):
        for c in range(2):
            arrival(c, n).start()
    for n in range(len(slots)):
        for c in range(2):
            arrival(c, n).wait()
            turned[c, n] = jnp.concatenate([taken[c, n, pl.ds(start, rows, step), :] for start, rows, step in runs]).T
        for k, window in enumerate(windows):
            if slots[n] == window.index + (1 if window.rim else 0):
                for c in range(2):
                    for copy in departures(c, k):
                        copy.start()
    for k in range(len(windows)):
        for c in range(2):
            for copy in departures(c, k):
                copy.wait()


def pieces_of(spec, level, windows, count):
    depth = spec.shape[2]
    slots = sorted({w.index for w in windows} | {w.index + 1 for w in windows if w.rim})
    return pl.pallas_call(
        functools.partial(pieces_kernel, windows, slots, count),
        in_specs=[pl.BlockSpec(memory_space=pltpu.SMEM), pl.BlockSpec(memory_space=pl.ANY)],
        out_specs=[pl.BlockSpec(memory_space=pl.ANY)] * len(windows),
        out_shape=[jax.ShapeDtypeStruct((2, w.rows, depth), jnp.float32) for w in windows],
        scratch_shapes=[
            pltpu.VMEM((2, len(slots), depth, LANE), jnp.float32),
            pltpu.VMEM((2, len(slots), LANE, depth), jnp.float32),
            pltpu.SemaphoreType.DMA((2, len(slots))),
            pltpu.SemaphoreType.DMA((len(windows), 2, 2)),
        ],
        compiler_params=pltpu.CompilerParams(vmem_limit_bytes=VMEM_LIMIT),
        cost_estimate=pl.CostEstimate(
            flops=0, transcendentals=0, bytes_accessed=4 * 2 * len(slots) * LANE * depth * 4
        ),
        name="pieces_of",
    )(level.reshape(1), spec)


def gate_kernel(*refs):
    pass


def gated(part, waits):
    return pl.pallas_call(
        gate_kernel,
        in_specs=[pl.BlockSpec(memory_space=pl.ANY)] * (1 + len(waits)),
        out_specs=pl.BlockSpec(memory_space=pl.ANY),
        out_shape=jax.ShapeDtypeStruct(part.shape, part.dtype),
        input_output_aliases={0: 0},
        cost_estimate=pl.CostEstimate(flops=0, transcendentals=0, bytes_accessed=1024),
        name="gated",
    )(part, *waits)


def east_of(x):
    return pltpu.roll(x, NLON - 1, axis=1) - pltpu.roll(x, 1, axis=1)


def north_of(before, here, after):
    row = lax.broadcasted_iota(jnp.int32, here.shape, 0)
    above = jnp.where(row == SUB - 1, pltpu.roll(after, SUB - 1, axis=0), pltpu.roll(here, SUB - 1, axis=0))
    below = jnp.where(row == 0, pltpu.roll(before, 1, axis=0), pltpu.roll(here, 1, axis=0))
    return above - below


def window_kernel(window, slot, waits, *refs):
    refs = list(refs)
    place_ref, local_ref, remote_ref, table_ref = refs[:4]
    refs = refs[4 + waits + (len(QUARTERS) if slot else 0) :]
    carry_ref = None if window.first else refs.pop(0)
    out_refs = [refs.pop(0) for _ in range(4)]
    carried_ref = None if window.last else refs.pop(0)
    table, lhs_high, lhs_low, wind, second, third, shift, results, carried, table_sem, out_sems = refs
    band, core, sides = place_ref[0], place_ref[1], (place_ref[2], place_ref[3])
    rows, extended = window.rows, window.extended

    def at(pair):
        return multiple(choose(band, pair), SUB)

    tables = pltpu.make_async_copy(table_ref, table, table_sem)
    tables.start()
    lane = lax.broadcasted_iota(jnp.int32, (rows, LANE), 1)
    even, odd = [], []
    for c in range(2):
        mine, theirs = local_ref[c], remote_ref[c]
        low, high = jnp.where(band == 0, mine, theirs), jnp.where(band == 0, theirs, mine)
        low_rest, high_rest = low[:, 4 * LANE :], high[:, 4 * LANE :]
        turn = functools.partial(pltpu.roll, shift=LANE // 2, axis=1)
        even_rest = jnp.where(lane < LANE // 2, low_rest, turn(high_rest))
        odd_rest = jnp.where(lane < LANE // 2, turn(low_rest), high_rest)
        even.append(jnp.concatenate([low[:, : 2 * LANE], high[:, : 2 * LANE], even_rest], axis=1))
        odd.append(jnp.concatenate([low[:, 2 * LANE : 4 * LANE], high[:, 2 * LANE : 4 * LANE], odd_rest], axis=1))
    for parity, parts in enumerate((even, odd)):
        lhs = jnp.concatenate(parts)
        lhs_high[parity] = lhs.astype(jnp.bfloat16)
        lhs_low[parity] = (lhs - lhs_high[parity].astype(jnp.float32)).astype(jnp.bfloat16)
    tables.wait()

    place = at(window.place)
    if window.first or window.last:
        for c in range(2):
            if window.first:
                wind[c, pl.ds(at((extended - SUB, 0)), SUB), :] = jnp.zeros((SUB, NLON), jnp.float32)
            if window.last:
                wind[c, pl.ds(at((0, extended - SUB)), SUB), :] = jnp.zeros((SUB, NLON), jnp.float32)
    if not window.first:
        for c in range(2):
            wind[c, pl.ds(at((extended - 2 * SUB, 0)), 2 * SUB), :] = carry_ref[c]

    dot = functools.partial(jnp.dot, preferred_element_type=jnp.float32)
    for start in range(0, NLON // 2, 2 * LANE):
        stop = min(start + 2 * LANE, NLON // 2)
        columns = slice(start, stop)
        sums = []
        for parity in range(2):
            total = dot(lhs_high[parity], table[2 * parity, :, columns])
            total += dot(lhs_low[parity], table[2 * parity, :, columns])
            total += dot(lhs_high[parity], table[2 * parity + 1, :, columns])
            sums.append(total)
        for c in range(2):
            even_sum, odd_sum = (total[c * rows : (c + 1) * rows] for total in sums)
            wind[c, pl.ds(place, rows), start:stop] = even_sum + odd_sum
            wind[c, pl.ds(place, rows), NLON // 2 + start : NLON // 2 + stop] = even_sum - odd_sum

    if not window.last:
        for c in range(2):
            carried[c] = wind[c, pl.ds(at((0, extended - 2 * SUB)), 2 * SUB), :]
        carry_on = pltpu.make_async_copy(carried, carried_ref, out_sems.at[4])
        carry_on.start()

    blocks = extended // SUB

    def rows_of(block):
        return pl.ds(pl.multiple_of(block * SUB, SUB), SUB)

    def derivatives(field, block):
        before, after = jnp.maximum(block - 1, 0), jnp.minimum(block + 1, blocks - 1)
        result = []
        for c in range(2):
            here = field[c, rows_of(block), :]
            result.append((east_of(here), north_of(field[c, rows_of(before), :], here, field[c, rows_of(after), :])))
        return result

    @pl.loop(0, blocks, unroll=6)
    def _(block):
        flow = [wind[c, rows_of(block), :] for c in range(2)]
        for c, (east, north) in enumerate(derivatives(wind, block)):
            second[c, rows_of(block), :] = 0.25 * (flow[0] * east + flow[1] * north) - flow[c]

    @pl.loop(0, blocks, unroll=6)
    def _(block):
        flow = [wind[c, rows_of(block), :] for c in range(2)]
        for c, (east, north) in enumerate(derivatives(second, block)):
            third[c, rows_of(block), :] = -flow[c] - 0.25 * (flow[0] * east + flow[1] * north)

    @pl.loop(0, blocks, unroll=6)
    def _(block):
        flow = [wind[c, rows_of(block), :] for c in range(2)]
        for c, (east, north) in enumerate(derivatives(third, block)):
            fourth = -flow[c] - 0.5 * (flow[0] * east + flow[1] * north)
            both = second[c, rows_of(block), :] + third[c, rows_of(block), :]
            shift[c, rows_of(block), :] = (2.0 * both + (fourth - flow[c])) * (1.0 / 6.0)

    quarter = window.width // 4 // SUB

    def entries(out, base):
        @pl.loop(0, quarter, unroll=4)
        def _(block):
            (e0, n0), (e1, n1) = derivatives(shift, base + block + 1)
            g_xx, g_xy, g_yx, g_yy = 1.0 + 0.5 * e0, 0.5 * n0, 0.5 * e1, 1.0 + 0.5 * n1
            out[0, rows_of(block), :] = g_xx * g_xx + g_yx * g_yx
            out[1, rows_of(block), :] = g_xx * g_xy + g_yx * g_yy
            out[2, rows_of(block), :] = g_xy * g_xy + g_yy * g_yy

    copies = []
    for n, (a, b) in reversed(list(enumerate(QUARTERS))):
        side = sides[a]
        entries(results.at[n], (2 * (core + a - 2 * core * a) + (side + b - 2 * side * b)) * quarter)
        copies.append(pltpu.make_async_copy(results.at[n], out_refs[n].at[slot], out_sems.at[n]))
        copies[-1].start()
    for copy in copies:
        copy.wait()
    if not window.last:
        carry_on.wait()


QUARTERS = ((0, 0), (0, 1), (1, 0), (1, 1))


def window_tensor(window, slot, slots, place, local, remote, table, made, waits, carry):
    depth = local.shape[2]
    vmem = pl.BlockSpec(memory_space=pltpu.VMEM)
    in_specs = [
        pl.BlockSpec(memory_space=pltpu.SMEM),
        vmem,
        vmem,
        pl.BlockSpec(memory_space=pl.ANY),
    ]
    in_specs += [pl.BlockSpec(memory_space=pl.ANY)] * len(waits)
    operands = [place, local, remote, table, *waits]
    aliases = {}
    if slot:
        aliases = {len(operands) + n: n for n in range(len(QUARTERS))}
        in_specs += [pl.BlockSpec(memory_space=pl.ANY)] * len(QUARTERS)
        operands += made
    if not window.first:
        in_specs.append(vmem)
        operands.append(carry)
    out_shape = [jax.ShapeDtypeStruct((slots, 3, window.width // 4, NLON), jnp.float32)] * len(QUARTERS)
    if not window.last:
        out_shape.append(jax.ShapeDtypeStruct((2, 2 * SUB, NLON), jnp.float32))
    field = pltpu.VMEM((2, window.extended, NLON), jnp.float32)
    lhs_shape = (2, 2 * window.rows, depth)
    out = pl.pallas_call(
        functools.partial(window_kernel, window, slot, len(waits)),
        out_shape=out_shape,
        in_specs=in_specs,
        out_specs=[pl.BlockSpec(memory_space=pl.ANY)] * len(out_shape),
        scratch_shapes=[
            pltpu.VMEM(table.shape, table.dtype),
            pltpu.VMEM(lhs_shape, jnp.bfloat16),
            pltpu.VMEM(lhs_shape, jnp.bfloat16),
            field,
            field,
            field,
            field,
            pltpu.VMEM((4, 3, window.width // 4, NLON), jnp.float32),
            pltpu.VMEM((2, 2 * SUB, NLON), jnp.float32),
            pltpu.SemaphoreType.DMA,
            pltpu.SemaphoreType.DMA((5,)),
        ],
        input_output_aliases=aliases,
        compiler_params=pltpu.CompilerParams(vmem_limit_bytes=VMEM_LIMIT),
        cost_estimate=pl.CostEstimate(
            flops=KERNEL_WORK * 3 * 2 * 2 * window.rows * depth * NLON,
            transcendentals=0,
            bytes_accessed=2 * table.size + 4 * window.rows * depth * 4 + 12 * window.width * NLON,
        ),
        name="window_tensor",
    )(*operands)
    return list(out[:4]), (None if window.last else out[4])


def by_levels(coeffs):
    spec = coeffs[0]
    levels, _, parts, waves_local, nlat = spec.shape
    members = lax.axis_size("mem")
    band = lax.axis_index("band").astype(jnp.int32)
    member = lax.axis_index("mem").astype(jnp.int32)
    core = member % 2
    half_of = [choose(core, [member // bits[step] % 2 for bits in ORDER]) for step in range(len(ORDER[0]))]
    half_beside = choose(1 - core, [member // bits[0] % 2 for bits in ORDER])
    place = jnp.stack([band, core, half_of[0], half_beside])
    spec = spec.reshape(levels, 2, parts * waves_local, nlat)
    count = nlat // LANE
    windows = [Window(k, count) for k in range(count)]
    table = jnp.asarray(wave_table(levels, waves_local))
    swap = [(0, 1), (1, 0)]

    (piece,) = pieces_of(spec, 1 - band, windows[:1], count)
    remotes = [lax.ppermute(piece, "band", swap)]
    outgoing = [None, *pieces_of(spec, 1 - band, windows[1:], count)]
    remotes.append(lax.ppermute(outgoing[1], "band", swap))
    local = pieces_of(spec, band, windows, count)

    cores = [(m, m ^ 1) for m in range(members)]
    ways = [[(m, m ^ ORDER[m % 2][step]) for m in range(members)] for step in range(len(ORDER[0]))]

    def halved(parts_of, step):
        half = parts_of[0].shape[2] // 2
        mine = half_of[step]

        def total(which):
            return sum(lax.dynamic_slice_in_dim(part, which * half, half, axis=2) for part in parts_of)

        leaves = total(1 - mine)
        return [total(mine), lax.ppermute(leaves, "mem", ways[step])], leaves

    def across(parts_of, step):
        kept, passed, kept_more, passed_more = parts_of
        leaves = passed + passed_more
        if len(sums) == 1:
            leaves = gated(leaves, [remotes[-1]])
        return [kept, kept_more, lax.ppermute(leaves, "mem", ways[step])], leaves

    def advanced(parts_of, step):
        return (across if step == 0 else halved)(parts_of, step)

    def doubled(part, step):
        beside = lax.ppermute(part, "mem", cores if step < 0 else ways[step])
        mine = core if step < 0 else half_of[step]
        return jnp.where(mine == 0, jnp.concatenate([part, beside], axis=1), jnp.concatenate([beside, part], axis=1))

    def gathered(part):
        for step in range(len(ways) - 1, -2, -1):
            part = doubled(part, step)
        return part

    carry = None
    sums, done = [], []
    for batch in BATCHES:
        made = None
        for slot, k in enumerate(batch):
            if k + 2 < count:
                piece = gated(outgoing[k + 2], [remotes[k]] if carry is None else [remotes[k], carry])
                remotes.append(lax.ppermute(piece, "band", swap))
            waits = []
            for j in AHEAD[k]:
                sums[j], left = advanced(sums[j], done[j])
                done[j] += 1
                waits.append(left)
            made, carry = window_tensor(
                windows[k], slot, len(batch), place, local[k], remotes[k], table, made, waits, carry
            )
        first = lax.ppermute(made[3], "mem", cores)
        second = lax.ppermute(made[2], "mem", cores)
        sums.append([made[0], made[1], second, first])
        done.append(0)
    results = []
    for j in range(len(BATCHES)):
        for step in range(done[j], len(ways)):
            sums[j], _ = advanced(sums[j], step)
        results.append(exponent_of(sum(sums[j]), members))

    other = lax.ppermute(results[0][:2], "band", swap)
    place_of = {}
    for m in range(members):
        for b in range(2):
            bits = ORDER[m % 2]
            piece = functools.reduce(lambda value, bit: 2 * value + m // bit % 2, bits, m % 2)
            place_of[piece, b] = m * 2 + b
    trades, half = [], members // 2
    for (piece, b), index in place_of.items():
        mate = (piece, b) if (piece < half) == (b == 0) else ((piece + half) % members, 1 - b)
        trades.append((index, place_of[mate]))
    both = lax.ppermute(results[0][2:], ("mem", "band"), trades)

    early = gathered(jnp.concatenate([other, both]))
    other, both = early[:-1], early[-1]
    middle = both.shape[0] // 2
    low, high = both[:middle], both[middle:]
    rest = jnp.zeros((nlat // 2 - middle, NLON), jnp.float32)
    down = jnp.stack([jnp.concatenate([rest, low]), jnp.concatenate([*other, high])])
    up = jnp.stack([jnp.concatenate([low, *other[::-1]]), jnp.concatenate([high, rest])])
    out = jnp.where(band == 0, down, up)

    own = gathered(results[1])
    for k, block in enumerate(own):
        width = block.shape[0]
        row = choose(band, (nlat // 2 - middle - (k + 1) * width, middle + k * width))
        out = lax.dynamic_update_slice(out, block[None], (band, row.astype(jnp.int32), jnp.int32(0)))
    return out


def per_device(coeffs):
    _, levels, _, _, _, nlat = coeffs.shape
    members = lax.axis_size("mem")
    rows = nlat // lax.axis_size("band")
    fits = coeffs.shape[4] == 5 * LANE // 2 and nlat % (2 * LANE) == LANE and rows > LANE
    if fits and levels == lax.axis_size("band") == 2 and members == 16:
        return by_levels(coeffs)
    return by_rows(coeffs)


def solution(mesh):
    placed = (P("mem", None, None, None, "band", None),)
    return jax.shard_map(
        per_device, mesh=mesh, in_specs=placed, out_specs=P(None, "band", None), check_vma=False
    )
```

```python
import functools
import math

import jax
import jax.numpy as jnp
import ml_dtypes
import numpy as np
from jax import lax
from jax.experimental import pallas as pl
from jax.experimental.pallas import tpu as pltpu
from jax.sharding import PartitionSpec as P

NLON = 1280
STEPS = 1
SUB = 8
LANE = 128
VMEM_LIMIT = 60 * 1024 * 1024
KERNEL_WORK = 8
ORDER = ((2, 4, 8), (4, 2, 8))
AHEAD = ((), (), (0,), (1, 0), (3, 2, 1))


def padded(cells, sides, width):
    for axis, dim in sides:
        count = lax.axis_size(axis)
        ends = count - 1
        head = lax.slice_in_dim(cells, 0, width, axis=dim)
        tail = lax.slice_in_dim(cells, cells.shape[dim] - width, cells.shape[dim], axis=dim)
        cells = jnp.concatenate(
            [
                lax.ppermute(tail, axis, [(i, (i + 1) % count) for i in range(ends)]),
                cells,
                lax.ppermute(head, axis, [((i + 1) % count, i) for i in range(ends)]),
            ],
            axis=dim,
        )
    return cells


def slope(extended, winds):
    center = extended[:, 1:-1]
    north = (extended[:, 2:] - extended[:, :-2]) * 0.5
    east = (jnp.roll(center, -1, 2) - jnp.roll(center, 1, 2)) * 0.5
    return -winds - (winds[0] * east + winds[1] * north)


def rimmed(field):
    return padded(field, (("band", 1),), 1)


def tensor(extended):
    center = extended[:, 1:-1]
    north = (extended[:, 2:] - extended[:, :-2]) * 0.5
    east = (jnp.roll(center, -1, 2) - jnp.roll(center, 1, 2)) * 0.5
    g_xx = 1.0 + east[0]
    g_xy = north[0]
    g_yx = east[1]
    g_yy = 1.0 + north[1]
    return jnp.stack(
        [g_xx * g_xx + g_yx * g_yx, g_xx * g_xy + g_yx * g_yy, g_xy * g_xy + g_yy * g_yy]
    )


def integrate(shift, flow, extend):
    first = slope(extend(shift), flow)
    second = slope(extend(0.5 * first), flow)
    third = slope(extend(0.5 * second), flow)
    fourth = slope(extend(third), flow)
    return (first + 2.0 * second + 2.0 * third + fourth) / 6.0


def exponent_of(summed, members):
    mean = summed / members
    first, cross, second = (mean[..., 0, :, :], mean[..., 1, :, :], mean[..., 2, :, :])
    half = (first + second) * 0.5
    differ = (first - second) * 0.5
    largest = half + jnp.sqrt(differ * differ + cross * cross)
    return jnp.log(largest + 1e-06) / (2.0 * STEPS)


def by_rows(coeffs):
    spec = coeffs[0]
    levels = spec.shape[0]
    nlat = spec.shape[4]
    waves = spec.shape[3] * lax.axis_size("band")
    members = lax.axis_size("mem")
    stacked = spec.reshape(levels * 2, 2, spec.shape[3], nlat)
    wave_index = lax.iota(jnp.int32, waves)
    column = lax.iota(jnp.int32, NLON)
    phase = wave_index[:, None] * column[None, :] % NLON
    angle = phase.astype(jnp.float32) * (2.0 * math.pi / NLON)
    weight = jnp.where(wave_index == 0, 1.0, 2.0).astype(jnp.float32)[:, None]
    table = jnp.stack([weight * jnp.cos(angle), -weight * jnp.sin(angle)], axis=0)
    winds = jnp.einsum(
        "crwh,rwn->chn",
        lax.all_to_all(stacked, "band", split_axis=3, concat_axis=2, tiled=True),
        table,
        precision=lax.Precision.HIGHEST,
        preferred_element_type=jnp.float32,
    )
    height = winds.shape[1]
    winds = winds.reshape(levels, 2, height, NLON)
    partials = []
    for level in range(levels):
        flow = winds[level]
        shift = integrate(jnp.zeros_like(flow), flow, rimmed)
        partials.append(tensor(rimmed(shift)))
    summed = lax.psum_scatter(jnp.stack(partials), "mem", scatter_dimension=3, tiled=True)
    return lax.all_gather(exponent_of(summed, members), "mem", axis=2, tiled=True)


def by_parity(waves_local):
    half = waves_local // 2
    whole = 2 * LANE - half
    runs = []
    for parity in range(2):
        runs += [(parity, half, 2), (waves_local + parity, whole, 2)]
    for parity in range(2):
        runs.append((waves_local + parity + 2 * whole, half - whole, 2))
    return runs


@functools.lru_cache(maxsize=None)
def wave_table(bands, waves_local):
    order = np.concatenate([start + step * np.arange(count) for start, count, step in by_parity(waves_local)])
    wave, part = order % waves_local, order // waves_local
    wave = wave[None, :] + waves_local * np.arange(bands)[:, None]
    part = np.broadcast_to(part, wave.shape)
    cut = [0, 2 * LANE, 4 * LANE, 4 * LANE + LANE // 2, 5 * LANE]
    result = []
    for parity in range(2):
        picks = [(band, slice(cut[parity], cut[parity + 1])) for band in range(bands)]
        picks += [(band, slice(cut[parity + 2], cut[parity + 3])) for band in range(bands)]
        waves = np.concatenate([wave[pick] for pick in picks])
        parts = np.concatenate([part[pick] for pick in picks])
        phase = (waves[:, None] * np.arange(NLON // 2)[None, :]) % NLON
        angle = phase.astype(np.float64) * (2.0 * np.pi / NLON)
        weight = np.where(waves == 0, 1.0, 2.0)[:, None]
        table = weight * np.where(parts[:, None] == 0, np.cos(angle), -np.sin(angle))
        high = table.astype(ml_dtypes.bfloat16)
        result += [high, (table - high.astype(np.float64)).astype(ml_dtypes.bfloat16)]
    return np.stack(result)


class Window:
    def __init__(self, index, count):
        self.first = index == 0
        self.last = index == count - 1
        self.index = index
        self.width = LANE
        self.extended = LANE + 2 * SUB
        self.main = LANE if self.first else LANE - SUB
        self.rim = 0 if self.last else SUB
        self.rows = self.main + self.rim
        up = SUB if self.first else 2 * SUB
        self.place = (self.extended - up - self.rows, up)
        self.side = "other" if 2 * (index + 1) <= count else "own" if 2 * index >= count else "both"


def choose(band, pair):
    return jnp.where(band == 0, pair[0], pair[1])


def multiple(value, of):
    return pl.multiple_of(value.astype(jnp.int32), of)


def pieces_kernel(windows, slots, count, level_ref, spec_ref, *refs):
    out_refs, (taken, turned, in_sems, out_sems) = refs[: len(windows)], refs[len(windows) :]
    level = level_ref[0]
    runs = by_parity(spec_ref.shape[2] // 2)

    def arrival(c, n):
        tile = choose(level, (count - 1 - slots[n], slots[n]))
        lanes = pl.ds(multiple(tile * LANE, LANE), LANE)
        return pltpu.make_async_copy(spec_ref.at[level, c, :, lanes], taken.at[c, n], in_sems.at[c, n])

    def departures(c, k):
        window, n = windows[k], slots.index(windows[k].index)
        rows = pl.ds(multiple(choose(level, (0, LANE - window.main)), SUB), window.main)
        at = pl.ds(multiple(choose(level, (window.rim, 0)), SUB), window.main)
        yield pltpu.make_async_copy(turned.at[c, n, rows], out_refs[k].at[c, at], out_sems.at[k, c, 0])
        if window.rim:
            rows = pl.ds(multiple(choose(level, (LANE - SUB, 0)), SUB), SUB)
            at = pl.ds(multiple(choose(level, (0, window.main)), SUB), SUB)
            yield pltpu.make_async_copy(turned.at[c, n + 1, rows], out_refs[k].at[c, at], out_sems.at[k, c, 1])

    for n in range(len(slots)):
        for c in range(2):
            arrival(c, n).start()
    for n in range(len(slots)):
        for c in range(2):
            arrival(c, n).wait()
            turned[c, n] = jnp.concatenate([taken[c, n, pl.ds(start, rows, step), :] for start, rows, step in runs]).T
        for k, window in enumerate(windows):
            if slots[n] == window.index + (1 if window.rim else 0):
                for c in range(2):
                    for copy in departures(c, k):
                        copy.start()
    for k in range(len(windows)):
        for c in range(2):
            for copy in departures(c, k):
                copy.wait()


def pieces_of(spec, level, windows, count):
    depth = spec.shape[2]
    slots = sorted({w.index for w in windows} | {w.index + 1 for w in windows if w.rim})
    return pl.pallas_call(
        functools.partial(pieces_kernel, windows, slots, count),
        in_specs=[pl.BlockSpec(memory_space=pltpu.SMEM), pl.BlockSpec(memory_space=pl.ANY)],
        out_specs=[pl.BlockSpec(memory_space=pl.ANY)] * len(windows),
        out_shape=[jax.ShapeDtypeStruct((2, w.rows, depth), jnp.float32) for w in windows],
        scratch_shapes=[
            pltpu.VMEM((2, len(slots), depth, LANE), jnp.float32),
            pltpu.VMEM((2, len(slots), LANE, depth), jnp.float32),
            pltpu.SemaphoreType.DMA((2, len(slots))),
            pltpu.SemaphoreType.DMA((len(windows), 2, 2)),
        ],
        compiler_params=pltpu.CompilerParams(vmem_limit_bytes=VMEM_LIMIT),
        cost_estimate=pl.CostEstimate(
            flops=0, transcendentals=0, bytes_accessed=4 * 2 * len(slots) * LANE * depth * 4
        ),
        name="pieces_of",
    )(level.reshape(1), spec)


def gate_kernel(*refs):
    pass


def gated(part, waits):
    return pl.pallas_call(
        gate_kernel,
        in_specs=[pl.BlockSpec(memory_space=pl.ANY)] * (1 + len(waits)),
        out_specs=pl.BlockSpec(memory_space=pl.ANY),
        out_shape=jax.ShapeDtypeStruct(part.shape, part.dtype),
        input_output_aliases={0: 0},
        cost_estimate=pl.CostEstimate(flops=0, transcendentals=0, bytes_accessed=1024),
        name="gated",
    )(part, *waits)


def east_of(x):
    return pltpu.roll(x, NLON - 1, axis=1) - pltpu.roll(x, 1, axis=1)


def north_of(before, here, after):
    row = lax.broadcasted_iota(jnp.int32, here.shape, 0)
    above = jnp.where(row == SUB - 1, pltpu.roll(after, SUB - 1, axis=0), pltpu.roll(here, SUB - 1, axis=0))
    below = jnp.where(row == 0, pltpu.roll(before, 1, axis=0), pltpu.roll(here, 1, axis=0))
    return above - below


def window_kernel(window, depth, waits, *refs):
    refs = list(refs)
    place_ref, local_ref, remote_ref, table_ref = refs[:4]
    refs = refs[4 + waits :]
    carry_ref = None if window.first else refs.pop(0)
    out_refs = [refs.pop(0) for _ in range(4)]
    carried_ref = None if window.last else refs.pop(0)
    table, lhs_high, lhs_low, wind, second, third, shift, results, carried, table_sem, out_sems = refs
    band, core, sides = place_ref[0], place_ref[1], (place_ref[2], place_ref[3])
    rows, extended = window.rows, window.extended

    def at(pair):
        return multiple(choose(band, pair), SUB)

    tables = pltpu.make_async_copy(table_ref, table, table_sem)
    tables.start()
    lane = lax.broadcasted_iota(jnp.int32, (rows, LANE), 1)
    even, odd = [], []
    for c in range(2):
        mine, theirs = local_ref[c], remote_ref[c]
        low, high = jnp.where(band == 0, mine, theirs), jnp.where(band == 0, theirs, mine)
        low_rest, high_rest = low[:, 4 * LANE :], high[:, 4 * LANE :]
        turn = functools.partial(pltpu.roll, shift=LANE // 2, axis=1)
        even_rest = jnp.where(lane < LANE // 2, low_rest, turn(high_rest))
        odd_rest = jnp.where(lane < LANE // 2, turn(low_rest), high_rest)
        even.append(jnp.concatenate([low[:, : 2 * LANE], high[:, : 2 * LANE], even_rest], axis=1))
        odd.append(jnp.concatenate([low[:, 2 * LANE : 4 * LANE], high[:, 2 * LANE : 4 * LANE], odd_rest], axis=1))
    for parity, parts in enumerate((even, odd)):
        lhs = jnp.concatenate(parts)
        lhs_high[parity] = lhs.astype(jnp.bfloat16)
        lhs_low[parity] = (lhs - lhs_high[parity].astype(jnp.float32)).astype(jnp.bfloat16)
    tables.wait()

    place = at(window.place)
    if window.first or window.last:
        for c in range(2):
            if window.first:
                wind[c, pl.ds(at((extended - SUB, 0)), SUB), :] = jnp.zeros((SUB, NLON), jnp.float32)
            if window.last:
                wind[c, pl.ds(at((0, extended - SUB)), SUB), :] = jnp.zeros((SUB, NLON), jnp.float32)
    if not window.first:
        for c in range(2):
            wind[c, pl.ds(at((extended - 2 * SUB, 0)), 2 * SUB), :] = carry_ref[c]

    dot = functools.partial(jnp.dot, preferred_element_type=jnp.float32)
    for start in range(0, NLON // 2, 2 * LANE):
        stop = min(start + 2 * LANE, NLON // 2)
        columns = slice(start, stop)
        sums = []
        for parity in range(2):
            total = dot(lhs_high[parity], table[2 * parity, :, columns])
            total += dot(lhs_low[parity], table[2 * parity, :, columns])
            total += dot(lhs_high[parity], table[2 * parity + 1, :, columns])
            sums.append(total)
        for c in range(2):
            even_sum, odd_sum = (total[c * rows : (c + 1) * rows] for total in sums)
            wind[c, pl.ds(place, rows), start:stop] = even_sum + odd_sum
            wind[c, pl.ds(place, rows), NLON // 2 + start : NLON // 2 + stop] = even_sum - odd_sum

    if not window.last:
        for c in range(2):
            carried[c] = wind[c, pl.ds(at((0, extended - 2 * SUB)), 2 * SUB), :]
        carry_on = pltpu.make_async_copy(carried, carried_ref, out_sems.at[4])
        carry_on.start()

    blocks = extended // SUB

    def rows_of(block):
        return pl.ds(pl.multiple_of(block * SUB, SUB), SUB)

    def derivatives(field, block):
        before, after = jnp.maximum(block - 1, 0), jnp.minimum(block + 1, blocks - 1)
        result = []
        for c in range(2):
            here = field[c, rows_of(block), :]
            result.append((east_of(here), north_of(field[c, rows_of(before), :], here, field[c, rows_of(after), :])))
        return result

    @pl.loop(0, blocks, unroll=6)
    def _(block):
        flow = [wind[c, rows_of(block), :] for c in range(2)]
        for c, (east, north) in enumerate(derivatives(wind, block)):
            second[c, rows_of(block), :] = 0.25 * (flow[0] * east + flow[1] * north) - flow[c]

    @pl.loop(0, blocks, unroll=6)
    def _(block):
        flow = [wind[c, rows_of(block), :] for c in range(2)]
        for c, (east, north) in enumerate(derivatives(second, block)):
            third[c, rows_of(block), :] = -flow[c] - 0.25 * (flow[0] * east + flow[1] * north)

    @pl.loop(0, blocks, unroll=6)
    def _(block):
        flow = [wind[c, rows_of(block), :] for c in range(2)]
        for c, (east, north) in enumerate(derivatives(third, block)):
            fourth = -flow[c] - 0.5 * (flow[0] * east + flow[1] * north)
            both = second[c, rows_of(block), :] + third[c, rows_of(block), :]
            shift[c, rows_of(block), :] = (2.0 * both + (fourth - flow[c])) * (1.0 / 6.0)

    quarter = window.width // 4 // SUB

    def entries(out, base):
        @pl.loop(0, quarter, unroll=4)
        def _(block):
            (e0, n0), (e1, n1) = derivatives(shift, base + block + 1)
            g_xx, g_xy, g_yx, g_yy = 1.0 + 0.5 * e0, 0.5 * n0, 0.5 * e1, 1.0 + 0.5 * n1
            out[0, rows_of(block), :] = g_xx * g_xx + g_yx * g_yx
            out[1, rows_of(block), :] = g_xx * g_xy + g_yx * g_yy
            out[2, rows_of(block), :] = g_xy * g_xy + g_yy * g_yy

    copies = []
    for n, (a, b) in reversed(list(enumerate(QUARTERS))):
        side = sides[a]
        entries(results.at[n], (2 * (core + a - 2 * core * a) + (side + b - 2 * side * b)) * quarter)
        copies.append(pltpu.make_async_copy(results.at[n], out_refs[n], out_sems.at[n]))
        copies[-1].start()
    for copy in copies:
        copy.wait()
    if not window.last:
        carry_on.wait()


QUARTERS = ((0, 0), (0, 1), (1, 0), (1, 1))


def window_tensor(window, place, local, remote, table, waits, carry):
    depth = local.shape[2]
    vmem = pl.BlockSpec(memory_space=pltpu.VMEM)
    in_specs = [
        pl.BlockSpec(memory_space=pltpu.SMEM),
        vmem,
        vmem,
        pl.BlockSpec(memory_space=pl.ANY),
    ]
    in_specs += [pl.BlockSpec(memory_space=pl.ANY)] * len(waits)
    operands = [place, local, remote, table, *waits]
    if not window.first:
        in_specs.append(vmem)
        operands.append(carry)
    out_shape = [jax.ShapeDtypeStruct((3, window.width // 4, NLON), jnp.float32)] * 4
    if not window.last:
        out_shape.append(jax.ShapeDtypeStruct((2, 2 * SUB, NLON), jnp.float32))
    field = pltpu.VMEM((2, window.extended, NLON), jnp.float32)
    lhs_shape = (2, 2 * window.rows, depth)
    out = pl.pallas_call(
        functools.partial(window_kernel, window, depth, len(waits)),
        out_shape=out_shape,
        in_specs=in_specs,
        out_specs=[pl.BlockSpec(memory_space=pl.ANY)] * len(out_shape),
        scratch_shapes=[
            pltpu.VMEM(table.shape, table.dtype),
            pltpu.VMEM(lhs_shape, jnp.bfloat16),
            pltpu.VMEM(lhs_shape, jnp.bfloat16),
            field,
            field,
            field,
            field,
            pltpu.VMEM((4, 3, window.width // 4, NLON), jnp.float32),
            pltpu.VMEM((2, 2 * SUB, NLON), jnp.float32),
            pltpu.SemaphoreType.DMA,
            pltpu.SemaphoreType.DMA((5,)),
        ],
        compiler_params=pltpu.CompilerParams(vmem_limit_bytes=VMEM_LIMIT),
        cost_estimate=pl.CostEstimate(
            flops=KERNEL_WORK * 3 * 2 * 2 * window.rows * depth * NLON,
            transcendentals=0,
            bytes_accessed=2 * table.size + 4 * window.rows * depth * 4 + 12 * window.width * NLON,
        ),
        name="window_tensor",
    )(*operands)
    return out[:4], (None if window.last else out[4])


def by_levels(coeffs):
    spec = coeffs[0]
    levels, _, parts, waves_local, nlat = spec.shape
    members = lax.axis_size("mem")
    band = lax.axis_index("band").astype(jnp.int32)
    member = lax.axis_index("mem").astype(jnp.int32)
    core = member % 2
    half_of = [choose(core, [member // bits[step] % 2 for bits in ORDER]) for step in range(len(ORDER[0]))]
    half_beside = choose(1 - core, [member // bits[0] % 2 for bits in ORDER])
    place = jnp.stack([band, core, half_of[0], half_beside])
    spec = spec.reshape(levels, 2, parts * waves_local, nlat)
    count = nlat // LANE
    windows = [Window(k, count) for k in range(count)]
    table = jnp.asarray(wave_table(levels, waves_local))
    swap = [(0, 1), (1, 0)]

    (piece,) = pieces_of(spec, 1 - band, windows[:1], count)
    remotes = [lax.ppermute(piece, "band", swap)]
    for k, piece in enumerate(pieces_of(spec, 1 - band, windows[1:], count), 1):
        if k > 1:
            piece = gated(piece, [remotes[k - 2]])
        remotes.append(lax.ppermute(piece, "band", swap))
    local = pieces_of(spec, band, windows, count)

    cores = [(m, m ^ 1) for m in range(members)]
    ways = [[(m, m ^ ORDER[m % 2][step]) for m in range(members)] for step in range(len(ORDER[0]))]

    def halved(parts_of, step, waits=()):
        half = parts_of[0].shape[1] // 2
        mine = half_of[step]

        def total(which):
            return sum(lax.dynamic_slice_in_dim(part, which * half, half, axis=1) for part in parts_of)

        leaves = total(1 - mine)
        if waits:
            leaves = gated(leaves, waits)
        return [total(mine), lax.ppermute(leaves, "mem", ways[step])], leaves

    def across(parts_of, step):
        kept, passed, kept_more, passed_more = parts_of
        leaves = passed + passed_more
        return [kept, kept_more, lax.ppermute(leaves, "mem", ways[step])], leaves

    def advanced(parts_of, step):
        return (across if step == 0 else halved)(parts_of, step)

    def doubled(part, step):
        beside = lax.ppermute(part, "mem", cores if step < 0 else ways[step])
        mine = core if step < 0 else half_of[step]
        return jnp.where(mine == 0, jnp.concatenate([part, beside], axis=1), jnp.concatenate([beside, part], axis=1))

    def gathered(part):
        for step in range(len(ways) - 1, -2, -1):
            part = doubled(part, step)
        return part

    carry = None
    sums, done = [], []
    for k, window in enumerate(windows):
        waits = []
        for j in AHEAD[k]:
            sums[j], left = advanced(sums[j], done[j])
            done[j] += 1
            waits.append(left)
        quarters, carry = window_tensor(window, place, local[k], remotes[k], table, waits, carry)
        first = lax.ppermute(quarters[3], "mem", cores)
        second = lax.ppermute(quarters[2], "mem", cores)
        sums.append([quarters[0], quarters[1], second, first])
        done.append(0)
    last = count - 1
    sums[last], _ = across(sums[last], 0)
    done[last] = 1
    over = sums[last][2]
    pieces = {"own": [], "both": [], "other": []}
    for k, window in enumerate(windows):
        for step in range(done[k], len(ways)):
            if window.side == "other":
                sums[k], _ = halved(sums[k], step, [first])
            else:
                sums[k], _ = advanced(sums[k], step)
        pieces[window.side].append(exponent_of(sum(sums[k]), members))

    other = lax.ppermute(gated(jnp.stack(pieces["other"]), [over]), "band", swap)
    place_of = {}
    for m in range(members):
        for b in range(2):
            bits = ORDER[m % 2]
            piece = functools.reduce(lambda value, bit: 2 * value + m // bit % 2, bits, m % 2)
            place_of[piece, b] = m * 2 + b
    trades, half = [], members // 2
    for (piece, b), index in place_of.items():
        mate = (piece, b) if (piece < half) == (b == 0) else ((piece + half) % members, 1 - b)
        trades.append((index, place_of[mate]))
    both = lax.ppermute(pieces["both"][0], ("mem", "band"), trades)

    far = gathered(other)
    near = gathered(jnp.concatenate([both[None], jnp.stack(pieces["own"])]))
    middle = near.shape[1] // 2
    rest = jnp.zeros((nlat // 2, NLON), jnp.float32)
    down = jnp.stack([rest, jnp.concatenate([*far, rest[:middle]])])
    up = jnp.stack([jnp.concatenate([rest[:middle], *far[::-1]]), rest])
    out = jnp.where(band == 0, down, up)

    def put(block, level, pair):
        return lax.dynamic_update_slice(out, block[None], (level, choose(band, pair).astype(jnp.int32), jnp.int32(0)))

    edge = nlat // 2 - middle
    out = put(near[0, :middle], 0, (edge, 0))
    out = put(near[0, middle:], 1, (edge, 0))
    for k, block in enumerate(near[1:]):
        out = put(block, band, (edge - (k + 1) * LANE, middle + k * LANE))
    return out


def per_device(coeffs):
    _, levels, _, _, _, nlat = coeffs.shape
    members = lax.axis_size("mem")
    rows = nlat // lax.axis_size("band")
    fits = coeffs.shape[4] == 5 * LANE // 2 and nlat % (2 * LANE) == LANE and rows > LANE
    if fits and levels == lax.axis_size("band") == 2 and members == 16:
        return by_levels(coeffs)
    return by_rows(coeffs)


def solution(mesh):
    placed = (P("mem", None, None, None, "band", None),)
    return jax.shard_map(
        per_device, mesh=mesh, in_specs=placed, out_specs=P(None, "band", None), check_vma=False
    )
```

```python
import functools
import math

import jax
import jax.numpy as jnp
import ml_dtypes
import numpy as np
from jax import lax
from jax.experimental import pallas as pl
from jax.experimental.pallas import tpu as pltpu
from jax.sharding import PartitionSpec as P

NLON = 1280
STEPS = 1
SUB = 8
LANE = 128
VMEM_LIMIT = 60 * 1024 * 1024
KERNEL_WORK = 8
ORDER = ((2, 4, 8), (4, 2, 8))
AHEAD = ((), (), (0,), (1, 0), (2, 1, 0))


def padded(cells, sides, width):
    for axis, dim in sides:
        count = lax.axis_size(axis)
        ends = count - 1
        head = lax.slice_in_dim(cells, 0, width, axis=dim)
        tail = lax.slice_in_dim(cells, cells.shape[dim] - width, cells.shape[dim], axis=dim)
        cells = jnp.concatenate(
            [
                lax.ppermute(tail, axis, [(i, (i + 1) % count) for i in range(ends)]),
                cells,
                lax.ppermute(head, axis, [((i + 1) % count, i) for i in range(ends)]),
            ],
            axis=dim,
        )
    return cells


def slope(extended, winds):
    center = extended[:, 1:-1]
    north = (extended[:, 2:] - extended[:, :-2]) * 0.5
    east = (jnp.roll(center, -1, 2) - jnp.roll(center, 1, 2)) * 0.5
    return -winds - (winds[0] * east + winds[1] * north)


def rimmed(field):
    return padded(field, (("band", 1),), 1)


def tensor(extended):
    center = extended[:, 1:-1]
    north = (extended[:, 2:] - extended[:, :-2]) * 0.5
    east = (jnp.roll(center, -1, 2) - jnp.roll(center, 1, 2)) * 0.5
    g_xx = 1.0 + east[0]
    g_xy = north[0]
    g_yx = east[1]
    g_yy = 1.0 + north[1]
    return jnp.stack(
        [g_xx * g_xx + g_yx * g_yx, g_xx * g_xy + g_yx * g_yy, g_xy * g_xy + g_yy * g_yy]
    )


def integrate(shift, flow, extend):
    first = slope(extend(shift), flow)
    second = slope(extend(0.5 * first), flow)
    third = slope(extend(0.5 * second), flow)
    fourth = slope(extend(third), flow)
    return (first + 2.0 * second + 2.0 * third + fourth) / 6.0


def exponent_of(summed, members):
    mean = summed / members
    first, cross, second = (mean[..., 0, :, :], mean[..., 1, :, :], mean[..., 2, :, :])
    half = (first + second) * 0.5
    differ = (first - second) * 0.5
    largest = half + jnp.sqrt(differ * differ + cross * cross)
    return jnp.log(largest + 1e-06) / (2.0 * STEPS)


def by_rows(coeffs):
    spec = coeffs[0]
    levels = spec.shape[0]
    nlat = spec.shape[4]
    waves = spec.shape[3] * lax.axis_size("band")
    members = lax.axis_size("mem")
    stacked = spec.reshape(levels * 2, 2, spec.shape[3], nlat)
    wave_index = lax.iota(jnp.int32, waves)
    column = lax.iota(jnp.int32, NLON)
    phase = wave_index[:, None] * column[None, :] % NLON
    angle = phase.astype(jnp.float32) * (2.0 * math.pi / NLON)
    weight = jnp.where(wave_index == 0, 1.0, 2.0).astype(jnp.float32)[:, None]
    table = jnp.stack([weight * jnp.cos(angle), -weight * jnp.sin(angle)], axis=0)
    winds = jnp.einsum(
        "crwh,rwn->chn",
        lax.all_to_all(stacked, "band", split_axis=3, concat_axis=2, tiled=True),
        table,
        precision=lax.Precision.HIGHEST,
        preferred_element_type=jnp.float32,
    )
    height = winds.shape[1]
    winds = winds.reshape(levels, 2, height, NLON)
    partials = []
    for level in range(levels):
        flow = winds[level]
        shift = integrate(jnp.zeros_like(flow), flow, rimmed)
        partials.append(tensor(rimmed(shift)))
    summed = lax.psum_scatter(jnp.stack(partials), "mem", scatter_dimension=3, tiled=True)
    return lax.all_gather(exponent_of(summed, members), "mem", axis=2, tiled=True)


def by_parity(waves_local):
    half = waves_local // 2
    whole = 2 * LANE - half
    runs = []
    for parity in range(2):
        runs += [(parity, half, 2), (waves_local + parity, whole, 2)]
    for parity in range(2):
        runs.append((waves_local + parity + 2 * whole, half - whole, 2))
    return runs


@functools.lru_cache(maxsize=None)
def wave_table(bands, waves_local):
    order = np.concatenate([start + step * np.arange(count) for start, count, step in by_parity(waves_local)])
    wave, part = order % waves_local, order // waves_local
    wave = wave[None, :] + waves_local * np.arange(bands)[:, None]
    part = np.broadcast_to(part, wave.shape)
    cut = [0, 2 * LANE, 4 * LANE, 4 * LANE + LANE // 2, 5 * LANE]
    result = []
    for parity in range(2):
        picks = [(band, slice(cut[parity], cut[parity + 1])) for band in range(bands)]
        picks += [(band, slice(cut[parity + 2], cut[parity + 3])) for band in range(bands)]
        waves = np.concatenate([wave[pick] for pick in picks])
        parts = np.concatenate([part[pick] for pick in picks])
        phase = (waves[:, None] * np.arange(NLON // 2)[None, :]) % NLON
        angle = phase.astype(np.float64) * (2.0 * np.pi / NLON)
        weight = np.where(waves == 0, 1.0, 2.0)[:, None]
        table = weight * np.where(parts[:, None] == 0, np.cos(angle), -np.sin(angle))
        high = table.astype(ml_dtypes.bfloat16)
        result += [high, (table - high.astype(np.float64)).astype(ml_dtypes.bfloat16)]
    return np.stack(result)


class Window:
    def __init__(self, index, count):
        self.first = index == 0
        self.last = index == count - 1
        self.index = index
        self.width = LANE
        self.extended = LANE + 2 * SUB
        self.main = LANE if self.first else LANE - SUB
        self.rim = 0 if self.last else SUB
        self.rows = self.main + self.rim
        up = SUB if self.first else 2 * SUB
        self.place = (self.extended - up - self.rows, up)
        self.side = "other" if 2 * (index + 1) <= count else "own" if 2 * index >= count else "both"


def choose(band, pair):
    return jnp.where(band == 0, pair[0], pair[1])


def multiple(value, of):
    return pl.multiple_of(value.astype(jnp.int32), of)


def pieces_kernel(windows, slots, count, level_ref, spec_ref, *refs):
    out_refs, (taken, turned, in_sems, out_sems) = refs[: len(windows)], refs[len(windows) :]
    level = level_ref[0]
    runs = by_parity(spec_ref.shape[2] // 2)

    def arrival(c, n):
        tile = choose(level, (count - 1 - slots[n], slots[n]))
        lanes = pl.ds(multiple(tile * LANE, LANE), LANE)
        return pltpu.make_async_copy(spec_ref.at[level, c, :, lanes], taken.at[c, n], in_sems.at[c, n])

    def departures(c, k):
        window, n = windows[k], slots.index(windows[k].index)
        rows = pl.ds(multiple(choose(level, (0, LANE - window.main)), SUB), window.main)
        at = pl.ds(multiple(choose(level, (window.rim, 0)), SUB), window.main)
        yield pltpu.make_async_copy(turned.at[c, n, rows], out_refs[k].at[c, at], out_sems.at[k, c, 0])
        if window.rim:
            rows = pl.ds(multiple(choose(level, (LANE - SUB, 0)), SUB), SUB)
            at = pl.ds(multiple(choose(level, (0, window.main)), SUB), SUB)
            yield pltpu.make_async_copy(turned.at[c, n + 1, rows], out_refs[k].at[c, at], out_sems.at[k, c, 1])

    for n in range(len(slots)):
        for c in range(2):
            arrival(c, n).start()
    for n in range(len(slots)):
        for c in range(2):
            arrival(c, n).wait()
            turned[c, n] = jnp.concatenate([taken[c, n, pl.ds(start, rows, step), :] for start, rows, step in runs]).T
        for k, window in enumerate(windows):
            if slots[n] == window.index + (1 if window.rim else 0):
                for c in range(2):
                    for copy in departures(c, k):
                        copy.start()
    for k in range(len(windows)):
        for c in range(2):
            for copy in departures(c, k):
                copy.wait()


def pieces_of(spec, level, windows, count):
    depth = spec.shape[2]
    slots = sorted({w.index for w in windows} | {w.index + 1 for w in windows if w.rim})
    return pl.pallas_call(
        functools.partial(pieces_kernel, windows, slots, count),
        in_specs=[pl.BlockSpec(memory_space=pltpu.SMEM), pl.BlockSpec(memory_space=pl.ANY)],
        out_specs=[pl.BlockSpec(memory_space=pl.ANY)] * len(windows),
        out_shape=[jax.ShapeDtypeStruct((2, w.rows, depth), jnp.float32) for w in windows],
        scratch_shapes=[
            pltpu.VMEM((2, len(slots), depth, LANE), jnp.float32),
            pltpu.VMEM((2, len(slots), LANE, depth), jnp.float32),
            pltpu.SemaphoreType.DMA((2, len(slots))),
            pltpu.SemaphoreType.DMA((len(windows), 2, 2)),
        ],
        compiler_params=pltpu.CompilerParams(vmem_limit_bytes=VMEM_LIMIT),
        cost_estimate=pl.CostEstimate(
            flops=0, transcendentals=0, bytes_accessed=4 * 2 * len(slots) * LANE * depth * 4
        ),
        name="pieces_of",
    )(level.reshape(1), spec)


def gate_kernel(*refs):
    pass


def gated(part, waits):
    return pl.pallas_call(
        gate_kernel,
        in_specs=[pl.BlockSpec(memory_space=pl.ANY)] * (1 + len(waits)),
        out_specs=pl.BlockSpec(memory_space=pl.ANY),
        out_shape=jax.ShapeDtypeStruct(part.shape, part.dtype),
        input_output_aliases={0: 0},
        cost_estimate=pl.CostEstimate(flops=0, transcendentals=0, bytes_accessed=1024),
        name="gated",
    )(part, *waits)


def east_of(x):
    return pltpu.roll(x, NLON - 1, axis=1) - pltpu.roll(x, 1, axis=1)


def north_of(before, here, after):
    row = lax.broadcasted_iota(jnp.int32, here.shape, 0)
    above = jnp.where(row == SUB - 1, pltpu.roll(after, SUB - 1, axis=0), pltpu.roll(here, SUB - 1, axis=0))
    below = jnp.where(row == 0, pltpu.roll(before, 1, axis=0), pltpu.roll(here, 1, axis=0))
    return above - below


def window_kernel(window, waits, *refs):
    refs = list(refs)
    place_ref, local_ref, remote_ref, table_ref = refs[:4]
    refs = refs[4 + waits :]
    carry_ref = None if window.first else refs.pop(0)
    out_refs = [refs.pop(0) for _ in range(4)]
    carried_ref = None if window.last else refs.pop(0)
    table, mine_buf, theirs_buf, lhs_high, lhs_low, wind, second, third, shift, results, carried, in_sems, out_sems = refs
    band, core, sides = place_ref[0], place_ref[1], (place_ref[2], place_ref[3])
    rows, extended = window.rows, window.extended

    def at(pair):
        return multiple(choose(band, pair), SUB)

    inputs = [pltpu.make_async_copy(local_ref, mine_buf, in_sems.at[0])]
    inputs.append(pltpu.make_async_copy(remote_ref, theirs_buf, in_sems.at[1]))
    tables = pltpu.make_async_copy(table_ref, table, in_sems.at[2])
    if not window.first:
        rows_before = wind.at[:, pl.ds(at((extended - 2 * SUB, 0)), 2 * SUB)]
        inputs.append(pltpu.make_async_copy(carry_ref, rows_before, in_sems.at[3]))
    for copy in [*inputs, tables]:
        copy.start()
    for copy in inputs:
        copy.wait()
    lane = lax.broadcasted_iota(jnp.int32, (rows, LANE), 1)
    even, odd = [], []
    for c in range(2):
        mine, theirs = mine_buf[c], theirs_buf[c]
        low, high = jnp.where(band == 0, mine, theirs), jnp.where(band == 0, theirs, mine)
        low_rest, high_rest = low[:, 4 * LANE :], high[:, 4 * LANE :]
        turn = functools.partial(pltpu.roll, shift=LANE // 2, axis=1)
        even_rest = jnp.where(lane < LANE // 2, low_rest, turn(high_rest))
        odd_rest = jnp.where(lane < LANE // 2, turn(low_rest), high_rest)
        even.append(jnp.concatenate([low[:, : 2 * LANE], high[:, : 2 * LANE], even_rest], axis=1))
        odd.append(jnp.concatenate([low[:, 2 * LANE : 4 * LANE], high[:, 2 * LANE : 4 * LANE], odd_rest], axis=1))
    for parity, parts in enumerate((even, odd)):
        lhs = jnp.concatenate(parts)
        lhs_high[parity] = lhs.astype(jnp.bfloat16)
        lhs_low[parity] = (lhs - lhs_high[parity].astype(jnp.float32)).astype(jnp.bfloat16)

    place = at(window.place)
    if window.first or window.last:
        for c in range(2):
            if window.first:
                wind[c, pl.ds(at((extended - SUB, 0)), SUB), :] = jnp.zeros((SUB, NLON), jnp.float32)
            if window.last:
                wind[c, pl.ds(at((0, extended - SUB)), SUB), :] = jnp.zeros((SUB, NLON), jnp.float32)
    tables.wait()

    dot = functools.partial(jnp.dot, preferred_element_type=jnp.float32)
    for start in range(0, NLON // 2, 2 * LANE):
        stop = min(start + 2 * LANE, NLON // 2)
        columns = slice(start, stop)
        sums = []
        for parity in range(2):
            total = dot(lhs_high[parity], table[2 * parity, :, columns])
            total += dot(lhs_low[parity], table[2 * parity, :, columns])
            total += dot(lhs_high[parity], table[2 * parity + 1, :, columns])
            sums.append(total)
        for c in range(2):
            even_sum, odd_sum = (total[c * rows : (c + 1) * rows] for total in sums)
            wind[c, pl.ds(place, rows), start:stop] = even_sum + odd_sum
            wind[c, pl.ds(place, rows), NLON // 2 + start : NLON // 2 + stop] = even_sum - odd_sum

    if not window.last:
        for c in range(2):
            carried[c] = wind[c, pl.ds(at((0, extended - 2 * SUB)), 2 * SUB), :]
        carry_on = pltpu.make_async_copy(carried, carried_ref, out_sems.at[4])
        carry_on.start()

    blocks = extended // SUB

    def rows_of(block):
        return pl.ds(pl.multiple_of(block * SUB, SUB), SUB)

    def derivatives(field, block):
        before, after = jnp.maximum(block - 1, 0), jnp.minimum(block + 1, blocks - 1)
        result = []
        for c in range(2):
            here = field[c, rows_of(block), :]
            result.append((east_of(here), north_of(field[c, rows_of(before), :], here, field[c, rows_of(after), :])))
        return result

    @pl.loop(0, blocks, unroll=9)
    def _(block):
        flow = [wind[c, rows_of(block), :] for c in range(2)]
        for c, (east, north) in enumerate(derivatives(wind, block)):
            second[c, rows_of(block), :] = 0.25 * (flow[0] * east + flow[1] * north) - flow[c]

    @pl.loop(0, blocks, unroll=9)
    def _(block):
        flow = [wind[c, rows_of(block), :] for c in range(2)]
        for c, (east, north) in enumerate(derivatives(second, block)):
            third[c, rows_of(block), :] = -flow[c] - 0.25 * (flow[0] * east + flow[1] * north)

    @pl.loop(0, blocks, unroll=9)
    def _(block):
        flow = [wind[c, rows_of(block), :] for c in range(2)]
        for c, (east, north) in enumerate(derivatives(third, block)):
            fourth = -flow[c] - 0.5 * (flow[0] * east + flow[1] * north)
            both = second[c, rows_of(block), :] + third[c, rows_of(block), :]
            shift[c, rows_of(block), :] = (2.0 * both + (fourth - flow[c])) * (1.0 / 6.0)

    quarter = window.width // 4 // SUB

    def entries(out, base):
        @pl.loop(0, quarter, unroll=4)
        def _(block):
            (e0, n0), (e1, n1) = derivatives(shift, base + block + 1)
            g_xx, g_xy, g_yx, g_yy = 1.0 + 0.5 * e0, 0.5 * n0, 0.5 * e1, 1.0 + 0.5 * n1
            out[0, rows_of(block), :] = g_xx * g_xx + g_yx * g_yx
            out[1, rows_of(block), :] = g_xx * g_xy + g_yx * g_yy
            out[2, rows_of(block), :] = g_xy * g_xy + g_yy * g_yy

    copies = []
    for n, (a, b) in reversed(list(enumerate(QUARTERS))):
        side = sides[a]
        entries(results.at[n], (2 * (core + a - 2 * core * a) + (side + b - 2 * side * b)) * quarter)
        copies.append(pltpu.make_async_copy(results.at[n], out_refs[n], out_sems.at[n]))
        copies[-1].start()
    for copy in copies:
        copy.wait()
    if not window.last:
        carry_on.wait()


QUARTERS = ((0, 0), (0, 1), (1, 0), (1, 1))


def window_tensor(window, place, local, remote, table, waits, carry):
    depth = local.shape[2]
    operands = [place, local, remote, table, *waits]
    if not window.first:
        operands.append(carry)
    in_specs = [pl.BlockSpec(memory_space=pltpu.SMEM)] + [pl.BlockSpec(memory_space=pl.ANY)] * (len(operands) - 1)
    out_shape = [jax.ShapeDtypeStruct((3, window.width // 4, NLON), jnp.float32)] * 4
    if not window.last:
        out_shape.append(jax.ShapeDtypeStruct((2, 2 * SUB, NLON), jnp.float32))
    field = pltpu.VMEM((2, window.extended, NLON), jnp.float32)
    lhs_shape = (2, 2 * window.rows, depth)
    out = pl.pallas_call(
        functools.partial(window_kernel, window, len(waits)),
        out_shape=out_shape,
        in_specs=in_specs,
        out_specs=[pl.BlockSpec(memory_space=pl.ANY)] * len(out_shape),
        scratch_shapes=[
            pltpu.VMEM(table.shape, table.dtype),
            pltpu.VMEM(local.shape, jnp.float32),
            pltpu.VMEM(local.shape, jnp.float32),
            pltpu.VMEM(lhs_shape, jnp.bfloat16),
            pltpu.VMEM(lhs_shape, jnp.bfloat16),
            field,
            field,
            field,
            field,
            pltpu.VMEM((4, 3, window.width // 4, NLON), jnp.float32),
            pltpu.VMEM((2, 2 * SUB, NLON), jnp.float32),
            pltpu.SemaphoreType.DMA((4,)),
            pltpu.SemaphoreType.DMA((5,)),
        ],
        compiler_params=pltpu.CompilerParams(vmem_limit_bytes=VMEM_LIMIT),
        cost_estimate=pl.CostEstimate(
            flops=KERNEL_WORK * 3 * 2 * 2 * window.rows * depth * NLON,
            transcendentals=0,
            bytes_accessed=2 * table.size + 4 * window.rows * depth * 4 + 12 * window.width * NLON,
        ),
        name="window_tensor",
    )(*operands)
    return out[:4], (None if window.last else out[4])


def by_levels(coeffs):
    spec = coeffs[0]
    levels, _, parts, waves_local, nlat = spec.shape
    members = lax.axis_size("mem")
    band = lax.axis_index("band").astype(jnp.int32)
    member = lax.axis_index("mem").astype(jnp.int32)
    core = member % 2
    half_of = [choose(core, [member // bits[step] % 2 for bits in ORDER]) for step in range(len(ORDER[0]))]
    half_beside = choose(1 - core, [member // bits[0] % 2 for bits in ORDER])
    place = jnp.stack([band, core, half_of[0], half_beside])
    spec = spec.reshape(levels, 2, parts * waves_local, nlat)
    count = nlat // LANE
    windows = [Window(k, count) for k in range(count)]
    table = jnp.asarray(wave_table(levels, waves_local))
    swap = [(0, 1), (1, 0)]

    (piece,) = pieces_of(spec, 1 - band, windows[:1], count)
    remotes = [lax.ppermute(piece, "band", swap)]
    for k, piece in enumerate(pieces_of(spec, 1 - band, windows[1:], count), 1):
        if k > 1:
            piece = gated(piece, [remotes[k - 2]])
        remotes.append(lax.ppermute(piece, "band", swap))
    local = pieces_of(spec, band, windows, count)

    cores = [(m, m ^ 1) for m in range(members)]
    ways = [[(m, m ^ ORDER[m % 2][step]) for m in range(members)] for step in range(len(ORDER[0]))]

    def halved(parts_of, step):
        half = parts_of[0].shape[1] // 2
        mine = half_of[step]

        def total(which):
            return sum(lax.dynamic_slice_in_dim(part, which * half, half, axis=1) for part in parts_of)

        leaves = total(1 - mine)
        return [total(mine), lax.ppermute(leaves, "mem", ways[step])], leaves

    def across(parts_of, step):
        kept, passed, kept_more, passed_more = parts_of
        leaves = passed + passed_more
        return [kept, kept_more, lax.ppermute(leaves, "mem", ways[step])], leaves

    def advanced(parts_of, step):
        return (across if step == 0 else halved)(parts_of, step)

    def doubled(part, step):
        beside = lax.ppermute(part, "mem", cores if step < 0 else ways[step])
        mine = core if step < 0 else half_of[step]
        return jnp.where(mine == 0, jnp.concatenate([part, beside], axis=1), jnp.concatenate([beside, part], axis=1))

    def gathered(part):
        for step in range(len(ways) - 1, -2, -1):
            part = doubled(part, step)
        return part

    carry = None
    sums, done = [], []
    for k, window in enumerate(windows):
        waits = []
        for j in AHEAD[k]:
            sums[j], left = advanced(sums[j], done[j])
            done[j] += 1
            waits.append(left)
        quarters, carry = window_tensor(window, place, local[k], remotes[k], table, waits, carry)
        first = lax.ppermute(quarters[3], "mem", cores)
        second = lax.ppermute(quarters[2], "mem", cores)
        sums.append([quarters[0], quarters[1], second, first])
        done.append(0)
    pieces = {"own": [], "both": [], "other": []}
    for k, window in enumerate(windows):
        for step in range(done[k], len(ways)):
            sums[k], _ = advanced(sums[k], step)
        pieces[window.side].append(exponent_of(sum(sums[k]), members))

    other = lax.ppermute(jnp.stack(pieces["other"]), "band", swap)
    place_of = {}
    for m in range(members):
        for b in range(2):
            bits = ORDER[m % 2]
            piece = functools.reduce(lambda value, bit: 2 * value + m // bit % 2, bits, m % 2)
            place_of[piece, b] = m * 2 + b
    trades, half = [], members // 2
    for (piece, b), index in place_of.items():
        mate = (piece, b) if (piece < half) == (b == 0) else ((piece + half) % members, 1 - b)
        trades.append((index, place_of[mate]))
    both = lax.ppermute(pieces["both"][0], ("mem", "band"), trades)

    early = gathered(jnp.concatenate([other, both[None]]))
    other, both = early[:-1], early[-1]
    middle = both.shape[0] // 2
    low, high = both[:middle], both[middle:]
    rest = jnp.zeros((nlat // 2 - middle, NLON), jnp.float32)
    down = jnp.stack([jnp.concatenate([rest, low]), jnp.concatenate([*other, high])])
    up = jnp.stack([jnp.concatenate([low, *other[::-1]]), jnp.concatenate([high, rest])])
    out = jnp.where(band == 0, down, up)

    own = gathered(jnp.stack(pieces["own"]))
    for k, block in enumerate(own):
        width = block.shape[0]
        row = choose(band, (nlat // 2 - middle - (k + 1) * width, middle + k * width))
        out = lax.dynamic_update_slice(out, block[None], (band, row.astype(jnp.int32), jnp.int32(0)))
    return out


def per_device(coeffs):
    _, levels, _, _, _, nlat = coeffs.shape
    members = lax.axis_size("mem")
    rows = nlat // lax.axis_size("band")
    fits = coeffs.shape[4] == 5 * LANE // 2 and nlat % (2 * LANE) == LANE and rows > LANE
    if fits and levels == lax.axis_size("band") == 2 and members == 16:
        return by_levels(coeffs)
    return by_rows(coeffs)


def solution(mesh):
    placed = (P("mem", None, None, None, "band", None),)
    return jax.shard_map(
        per_device, mesh=mesh, in_specs=placed, out_specs=P(None, "band", None), check_vma=False
    )
```

```python
import functools
import math

import jax
import jax.numpy as jnp
import ml_dtypes
import numpy as np
from jax import lax
from jax.experimental import pallas as pl
from jax.experimental.pallas import tpu as pltpu
from jax.sharding import PartitionSpec as P

NLON = 1280
STEPS = 1
SUB = 8
LANE = 128
VMEM_LIMIT = 60 * 1024 * 1024
KERNEL_WORK = 8
ORDER = ((2, 4, 8), (4, 2, 8))
AHEAD = ((), (), (0,), (1,), (2, 1, 0))


def padded(cells, sides, width):
    for axis, dim in sides:
        count = lax.axis_size(axis)
        ends = count - 1
        head = lax.slice_in_dim(cells, 0, width, axis=dim)
        tail = lax.slice_in_dim(cells, cells.shape[dim] - width, cells.shape[dim], axis=dim)
        cells = jnp.concatenate(
            [
                lax.ppermute(tail, axis, [(i, (i + 1) % count) for i in range(ends)]),
                cells,
                lax.ppermute(head, axis, [((i + 1) % count, i) for i in range(ends)]),
            ],
            axis=dim,
        )
    return cells


def slope(extended, winds):
    center = extended[:, 1:-1]
    north = (extended[:, 2:] - extended[:, :-2]) * 0.5
    east = (jnp.roll(center, -1, 2) - jnp.roll(center, 1, 2)) * 0.5
    return -winds - (winds[0] * east + winds[1] * north)


def rimmed(field):
    return padded(field, (("band", 1),), 1)


def tensor(extended):
    center = extended[:, 1:-1]
    north = (extended[:, 2:] - extended[:, :-2]) * 0.5
    east = (jnp.roll(center, -1, 2) - jnp.roll(center, 1, 2)) * 0.5
    g_xx = 1.0 + east[0]
    g_xy = north[0]
    g_yx = east[1]
    g_yy = 1.0 + north[1]
    return jnp.stack(
        [g_xx * g_xx + g_yx * g_yx, g_xx * g_xy + g_yx * g_yy, g_xy * g_xy + g_yy * g_yy]
    )


def integrate(shift, flow, extend):
    first = slope(extend(shift), flow)
    second = slope(extend(0.5 * first), flow)
    third = slope(extend(0.5 * second), flow)
    fourth = slope(extend(third), flow)
    return (first + 2.0 * second + 2.0 * third + fourth) / 6.0


def exponent_of(summed, members):
    mean = summed / members
    first, cross, second = (mean[..., 0, :, :], mean[..., 1, :, :], mean[..., 2, :, :])
    half = (first + second) * 0.5
    differ = (first - second) * 0.5
    largest = half + jnp.sqrt(differ * differ + cross * cross)
    return jnp.log(largest + 1e-06) / (2.0 * STEPS)


def by_rows(coeffs):
    spec = coeffs[0]
    levels = spec.shape[0]
    nlat = spec.shape[4]
    waves = spec.shape[3] * lax.axis_size("band")
    members = lax.axis_size("mem")
    stacked = spec.reshape(levels * 2, 2, spec.shape[3], nlat)
    wave_index = lax.iota(jnp.int32, waves)
    column = lax.iota(jnp.int32, NLON)
    phase = wave_index[:, None] * column[None, :] % NLON
    angle = phase.astype(jnp.float32) * (2.0 * math.pi / NLON)
    weight = jnp.where(wave_index == 0, 1.0, 2.0).astype(jnp.float32)[:, None]
    table = jnp.stack([weight * jnp.cos(angle), -weight * jnp.sin(angle)], axis=0)
    winds = jnp.einsum(
        "crwh,rwn->chn",
        lax.all_to_all(stacked, "band", split_axis=3, concat_axis=2, tiled=True),
        table,
        precision=lax.Precision.HIGHEST,
        preferred_element_type=jnp.float32,
    )
    height = winds.shape[1]
    winds = winds.reshape(levels, 2, height, NLON)
    partials = []
    for level in range(levels):
        flow = winds[level]
        shift = integrate(jnp.zeros_like(flow), flow, rimmed)
        partials.append(tensor(rimmed(shift)))
    summed = lax.psum_scatter(jnp.stack(partials), "mem", scatter_dimension=3, tiled=True)
    return lax.all_gather(exponent_of(summed, members), "mem", axis=2, tiled=True)


def by_parity(waves_local):
    half = waves_local // 2
    whole = 2 * LANE - half
    runs = []
    for parity in range(2):
        runs += [(parity, half, 2), (waves_local + parity, whole, 2)]
    for parity in range(2):
        runs.append((waves_local + parity + 2 * whole, half - whole, 2))
    return runs


@functools.lru_cache(maxsize=None)
def wave_table(bands, waves_local):
    order = np.concatenate([start + step * np.arange(count) for start, count, step in by_parity(waves_local)])
    wave, part = order % waves_local, order // waves_local
    wave = wave[None, :] + waves_local * np.arange(bands)[:, None]
    part = np.broadcast_to(part, wave.shape)
    cut = [0, 2 * LANE, 4 * LANE, 4 * LANE + LANE // 2, 5 * LANE]
    result = []
    for parity in range(2):
        picks = [(band, slice(cut[parity], cut[parity + 1])) for band in range(bands)]
        picks += [(band, slice(cut[parity + 2], cut[parity + 3])) for band in range(bands)]
        waves = np.concatenate([wave[pick] for pick in picks])
        parts = np.concatenate([part[pick] for pick in picks])
        phase = (waves[:, None] * np.arange(NLON // 2)[None, :]) % NLON
        angle = phase.astype(np.float64) * (2.0 * np.pi / NLON)
        weight = np.where(waves == 0, 1.0, 2.0)[:, None]
        table = weight * np.where(parts[:, None] == 0, np.cos(angle), -np.sin(angle))
        high = table.astype(ml_dtypes.bfloat16)
        result += [high, (table - high.astype(np.float64)).astype(ml_dtypes.bfloat16)]
    return np.stack(result)


class Window:
    def __init__(self, index, count):
        self.first = index == 0
        self.last = index == count - 1
        self.index = index
        self.width = LANE
        self.extended = LANE + 2 * SUB
        self.main = LANE if self.first else LANE - SUB
        self.rim = 0 if self.last else SUB
        self.rows = self.main + self.rim
        up = SUB if self.first else 2 * SUB
        self.place = (self.extended - up - self.rows, up)
        self.side = "other" if 2 * (index + 1) <= count else "own" if 2 * index >= count else "both"


def choose(band, pair):
    return jnp.where(band == 0, pair[0], pair[1])


def multiple(value, of):
    return pl.multiple_of(value.astype(jnp.int32), of)


def pieces_kernel(windows, slots, count, level_ref, spec_ref, *refs):
    out_refs, (taken, turned, in_sems, out_sems) = refs[: len(windows)], refs[len(windows) :]
    level = level_ref[0]
    runs = by_parity(spec_ref.shape[2] // 2)

    def arrival(c, n):
        tile = choose(level, (count - 1 - slots[n], slots[n]))
        lanes = pl.ds(multiple(tile * LANE, LANE), LANE)
        return pltpu.make_async_copy(spec_ref.at[level, c, :, lanes], taken.at[c, n], in_sems.at[c, n])

    def departures(c, k):
        window, n = windows[k], slots.index(windows[k].index)
        rows = pl.ds(multiple(choose(level, (0, LANE - window.main)), SUB), window.main)
        at = pl.ds(multiple(choose(level, (window.rim, 0)), SUB), window.main)
        yield pltpu.make_async_copy(turned.at[c, n, rows], out_refs[k].at[c, at], out_sems.at[k, c, 0])
        if window.rim:
            rows = pl.ds(multiple(choose(level, (LANE - SUB, 0)), SUB), SUB)
            at = pl.ds(multiple(choose(level, (0, window.main)), SUB), SUB)
            yield pltpu.make_async_copy(turned.at[c, n + 1, rows], out_refs[k].at[c, at], out_sems.at[k, c, 1])

    for n in range(len(slots)):
        for c in range(2):
            arrival(c, n).start()
    for n in range(len(slots)):
        for c in range(2):
            arrival(c, n).wait()
            turned[c, n] = jnp.concatenate([taken[c, n, pl.ds(start, rows, step), :] for start, rows, step in runs]).T
        for k, window in enumerate(windows):
            if slots[n] == window.index + (1 if window.rim else 0):
                for c in range(2):
                    for copy in departures(c, k):
                        copy.start()
    for k in range(len(windows)):
        for c in range(2):
            for copy in departures(c, k):
                copy.wait()


def pieces_of(spec, level, windows, count):
    depth = spec.shape[2]
    slots = sorted({w.index for w in windows} | {w.index + 1 for w in windows if w.rim})
    return pl.pallas_call(
        functools.partial(pieces_kernel, windows, slots, count),
        in_specs=[pl.BlockSpec(memory_space=pltpu.SMEM), pl.BlockSpec(memory_space=pl.ANY)],
        out_specs=[pl.BlockSpec(memory_space=pl.ANY)] * len(windows),
        out_shape=[jax.ShapeDtypeStruct((2, w.rows, depth), jnp.float32) for w in windows],
        scratch_shapes=[
            pltpu.VMEM((2, len(slots), depth, LANE), jnp.float32),
            pltpu.VMEM((2, len(slots), LANE, depth), jnp.float32),
            pltpu.SemaphoreType.DMA((2, len(slots))),
            pltpu.SemaphoreType.DMA((len(windows), 2, 2)),
        ],
        compiler_params=pltpu.CompilerParams(vmem_limit_bytes=VMEM_LIMIT),
        cost_estimate=pl.CostEstimate(
            flops=0, transcendentals=0, bytes_accessed=4 * 2 * len(slots) * LANE * depth * 4
        ),
        name="pieces_of",
    )(level.reshape(1), spec)


def gate_kernel(*refs):
    pass


def gated(part, waits):
    return pl.pallas_call(
        gate_kernel,
        in_specs=[pl.BlockSpec(memory_space=pl.ANY)] * (1 + len(waits)),
        out_specs=pl.BlockSpec(memory_space=pl.ANY),
        out_shape=jax.ShapeDtypeStruct(part.shape, part.dtype),
        input_output_aliases={0: 0},
        cost_estimate=pl.CostEstimate(flops=0, transcendentals=0, bytes_accessed=1024),
        name="gated",
    )(part, *waits)


def east_of(x):
    return pltpu.roll(x, NLON - 1, axis=1) - pltpu.roll(x, 1, axis=1)


def north_of(before, here, after):
    row = lax.broadcasted_iota(jnp.int32, here.shape, 0)
    above = jnp.where(row == SUB - 1, pltpu.roll(after, SUB - 1, axis=0), pltpu.roll(here, SUB - 1, axis=0))
    below = jnp.where(row == 0, pltpu.roll(before, 1, axis=0), pltpu.roll(here, 1, axis=0))
    return above - below


def window_kernel(window, waits, *refs):
    refs = list(refs)
    place_ref, local_ref, remote_ref, table_ref = refs[:4]
    refs = refs[4 + waits :]
    carry_ref = None if window.first else refs.pop(0)
    out_refs = [refs.pop(0) for _ in range(4)]
    carried_ref = None if window.last else refs.pop(0)
    table, mine_buf, theirs_buf, lhs_high, lhs_low, wind, second, third, shift, results, carried, in_sems, out_sems = refs
    band, core, sides = place_ref[0], place_ref[1], (place_ref[2], place_ref[3])
    rows, extended = window.rows, window.extended

    def at(pair):
        return multiple(choose(band, pair), SUB)

    inputs = [pltpu.make_async_copy(local_ref, mine_buf, in_sems.at[0])]
    inputs.append(pltpu.make_async_copy(remote_ref, theirs_buf, in_sems.at[1]))
    tables = pltpu.make_async_copy(table_ref, table, in_sems.at[2])
    if not window.first:
        rows_before = wind.at[:, pl.ds(at((extended - 2 * SUB, 0)), 2 * SUB)]
        inputs.append(pltpu.make_async_copy(carry_ref, rows_before, in_sems.at[3]))
    for copy in [*inputs, tables]:
        copy.start()
    for copy in inputs:
        copy.wait()
    lane = lax.broadcasted_iota(jnp.int32, (rows, LANE), 1)
    even, odd = [], []
    for c in range(2):
        mine, theirs = mine_buf[c], theirs_buf[c]
        low, high = jnp.where(band == 0, mine, theirs), jnp.where(band == 0, theirs, mine)
        low_rest, high_rest = low[:, 4 * LANE :], high[:, 4 * LANE :]
        turn = functools.partial(pltpu.roll, shift=LANE // 2, axis=1)
        even_rest = jnp.where(lane < LANE // 2, low_rest, turn(high_rest))
        odd_rest = jnp.where(lane < LANE // 2, turn(low_rest), high_rest)
        even.append(jnp.concatenate([low[:, : 2 * LANE], high[:, : 2 * LANE], even_rest], axis=1))
        odd.append(jnp.concatenate([low[:, 2 * LANE : 4 * LANE], high[:, 2 * LANE : 4 * LANE], odd_rest], axis=1))
    for parity, parts in enumerate((even, odd)):
        lhs = jnp.concatenate(parts)
        lhs_high[parity] = lhs.astype(jnp.bfloat16)
        lhs_low[parity] = (lhs - lhs_high[parity].astype(jnp.float32)).astype(jnp.bfloat16)

    place = at(window.place)
    if window.first or window.last:
        for c in range(2):
            if window.first:
                wind[c, pl.ds(at((extended - SUB, 0)), SUB), :] = jnp.zeros((SUB, NLON), jnp.float32)
            if window.last:
                wind[c, pl.ds(at((0, extended - SUB)), SUB), :] = jnp.zeros((SUB, NLON), jnp.float32)
    tables.wait()

    dot = functools.partial(jnp.dot, preferred_element_type=jnp.float32)
    for start in range(0, NLON // 2, 2 * LANE):
        stop = min(start + 2 * LANE, NLON // 2)
        columns = slice(start, stop)
        sums = []
        for parity in range(2):
            total = dot(lhs_high[parity], table[2 * parity, :, columns])
            total += dot(lhs_low[parity], table[2 * parity, :, columns])
            total += dot(lhs_high[parity], table[2 * parity + 1, :, columns])
            sums.append(total)
        for c in range(2):
            even_sum, odd_sum = (total[c * rows : (c + 1) * rows] for total in sums)
            wind[c, pl.ds(place, rows), start:stop] = even_sum + odd_sum
            wind[c, pl.ds(place, rows), NLON // 2 + start : NLON // 2 + stop] = even_sum - odd_sum

    if not window.last:
        for c in range(2):
            carried[c] = wind[c, pl.ds(at((0, extended - 2 * SUB)), 2 * SUB), :]
        carry_on = pltpu.make_async_copy(carried, carried_ref, out_sems.at[4])
        carry_on.start()

    blocks = extended // SUB

    def rows_of(block):
        return pl.ds(pl.multiple_of(block * SUB, SUB), SUB)

    def derivatives(field, block):
        before, after = jnp.maximum(block - 1, 0), jnp.minimum(block + 1, blocks - 1)
        result = []
        for c in range(2):
            here = field[c, rows_of(block), :]
            result.append((east_of(here), north_of(field[c, rows_of(before), :], here, field[c, rows_of(after), :])))
        return result

    @pl.loop(0, blocks, unroll=9)
    def _(block):
        flow = [wind[c, rows_of(block), :] for c in range(2)]
        for c, (east, north) in enumerate(derivatives(wind, block)):
            second[c, rows_of(block), :] = 0.25 * (flow[0] * east + flow[1] * north) - flow[c]

    @pl.loop(0, blocks, unroll=9)
    def _(block):
        flow = [wind[c, rows_of(block), :] for c in range(2)]
        for c, (east, north) in enumerate(derivatives(second, block)):
            third[c, rows_of(block), :] = -flow[c] - 0.25 * (flow[0] * east + flow[1] * north)

    @pl.loop(0, blocks, unroll=9)
    def _(block):
        flow = [wind[c, rows_of(block), :] for c in range(2)]
        for c, (east, north) in enumerate(derivatives(third, block)):
            fourth = -flow[c] - 0.5 * (flow[0] * east + flow[1] * north)
            both = second[c, rows_of(block), :] + third[c, rows_of(block), :]
            shift[c, rows_of(block), :] = (2.0 * both + (fourth - flow[c])) * (1.0 / 6.0)

    quarter = window.width // 4 // SUB

    def entries(out, base):
        @pl.loop(0, quarter, unroll=4)
        def _(block):
            (e0, n0), (e1, n1) = derivatives(shift, base + block + 1)
            g_xx, g_xy, g_yx, g_yy = 1.0 + 0.5 * e0, 0.5 * n0, 0.5 * e1, 1.0 + 0.5 * n1
            out[0, rows_of(block), :] = g_xx * g_xx + g_yx * g_yx
            out[1, rows_of(block), :] = g_xx * g_xy + g_yx * g_yy
            out[2, rows_of(block), :] = g_xy * g_xy + g_yy * g_yy

    copies = []
    for n, (a, b) in reversed(list(enumerate(QUARTERS))):
        side = sides[a]
        entries(results.at[n], (2 * (core + a - 2 * core * a) + (side + b - 2 * side * b)) * quarter)
        copies.append(pltpu.make_async_copy(results.at[n], out_refs[n], out_sems.at[n]))
        copies[-1].start()
    for copy in copies:
        copy.wait()
    if not window.last:
        carry_on.wait()


QUARTERS = ((0, 0), (0, 1), (1, 0), (1, 1))


def window_tensor(window, place, local, remote, table, waits, carry):
    depth = local.shape[2]
    operands = [place, local, remote, table, *waits]
    if not window.first:
        operands.append(carry)
    in_specs = [pl.BlockSpec(memory_space=pltpu.SMEM)] + [pl.BlockSpec(memory_space=pl.ANY)] * (len(operands) - 1)
    out_shape = [jax.ShapeDtypeStruct((3, window.width // 4, NLON), jnp.float32)] * 4
    if not window.last:
        out_shape.append(jax.ShapeDtypeStruct((2, 2 * SUB, NLON), jnp.float32))
    field = pltpu.VMEM((2, window.extended, NLON), jnp.float32)
    lhs_shape = (2, 2 * window.rows, depth)
    out = pl.pallas_call(
        functools.partial(window_kernel, window, len(waits)),
        out_shape=out_shape,
        in_specs=in_specs,
        out_specs=[pl.BlockSpec(memory_space=pl.ANY)] * len(out_shape),
        scratch_shapes=[
            pltpu.VMEM(table.shape, table.dtype),
            pltpu.VMEM(local.shape, jnp.float32),
            pltpu.VMEM(local.shape, jnp.float32),
            pltpu.VMEM(lhs_shape, jnp.bfloat16),
            pltpu.VMEM(lhs_shape, jnp.bfloat16),
            field,
            field,
            field,
            field,
            pltpu.VMEM((4, 3, window.width // 4, NLON), jnp.float32),
            pltpu.VMEM((2, 2 * SUB, NLON), jnp.float32),
            pltpu.SemaphoreType.DMA((4,)),
            pltpu.SemaphoreType.DMA((5,)),
        ],
        compiler_params=pltpu.CompilerParams(vmem_limit_bytes=VMEM_LIMIT),
        cost_estimate=pl.CostEstimate(
            flops=KERNEL_WORK * 3 * 2 * 2 * window.rows * depth * NLON,
            transcendentals=0,
            bytes_accessed=2 * table.size + 4 * window.rows * depth * 4 + 12 * window.width * NLON,
        ),
        name="window_tensor",
    )(*operands)
    return out[:4], (None if window.last else out[4])


def by_levels(coeffs):
    spec = coeffs[0]
    levels, _, parts, waves_local, nlat = spec.shape
    members = lax.axis_size("mem")
    band = lax.axis_index("band").astype(jnp.int32)
    member = lax.axis_index("mem").astype(jnp.int32)
    core = member % 2
    half_of = [choose(core, [member // bits[step] % 2 for bits in ORDER]) for step in range(len(ORDER[0]))]
    half_beside = choose(1 - core, [member // bits[0] % 2 for bits in ORDER])
    place = jnp.stack([band, core, half_of[0], half_beside])
    spec = spec.reshape(levels, 2, parts * waves_local, nlat)
    count = nlat // LANE
    windows = [Window(k, count) for k in range(count)]
    table = jnp.asarray(wave_table(levels, waves_local))
    swap = [(0, 1), (1, 0)]

    (piece,) = pieces_of(spec, 1 - band, windows[:1], count)
    remotes = [lax.ppermute(piece, "band", swap)]
    for k, piece in enumerate(pieces_of(spec, 1 - band, windows[1:], count), 1):
        if k > 1:
            piece = gated(piece, [remotes[k - 2]])
        remotes.append(lax.ppermute(piece, "band", swap))
    local = pieces_of(spec, band, windows, count)

    cores = [(m, m ^ 1) for m in range(members)]
    ways = [[(m, m ^ ORDER[m % 2][step]) for m in range(members)] for step in range(len(ORDER[0]))]

    def halved(parts_of, step):
        half = parts_of[0].shape[1] // 2
        mine = half_of[step]

        def total(which):
            return sum(lax.dynamic_slice_in_dim(part, which * half, half, axis=1) for part in parts_of)

        leaves = total(1 - mine)
        return [total(mine), lax.ppermute(leaves, "mem", ways[step])], leaves

    def across(parts_of, step):
        kept, passed, kept_more, passed_more = parts_of
        leaves = passed + passed_more
        return [kept, kept_more, lax.ppermute(leaves, "mem", ways[step])], leaves

    def advanced(parts_of, step):
        return (across if step == 0 else halved)(parts_of, step)

    def doubled(part, step):
        beside = lax.ppermute(part, "mem", cores if step < 0 else ways[step])
        mine = core if step < 0 else half_of[step]
        return jnp.where(mine == 0, jnp.concatenate([part, beside], axis=1), jnp.concatenate([beside, part], axis=1))

    def gathered(part):
        for step in range(len(ways) - 1, -2, -1):
            part = doubled(part, step)
        return part

    carry = None
    sums, done = [], []
    for k, window in enumerate(windows):
        waits = []
        for j in AHEAD[k]:
            sums[j], left = advanced(sums[j], done[j])
            done[j] += 1
            waits.append(left)
        quarters, carry = window_tensor(window, place, local[k], remotes[k], table, waits, carry)
        first = lax.ppermute(quarters[3], "mem", cores)
        second = lax.ppermute(quarters[2], "mem", cores)
        sums.append([quarters[0], quarters[1], second, first])
        done.append(0)
    pieces = {"own": [], "both": [], "other": []}
    for k, window in enumerate(windows):
        for step in range(done[k], len(ways)):
            sums[k], _ = advanced(sums[k], step)
        pieces[window.side].append(exponent_of(sum(sums[k]), members))

    other = lax.ppermute(jnp.stack(pieces["other"]), "band", swap)
    place_of = {}
    for m in range(members):
        for b in range(2):
            bits = ORDER[m % 2]
            piece = functools.reduce(lambda value, bit: 2 * value + m // bit % 2, bits, m % 2)
            place_of[piece, b] = m * 2 + b
    trades, half = [], members // 2
    for (piece, b), index in place_of.items():
        mate = (piece, b) if (piece < half) == (b == 0) else ((piece + half) % members, 1 - b)
        trades.append((index, place_of[mate]))
    both = lax.ppermute(pieces["both"][0], ("mem", "band"), trades)

    early = gathered(jnp.concatenate([other, both[None]]))
    other, both = early[:-1], early[-1]
    middle = both.shape[0] // 2
    low, high = both[:middle], both[middle:]
    rest = jnp.zeros((nlat // 2 - middle, NLON), jnp.float32)
    down = jnp.stack([jnp.concatenate([rest, low]), jnp.concatenate([*other, high])])
    up = jnp.stack([jnp.concatenate([low, *other[::-1]]), jnp.concatenate([high, rest])])
    out = jnp.where(band == 0, down, up)

    own = gathered(jnp.stack(pieces["own"]))
    for k, block in enumerate(own):
        width = block.shape[0]
        row = choose(band, (nlat // 2 - middle - (k + 1) * width, middle + k * width))
        out = lax.dynamic_update_slice(out, block[None], (band, row.astype(jnp.int32), jnp.int32(0)))
    return out


def per_device(coeffs):
    _, levels, _, _, _, nlat = coeffs.shape
    members = lax.axis_size("mem")
    rows = nlat // lax.axis_size("band")
    fits = coeffs.shape[4] == 5 * LANE // 2 and nlat % (2 * LANE) == LANE and rows > LANE
    if fits and levels == lax.axis_size("band") == 2 and members == 16:
        return by_levels(coeffs)
    return by_rows(coeffs)


def solution(mesh):
    placed = (P("mem", None, None, None, "band", None),)
    return jax.shard_map(
        per_device, mesh=mesh, in_specs=placed, out_specs=P(None, "band", None), check_vma=False
    )
```

```python
import functools
import math

import jax
import jax.numpy as jnp
import ml_dtypes
import numpy as np
from jax import lax
from jax.experimental import pallas as pl
from jax.experimental.pallas import tpu as pltpu
from jax.sharding import PartitionSpec as P

NLON = 1280
STEPS = 1
SUB = 8
LANE = 128
VMEM_LIMIT = 60 * 1024 * 1024
KERNEL_WORK = 8
ORDER = ((2, 4, 8), (4, 2, 8))
AHEAD = ((), (), (0,), (1,), (2, 1, 0))


def padded(cells, sides, width):
    for axis, dim in sides:
        count = lax.axis_size(axis)
        ends = count - 1
        head = lax.slice_in_dim(cells, 0, width, axis=dim)
        tail = lax.slice_in_dim(cells, cells.shape[dim] - width, cells.shape[dim], axis=dim)
        cells = jnp.concatenate(
            [
                lax.ppermute(tail, axis, [(i, (i + 1) % count) for i in range(ends)]),
                cells,
                lax.ppermute(head, axis, [((i + 1) % count, i) for i in range(ends)]),
            ],
            axis=dim,
        )
    return cells


def slope(extended, winds):
    center = extended[:, 1:-1]
    north = (extended[:, 2:] - extended[:, :-2]) * 0.5
    east = (jnp.roll(center, -1, 2) - jnp.roll(center, 1, 2)) * 0.5
    return -winds - (winds[0] * east + winds[1] * north)


def rimmed(field):
    return padded(field, (("band", 1),), 1)


def tensor(extended):
    center = extended[:, 1:-1]
    north = (extended[:, 2:] - extended[:, :-2]) * 0.5
    east = (jnp.roll(center, -1, 2) - jnp.roll(center, 1, 2)) * 0.5
    g_xx = 1.0 + east[0]
    g_xy = north[0]
    g_yx = east[1]
    g_yy = 1.0 + north[1]
    return jnp.stack(
        [g_xx * g_xx + g_yx * g_yx, g_xx * g_xy + g_yx * g_yy, g_xy * g_xy + g_yy * g_yy]
    )


def integrate(shift, flow, extend):
    first = slope(extend(shift), flow)
    second = slope(extend(0.5 * first), flow)
    third = slope(extend(0.5 * second), flow)
    fourth = slope(extend(third), flow)
    return (first + 2.0 * second + 2.0 * third + fourth) / 6.0


def exponent_of(summed, members):
    mean = summed / members
    first, cross, second = (mean[..., 0, :, :], mean[..., 1, :, :], mean[..., 2, :, :])
    half = (first + second) * 0.5
    differ = (first - second) * 0.5
    largest = half + jnp.sqrt(differ * differ + cross * cross)
    return jnp.log(largest + 1e-06) / (2.0 * STEPS)


def by_rows(coeffs):
    spec = coeffs[0]
    levels = spec.shape[0]
    nlat = spec.shape[4]
    waves = spec.shape[3] * lax.axis_size("band")
    members = lax.axis_size("mem")
    stacked = spec.reshape(levels * 2, 2, spec.shape[3], nlat)
    wave_index = lax.iota(jnp.int32, waves)
    column = lax.iota(jnp.int32, NLON)
    phase = wave_index[:, None] * column[None, :] % NLON
    angle = phase.astype(jnp.float32) * (2.0 * math.pi / NLON)
    weight = jnp.where(wave_index == 0, 1.0, 2.0).astype(jnp.float32)[:, None]
    table = jnp.stack([weight * jnp.cos(angle), -weight * jnp.sin(angle)], axis=0)
    winds = jnp.einsum(
        "crwh,rwn->chn",
        lax.all_to_all(stacked, "band", split_axis=3, concat_axis=2, tiled=True),
        table,
        precision=lax.Precision.HIGHEST,
        preferred_element_type=jnp.float32,
    )
    height = winds.shape[1]
    winds = winds.reshape(levels, 2, height, NLON)
    partials = []
    for level in range(levels):
        flow = winds[level]
        shift = integrate(jnp.zeros_like(flow), flow, rimmed)
        partials.append(tensor(rimmed(shift)))
    summed = lax.psum_scatter(jnp.stack(partials), "mem", scatter_dimension=3, tiled=True)
    return lax.all_gather(exponent_of(summed, members), "mem", axis=2, tiled=True)


def by_parity(waves_local):
    half = waves_local // 2
    whole = 2 * LANE - half
    runs = []
    for parity in range(2):
        runs += [(parity, half, 2), (waves_local + parity, whole, 2)]
    for parity in range(2):
        runs.append((waves_local + parity + 2 * whole, half - whole, 2))
    return runs


@functools.lru_cache(maxsize=None)
def wave_table(bands, waves_local):
    order = np.concatenate([start + step * np.arange(count) for start, count, step in by_parity(waves_local)])
    wave, part = order % waves_local, order // waves_local
    wave = wave[None, :] + waves_local * np.arange(bands)[:, None]
    part = np.broadcast_to(part, wave.shape)
    cut = [0, 2 * LANE, 4 * LANE, 4 * LANE + LANE // 2, 5 * LANE]
    result = []
    for parity in range(2):
        picks = [(band, slice(cut[parity], cut[parity + 1])) for band in range(bands)]
        picks += [(band, slice(cut[parity + 2], cut[parity + 3])) for band in range(bands)]
        waves = np.concatenate([wave[pick] for pick in picks])
        parts = np.concatenate([part[pick] for pick in picks])
        phase = (waves[:, None] * np.arange(NLON // 2)[None, :]) % NLON
        angle = phase.astype(np.float64) * (2.0 * np.pi / NLON)
        weight = np.where(waves == 0, 1.0, 2.0)[:, None]
        table = weight * np.where(parts[:, None] == 0, np.cos(angle), -np.sin(angle))
        high = table.astype(ml_dtypes.bfloat16)
        result += [high, (table - high.astype(np.float64)).astype(ml_dtypes.bfloat16)]
    return np.stack(result)


class Window:
    def __init__(self, index, count):
        self.first = index == 0
        self.last = index == count - 1
        self.index = index
        self.width = LANE
        self.extended = LANE + 2 * SUB
        self.main = LANE if self.first else LANE - SUB
        self.rim = 0 if self.last else SUB
        self.rows = self.main + self.rim
        up = SUB if self.first else 2 * SUB
        self.place = (self.extended - up - self.rows, up)
        self.side = "other" if 2 * (index + 1) <= count else "own" if 2 * index >= count else "both"


def choose(band, pair):
    return jnp.where(band == 0, pair[0], pair[1])


def multiple(value, of):
    return pl.multiple_of(value.astype(jnp.int32), of)


def pieces_kernel(windows, slots, count, level_ref, spec_ref, *refs):
    out_refs, (taken, turned, in_sems, out_sems) = refs[: len(windows)], refs[len(windows) :]
    level = level_ref[0]
    runs = by_parity(spec_ref.shape[2] // 2)

    def arrival(c, n):
        tile = choose(level, (count - 1 - slots[n], slots[n]))
        lanes = pl.ds(multiple(tile * LANE, LANE), LANE)
        return pltpu.make_async_copy(spec_ref.at[level, c, :, lanes], taken.at[c, n], in_sems.at[c, n])

    def departures(c, k):
        window, n = windows[k], slots.index(windows[k].index)
        rows = pl.ds(multiple(choose(level, (0, LANE - window.main)), SUB), window.main)
        at = pl.ds(multiple(choose(level, (window.rim, 0)), SUB), window.main)
        yield pltpu.make_async_copy(turned.at[c, n, rows], out_refs[k].at[c, at], out_sems.at[k, c, 0])
        if window.rim:
            rows = pl.ds(multiple(choose(level, (LANE - SUB, 0)), SUB), SUB)
            at = pl.ds(multiple(choose(level, (0, window.main)), SUB), SUB)
            yield pltpu.make_async_copy(turned.at[c, n + 1, rows], out_refs[k].at[c, at], out_sems.at[k, c, 1])

    for n in range(len(slots)):
        for c in range(2):
            arrival(c, n).start()
    for n in range(len(slots)):
        for c in range(2):
            arrival(c, n).wait()
            turned[c, n] = jnp.concatenate([taken[c, n, pl.ds(start, rows, step), :] for start, rows, step in runs]).T
        for k, window in enumerate(windows):
            if slots[n] == window.index + (1 if window.rim else 0):
                for c in range(2):
                    for copy in departures(c, k):
                        copy.start()
    for k in range(len(windows)):
        for c in range(2):
            for copy in departures(c, k):
                copy.wait()


def pieces_of(spec, level, windows, count):
    depth = spec.shape[2]
    slots = sorted({w.index for w in windows} | {w.index + 1 for w in windows if w.rim})
    return pl.pallas_call(
        functools.partial(pieces_kernel, windows, slots, count),
        in_specs=[pl.BlockSpec(memory_space=pltpu.SMEM), pl.BlockSpec(memory_space=pl.ANY)],
        out_specs=[pl.BlockSpec(memory_space=pl.ANY)] * len(windows),
        out_shape=[jax.ShapeDtypeStruct((2, w.rows, depth), jnp.float32) for w in windows],
        scratch_shapes=[
            pltpu.VMEM((2, len(slots), depth, LANE), jnp.float32),
            pltpu.VMEM((2, len(slots), LANE, depth), jnp.float32),
            pltpu.SemaphoreType.DMA((2, len(slots))),
            pltpu.SemaphoreType.DMA((len(windows), 2, 2)),
        ],
        compiler_params=pltpu.CompilerParams(vmem_limit_bytes=VMEM_LIMIT),
        cost_estimate=pl.CostEstimate(
            flops=0, transcendentals=0, bytes_accessed=4 * 2 * len(slots) * LANE * depth * 4
        ),
        name="pieces_of",
    )(level.reshape(1), spec)


def gate_kernel(*refs):
    pass


def gated(part, waits):
    return pl.pallas_call(
        gate_kernel,
        in_specs=[pl.BlockSpec(memory_space=pl.ANY)] * (1 + len(waits)),
        out_specs=pl.BlockSpec(memory_space=pl.ANY),
        out_shape=jax.ShapeDtypeStruct(part.shape, part.dtype),
        input_output_aliases={0: 0},
        cost_estimate=pl.CostEstimate(flops=0, transcendentals=0, bytes_accessed=1024),
        name="gated",
    )(part, *waits)


def east_of(x):
    return pltpu.roll(x, NLON - 1, axis=1) - pltpu.roll(x, 1, axis=1)


def north_of(before, here, after):
    row = lax.broadcasted_iota(jnp.int32, here.shape, 0)
    above = jnp.where(row == SUB - 1, pltpu.roll(after, SUB - 1, axis=0), pltpu.roll(here, SUB - 1, axis=0))
    below = jnp.where(row == 0, pltpu.roll(before, 1, axis=0), pltpu.roll(here, 1, axis=0))
    return above - below


def window_kernel(window, waits, *refs):
    refs = list(refs)
    place_ref, local_ref, remote_ref, table_ref = refs[:4]
    refs = refs[4 + waits :]
    carry_ref = None if window.first else refs.pop(0)
    out_refs = [refs.pop(0) for _ in range(4)]
    carried_ref = None if window.last else refs.pop(0)
    table, mine_buf, theirs_buf, lhs_high, lhs_low, wind, second, third, shift, results, carried, in_sems, out_sems = refs
    band, core, sides = place_ref[0], place_ref[1], (place_ref[2], place_ref[3])
    rows, extended = window.rows, window.extended

    def at(pair):
        return multiple(choose(band, pair), SUB)

    inputs = [pltpu.make_async_copy(local_ref, mine_buf, in_sems.at[0])]
    inputs.append(pltpu.make_async_copy(remote_ref, theirs_buf, in_sems.at[1]))
    tables = pltpu.make_async_copy(table_ref, table, in_sems.at[2])
    if not window.first:
        rows_before = wind.at[:, pl.ds(at((extended - 2 * SUB, 0)), 2 * SUB)]
        inputs.append(pltpu.make_async_copy(carry_ref, rows_before, in_sems.at[3]))
    for copy in [*inputs, tables]:
        copy.start()
    for copy in inputs:
        copy.wait()
    lane = lax.broadcasted_iota(jnp.int32, (rows, LANE), 1)
    even, odd = [], []
    for c in range(2):
        mine, theirs = mine_buf[c], theirs_buf[c]
        low, high = jnp.where(band == 0, mine, theirs), jnp.where(band == 0, theirs, mine)
        low_rest, high_rest = low[:, 4 * LANE :], high[:, 4 * LANE :]
        turn = functools.partial(pltpu.roll, shift=LANE // 2, axis=1)
        even_rest = jnp.where(lane < LANE // 2, low_rest, turn(high_rest))
        odd_rest = jnp.where(lane < LANE // 2, turn(low_rest), high_rest)
        even.append(jnp.concatenate([low[:, : 2 * LANE], high[:, : 2 * LANE], even_rest], axis=1))
        odd.append(jnp.concatenate([low[:, 2 * LANE : 4 * LANE], high[:, 2 * LANE : 4 * LANE], odd_rest], axis=1))
    for parity, parts in enumerate((even, odd)):
        lhs = jnp.concatenate(parts)
        lhs_high[parity] = lhs.astype(jnp.bfloat16)
        lhs_low[parity] = (lhs - lhs_high[parity].astype(jnp.float32)).astype(jnp.bfloat16)

    place = at(window.place)
    if window.first or window.last:
        for c in range(2):
            if window.first:
                wind[c, pl.ds(at((extended - SUB, 0)), SUB), :] = jnp.zeros((SUB, NLON), jnp.float32)
            if window.last:
                wind[c, pl.ds(at((0, extended - SUB)), SUB), :] = jnp.zeros((SUB, NLON), jnp.float32)
    tables.wait()

    dot = functools.partial(jnp.dot, preferred_element_type=jnp.float32)
    for start in range(0, NLON // 2, 2 * LANE):
        stop = min(start + 2 * LANE, NLON // 2)
        columns = slice(start, stop)
        sums = []
        for parity in range(2):
            total = dot(lhs_high[parity], table[2 * parity, :, columns])
            total += dot(lhs_low[parity], table[2 * parity, :, columns])
            total += dot(lhs_high[parity], table[2 * parity + 1, :, columns])
            sums.append(total)
        for c in range(2):
            even_sum, odd_sum = (total[c * rows : (c + 1) * rows] for total in sums)
            wind[c, pl.ds(place, rows), start:stop] = even_sum + odd_sum
            wind[c, pl.ds(place, rows), NLON // 2 + start : NLON // 2 + stop] = even_sum - odd_sum

    if not window.last:
        for c in range(2):
            carried[c] = wind[c, pl.ds(at((0, extended - 2 * SUB)), 2 * SUB), :]
        carry_on = pltpu.make_async_copy(carried, carried_ref, out_sems.at[4])
        carry_on.start()

    blocks = extended // SUB

    def rows_of(block):
        return pl.ds(pl.multiple_of(block * SUB, SUB), SUB)

    def derivatives(field, block):
        before, after = jnp.maximum(block - 1, 0), jnp.minimum(block + 1, blocks - 1)
        result = []
        for c in range(2):
            here = field[c, rows_of(block), :]
            result.append((east_of(here), north_of(field[c, rows_of(before), :], here, field[c, rows_of(after), :])))
        return result

    @pl.loop(0, blocks, unroll=9)
    def _(block):
        flow = [wind[c, rows_of(block), :] for c in range(2)]
        for c, (east, north) in enumerate(derivatives(wind, block)):
            second[c, rows_of(block), :] = 0.25 * (flow[0] * east + flow[1] * north) - flow[c]

    @pl.loop(0, blocks, unroll=9)
    def _(block):
        flow = [wind[c, rows_of(block), :] for c in range(2)]
        for c, (east, north) in enumerate(derivatives(second, block)):
            third[c, rows_of(block), :] = -flow[c] - 0.25 * (flow[0] * east + flow[1] * north)

    @pl.loop(0, blocks, unroll=9)
    def _(block):
        flow = [wind[c, rows_of(block), :] for c in range(2)]
        for c, (east, north) in enumerate(derivatives(third, block)):
            fourth = -flow[c] - 0.5 * (flow[0] * east + flow[1] * north)
            both = second[c, rows_of(block), :] + third[c, rows_of(block), :]
            shift[c, rows_of(block), :] = (2.0 * both + (fourth - flow[c])) * (1.0 / 6.0)

    quarter = window.width // 4 // SUB

    def entries(out, base):
        @pl.loop(0, quarter, unroll=4)
        def _(block):
            (e0, n0), (e1, n1) = derivatives(shift, base + block + 1)
            g_xx, g_xy, g_yx, g_yy = 1.0 + 0.5 * e0, 0.5 * n0, 0.5 * e1, 1.0 + 0.5 * n1
            out[0, rows_of(block), :] = g_xx * g_xx + g_yx * g_yx
            out[1, rows_of(block), :] = g_xx * g_xy + g_yx * g_yy
            out[2, rows_of(block), :] = g_xy * g_xy + g_yy * g_yy

    copies = []
    for n, (a, b) in reversed(list(enumerate(QUARTERS))):
        side = sides[a]
        entries(results.at[n], (2 * (core + a - 2 * core * a) + (side + b - 2 * side * b)) * quarter)
        copies.append(pltpu.make_async_copy(results.at[n], out_refs[n], out_sems.at[n]))
        copies[-1].start()
    for copy in copies:
        copy.wait()
    if not window.last:
        carry_on.wait()


QUARTERS = ((0, 0), (0, 1), (1, 0), (1, 1))


def window_tensor(window, place, local, remote, table, waits, carry):
    depth = local.shape[2]
    operands = [place, local, remote, table, *waits]
    if not window.first:
        operands.append(carry)
    in_specs = [pl.BlockSpec(memory_space=pltpu.SMEM)] + [pl.BlockSpec(memory_space=pl.ANY)] * (len(operands) - 1)
    out_shape = [jax.ShapeDtypeStruct((3, window.width // 4, NLON), jnp.float32)] * 4
    if not window.last:
        out_shape.append(jax.ShapeDtypeStruct((2, 2 * SUB, NLON), jnp.float32))
    field = pltpu.VMEM((2, window.extended, NLON), jnp.float32)
    lhs_shape = (2, 2 * window.rows, depth)
    out = pl.pallas_call(
        functools.partial(window_kernel, window, len(waits)),
        out_shape=out_shape,
        in_specs=in_specs,
        out_specs=[pl.BlockSpec(memory_space=pl.ANY)] * len(out_shape),
        scratch_shapes=[
            pltpu.VMEM(table.shape, table.dtype),
            pltpu.VMEM(local.shape, jnp.float32),
            pltpu.VMEM(local.shape, jnp.float32),
            pltpu.VMEM(lhs_shape, jnp.bfloat16),
            pltpu.VMEM(lhs_shape, jnp.bfloat16),
            field,
            field,
            field,
            field,
            pltpu.VMEM((4, 3, window.width // 4, NLON), jnp.float32),
            pltpu.VMEM((2, 2 * SUB, NLON), jnp.float32),
            pltpu.SemaphoreType.DMA((4,)),
            pltpu.SemaphoreType.DMA((5,)),
        ],
        compiler_params=pltpu.CompilerParams(vmem_limit_bytes=VMEM_LIMIT),
        cost_estimate=pl.CostEstimate(
            flops=KERNEL_WORK * 3 * 2 * 2 * window.rows * depth * NLON,
            transcendentals=0,
            bytes_accessed=2 * table.size + 4 * window.rows * depth * 4 + 12 * window.width * NLON,
        ),
        name="window_tensor",
    )(*operands)
    return out[:4], (None if window.last else out[4])


def by_levels(coeffs):
    spec = coeffs[0]
    levels, _, parts, waves_local, nlat = spec.shape
    members = lax.axis_size("mem")
    band = lax.axis_index("band").astype(jnp.int32)
    member = lax.axis_index("mem").astype(jnp.int32)
    core = member % 2
    half_of = [choose(core, [member // bits[step] % 2 for bits in ORDER]) for step in range(len(ORDER[0]))]
    half_beside = choose(1 - core, [member // bits[0] % 2 for bits in ORDER])
    place = jnp.stack([band, core, half_of[0], half_beside])
    spec = spec.reshape(levels, 2, parts * waves_local, nlat)
    count = nlat // LANE
    windows = [Window(k, count) for k in range(count)]
    table = jnp.asarray(wave_table(levels, waves_local))
    swap = [(0, 1), (1, 0)]

    (piece,) = pieces_of(spec, 1 - band, windows[:1], count)
    remotes = [lax.ppermute(piece, "band", swap)]
    for k, piece in enumerate(pieces_of(spec, 1 - band, windows[1:], count), 1):
        if k > 1:
            piece = gated(piece, [remotes[k - 2]])
        remotes.append(lax.ppermute(piece, "band", swap))
    local = pieces_of(spec, band, windows, count)

    cores = [(m, m ^ 1) for m in range(members)]
    ways = [[(m, m ^ ORDER[m % 2][step]) for m in range(members)] for step in range(len(ORDER[0]))]

    def halved(parts_of, step):
        half = parts_of[0].shape[1] // 2
        mine = half_of[step]

        def total(which):
            return sum(lax.dynamic_slice_in_dim(part, which * half, half, axis=1) for part in parts_of)

        leaves = total(1 - mine)
        return [total(mine), lax.ppermute(leaves, "mem", ways[step])], leaves

    def across(parts_of, step):
        kept, passed, kept_more, passed_more = parts_of
        leaves = passed + passed_more
        return [kept, kept_more, lax.ppermute(leaves, "mem", ways[step])], leaves

    def advanced(parts_of, step):
        return (across if step == 0 else halved)(parts_of, step)

    def doubled(part, step):
        beside = lax.ppermute(part, "mem", cores if step < 0 else ways[step])
        mine = core if step < 0 else half_of[step]
        return jnp.where(mine == 0, jnp.concatenate([part, beside], axis=1), jnp.concatenate([beside, part], axis=1))

    def gathered(part):
        for step in range(len(ways) - 1, -2, -1):
            part = doubled(part, step)
        return part

    carry = None
    sums, done = [], []
    for k, window in enumerate(windows):
        waits = []
        for j in AHEAD[k]:
            sums[j], left = advanced(sums[j], done[j])
            done[j] += 1
            waits.append(left)
        quarters, carry = window_tensor(window, place, local[k], remotes[k], table, waits, carry)
        first = lax.ppermute(quarters[3], "mem", cores)
        second = lax.ppermute(quarters[2], "mem", cores)
        sums.append([quarters[0], quarters[1], second, first])
        done.append(0)
    pieces = {"own": [], "both": [], "other": []}
    for k, window in enumerate(windows):
        for step in range(done[k], len(ways)):
            if window.side == "other" and step + 1 == len(ways):
                sums[k] = [sums[k][0], gated(sums[k][1], [quarters[0]])]
            sums[k], _ = advanced(sums[k], step)
        pieces[window.side].append(exponent_of(sum(sums[k]), members))

    other = lax.ppermute(jnp.stack(pieces["other"]), "band", swap)
    place_of = {}
    for m in range(members):
        for b in range(2):
            bits = ORDER[m % 2]
            piece = functools.reduce(lambda value, bit: 2 * value + m // bit % 2, bits, m % 2)
            place_of[piece, b] = m * 2 + b
    trades, half = [], members // 2
    for (piece, b), index in place_of.items():
        mate = (piece, b) if (piece < half) == (b == 0) else ((piece + half) % members, 1 - b)
        trades.append((index, place_of[mate]))
    both = lax.ppermute(pieces["both"][0], ("mem", "band"), trades)

    early = gathered(jnp.concatenate([other, both[None]]))
    other, both = early[:-1], early[-1]
    middle = both.shape[0] // 2
    low, high = both[:middle], both[middle:]
    rest = jnp.zeros((nlat // 2 - middle, NLON), jnp.float32)
    down = jnp.stack([jnp.concatenate([rest, low]), jnp.concatenate([*other, high])])
    up = jnp.stack([jnp.concatenate([low, *other[::-1]]), jnp.concatenate([high, rest])])
    out = jnp.where(band == 0, down, up)

    own = gathered(jnp.stack(pieces["own"]))
    for k, block in enumerate(own):
        width = block.shape[0]
        row = choose(band, (nlat // 2 - middle - (k + 1) * width, middle + k * width))
        out = lax.dynamic_update_slice(out, block[None], (band, row.astype(jnp.int32), jnp.int32(0)))
    return out


def per_device(coeffs):
    _, levels, _, _, _, nlat = coeffs.shape
    members = lax.axis_size("mem")
    rows = nlat // lax.axis_size("band")
    fits = coeffs.shape[4] == 5 * LANE // 2 and nlat % (2 * LANE) == LANE and rows > LANE
    if fits and levels == lax.axis_size("band") == 2 and members == 16:
        return by_levels(coeffs)
    return by_rows(coeffs)


def solution(mesh):
    placed = (P("mem", None, None, None, "band", None),)
    return jax.shard_map(
        per_device, mesh=mesh, in_specs=placed, out_specs=P(None, "band", None), check_vma=False
    )
```

```python
import functools
import math

import jax
import jax.numpy as jnp
import ml_dtypes
import numpy as np
from jax import lax
from jax.experimental import pallas as pl
from jax.experimental.pallas import tpu as pltpu
from jax.sharding import PartitionSpec as P

NLON = 1280
STEPS = 1
SUB = 8
LANE = 128
VMEM_LIMIT = 60 * 1024 * 1024
KERNEL_WORK = 8
ORDER = ((2, 4, 8), (4, 2, 8))
AHEAD = ((), (), (0,), (1, 0), (2, 1, 0))


def padded(cells, sides, width):
    for axis, dim in sides:
        count = lax.axis_size(axis)
        ends = count - 1
        head = lax.slice_in_dim(cells, 0, width, axis=dim)
        tail = lax.slice_in_dim(cells, cells.shape[dim] - width, cells.shape[dim], axis=dim)
        cells = jnp.concatenate(
            [
                lax.ppermute(tail, axis, [(i, (i + 1) % count) for i in range(ends)]),
                cells,
                lax.ppermute(head, axis, [((i + 1) % count, i) for i in range(ends)]),
            ],
            axis=dim,
        )
    return cells


def slope(extended, winds):
    center = extended[:, 1:-1]
    north = (extended[:, 2:] - extended[:, :-2]) * 0.5
    east = (jnp.roll(center, -1, 2) - jnp.roll(center, 1, 2)) * 0.5
    return -winds - (winds[0] * east + winds[1] * north)


def rimmed(field):
    return padded(field, (("band", 1),), 1)


def tensor(extended):
    center = extended[:, 1:-1]
    north = (extended[:, 2:] - extended[:, :-2]) * 0.5
    east = (jnp.roll(center, -1, 2) - jnp.roll(center, 1, 2)) * 0.5
    g_xx = 1.0 + east[0]
    g_xy = north[0]
    g_yx = east[1]
    g_yy = 1.0 + north[1]
    return jnp.stack(
        [g_xx * g_xx + g_yx * g_yx, g_xx * g_xy + g_yx * g_yy, g_xy * g_xy + g_yy * g_yy]
    )


def integrate(shift, flow, extend):
    first = slope(extend(shift), flow)
    second = slope(extend(0.5 * first), flow)
    third = slope(extend(0.5 * second), flow)
    fourth = slope(extend(third), flow)
    return (first + 2.0 * second + 2.0 * third + fourth) / 6.0


def exponent_of(summed, members):
    mean = summed / members
    first, cross, second = (mean[..., 0, :, :], mean[..., 1, :, :], mean[..., 2, :, :])
    half = (first + second) * 0.5
    differ = (first - second) * 0.5
    largest = half + jnp.sqrt(differ * differ + cross * cross)
    return jnp.log(largest + 1e-06) / (2.0 * STEPS)


def by_rows(coeffs):
    spec = coeffs[0]
    levels = spec.shape[0]
    nlat = spec.shape[4]
    waves = spec.shape[3] * lax.axis_size("band")
    members = lax.axis_size("mem")
    stacked = spec.reshape(levels * 2, 2, spec.shape[3], nlat)
    wave_index = lax.iota(jnp.int32, waves)
    column = lax.iota(jnp.int32, NLON)
    phase = wave_index[:, None] * column[None, :] % NLON
    angle = phase.astype(jnp.float32) * (2.0 * math.pi / NLON)
    weight = jnp.where(wave_index == 0, 1.0, 2.0).astype(jnp.float32)[:, None]
    table = jnp.stack([weight * jnp.cos(angle), -weight * jnp.sin(angle)], axis=0)
    winds = jnp.einsum(
        "crwh,rwn->chn",
        lax.all_to_all(stacked, "band", split_axis=3, concat_axis=2, tiled=True),
        table,
        precision=lax.Precision.HIGHEST,
        preferred_element_type=jnp.float32,
    )
    height = winds.shape[1]
    winds = winds.reshape(levels, 2, height, NLON)
    partials = []
    for level in range(levels):
        flow = winds[level]
        shift = integrate(jnp.zeros_like(flow), flow, rimmed)
        partials.append(tensor(rimmed(shift)))
    summed = lax.psum_scatter(jnp.stack(partials), "mem", scatter_dimension=3, tiled=True)
    return lax.all_gather(exponent_of(summed, members), "mem", axis=2, tiled=True)


def by_parity(waves_local):
    half = waves_local // 2
    whole = 2 * LANE - half
    runs = []
    for parity in range(2):
        runs += [(parity, half, 2), (waves_local + parity, whole, 2)]
    for parity in range(2):
        runs.append((waves_local + parity + 2 * whole, half - whole, 2))
    return runs


@functools.lru_cache(maxsize=None)
def wave_table(bands, waves_local):
    order = np.concatenate([start + step * np.arange(count) for start, count, step in by_parity(waves_local)])
    wave, part = order % waves_local, order // waves_local
    wave = wave[None, :] + waves_local * np.arange(bands)[:, None]
    part = np.broadcast_to(part, wave.shape)
    cut = [0, 2 * LANE, 4 * LANE, 4 * LANE + LANE // 2, 5 * LANE]
    result = []
    for parity in range(2):
        picks = [(band, slice(cut[parity], cut[parity + 1])) for band in range(bands)]
        picks += [(band, slice(cut[parity + 2], cut[parity + 3])) for band in range(bands)]
        waves = np.concatenate([wave[pick] for pick in picks])
        parts = np.concatenate([part[pick] for pick in picks])
        phase = (waves[:, None] * np.arange(NLON // 2)[None, :]) % NLON
        angle = phase.astype(np.float64) * (2.0 * np.pi / NLON)
        weight = np.where(waves == 0, 1.0, 2.0)[:, None]
        table = weight * np.where(parts[:, None] == 0, np.cos(angle), -np.sin(angle))
        high = table.astype(ml_dtypes.bfloat16)
        result += [high, (table - high.astype(np.float64)).astype(ml_dtypes.bfloat16)]
    return np.stack(result)


class Window:
    def __init__(self, index, count):
        self.first = index == 0
        self.last = index == count - 1
        self.index = index
        self.width = LANE
        self.extended = LANE + 2 * SUB
        self.main = LANE if self.first else LANE - SUB
        self.rim = 0 if self.last else SUB
        self.rows = self.main + self.rim
        up = SUB if self.first else 2 * SUB
        self.place = (self.extended - up - self.rows, up)
        self.side = "other" if 2 * (index + 1) <= count else "own" if 2 * index >= count else "both"


def choose(band, pair):
    return jnp.where(band == 0, pair[0], pair[1])


def multiple(value, of):
    return pl.multiple_of(value.astype(jnp.int32), of)


def pieces_kernel(windows, slots, count, level_ref, spec_ref, *refs):
    out_refs, (taken, turned, in_sems, out_sems) = refs[: len(windows)], refs[len(windows) :]
    level = level_ref[0]
    runs = by_parity(spec_ref.shape[2] // 2)

    def arrival(c, n):
        tile = choose(level, (count - 1 - slots[n], slots[n]))
        lanes = pl.ds(multiple(tile * LANE, LANE), LANE)
        return pltpu.make_async_copy(spec_ref.at[level, c, :, lanes], taken.at[c, n], in_sems.at[c, n])

    def departures(c, k):
        window, n = windows[k], slots.index(windows[k].index)
        rows = pl.ds(multiple(choose(level, (0, LANE - window.main)), SUB), window.main)
        at = pl.ds(multiple(choose(level, (window.rim, 0)), SUB), window.main)
        yield pltpu.make_async_copy(turned.at[c, n, rows], out_refs[k].at[c, at], out_sems.at[k, c, 0])
        if window.rim:
            rows = pl.ds(multiple(choose(level, (LANE - SUB, 0)), SUB), SUB)
            at = pl.ds(multiple(choose(level, (0, window.main)), SUB), SUB)
            yield pltpu.make_async_copy(turned.at[c, n + 1, rows], out_refs[k].at[c, at], out_sems.at[k, c, 1])

    for n in range(len(slots)):
        for c in range(2):
            arrival(c, n).start()
    for n in range(len(slots)):
        for c in range(2):
            arrival(c, n).wait()
            turned[c, n] = jnp.concatenate([taken[c, n, pl.ds(start, rows, step), :] for start, rows, step in runs]).T
        for k, window in enumerate(windows):
            if slots[n] == window.index + (1 if window.rim else 0):
                for c in range(2):
                    for copy in departures(c, k):
                        copy.start()
    for k in range(len(windows)):
        for c in range(2):
            for copy in departures(c, k):
                copy.wait()


def pieces_of(spec, level, windows, count):
    depth = spec.shape[2]
    slots = sorted({w.index for w in windows} | {w.index + 1 for w in windows if w.rim})
    return pl.pallas_call(
        functools.partial(pieces_kernel, windows, slots, count),
        in_specs=[pl.BlockSpec(memory_space=pltpu.SMEM), pl.BlockSpec(memory_space=pl.ANY)],
        out_specs=[pl.BlockSpec(memory_space=pl.ANY)] * len(windows),
        out_shape=[jax.ShapeDtypeStruct((2, w.rows, depth), jnp.float32) for w in windows],
        scratch_shapes=[
            pltpu.VMEM((2, len(slots), depth, LANE), jnp.float32),
            pltpu.VMEM((2, len(slots), LANE, depth), jnp.float32),
            pltpu.SemaphoreType.DMA((2, len(slots))),
            pltpu.SemaphoreType.DMA((len(windows), 2, 2)),
        ],
        compiler_params=pltpu.CompilerParams(vmem_limit_bytes=VMEM_LIMIT),
        cost_estimate=pl.CostEstimate(
            flops=0, transcendentals=0, bytes_accessed=4 * 2 * len(slots) * LANE * depth * 4
        ),
        name="pieces_of",
    )(level.reshape(1), spec)


def gate_kernel(*refs):
    pass


def gated(part, waits):
    return pl.pallas_call(
        gate_kernel,
        in_specs=[pl.BlockSpec(memory_space=pl.ANY)] * (1 + len(waits)),
        out_specs=pl.BlockSpec(memory_space=pl.ANY),
        out_shape=jax.ShapeDtypeStruct(part.shape, part.dtype),
        input_output_aliases={0: 0},
        cost_estimate=pl.CostEstimate(flops=0, transcendentals=0, bytes_accessed=1024),
        name="gated",
    )(part, *waits)


def east_of(x):
    return pltpu.roll(x, NLON - 1, axis=1) - pltpu.roll(x, 1, axis=1)


def north_of(before, here, after):
    row = lax.broadcasted_iota(jnp.int32, here.shape, 0)
    above = jnp.where(row == SUB - 1, pltpu.roll(after, SUB - 1, axis=0), pltpu.roll(here, SUB - 1, axis=0))
    below = jnp.where(row == 0, pltpu.roll(before, 1, axis=0), pltpu.roll(here, 1, axis=0))
    return above - below


def window_kernel(window, waits, *refs):
    refs = list(refs)
    place_ref, local_ref, remote_ref, table_ref = refs[:4]
    refs = refs[4 + waits :]
    carry_ref = None if window.first else refs.pop(0)
    out_refs = [refs.pop(0) for _ in range(4)]
    carried_ref = None if window.last else refs.pop(0)
    table, mine_buf, theirs_buf, lhs_high, lhs_low, wind, second, third, shift, results, carried, in_sems, out_sems = refs
    band, core, sides = place_ref[0], place_ref[1], (place_ref[2], place_ref[3])
    rows, extended = window.rows, window.extended

    def at(pair):
        return multiple(choose(band, pair), SUB)

    inputs = [pltpu.make_async_copy(local_ref, mine_buf, in_sems.at[0])]
    inputs.append(pltpu.make_async_copy(remote_ref, theirs_buf, in_sems.at[1]))
    tables = pltpu.make_async_copy(table_ref, table, in_sems.at[2])
    if not window.first:
        rows_before = wind.at[:, pl.ds(at((extended - 2 * SUB, 0)), 2 * SUB)]
        inputs.append(pltpu.make_async_copy(carry_ref, rows_before, in_sems.at[3]))
    for copy in [*inputs, tables]:
        copy.start()
    for copy in inputs:
        copy.wait()
    lane = lax.broadcasted_iota(jnp.int32, (rows, LANE), 1)
    even, odd = [], []
    for c in range(2):
        mine, theirs = mine_buf[c], theirs_buf[c]
        low, high = jnp.where(band == 0, mine, theirs), jnp.where(band == 0, theirs, mine)
        low_rest, high_rest = low[:, 4 * LANE :], high[:, 4 * LANE :]
        turn = functools.partial(pltpu.roll, shift=LANE // 2, axis=1)
        even_rest = jnp.where(lane < LANE // 2, low_rest, turn(high_rest))
        odd_rest = jnp.where(lane < LANE // 2, turn(low_rest), high_rest)
        even.append(jnp.concatenate([low[:, : 2 * LANE], high[:, : 2 * LANE], even_rest], axis=1))
        odd.append(jnp.concatenate([low[:, 2 * LANE : 4 * LANE], high[:, 2 * LANE : 4 * LANE], odd_rest], axis=1))
    for parity, parts in enumerate((even, odd)):
        lhs = jnp.concatenate(parts)
        lhs_high[parity] = lhs.astype(jnp.bfloat16)
        lhs_low[parity] = (lhs - lhs_high[parity].astype(jnp.float32)).astype(jnp.bfloat16)

    place = at(window.place)
    if window.first or window.last:
        for c in range(2):
            if window.first:
                wind[c, pl.ds(at((extended - SUB, 0)), SUB), :] = jnp.zeros((SUB, NLON), jnp.float32)
            if window.last:
                wind[c, pl.ds(at((0, extended - SUB)), SUB), :] = jnp.zeros((SUB, NLON), jnp.float32)
    tables.wait()

    dot = functools.partial(jnp.dot, preferred_element_type=jnp.float32)
    for start in range(0, NLON // 2, 2 * LANE):
        stop = min(start + 2 * LANE, NLON // 2)
        columns = slice(start, stop)
        sums = []
        for parity in range(2):
            total = dot(lhs_high[parity], table[2 * parity, :, columns])
            total += dot(lhs_low[parity], table[2 * parity, :, columns])
            total += dot(lhs_high[parity], table[2 * parity + 1, :, columns])
            sums.append(total)
        for c in range(2):
            even_sum, odd_sum = (total[c * rows : (c + 1) * rows] for total in sums)
            wind[c, pl.ds(place, rows), start:stop] = even_sum + odd_sum
            wind[c, pl.ds(place, rows), NLON // 2 + start : NLON // 2 + stop] = even_sum - odd_sum

    if not window.last:
        for c in range(2):
            carried[c] = wind[c, pl.ds(at((0, extended - 2 * SUB)), 2 * SUB), :]
        carry_on = pltpu.make_async_copy(carried, carried_ref, out_sems.at[4])
        carry_on.start()

    blocks = extended // SUB

    def rows_of(block):
        return pl.ds(pl.multiple_of(block * SUB, SUB), SUB)

    def derivatives(field, block):
        before, after = jnp.maximum(block - 1, 0), jnp.minimum(block + 1, blocks - 1)
        result = []
        for c in range(2):
            here = field[c, rows_of(block), :]
            result.append((east_of(here), north_of(field[c, rows_of(before), :], here, field[c, rows_of(after), :])))
        return result

    @pl.loop(0, blocks, unroll=9)
    def _(block):
        flow = [wind[c, rows_of(block), :] for c in range(2)]
        for c, (east, north) in enumerate(derivatives(wind, block)):
            second[c, rows_of(block), :] = 0.25 * (flow[0] * east + flow[1] * north) - flow[c]

    @pl.loop(0, blocks, unroll=9)
    def _(block):
        flow = [wind[c, rows_of(block), :] for c in range(2)]
        for c, (east, north) in enumerate(derivatives(second, block)):
            third[c, rows_of(block), :] = -flow[c] - 0.25 * (flow[0] * east + flow[1] * north)

    @pl.loop(0, blocks, unroll=9)
    def _(block):
        flow = [wind[c, rows_of(block), :] for c in range(2)]
        for c, (east, north) in enumerate(derivatives(third, block)):
            fourth = -flow[c] - 0.5 * (flow[0] * east + flow[1] * north)
            both = second[c, rows_of(block), :] + third[c, rows_of(block), :]
            shift[c, rows_of(block), :] = (2.0 * both + (fourth - flow[c])) * (1.0 / 6.0)

    quarter = window.width // 4 // SUB

    def entries(out, base):
        @pl.loop(0, quarter, unroll=4)
        def _(block):
            (e0, n0), (e1, n1) = derivatives(shift, base + block + 1)
            g_xx, g_xy, g_yx, g_yy = 1.0 + 0.5 * e0, 0.5 * n0, 0.5 * e1, 1.0 + 0.5 * n1
            out[0, rows_of(block), :] = g_xx * g_xx + g_yx * g_yx
            out[1, rows_of(block), :] = g_xx * g_xy + g_yx * g_yy
            out[2, rows_of(block), :] = g_xy * g_xy + g_yy * g_yy

    copies = []
    for n, (a, b) in reversed(list(enumerate(QUARTERS))):
        side = sides[a]
        entries(results.at[n], (2 * (core + a - 2 * core * a) + (side + b - 2 * side * b)) * quarter)
        copies.append(pltpu.make_async_copy(results.at[n], out_refs[n], out_sems.at[n]))
        copies[-1].start()
    for copy in copies:
        copy.wait()
    if not window.last:
        carry_on.wait()


QUARTERS = ((0, 0), (0, 1), (1, 0), (1, 1))


def window_tensor(window, place, local, remote, table, waits, carry):
    depth = local.shape[2]
    operands = [place, local, remote, table, *waits]
    if not window.first:
        operands.append(carry)
    in_specs = [pl.BlockSpec(memory_space=pltpu.SMEM)] + [pl.BlockSpec(memory_space=pl.ANY)] * (len(operands) - 1)
    out_shape = [jax.ShapeDtypeStruct((3, window.width // 4, NLON), jnp.float32)] * 4
    if not window.last:
        out_shape.append(jax.ShapeDtypeStruct((2, 2 * SUB, NLON), jnp.float32))
    field = pltpu.VMEM((2, window.extended, NLON), jnp.float32)
    lhs_shape = (2, 2 * window.rows, depth)
    out = pl.pallas_call(
        functools.partial(window_kernel, window, len(waits)),
        out_shape=out_shape,
        in_specs=in_specs,
        out_specs=[pl.BlockSpec(memory_space=pl.ANY)] * len(out_shape),
        scratch_shapes=[
            pltpu.VMEM(table.shape, table.dtype),
            pltpu.VMEM(local.shape, jnp.float32),
            pltpu.VMEM(local.shape, jnp.float32),
            pltpu.VMEM(lhs_shape, jnp.bfloat16),
            pltpu.VMEM(lhs_shape, jnp.bfloat16),
            field,
            field,
            field,
            field,
            pltpu.VMEM((4, 3, window.width // 4, NLON), jnp.float32),
            pltpu.VMEM((2, 2 * SUB, NLON), jnp.float32),
            pltpu.SemaphoreType.DMA((4,)),
            pltpu.SemaphoreType.DMA((5,)),
        ],
        compiler_params=pltpu.CompilerParams(vmem_limit_bytes=VMEM_LIMIT),
        cost_estimate=pl.CostEstimate(
            flops=KERNEL_WORK * 3 * 2 * 2 * window.rows * depth * NLON,
            transcendentals=0,
            bytes_accessed=2 * table.size + 4 * window.rows * depth * 4 + 12 * window.width * NLON,
        ),
        name="window_tensor",
    )(*operands)
    return out[:4], (None if window.last else out[4])


def by_levels(coeffs):
    spec = coeffs[0]
    levels, _, parts, waves_local, nlat = spec.shape
    members = lax.axis_size("mem")
    band = lax.axis_index("band").astype(jnp.int32)
    member = lax.axis_index("mem").astype(jnp.int32)
    core = member % 2
    half_of = [choose(core, [member // bits[step] % 2 for bits in ORDER]) for step in range(len(ORDER[0]))]
    half_beside = choose(1 - core, [member // bits[0] % 2 for bits in ORDER])
    place = jnp.stack([band, core, half_of[0], half_beside])
    spec = spec.reshape(levels, 2, parts * waves_local, nlat)
    count = nlat // LANE
    windows = [Window(k, count) for k in range(count)]
    table = jnp.asarray(wave_table(levels, waves_local))
    swap = [(0, 1), (1, 0)]

    (piece,) = pieces_of(spec, 1 - band, windows[:1], count)
    remotes = [lax.ppermute(piece, "band", swap)]
    for k, piece in enumerate(pieces_of(spec, 1 - band, windows[1:], count), 1):
        if k > 1:
            piece = gated(piece, [remotes[k - 2]])
        remotes.append(lax.ppermute(piece, "band", swap))
    local = pieces_of(spec, band, windows, count)

    cores = [(m, m ^ 1) for m in range(members)]
    ways = [[(m, m ^ ORDER[m % 2][step]) for m in range(members)] for step in range(len(ORDER[0]))]

    def halved(parts_of, step):
        half = parts_of[0].shape[1] // 2
        mine = half_of[step]

        def total(which):
            return sum(lax.dynamic_slice_in_dim(part, which * half, half, axis=1) for part in parts_of)

        leaves = total(1 - mine)
        return [total(mine), lax.ppermute(leaves, "mem", ways[step])], leaves

    def across(parts_of, step):
        kept, passed, kept_more, passed_more = parts_of
        leaves = passed + passed_more
        return [kept, kept_more, lax.ppermute(leaves, "mem", ways[step])], leaves

    def advanced(parts_of, step):
        return (across if step == 0 else halved)(parts_of, step)

    def doubled(part, step):
        beside = lax.ppermute(part, "mem", cores if step < 0 else ways[step])
        mine = core if step < 0 else half_of[step]
        return jnp.where(mine == 0, jnp.concatenate([part, beside], axis=1), jnp.concatenate([beside, part], axis=1))

    def gathered(part):
        for step in range(len(ways) - 1, -2, -1):
            part = doubled(part, step)
        return part

    carry = None
    sums, done = [], []
    for k, window in enumerate(windows):
        waits = []
        for j in AHEAD[k]:
            sums[j], left = advanced(sums[j], done[j])
            done[j] += 1
            waits.append(left)
        quarters, carry = window_tensor(window, place, local[k], remotes[k], table, waits, carry)
        first = lax.ppermute(quarters[3], "mem", cores)
        second = lax.ppermute(quarters[2], "mem", cores)
        sums.append([quarters[0], quarters[1], second, first])
        done.append(0)
    pieces = {"own": [], "both": [], "other": []}
    for k, window in enumerate(windows):
        for step in range(done[k], len(ways)):
            sums[k], _ = advanced(sums[k], step)
        pieces[window.side].append(exponent_of(sum(sums[k]), members))

    other = lax.ppermute(jnp.stack(pieces["other"]), "band", swap)
    place_of = {}
    for m in range(members):
        for b in range(2):
            bits = ORDER[m % 2]
            piece = functools.reduce(lambda value, bit: 2 * value + m // bit % 2, bits, m % 2)
            place_of[piece, b] = m * 2 + b
    trades, half = [], members // 2
    for (piece, b), index in place_of.items():
        mate = (piece, b) if (piece < half) == (b == 0) else ((piece + half) % members, 1 - b)
        trades.append((index, place_of[mate]))
    both = lax.ppermute(pieces["both"][0], ("mem", "band"), trades)

    early = gathered(jnp.concatenate([other, both[None]]))
    other, both = early[:-1], early[-1]
    middle = both.shape[0] // 2
    low, high = both[:middle], both[middle:]
    rest = jnp.zeros((nlat // 2 - middle, NLON), jnp.float32)
    down = jnp.stack([jnp.concatenate([rest, low]), jnp.concatenate([*other, high])])
    up = jnp.stack([jnp.concatenate([low, *other[::-1]]), jnp.concatenate([high, rest])])
    out = jnp.where(band == 0, down, up)

    own = jnp.stack(pieces["own"])
    for step in range(len(ways) - 1, -2, -1):
        own = doubled(gated(own, [out]) if step < 0 else own, step)
    for k, block in enumerate(own):
        width = block.shape[0]
        row = choose(band, (nlat // 2 - middle - (k + 1) * width, middle + k * width))
        out = lax.dynamic_update_slice(out, block[None], (band, row.astype(jnp.int32), jnp.int32(0)))
    return out


def per_device(coeffs):
    _, levels, _, _, _, nlat = coeffs.shape
    members = lax.axis_size("mem")
    rows = nlat // lax.axis_size("band")
    fits = coeffs.shape[4] == 5 * LANE // 2 and nlat % (2 * LANE) == LANE and rows > LANE
    if fits and levels == lax.axis_size("band") == 2 and members == 16:
        return by_levels(coeffs)
    return by_rows(coeffs)


def solution(mesh):
    placed = (P("mem", None, None, None, "band", None),)
    return jax.shard_map(
        per_device, mesh=mesh, in_specs=placed, out_specs=P(None, "band", None), check_vma=False
    )
```

```python
import functools
import math

import jax
import jax.numpy as jnp
import ml_dtypes
import numpy as np
from jax import lax
from jax.experimental import pallas as pl
from jax.experimental.pallas import tpu as pltpu
from jax.sharding import PartitionSpec as P

NLON = 1280
STEPS = 1
SUB = 8
LANE = 128
VMEM_LIMIT = 60 * 1024 * 1024
KERNEL_WORK = 8
ORDER = ((2, 4, 8), (4, 2, 8))
AHEAD = ((), (), (0,), (1, 0), (2, 1, 0))


def padded(cells, sides, width):
    for axis, dim in sides:
        count = lax.axis_size(axis)
        ends = count - 1
        head = lax.slice_in_dim(cells, 0, width, axis=dim)
        tail = lax.slice_in_dim(cells, cells.shape[dim] - width, cells.shape[dim], axis=dim)
        cells = jnp.concatenate(
            [
                lax.ppermute(tail, axis, [(i, (i + 1) % count) for i in range(ends)]),
                cells,
                lax.ppermute(head, axis, [((i + 1) % count, i) for i in range(ends)]),
            ],
            axis=dim,
        )
    return cells


def slope(extended, winds):
    center = extended[:, 1:-1]
    north = (extended[:, 2:] - extended[:, :-2]) * 0.5
    east = (jnp.roll(center, -1, 2) - jnp.roll(center, 1, 2)) * 0.5
    return -winds - (winds[0] * east + winds[1] * north)


def rimmed(field):
    return padded(field, (("band", 1),), 1)


def tensor(extended):
    center = extended[:, 1:-1]
    north = (extended[:, 2:] - extended[:, :-2]) * 0.5
    east = (jnp.roll(center, -1, 2) - jnp.roll(center, 1, 2)) * 0.5
    g_xx = 1.0 + east[0]
    g_xy = north[0]
    g_yx = east[1]
    g_yy = 1.0 + north[1]
    return jnp.stack(
        [g_xx * g_xx + g_yx * g_yx, g_xx * g_xy + g_yx * g_yy, g_xy * g_xy + g_yy * g_yy]
    )


def integrate(shift, flow, extend):
    first = slope(extend(shift), flow)
    second = slope(extend(0.5 * first), flow)
    third = slope(extend(0.5 * second), flow)
    fourth = slope(extend(third), flow)
    return (first + 2.0 * second + 2.0 * third + fourth) / 6.0


def exponent_of(summed, members):
    mean = summed / members
    first, cross, second = (mean[..., 0, :, :], mean[..., 1, :, :], mean[..., 2, :, :])
    half = (first + second) * 0.5
    differ = (first - second) * 0.5
    largest = half + jnp.sqrt(differ * differ + cross * cross)
    return jnp.log(largest + 1e-06) / (2.0 * STEPS)


def by_rows(coeffs):
    spec = coeffs[0]
    levels = spec.shape[0]
    nlat = spec.shape[4]
    waves = spec.shape[3] * lax.axis_size("band")
    members = lax.axis_size("mem")
    stacked = spec.reshape(levels * 2, 2, spec.shape[3], nlat)
    wave_index = lax.iota(jnp.int32, waves)
    column = lax.iota(jnp.int32, NLON)
    phase = wave_index[:, None] * column[None, :] % NLON
    angle = phase.astype(jnp.float32) * (2.0 * math.pi / NLON)
    weight = jnp.where(wave_index == 0, 1.0, 2.0).astype(jnp.float32)[:, None]
    table = jnp.stack([weight * jnp.cos(angle), -weight * jnp.sin(angle)], axis=0)
    winds = jnp.einsum(
        "crwh,rwn->chn",
        lax.all_to_all(stacked, "band", split_axis=3, concat_axis=2, tiled=True),
        table,
        precision=lax.Precision.HIGHEST,
        preferred_element_type=jnp.float32,
    )
    height = winds.shape[1]
    winds = winds.reshape(levels, 2, height, NLON)
    partials = []
    for level in range(levels):
        flow = winds[level]
        shift = integrate(jnp.zeros_like(flow), flow, rimmed)
        partials.append(tensor(rimmed(shift)))
    summed = lax.psum_scatter(jnp.stack(partials), "mem", scatter_dimension=3, tiled=True)
    return lax.all_gather(exponent_of(summed, members), "mem", axis=2, tiled=True)


def by_parity(waves_local):
    half = waves_local // 2
    whole = 2 * LANE - half
    runs = []
    for parity in range(2):
        runs += [(parity, half, 2), (waves_local + parity, whole, 2)]
    for parity in range(2):
        runs.append((waves_local + parity + 2 * whole, half - whole, 2))
    return runs


@functools.lru_cache(maxsize=None)
def wave_table(bands, waves_local):
    order = np.concatenate([start + step * np.arange(count) for start, count, step in by_parity(waves_local)])
    wave, part = order % waves_local, order // waves_local
    wave = wave[None, :] + waves_local * np.arange(bands)[:, None]
    part = np.broadcast_to(part, wave.shape)
    cut = [0, 2 * LANE, 4 * LANE, 4 * LANE + LANE // 2, 5 * LANE]
    result = []
    for parity in range(2):
        picks = [(band, slice(cut[parity], cut[parity + 1])) for band in range(bands)]
        picks += [(band, slice(cut[parity + 2], cut[parity + 3])) for band in range(bands)]
        waves = np.concatenate([wave[pick] for pick in picks])
        parts = np.concatenate([part[pick] for pick in picks])
        phase = (waves[:, None] * np.arange(NLON // 2)[None, :]) % NLON
        angle = phase.astype(np.float64) * (2.0 * np.pi / NLON)
        weight = np.where(waves == 0, 1.0, 2.0)[:, None]
        table = weight * np.where(parts[:, None] == 0, np.cos(angle), -np.sin(angle))
        high = table.astype(ml_dtypes.bfloat16)
        result += [high, (table - high.astype(np.float64)).astype(ml_dtypes.bfloat16)]
    return np.stack(result)


class Window:
    def __init__(self, index, count):
        self.first = index == 0
        self.last = index == count - 1
        self.index = index
        self.width = LANE
        self.extended = LANE + 2 * SUB
        self.main = LANE if self.first else LANE - SUB
        self.rim = 0 if self.last else SUB
        self.rows = self.main + self.rim
        up = SUB if self.first else 2 * SUB
        self.place = (self.extended - up - self.rows, up)
        self.side = "other" if 2 * (index + 1) <= count else "own" if 2 * index >= count else "both"


def choose(band, pair):
    return jnp.where(band == 0, pair[0], pair[1])


def multiple(value, of):
    return pl.multiple_of(value.astype(jnp.int32), of)


def pieces_kernel(windows, slots, count, level_ref, spec_ref, *refs):
    out_refs, (taken, turned, in_sems, out_sems) = refs[: len(windows)], refs[len(windows) :]
    level = level_ref[0]
    runs = by_parity(spec_ref.shape[2] // 2)

    def arrival(c, n):
        tile = choose(level, (count - 1 - slots[n], slots[n]))
        lanes = pl.ds(multiple(tile * LANE, LANE), LANE)
        return pltpu.make_async_copy(spec_ref.at[level, c, :, lanes], taken.at[c, n], in_sems.at[c, n])

    def departures(c, k):
        window, n = windows[k], slots.index(windows[k].index)
        rows = pl.ds(multiple(choose(level, (0, LANE - window.main)), SUB), window.main)
        at = pl.ds(multiple(choose(level, (window.rim, 0)), SUB), window.main)
        yield pltpu.make_async_copy(turned.at[c, n, rows], out_refs[k].at[c, at], out_sems.at[k, c, 0])
        if window.rim:
            rows = pl.ds(multiple(choose(level, (LANE - SUB, 0)), SUB), SUB)
            at = pl.ds(multiple(choose(level, (0, window.main)), SUB), SUB)
            yield pltpu.make_async_copy(turned.at[c, n + 1, rows], out_refs[k].at[c, at], out_sems.at[k, c, 1])

    for n in range(len(slots)):
        for c in range(2):
            arrival(c, n).start()
    for n in range(len(slots)):
        for c in range(2):
            arrival(c, n).wait()
            turned[c, n] = jnp.concatenate([taken[c, n, pl.ds(start, rows, step), :] for start, rows, step in runs]).T
        for k, window in enumerate(windows):
            if slots[n] == window.index + (1 if window.rim else 0):
                for c in range(2):
                    for copy in departures(c, k):
                        copy.start()
    for k in range(len(windows)):
        for c in range(2):
            for copy in departures(c, k):
                copy.wait()


def pieces_of(spec, level, windows, count):
    depth = spec.shape[2]
    slots = sorted({w.index for w in windows} | {w.index + 1 for w in windows if w.rim})
    return pl.pallas_call(
        functools.partial(pieces_kernel, windows, slots, count),
        in_specs=[pl.BlockSpec(memory_space=pltpu.SMEM), pl.BlockSpec(memory_space=pl.ANY)],
        out_specs=[pl.BlockSpec(memory_space=pl.ANY)] * len(windows),
        out_shape=[jax.ShapeDtypeStruct((2, w.rows, depth), jnp.float32) for w in windows],
        scratch_shapes=[
            pltpu.VMEM((2, len(slots), depth, LANE), jnp.float32),
            pltpu.VMEM((2, len(slots), LANE, depth), jnp.float32),
            pltpu.SemaphoreType.DMA((2, len(slots))),
            pltpu.SemaphoreType.DMA((len(windows), 2, 2)),
        ],
        compiler_params=pltpu.CompilerParams(vmem_limit_bytes=VMEM_LIMIT),
        cost_estimate=pl.CostEstimate(
            flops=0, transcendentals=0, bytes_accessed=4 * 2 * len(slots) * LANE * depth * 4
        ),
        name="pieces_of",
    )(level.reshape(1), spec)


def gate_kernel(*refs):
    pass


def gated(part, waits):
    return pl.pallas_call(
        gate_kernel,
        in_specs=[pl.BlockSpec(memory_space=pl.ANY)] * (1 + len(waits)),
        out_specs=pl.BlockSpec(memory_space=pl.ANY),
        out_shape=jax.ShapeDtypeStruct(part.shape, part.dtype),
        input_output_aliases={0: 0},
        cost_estimate=pl.CostEstimate(flops=0, transcendentals=0, bytes_accessed=1024),
        name="gated",
    )(part, *waits)


def east_of(x):
    return pltpu.roll(x, NLON - 1, axis=1) - pltpu.roll(x, 1, axis=1)


def north_of(before, here, after):
    row = lax.broadcasted_iota(jnp.int32, here.shape, 0)
    above = jnp.where(row == SUB - 1, pltpu.roll(after, SUB - 1, axis=0), pltpu.roll(here, SUB - 1, axis=0))
    below = jnp.where(row == 0, pltpu.roll(before, 1, axis=0), pltpu.roll(here, 1, axis=0))
    return above - below


def window_kernel(window, waits, *refs):
    refs = list(refs)
    place_ref, local_ref, remote_ref, table_ref = refs[:4]
    refs = refs[4 + waits :]
    carry_ref = None if window.first else refs.pop(0)
    out_refs = [refs.pop(0) for _ in range(4)]
    carried_ref = None if window.last else refs.pop(0)
    table, mine_buf, theirs_buf, lhs_high, lhs_low, wind, second, third, shift, results, carried, in_sems, out_sems = refs
    band, core, sides = place_ref[0], place_ref[1], (place_ref[2], place_ref[3])
    rows, extended = window.rows, window.extended

    def at(pair):
        return multiple(choose(band, pair), SUB)

    inputs = [pltpu.make_async_copy(local_ref, mine_buf, in_sems.at[0])]
    inputs.append(pltpu.make_async_copy(remote_ref, theirs_buf, in_sems.at[1]))
    tables = pltpu.make_async_copy(table_ref, table, in_sems.at[2])
    if not window.first:
        rows_before = wind.at[:, pl.ds(at((extended - 2 * SUB, 0)), 2 * SUB)]
        inputs.append(pltpu.make_async_copy(carry_ref, rows_before, in_sems.at[3]))
    for copy in [*inputs, tables]:
        copy.start()
    for copy in inputs:
        copy.wait()
    lane = lax.broadcasted_iota(jnp.int32, (rows, LANE), 1)
    even, odd = [], []
    for c in range(2):
        mine, theirs = mine_buf[c], theirs_buf[c]
        low, high = jnp.where(band == 0, mine, theirs), jnp.where(band == 0, theirs, mine)
        low_rest, high_rest = low[:, 4 * LANE :], high[:, 4 * LANE :]
        turn = functools.partial(pltpu.roll, shift=LANE // 2, axis=1)
        even_rest = jnp.where(lane < LANE // 2, low_rest, turn(high_rest))
        odd_rest = jnp.where(lane < LANE // 2, turn(low_rest), high_rest)
        even.append(jnp.concatenate([low[:, : 2 * LANE], high[:, : 2 * LANE], even_rest], axis=1))
        odd.append(jnp.concatenate([low[:, 2 * LANE : 4 * LANE], high[:, 2 * LANE : 4 * LANE], odd_rest], axis=1))
    for parity, parts in enumerate((even, odd)):
        lhs = jnp.concatenate(parts)
        lhs_high[parity] = lhs.astype(jnp.bfloat16)
        lhs_low[parity] = (lhs - lhs_high[parity].astype(jnp.float32)).astype(jnp.bfloat16)

    place = at(window.place)
    if window.first or window.last:
        for c in range(2):
            if window.first:
                wind[c, pl.ds(at((extended - SUB, 0)), SUB), :] = jnp.zeros((SUB, NLON), jnp.float32)
            if window.last:
                wind[c, pl.ds(at((0, extended - SUB)), SUB), :] = jnp.zeros((SUB, NLON), jnp.float32)
    tables.wait()

    dot = functools.partial(jnp.dot, preferred_element_type=jnp.float32)
    for start in range(0, NLON // 2, 2 * LANE):
        stop = min(start + 2 * LANE, NLON // 2)
        columns = slice(start, stop)
        sums = []
        for parity in range(2):
            total = dot(lhs_high[parity], table[2 * parity, :, columns])
            total += dot(lhs_low[parity], table[2 * parity, :, columns])
            total += dot(lhs_high[parity], table[2 * parity + 1, :, columns])
            sums.append(total)
        for c in range(2):
            even_sum, odd_sum = (total[c * rows : (c + 1) * rows] for total in sums)
            wind[c, pl.ds(place, rows), start:stop] = even_sum + odd_sum
            wind[c, pl.ds(place, rows), NLON // 2 + start : NLON // 2 + stop] = even_sum - odd_sum

    if not window.last:
        for c in range(2):
            carried[c] = wind[c, pl.ds(at((0, extended - 2 * SUB)), 2 * SUB), :]
        carry_on = pltpu.make_async_copy(carried, carried_ref, out_sems.at[4])
        carry_on.start()

    blocks = extended // SUB

    def rows_of(block):
        return pl.ds(pl.multiple_of(block * SUB, SUB), SUB)

    def derivatives(field, block):
        before, after = jnp.maximum(block - 1, 0), jnp.minimum(block + 1, blocks - 1)
        result = []
        for c in range(2):
            here = field[c, rows_of(block), :]
            result.append((east_of(here), north_of(field[c, rows_of(before), :], here, field[c, rows_of(after), :])))
        return result

    @pl.loop(0, blocks, unroll=9)
    def _(block):
        flow = [wind[c, rows_of(block), :] for c in range(2)]
        for c, (east, north) in enumerate(derivatives(wind, block)):
            second[c, rows_of(block), :] = 0.25 * (flow[0] * east + flow[1] * north) - flow[c]

    @pl.loop(0, blocks, unroll=9)
    def _(block):
        flow = [wind[c, rows_of(block), :] for c in range(2)]
        for c, (east, north) in enumerate(derivatives(second, block)):
            third[c, rows_of(block), :] = -flow[c] - 0.25 * (flow[0] * east + flow[1] * north)

    @pl.loop(0, blocks, unroll=9)
    def _(block):
        flow = [wind[c, rows_of(block), :] for c in range(2)]
        for c, (east, north) in enumerate(derivatives(third, block)):
            fourth = -flow[c] - 0.5 * (flow[0] * east + flow[1] * north)
            both = second[c, rows_of(block), :] + third[c, rows_of(block), :]
            shift[c, rows_of(block), :] = (2.0 * both + (fourth - flow[c])) * (1.0 / 6.0)

    quarter = window.width // 4 // SUB

    def entries(out, base):
        @pl.loop(0, quarter, unroll=4)
        def _(block):
            (e0, n0), (e1, n1) = derivatives(shift, base + block + 1)
            g_xx, g_xy, g_yx, g_yy = 1.0 + 0.5 * e0, 0.5 * n0, 0.5 * e1, 1.0 + 0.5 * n1
            out[0, rows_of(block), :] = g_xx * g_xx + g_yx * g_yx
            out[1, rows_of(block), :] = g_xx * g_xy + g_yx * g_yy
            out[2, rows_of(block), :] = g_xy * g_xy + g_yy * g_yy

    copies = []
    for n, (a, b) in reversed(list(enumerate(QUARTERS))):
        side = sides[a]
        entries(results.at[n], (2 * (core + a - 2 * core * a) + (side + b - 2 * side * b)) * quarter)
        copies.append(pltpu.make_async_copy(results.at[n], out_refs[n], out_sems.at[n]))
        copies[-1].start()
    for copy in copies:
        copy.wait()
    if not window.last:
        carry_on.wait()


QUARTERS = ((0, 0), (0, 1), (1, 0), (1, 1))


def window_tensor(window, place, local, remote, table, waits, carry):
    depth = local.shape[2]
    operands = [place, local, remote, table, *waits]
    if not window.first:
        operands.append(carry)
    in_specs = [pl.BlockSpec(memory_space=pltpu.SMEM)] + [pl.BlockSpec(memory_space=pl.ANY)] * (len(operands) - 1)
    out_shape = [jax.ShapeDtypeStruct((3, window.width // 4, NLON), jnp.float32)] * 4
    if not window.last:
        out_shape.append(jax.ShapeDtypeStruct((2, 2 * SUB, NLON), jnp.float32))
    field = pltpu.VMEM((2, window.extended, NLON), jnp.float32)
    lhs_shape = (2, 2 * window.rows, depth)
    out = pl.pallas_call(
        functools.partial(window_kernel, window, len(waits)),
        out_shape=out_shape,
        in_specs=in_specs,
        out_specs=[pl.BlockSpec(memory_space=pl.ANY)] * len(out_shape),
        scratch_shapes=[
            pltpu.VMEM(table.shape, table.dtype),
            pltpu.VMEM(local.shape, jnp.float32),
            pltpu.VMEM(local.shape, jnp.float32),
            pltpu.VMEM(lhs_shape, jnp.bfloat16),
            pltpu.VMEM(lhs_shape, jnp.bfloat16),
            field,
            field,
            field,
            field,
            pltpu.VMEM((4, 3, window.width // 4, NLON), jnp.float32),
            pltpu.VMEM((2, 2 * SUB, NLON), jnp.float32),
            pltpu.SemaphoreType.DMA((4,)),
            pltpu.SemaphoreType.DMA((5,)),
        ],
        compiler_params=pltpu.CompilerParams(vmem_limit_bytes=VMEM_LIMIT),
        cost_estimate=pl.CostEstimate(
            flops=KERNEL_WORK * 3 * 2 * 2 * window.rows * depth * NLON,
            transcendentals=0,
            bytes_accessed=2 * table.size + 4 * window.rows * depth * 4 + 12 * window.width * NLON,
        ),
        name="window_tensor",
    )(*operands)
    return out[:4], (None if window.last else out[4])


def by_levels(coeffs):
    spec = coeffs[0]
    levels, _, parts, waves_local, nlat = spec.shape
    members = lax.axis_size("mem")
    band = lax.axis_index("band").astype(jnp.int32)
    member = lax.axis_index("mem").astype(jnp.int32)
    core = member % 2
    half_of = [choose(core, [member // bits[step] % 2 for bits in ORDER]) for step in range(len(ORDER[0]))]
    half_beside = choose(1 - core, [member // bits[0] % 2 for bits in ORDER])
    place = jnp.stack([band, core, half_of[0], half_beside])
    spec = spec.reshape(levels, 2, parts * waves_local, nlat)
    count = nlat // LANE
    windows = [Window(k, count) for k in range(count)]
    table = jnp.asarray(wave_table(levels, waves_local))
    swap = [(0, 1), (1, 0)]

    (piece,) = pieces_of(spec, 1 - band, windows[:1], count)
    remotes = [lax.ppermute(piece, "band", swap)]
    for k, piece in enumerate(pieces_of(spec, 1 - band, windows[1:], count), 1):
        if k > 1:
            piece = gated(piece, [remotes[k - 2]])
        remotes.append(lax.ppermute(piece, "band", swap))
    local = pieces_of(spec, band, windows, count)

    cores = [(m, m ^ 1) for m in range(members)]
    ways = [[(m, m ^ ORDER[m % 2][step]) for m in range(members)] for step in range(len(ORDER[0]))]

    def halved(parts_of, step):
        half = parts_of[0].shape[1] // 2
        mine = half_of[step]

        def total(which):
            return sum(lax.dynamic_slice_in_dim(part, which * half, half, axis=1) for part in parts_of)

        leaves = total(1 - mine)
        return [total(mine), lax.ppermute(leaves, "mem", ways[step])], leaves

    def across(parts_of, step):
        kept, passed, kept_more, passed_more = parts_of
        leaves = passed + passed_more
        return [kept, kept_more, lax.ppermute(leaves, "mem", ways[step])], leaves

    def advanced(parts_of, step):
        return (across if step == 0 else halved)(parts_of, step)

    def doubled(part, step):
        beside = lax.ppermute(part, "mem", cores if step < 0 else ways[step])
        mine = core if step < 0 else half_of[step]
        return jnp.where(mine == 0, jnp.concatenate([part, beside], axis=1), jnp.concatenate([beside, part], axis=1))

    def gathered(part):
        for step in range(len(ways) - 1, -2, -1):
            part = doubled(part, step)
        return part

    carry = None
    sums, done = [], []
    for k, window in enumerate(windows):
        waits = []
        for j in AHEAD[k]:
            sums[j], left = advanced(sums[j], done[j])
            done[j] += 1
            waits.append(left)
        quarters, carry = window_tensor(window, place, local[k], remotes[k], table, waits, carry)
        first = lax.ppermute(quarters[3], "mem", cores)
        second = lax.ppermute(quarters[2], "mem", cores)
        sums.append([quarters[0], quarters[1], second, first])
        done.append(0)
    pieces = {"own": [], "both": [], "other": []}
    for k, window in enumerate(windows):
        for step in range(done[k], len(ways)):
            sums[k], _ = advanced(sums[k], step)
        pieces[window.side].append(exponent_of(sum(sums[k]), members))

    other = lax.ppermute(jnp.stack(pieces["other"]), "band", swap)
    place_of = {}
    for m in range(members):
        for b in range(2):
            bits = ORDER[m % 2]
            piece = functools.reduce(lambda value, bit: 2 * value + m // bit % 2, bits, m % 2)
            place_of[piece, b] = m * 2 + b
    trades, half = [], members // 2
    for (piece, b), index in place_of.items():
        mate = (piece, b) if (piece < half) == (b == 0) else ((piece + half) % members, 1 - b)
        trades.append((index, place_of[mate]))
    both = lax.ppermute(pieces["both"][0], ("mem", "band"), trades)

    far = gathered(other)
    near = gathered(jnp.concatenate([both[None], jnp.stack(pieces["own"])]))
    middle = near.shape[1] // 2
    rest = jnp.zeros((nlat // 2, NLON), jnp.float32)
    down = jnp.stack([rest, jnp.concatenate([*far, rest[:middle]])])
    up = jnp.stack([jnp.concatenate([rest[:middle], *far[::-1]]), rest])
    out = jnp.where(band == 0, down, up)

    def put(block, level, pair):
        return lax.dynamic_update_slice(out, block[None], (level, choose(band, pair).astype(jnp.int32), jnp.int32(0)))

    edge = nlat // 2 - middle
    out = put(near[0, :middle], 0, (edge, 0))
    out = put(near[0, middle:], 1, (edge, 0))
    for k, block in enumerate(near[1:]):
        out = put(block, band, (edge - (k + 1) * LANE, middle + k * LANE))
    return out


def per_device(coeffs):
    _, levels, _, _, _, nlat = coeffs.shape
    members = lax.axis_size("mem")
    rows = nlat // lax.axis_size("band")
    fits = coeffs.shape[4] == 5 * LANE // 2 and nlat % (2 * LANE) == LANE and rows > LANE
    if fits and levels == lax.axis_size("band") == 2 and members == 16:
        return by_levels(coeffs)
    return by_rows(coeffs)


def solution(mesh):
    placed = (P("mem", None, None, None, "band", None),)
    return jax.shard_map(
        per_device, mesh=mesh, in_specs=placed, out_specs=P(None, "band", None), check_vma=False
    )
```

```python
import functools
import math

import jax
import jax.numpy as jnp
import ml_dtypes
import numpy as np
from jax import lax
from jax.experimental import pallas as pl
from jax.experimental.pallas import tpu as pltpu
from jax.sharding import PartitionSpec as P

NLON = 1280
STEPS = 1
SUB = 8
LANE = 128
VMEM_LIMIT = 60 * 1024 * 1024
KERNEL_WORK = 8
ORDER = ((2, 4, 8), (4, 2, 8))
AHEAD = ((), (), (0,), (1, 0), (2, 1, 0))


def padded(cells, sides, width):
    for axis, dim in sides:
        count = lax.axis_size(axis)
        ends = count - 1
        head = lax.slice_in_dim(cells, 0, width, axis=dim)
        tail = lax.slice_in_dim(cells, cells.shape[dim] - width, cells.shape[dim], axis=dim)
        cells = jnp.concatenate(
            [
                lax.ppermute(tail, axis, [(i, (i + 1) % count) for i in range(ends)]),
                cells,
                lax.ppermute(head, axis, [((i + 1) % count, i) for i in range(ends)]),
            ],
            axis=dim,
        )
    return cells


def slope(extended, winds):
    center = extended[:, 1:-1]
    north = (extended[:, 2:] - extended[:, :-2]) * 0.5
    east = (jnp.roll(center, -1, 2) - jnp.roll(center, 1, 2)) * 0.5
    return -winds - (winds[0] * east + winds[1] * north)


def rimmed(field):
    return padded(field, (("band", 1),), 1)


def tensor(extended):
    center = extended[:, 1:-1]
    north = (extended[:, 2:] - extended[:, :-2]) * 0.5
    east = (jnp.roll(center, -1, 2) - jnp.roll(center, 1, 2)) * 0.5
    g_xx = 1.0 + east[0]
    g_xy = north[0]
    g_yx = east[1]
    g_yy = 1.0 + north[1]
    return jnp.stack(
        [g_xx * g_xx + g_yx * g_yx, g_xx * g_xy + g_yx * g_yy, g_xy * g_xy + g_yy * g_yy]
    )


def integrate(shift, flow, extend):
    first = slope(extend(shift), flow)
    second = slope(extend(0.5 * first), flow)
    third = slope(extend(0.5 * second), flow)
    fourth = slope(extend(third), flow)
    return (first + 2.0 * second + 2.0 * third + fourth) / 6.0


def exponent_of(summed, members):
    mean = summed / members
    first, cross, second = (mean[..., 0, :, :], mean[..., 1, :, :], mean[..., 2, :, :])
    half = (first + second) * 0.5
    differ = (first - second) * 0.5
    largest = half + jnp.sqrt(differ * differ + cross * cross)
    return jnp.log(largest + 1e-06) / (2.0 * STEPS)


def by_rows(coeffs):
    spec = coeffs[0]
    levels = spec.shape[0]
    nlat = spec.shape[4]
    waves = spec.shape[3] * lax.axis_size("band")
    members = lax.axis_size("mem")
    stacked = spec.reshape(levels * 2, 2, spec.shape[3], nlat)
    wave_index = lax.iota(jnp.int32, waves)
    column = lax.iota(jnp.int32, NLON)
    phase = wave_index[:, None] * column[None, :] % NLON
    angle = phase.astype(jnp.float32) * (2.0 * math.pi / NLON)
    weight = jnp.where(wave_index == 0, 1.0, 2.0).astype(jnp.float32)[:, None]
    table = jnp.stack([weight * jnp.cos(angle), -weight * jnp.sin(angle)], axis=0)
    winds = jnp.einsum(
        "crwh,rwn->chn",
        lax.all_to_all(stacked, "band", split_axis=3, concat_axis=2, tiled=True),
        table,
        precision=lax.Precision.HIGHEST,
        preferred_element_type=jnp.float32,
    )
    height = winds.shape[1]
    winds = winds.reshape(levels, 2, height, NLON)
    partials = []
    for level in range(levels):
        flow = winds[level]
        shift = integrate(jnp.zeros_like(flow), flow, rimmed)
        partials.append(tensor(rimmed(shift)))
    summed = lax.psum_scatter(jnp.stack(partials), "mem", scatter_dimension=3, tiled=True)
    return lax.all_gather(exponent_of(summed, members), "mem", axis=2, tiled=True)


def by_parity(waves_local):
    half = waves_local // 2
    whole = 2 * LANE - half
    runs = []
    for parity in range(2):
        runs += [(parity, half, 2), (waves_local + parity, whole, 2)]
    for parity in range(2):
        runs.append((waves_local + parity + 2 * whole, half - whole, 2))
    return runs


@functools.lru_cache(maxsize=None)
def wave_table(bands, waves_local):
    order = np.concatenate([start + step * np.arange(count) for start, count, step in by_parity(waves_local)])
    wave, part = order % waves_local, order // waves_local
    wave = wave[None, :] + waves_local * np.arange(bands)[:, None]
    part = np.broadcast_to(part, wave.shape)
    cut = [0, 2 * LANE, 4 * LANE, 4 * LANE + LANE // 2, 5 * LANE]
    result = []
    for parity in range(2):
        picks = [(band, slice(cut[parity], cut[parity + 1])) for band in range(bands)]
        picks += [(band, slice(cut[parity + 2], cut[parity + 3])) for band in range(bands)]
        waves = np.concatenate([wave[pick] for pick in picks])
        parts = np.concatenate([part[pick] for pick in picks])
        phase = (waves[:, None] * np.arange(NLON // 2)[None, :]) % NLON
        angle = phase.astype(np.float64) * (2.0 * np.pi / NLON)
        weight = np.where(waves == 0, 1.0, 2.0)[:, None]
        table = weight * np.where(parts[:, None] == 0, np.cos(angle), -np.sin(angle))
        high = table.astype(ml_dtypes.bfloat16)
        result += [high, (table - high.astype(np.float64)).astype(ml_dtypes.bfloat16)]
    return np.stack(result)


class Window:
    def __init__(self, index, count):
        self.first = index == 0
        self.last = index == count - 1
        self.index = index
        self.width = LANE
        self.extended = LANE + 2 * SUB
        self.main = LANE if self.first else LANE - SUB
        self.rim = 0 if self.last else SUB
        self.rows = self.main + self.rim
        up = SUB if self.first else 2 * SUB
        self.place = (self.extended - up - self.rows, up)
        self.side = "other" if 2 * (index + 1) <= count else "own" if 2 * index >= count else "both"


def choose(band, pair):
    return jnp.where(band == 0, pair[0], pair[1])


def multiple(value, of):
    return pl.multiple_of(value.astype(jnp.int32), of)


def pieces_kernel(windows, slots, count, level_ref, spec_ref, *refs):
    out_refs, (taken, turned, in_sems, out_sems) = refs[: len(windows)], refs[len(windows) :]
    level = level_ref[0]
    runs = by_parity(spec_ref.shape[2] // 2)

    def arrival(c, n):
        tile = choose(level, (count - 1 - slots[n], slots[n]))
        lanes = pl.ds(multiple(tile * LANE, LANE), LANE)
        return pltpu.make_async_copy(spec_ref.at[level, c, :, lanes], taken.at[c, n], in_sems.at[c, n])

    def departures(c, k):
        window, n = windows[k], slots.index(windows[k].index)
        rows = pl.ds(multiple(choose(level, (0, LANE - window.main)), SUB), window.main)
        at = pl.ds(multiple(choose(level, (window.rim, 0)), SUB), window.main)
        yield pltpu.make_async_copy(turned.at[c, n, rows], out_refs[k].at[c, at], out_sems.at[k, c, 0])
        if window.rim:
            rows = pl.ds(multiple(choose(level, (LANE - SUB, 0)), SUB), SUB)
            at = pl.ds(multiple(choose(level, (0, window.main)), SUB), SUB)
            yield pltpu.make_async_copy(turned.at[c, n + 1, rows], out_refs[k].at[c, at], out_sems.at[k, c, 1])

    for n in range(len(slots)):
        for c in range(2):
            arrival(c, n).start()
    for n in range(len(slots)):
        for c in range(2):
            arrival(c, n).wait()
            turned[c, n] = jnp.concatenate([taken[c, n, pl.ds(start, rows, step), :] for start, rows, step in runs]).T
        for k, window in enumerate(windows):
            if slots[n] == window.index + (1 if window.rim else 0):
                for c in range(2):
                    for copy in departures(c, k):
                        copy.start()
    for k in range(len(windows)):
        for c in range(2):
            for copy in departures(c, k):
                copy.wait()


def pieces_of(spec, level, windows, count):
    depth = spec.shape[2]
    slots = sorted({w.index for w in windows} | {w.index + 1 for w in windows if w.rim})
    return pl.pallas_call(
        functools.partial(pieces_kernel, windows, slots, count),
        in_specs=[pl.BlockSpec(memory_space=pltpu.SMEM), pl.BlockSpec(memory_space=pl.ANY)],
        out_specs=[pl.BlockSpec(memory_space=pl.ANY)] * len(windows),
        out_shape=[jax.ShapeDtypeStruct((2, w.rows, depth), jnp.float32) for w in windows],
        scratch_shapes=[
            pltpu.VMEM((2, len(slots), depth, LANE), jnp.float32),
            pltpu.VMEM((2, len(slots), LANE, depth), jnp.float32),
            pltpu.SemaphoreType.DMA((2, len(slots))),
            pltpu.SemaphoreType.DMA((len(windows), 2, 2)),
        ],
        compiler_params=pltpu.CompilerParams(vmem_limit_bytes=VMEM_LIMIT),
        cost_estimate=pl.CostEstimate(
            flops=0, transcendentals=0, bytes_accessed=4 * 2 * len(slots) * LANE * depth * 4
        ),
        name="pieces_of",
    )(level.reshape(1), spec)


def gate_kernel(*refs):
    pass


def gated(part, waits):
    return pl.pallas_call(
        gate_kernel,
        in_specs=[pl.BlockSpec(memory_space=pl.ANY)] * (1 + len(waits)),
        out_specs=pl.BlockSpec(memory_space=pl.ANY),
        out_shape=jax.ShapeDtypeStruct(part.shape, part.dtype),
        input_output_aliases={0: 0},
        cost_estimate=pl.CostEstimate(flops=0, transcendentals=0, bytes_accessed=1024),
        name="gated",
    )(part, *waits)


def east_of(x):
    return pltpu.roll(x, NLON - 1, axis=1) - pltpu.roll(x, 1, axis=1)


def north_of(before, here, after):
    row = lax.broadcasted_iota(jnp.int32, here.shape, 0)
    above = jnp.where(row == SUB - 1, pltpu.roll(after, SUB - 1, axis=0), pltpu.roll(here, SUB - 1, axis=0))
    below = jnp.where(row == 0, pltpu.roll(before, 1, axis=0), pltpu.roll(here, 1, axis=0))
    return above - below


def window_kernel(window, waits, *refs):
    refs = list(refs)
    place_ref, local_ref, remote_ref, table_ref = refs[:4]
    refs = refs[4 + waits :]
    carry_ref = None if window.first else refs.pop(0)
    out_refs = [refs.pop(0) for _ in range(4)]
    carried_ref = None if window.last else refs.pop(0)
    table, mine_buf, theirs_buf, lhs_high, lhs_low, wind, second, third, shift, results, carried, in_sems, out_sems = refs
    band, core, sides = place_ref[0], place_ref[1], (place_ref[2], place_ref[3])
    rows, extended = window.rows, window.extended

    def at(pair):
        return multiple(choose(band, pair), SUB)

    inputs = [pltpu.make_async_copy(local_ref, mine_buf, in_sems.at[0])]
    inputs.append(pltpu.make_async_copy(remote_ref, theirs_buf, in_sems.at[1]))
    tables = pltpu.make_async_copy(table_ref, table, in_sems.at[2])
    if not window.first:
        rows_before = wind.at[:, pl.ds(at((extended - 2 * SUB, 0)), 2 * SUB)]
        inputs.append(pltpu.make_async_copy(carry_ref, rows_before, in_sems.at[3]))
    for copy in [*inputs, tables]:
        copy.start()
    for copy in inputs:
        copy.wait()
    lane = lax.broadcasted_iota(jnp.int32, (rows, LANE), 1)
    even, odd = [], []
    for c in range(2):
        mine, theirs = mine_buf[c], theirs_buf[c]
        low, high = jnp.where(band == 0, mine, theirs), jnp.where(band == 0, theirs, mine)
        low_rest, high_rest = low[:, 4 * LANE :], high[:, 4 * LANE :]
        turn = functools.partial(pltpu.roll, shift=LANE // 2, axis=1)
        even_rest = jnp.where(lane < LANE // 2, low_rest, turn(high_rest))
        odd_rest = jnp.where(lane < LANE // 2, turn(low_rest), high_rest)
        even.append(jnp.concatenate([low[:, : 2 * LANE], high[:, : 2 * LANE], even_rest], axis=1))
        odd.append(jnp.concatenate([low[:, 2 * LANE : 4 * LANE], high[:, 2 * LANE : 4 * LANE], odd_rest], axis=1))
    for parity, parts in enumerate((even, odd)):
        lhs = jnp.concatenate(parts)
        lhs_high[parity] = lhs.astype(jnp.bfloat16)
        lhs_low[parity] = (lhs - lhs_high[parity].astype(jnp.float32)).astype(jnp.bfloat16)

    place = at(window.place)
    if window.first or window.last:
        for c in range(2):
            if window.first:
                wind[c, pl.ds(at((extended - SUB, 0)), SUB), :] = jnp.zeros((SUB, NLON), jnp.float32)
            if window.last:
                wind[c, pl.ds(at((0, extended - SUB)), SUB), :] = jnp.zeros((SUB, NLON), jnp.float32)
    tables.wait()

    dot = functools.partial(jnp.dot, preferred_element_type=jnp.float32)
    for start in range(0, NLON // 2, 2 * LANE):
        stop = min(start + 2 * LANE, NLON // 2)
        columns = slice(start, stop)
        sums = []
        for parity in range(2):
            terms = jnp.concatenate([lhs_high[parity], lhs_low[parity]])
            both = dot(terms, table[2 * parity, :, columns])
            total = both[: 2 * rows] + both[2 * rows :]
            total += dot(lhs_high[parity], table[2 * parity + 1, :, columns])
            sums.append(total)
        for c in range(2):
            even_sum, odd_sum = (total[c * rows : (c + 1) * rows] for total in sums)
            wind[c, pl.ds(place, rows), start:stop] = even_sum + odd_sum
            wind[c, pl.ds(place, rows), NLON // 2 + start : NLON // 2 + stop] = even_sum - odd_sum

    if not window.last:
        for c in range(2):
            carried[c] = wind[c, pl.ds(at((0, extended - 2 * SUB)), 2 * SUB), :]
        carry_on = pltpu.make_async_copy(carried, carried_ref, out_sems.at[4])
        carry_on.start()

    blocks = extended // SUB

    def rows_of(block):
        return pl.ds(pl.multiple_of(block * SUB, SUB), SUB)

    def derivatives(field, block):
        before, after = jnp.maximum(block - 1, 0), jnp.minimum(block + 1, blocks - 1)
        result = []
        for c in range(2):
            here = field[c, rows_of(block), :]
            result.append((east_of(here), north_of(field[c, rows_of(before), :], here, field[c, rows_of(after), :])))
        return result

    @pl.loop(0, blocks, unroll=9)
    def _(block):
        flow = [wind[c, rows_of(block), :] for c in range(2)]
        for c, (east, north) in enumerate(derivatives(wind, block)):
            second[c, rows_of(block), :] = 0.25 * (flow[0] * east + flow[1] * north) - flow[c]

    @pl.loop(0, blocks, unroll=9)
    def _(block):
        flow = [wind[c, rows_of(block), :] for c in range(2)]
        for c, (east, north) in enumerate(derivatives(second, block)):
            third[c, rows_of(block), :] = -flow[c] - 0.25 * (flow[0] * east + flow[1] * north)

    @pl.loop(0, blocks, unroll=9)
    def _(block):
        flow = [wind[c, rows_of(block), :] for c in range(2)]
        for c, (east, north) in enumerate(derivatives(third, block)):
            fourth = -flow[c] - 0.5 * (flow[0] * east + flow[1] * north)
            both = second[c, rows_of(block), :] + third[c, rows_of(block), :]
            shift[c, rows_of(block), :] = (2.0 * both + (fourth - flow[c])) * (1.0 / 6.0)

    quarter = window.width // 4 // SUB

    def entries(out, base):
        @pl.loop(0, quarter, unroll=4)
        def _(block):
            (e0, n0), (e1, n1) = derivatives(shift, base + block + 1)
            g_xx, g_xy, g_yx, g_yy = 1.0 + 0.5 * e0, 0.5 * n0, 0.5 * e1, 1.0 + 0.5 * n1
            out[0, rows_of(block), :] = g_xx * g_xx + g_yx * g_yx
            out[1, rows_of(block), :] = g_xx * g_xy + g_yx * g_yy
            out[2, rows_of(block), :] = g_xy * g_xy + g_yy * g_yy

    copies = []
    for n, (a, b) in reversed(list(enumerate(QUARTERS))):
        side = sides[a]
        entries(results.at[n], (2 * (core + a - 2 * core * a) + (side + b - 2 * side * b)) * quarter)
        copies.append(pltpu.make_async_copy(results.at[n], out_refs[n], out_sems.at[n]))
        copies[-1].start()
    for copy in copies:
        copy.wait()
    if not window.last:
        carry_on.wait()


QUARTERS = ((0, 0), (0, 1), (1, 0), (1, 1))


def window_tensor(window, place, local, remote, table, waits, carry):
    depth = local.shape[2]
    operands = [place, local, remote, table, *waits]
    if not window.first:
        operands.append(carry)
    in_specs = [pl.BlockSpec(memory_space=pltpu.SMEM)] + [pl.BlockSpec(memory_space=pl.ANY)] * (len(operands) - 1)
    out_shape = [jax.ShapeDtypeStruct((3, window.width // 4, NLON), jnp.float32)] * 4
    if not window.last:
        out_shape.append(jax.ShapeDtypeStruct((2, 2 * SUB, NLON), jnp.float32))
    field = pltpu.VMEM((2, window.extended, NLON), jnp.float32)
    lhs_shape = (2, 2 * window.rows, depth)
    out = pl.pallas_call(
        functools.partial(window_kernel, window, len(waits)),
        out_shape=out_shape,
        in_specs=in_specs,
        out_specs=[pl.BlockSpec(memory_space=pl.ANY)] * len(out_shape),
        scratch_shapes=[
            pltpu.VMEM(table.shape, table.dtype),
            pltpu.VMEM(local.shape, jnp.float32),
            pltpu.VMEM(local.shape, jnp.float32),
            pltpu.VMEM(lhs_shape, jnp.bfloat16),
            pltpu.VMEM(lhs_shape, jnp.bfloat16),
            field,
            field,
            field,
            field,
            pltpu.VMEM((4, 3, window.width // 4, NLON), jnp.float32),
            pltpu.VMEM((2, 2 * SUB, NLON), jnp.float32),
            pltpu.SemaphoreType.DMA((4,)),
            pltpu.SemaphoreType.DMA((5,)),
        ],
        compiler_params=pltpu.CompilerParams(vmem_limit_bytes=VMEM_LIMIT),
        cost_estimate=pl.CostEstimate(
            flops=KERNEL_WORK * 3 * 2 * 2 * window.rows * depth * NLON,
            transcendentals=0,
            bytes_accessed=2 * table.size + 4 * window.rows * depth * 4 + 12 * window.width * NLON,
        ),
        name="window_tensor",
    )(*operands)
    return out[:4], (None if window.last else out[4])


def by_levels(coeffs):
    spec = coeffs[0]
    levels, _, parts, waves_local, nlat = spec.shape
    members = lax.axis_size("mem")
    band = lax.axis_index("band").astype(jnp.int32)
    member = lax.axis_index("mem").astype(jnp.int32)
    core = member % 2
    half_of = [choose(core, [member // bits[step] % 2 for bits in ORDER]) for step in range(len(ORDER[0]))]
    half_beside = choose(1 - core, [member // bits[0] % 2 for bits in ORDER])
    place = jnp.stack([band, core, half_of[0], half_beside])
    spec = spec.reshape(levels, 2, parts * waves_local, nlat)
    count = nlat // LANE
    windows = [Window(k, count) for k in range(count)]
    table = jnp.asarray(wave_table(levels, waves_local))
    swap = [(0, 1), (1, 0)]

    (piece,) = pieces_of(spec, 1 - band, windows[:1], count)
    remotes = [lax.ppermute(piece, "band", swap)]
    for k, piece in enumerate(pieces_of(spec, 1 - band, windows[1:], count), 1):
        if k > 1:
            piece = gated(piece, [remotes[k - 2]])
        remotes.append(lax.ppermute(piece, "band", swap))
    local = pieces_of(spec, band, windows, count)

    cores = [(m, m ^ 1) for m in range(members)]
    ways = [[(m, m ^ ORDER[m % 2][step]) for m in range(members)] for step in range(len(ORDER[0]))]

    def halved(parts_of, step):
        half = parts_of[0].shape[1] // 2
        mine = half_of[step]

        def total(which):
            return sum(lax.dynamic_slice_in_dim(part, which * half, half, axis=1) for part in parts_of)

        leaves = total(1 - mine)
        return [total(mine), lax.ppermute(leaves, "mem", ways[step])], leaves

    def across(parts_of, step):
        kept, passed, kept_more, passed_more = parts_of
        leaves = passed + passed_more
        return [kept, kept_more, lax.ppermute(leaves, "mem", ways[step])], leaves

    def advanced(parts_of, step):
        return (across if step == 0 else halved)(parts_of, step)

    def doubled(part, step):
        beside = lax.ppermute(part, "mem", cores if step < 0 else ways[step])
        mine = core if step < 0 else half_of[step]
        return jnp.where(mine == 0, jnp.concatenate([part, beside], axis=1), jnp.concatenate([beside, part], axis=1))

    def gathered(part):
        for step in range(len(ways) - 1, -2, -1):
            part = doubled(part, step)
        return part

    carry = None
    sums, done = [], []
    for k, window in enumerate(windows):
        waits = []
        for j in AHEAD[k]:
            sums[j], left = advanced(sums[j], done[j])
            done[j] += 1
            waits.append(left)
        quarters, carry = window_tensor(window, place, local[k], remotes[k], table, waits, carry)
        first = lax.ppermute(quarters[3], "mem", cores)
        second = lax.ppermute(quarters[2], "mem", cores)
        sums.append([quarters[0], quarters[1], second, first])
        done.append(0)
    pieces = {"own": [], "both": [], "other": []}
    for k, window in enumerate(windows):
        for step in range(done[k], len(ways)):
            sums[k], _ = advanced(sums[k], step)
        pieces[window.side].append(exponent_of(sum(sums[k]), members))

    other = lax.ppermute(jnp.stack(pieces["other"]), "band", swap)
    place_of = {}
    for m in range(members):
        for b in range(2):
            bits = ORDER[m % 2]
            piece = functools.reduce(lambda value, bit: 2 * value + m // bit % 2, bits, m % 2)
            place_of[piece, b] = m * 2 + b
    trades, half = [], members // 2
    for (piece, b), index in place_of.items():
        mate = (piece, b) if (piece < half) == (b == 0) else ((piece + half) % members, 1 - b)
        trades.append((index, place_of[mate]))
    both = lax.ppermute(pieces["both"][0], ("mem", "band"), trades)

    early = gathered(jnp.concatenate([other, both[None]]))
    other, both = early[:-1], early[-1]
    middle = both.shape[0] // 2
    low, high = both[:middle], both[middle:]
    rest = jnp.zeros((nlat // 2 - middle, NLON), jnp.float32)
    down = jnp.stack([jnp.concatenate([rest, low]), jnp.concatenate([*other, high])])
    up = jnp.stack([jnp.concatenate([low, *other[::-1]]), jnp.concatenate([high, rest])])
    out = jnp.where(band == 0, down, up)

    own = gathered(jnp.stack(pieces["own"]))
    for k, block in enumerate(own):
        width = block.shape[0]
        row = choose(band, (nlat // 2 - middle - (k + 1) * width, middle + k * width))
        out = lax.dynamic_update_slice(out, block[None], (band, row.astype(jnp.int32), jnp.int32(0)))
    return out


def per_device(coeffs):
    _, levels, _, _, _, nlat = coeffs.shape
    members = lax.axis_size("mem")
    rows = nlat // lax.axis_size("band")
    fits = coeffs.shape[4] == 5 * LANE // 2 and nlat % (2 * LANE) == LANE and rows > LANE
    if fits and levels == lax.axis_size("band") == 2 and members == 16:
        return by_levels(coeffs)
    return by_rows(coeffs)


def solution(mesh):
    placed = (P("mem", None, None, None, "band", None),)
    return jax.shard_map(
        per_device, mesh=mesh, in_specs=placed, out_specs=P(None, "band", None), check_vma=False
    )
```
